32 devices in a mesh: ctx: 16 (over z, y, core), head: 2 (over x).
Axes of the slice: x: 2, y: 2, z: 4, core: 2. Of those that a mesh axis runs over, the one named last changes fastest.
Arguments:
- queries: bfloat16 [64, 16384], P('ctx', 'head'), may hold values from -7 to 7
- grad_out: bfloat16 [64, 16384], P('ctx', 'head'), may hold values from -384 to 384
- outputs: bfloat16 [64, 16384], P('ctx', 'head'), may hold values from -6 to 6
- lse_self: float32 [64, 128], P('ctx', 'head'), may hold values from 0 to 20
- prompt_keys: bfloat16 [4096, 1024], P(('ctx', 'head')), may hold values from -11 to 11
- prompt_values: bfloat16 [4096, 1024], P(('ctx', 'head')), may hold values from -6 to 6
- resp_len: int32 [1], replicated, may hold values from 16 to 64, as said below
- prompt_end: int32 [1], replicated, may hold values from 2048 to 4096, as said below
Outputs:
- query_grad: bfloat16 [64, 16384], P('ctx', 'head')
- prompt_key_grad: bfloat16 [4096, 1024], P(('ctx', 'head'))
- prompt_value_grad: bfloat16 [4096, 1024], P(('ctx', 'head'))
The draws below stay inside these ranges and needn't reach their ends.
Inputs may be any that keep to these rules, and one draw needn't show every extreme that they name: `resp_len`: at least one response has all 64 rows live. `prompt_end`: at least one response sees the whole prompt.
All inputs are finite; a program needn't handle non-finite values.
Results may differ from the reference program's by a relative error of at most 0.013.
Values may be sent and summed in bfloat16 or wider, within the bound.
No kernel may reach another device: no remote copies, remote signals or barrier semaphores. Data moves between devices by JAX's collectives and lax.ppermute only.
A program may use at most 64 MiB of HBM per device.

```python
import math
import jax
import jax.numpy as jnp
from jax import lax

QH = 128
KVH = 8
DH = 128
RESP_LEN = 64
PROMPT = 4096
ROWS = 64
NRESP = 1


def draw_queries(key, part):
    key = jax.random.fold_in(key, 5)
    key_base, key_rows = jax.random.split(key)
    base = jax.random.truncated_normal(key_base, -4.0, 4.0, (ROWS, QH * DH), jnp.float32)
    row_scale = jnp.exp(jax.random.uniform(key_rows, (ROWS, 1), jnp.float32, -0.5, 0.5))
    values = base * row_scale
    return values.astype(jnp.bfloat16)


def draw_prompt_keys(key, part):
    key = jax.random.fold_in(key, 7)
    key_base, key_rows = jax.random.split(key)
    position = jnp.arange(PROMPT, dtype=jnp.float32)[:, None] / PROMPT
    rough = jnp.exp(jax.random.uniform(key_rows, (PROMPT, 1), jnp.float32, -0.6, 0.6))
    base = jax.random.truncated_normal(key_base, -4.0, 4.0, (PROMPT, KVH * DH), jnp.float32)
    values = base * (0.5 + position) * rough
    return values.astype(jnp.bfloat16)


def draw_lse_self(key, part):
    key = jax.random.fold_in(key, 9)
    offset = jax.random.uniform(key, (ROWS, QH), jnp.float32, -1.0, 2.5)
    return (math.log(PROMPT) + offset).astype(jnp.float32)


def draw_resp_len(key, part):
    key = jax.random.fold_in(key, 13)
    key_vals, key_full = jax.random.split(key)
    values = jax.random.randint(key_vals, (NRESP,), RESP_LEN // 4, RESP_LEN + 1, jnp.int32)
    chosen = jax.random.randint(key_full, (), 0, NRESP, jnp.int32)
    return jnp.where(jnp.arange(NRESP, dtype=jnp.int32) == chosen, RESP_LEN, values).astype(jnp.int32)


def draw_prompt_end(key, part):
    key = jax.random.fold_in(key, 17)
    key_vals, key_full = jax.random.split(key)
    values = jax.random.randint(key_vals, (NRESP,), PROMPT // 2, PROMPT + 1, jnp.int32)
    chosen = jax.random.randint(key_full, (), 0, NRESP, jnp.int32)
    return jnp.where(jnp.arange(NRESP, dtype=jnp.int32) == chosen, PROMPT, values).astype(jnp.int32)


def levels(own_key, extent, pieces, smallest, largest):
    factor_of = 1.0
    for dim, blocks in pieces:
        heights = jax.random.uniform(jax.random.fold_in(jax.random.fold_in(own_key, 6), dim), (blocks,), jnp.float32, smallest / len(pieces), largest / len(pieces))
        factor_of = factor_of * jnp.repeat(jnp.exp(heights), extent[dim] // blocks).reshape((-1,) + (1,) * (len(extent) - 1 - dim))
    return factor_of


def gaussian(stream_key, dims, width, limit, cuts=(), kind=jnp.bfloat16):
    values = jax.random.normal(stream_key, dims, jnp.float32) * width
    if len(cuts) > 0:
        values = levels(stream_key, dims, cuts, -0.22, 0.18) * values
    return jnp.clip(values, min=-limit, max=limit).astype(kind)


def setup_inputs(seed: int = 0) -> dict:
    key_list = jax.random.split(jax.random.key(seed), 9)
    return {
        "queries": draw_queries(jax.random.fold_in(key_list[8], 71), 0),
        "grad_out": gaussian(key_list[1], (ROWS, QH * DH), 64.0, 384.0, ((0, 16), (1, 2))),
        "outputs": gaussian(key_list[2], (ROWS, QH * DH), 1.0, 6.0, ((0, 16), (1, 2))),
        "lse_self": draw_lse_self(jax.random.fold_in(key_list[8], 71), 0),
        "prompt_keys": draw_prompt_keys(jax.random.fold_in(key_list[8], 71), 0),
        "prompt_values": gaussian(key_list[5], (PROMPT, KVH * DH), 1.0, 6.0, ((0, 32),)),
        "resp_len": draw_resp_len(jax.random.fold_in(key_list[8], 71), 0),
        "prompt_end": draw_prompt_end(jax.random.fold_in(key_list[8], 71), 0),
    }


MASKED_SCORE = -1.0e30


def head_terms(query_head, grad_head, output_head, self_lse, key_group, value_group, visible, live_rows):
    score_scale = DH ** -0.5
    scores = jnp.dot(query_head, key_group.T, preferred_element_type=jnp.float32) * score_scale
    scores = jnp.where(visible, scores, MASKED_SCORE)
    row_peak = jnp.max(scores, axis=1)
    prompt_lse = row_peak + jnp.log(jnp.sum(jnp.where(visible, jnp.exp(scores - row_peak[:, None]), 0.0), axis=1))
    higher = jnp.maximum(prompt_lse, self_lse)
    full_lse = higher + jnp.log(jnp.exp(prompt_lse - higher) + jnp.exp(self_lse - higher))
    prob = jnp.where(visible, jnp.exp(scores - full_lse[:, None]), 0.0) * live_rows[:, None]
    row_dots = jnp.sum(grad_head.astype(jnp.float32) * output_head.astype(jnp.float32), axis=1)
    dprob = jnp.dot(grad_head, value_group.T, preferred_element_type=jnp.float32)
    dscore = (prob * (dprob - row_dots[:, None])).astype(jnp.bfloat16)
    value_grad = jnp.dot(prob.astype(jnp.bfloat16).T, grad_head, preferred_element_type=jnp.float32)
    key_grad = jnp.dot(dscore.T, query_head, preferred_element_type=jnp.float32) * score_scale
    query_grad = jnp.dot(dscore, key_group, preferred_element_type=jnp.float32) * score_scale
    return query_grad, key_grad, value_grad


def reference(queries, grad_out, outputs, lse_self, prompt_keys, prompt_values, resp_len, prompt_end):
    row_count = queries.shape[0]
    prompt_len = prompt_keys.shape[0]
    per_group = QH // KVH
    row_ids = jnp.arange(row_count, dtype=jnp.int32)
    resp_index = row_ids // RESP_LEN
    live_rows = ((row_ids % RESP_LEN) < resp_len[resp_index]).astype(jnp.float32)
    visible = jnp.arange(prompt_len, dtype=jnp.int32)[None, :] < prompt_end[resp_index][:, None]

    def group_step(unused, group_index):
        key_group = lax.dynamic_slice_in_dim(prompt_keys, group_index * DH, DH, 1)
        value_group = lax.dynamic_slice_in_dim(prompt_values, group_index * DH, DH, 1)

        def head_step(totals, head_index):
            head_number = group_index * per_group + head_index
            query_head = lax.dynamic_slice_in_dim(queries, head_number * DH, DH, 1)
            grad_head = lax.dynamic_slice_in_dim(grad_out, head_number * DH, DH, 1)
            output_head = lax.dynamic_slice_in_dim(outputs, head_number * DH, DH, 1)
            self_lse = lax.dynamic_index_in_dim(lse_self, head_number, 1, keepdims=False)
            query_grad, key_grad, value_grad = head_terms(query_head, grad_head, output_head, self_lse, key_group, value_group, visible, live_rows)
            return (totals[0] + key_grad, totals[1] + value_grad), query_grad

        zero_sums = (jnp.zeros((prompt_len, DH), jnp.float32), jnp.zeros((prompt_len, DH), jnp.float32))
        (key_sum, value_sum), query_grads = lax.scan(head_step, zero_sums, jnp.arange(per_group, dtype=jnp.int32))
        return unused, (query_grads, key_sum, value_sum)

    _, (query_grads, key_sums, value_sums) = lax.scan(group_step, jnp.zeros((), jnp.float32), jnp.arange(KVH, dtype=jnp.int32))
    query_grad = jnp.transpose(query_grads, (2, 0, 1, 3)).reshape(row_count, QH * DH).astype(jnp.bfloat16)
    key_grad = jnp.transpose(key_sums, (1, 0, 2)).reshape(prompt_len, KVH * DH).astype(jnp.bfloat16)
    value_grad = jnp.transpose(value_sums, (1, 0, 2)).reshape(prompt_len, KVH * DH).astype(jnp.bfloat16)
    return (query_grad, key_grad, value_grad)
```

```python
import functools

import jax
import jax.numpy as jnp
from jax import lax
from jax.experimental import pallas as pl
from jax.experimental.pallas import tpu as pltpu
from jax.sharding import Mesh, PartitionSpec as P

DH = 128
KVH = 8
RESP_LEN = 64
SCALE = DH ** (-0.5)
MASKED_SCORE = -1e30
DEAD_LSE = 1e30
PIECES = 3
STAT_ROWS = 16
PARAMS = pltpu.CompilerParams(vmem_limit_bytes=48 * 1024 * 1024)
ANY = pl.BlockSpec(memory_space=pl.ANY)
SMEM = pl.BlockSpec(memory_space=pltpu.SMEM)
VMEM = pl.BlockSpec(memory_space=pltpu.VMEM)


def split_pieces(x):
    first = x.astype(jnp.bfloat16)
    rest = x - first.astype(jnp.float32)
    second = rest.astype(jnp.bfloat16)
    third = (rest - second.astype(jnp.float32)).astype(jnp.bfloat16)
    return first, second, third


def group_of(member, groups, heads):
    return member % heads * groups + member // heads


def pack_kv_kernel(groups, heads, scalars, k_ref, v_ref, *rest):
    out_refs, sems = rest[:-1], rest[-1]
    tokens = k_ref.shape[0]
    copies = []
    for j in range(KVH):
        column = pl.multiple_of(group_of(scalars[0] ^ j, groups, heads) * DH, DH)
        for n, ref in enumerate((k_ref, v_ref)):
            copies.append(
                pltpu.make_async_copy(
                    ref.at[:, pl.ds(column, DH)],
                    out_refs[j].at[pl.ds(n * tokens, tokens), :],
                    sems.at[2 * j + n],
                )
            )
    for copy in copies:
        copy.start()
    for copy in copies:
        copy.wait()


def pack_rows_kernel(parts, groups, q_hbm, o_grad_hbm, o_hbm, lse_hbm, rows_ref, q_ref, o_grad_ref, o_ref, lse_ref, sems):
    copies = [
        pltpu.make_async_copy(source, target, sems.at[n])
        for n, (source, target) in enumerate(
            ((lse_hbm, lse_ref), (q_hbm, q_ref), (o_grad_hbm, o_grad_ref), (o_hbm, o_ref))
        )
    ]
    for copy in copies:
        copy.start()
    group_lines = q_ref.shape[0] // groups
    rows = lse_ref.shape[0]
    group_heads = group_lines // rows
    head_ids = lax.broadcasted_iota(jnp.int32, (lse_ref.shape[1], 2 * group_lines), 0)
    line_ids = lax.broadcasted_iota(jnp.int32, (lse_ref.shape[1], 2 * group_lines), 1) % group_lines
    row_ids = lax.broadcasted_iota(jnp.int32, (rows, 2 * group_lines), 0)
    row_of_line = lax.broadcasted_iota(jnp.int32, (rows, 2 * group_lines), 1) % rows
    for copy in copies:
        copy.wait()
    lse_pieces = [piece.astype(jnp.float32) for piece in split_pieces(lse_ref[...])]
    for g in range(groups):
        lines = pl.ds(g * group_lines, group_lines)
        q = q_ref[lines, :]
        o_grad = o_grad_ref[lines, :]
        product = o_grad.astype(jnp.float32) * o_ref[lines, :].astype(jnp.float32)
        dots = jnp.sum(jnp.concatenate([product, product], axis=0).T, axis=0, keepdims=True)
        chosen = (head_ids == g * group_heads + line_ids // rows).astype(jnp.float32)
        stats = []
        for piece in lse_pieces:
            spread = jnp.dot(piece, chosen, preferred_element_type=jnp.float32)
            stats.append(
                jnp.sum(jnp.where(row_ids == row_of_line, spread, 0.0), axis=0, keepdims=True)
            )
        stats += [piece.astype(jnp.float32) for piece in split_pieces(dots)]
        stats.append(jnp.zeros((STAT_ROWS - 2 * PIECES, 2 * group_lines), jnp.float32))
        stat_block = jnp.concatenate(stats, axis=0).astype(jnp.bfloat16)
        for part in range(parts):
            rows_ref[part * groups + g, 0:group_lines, :] = q
            rows_ref[part * groups + g, group_lines : 2 * group_lines, :] = o_grad
            rows_ref[part * groups + g, 2 * group_lines :, :] = stat_block


def line_limits(first_line, count, lines, rows, resp_len, prompt_end):
    line = first_line + lax.broadcasted_iota(jnp.int32, (1, count), 1)
    row = line // lines * rows + line % rows
    resp = row // RESP_LEN
    end = jnp.zeros_like(line)
    length = jnp.zeros_like(line)
    for r in range(resp_len.shape[0]):
        end = jnp.where(resp == r, prompt_end[r], end)
        length = jnp.where(resp == r, resp_len[r], length)
    return end, row % RESP_LEN < length


def line_values(rows_ref, first_source, count, lines, first_piece):
    low = lax.broadcasted_iota(jnp.int32, (1, 2 * lines), 1) < lines
    out = []
    for s in range(first_source, first_source + count, 2):
        total = None
        for k in range(first_piece, first_piece + PIECES):
            even = rows_ref[s, 2 * lines : 2 * lines + STAT_ROWS, :].astype(jnp.float32)[k : k + 1]
            odd = rows_ref[s + 1, 2 * lines : 2 * lines + STAT_ROWS, :].astype(jnp.float32)[k : k + 1]
            piece = jnp.where(low, even, odd)
            total = piece if total is None else total + piece
        out.append(total)
    return jnp.concatenate(out, axis=1)


def stat_kernel(rows, tokens, scalars, resp_len, prompt_end, rows_ref, *rest):
    kv_refs, lse_ref = rest[:-1], rest[-1]
    sources, lines = rows_ref.shape[0], (rows_ref.shape[1] - STAT_ROWS) // 2
    step = 256 // lines
    for c in range(sources // step):
        q = rows_ref[c * step : (c + 1) * step, 0:lines, :].reshape(step * lines, DH)
        end, _ = line_limits(c * step * lines, step * lines, lines, rows, resp_len, prompt_end)
        scores = []
        for j, ref in enumerate(kv_refs):
            part = lax.dot_general(
                ref[0:tokens, :], q, (((1,), (1,)), ((), ())), preferred_element_type=jnp.float32
            )
            offset = lax.broadcasted_iota(jnp.int32, part.shape, 0)
            visible = offset < end - scalars[1 + j]
            scores.append(jnp.where(visible, part * SCALE, MASKED_SCORE))
        scores = jnp.concatenate(scores, axis=0)
        peak = jnp.max(scores, axis=0, keepdims=True)
        total = jnp.sum(jnp.exp(scores - peak), axis=0, keepdims=True)
        lse = peak + jnp.log(total)
        for n in range(step * lines // DH):
            lse_ref[c * (step * lines // DH) + n, :] = lse[0, n * DH : (n + 1) * DH]


def grad_kernel(parts, rows, tokens, scalars, resp_len, prompt_end, rows_ref, *rest):
    kv_refs, lse_refs = rest[:KVH], rest[KVH : KVH + parts]
    dq_ref, dkv_refs = rest[KVH + parts], rest[KVH + parts + 1 : KVH + parts + 1 + KVH]
    dk_acc, dv_acc = rest[-2:]
    sources, lines = rows_ref.shape[0], (rows_ref.shape[1] - STAT_ROWS) // 2
    step = min(sources, 1024 // lines)
    count = step * lines
    pair = 2
    for c in range(sources // step):
        q = rows_ref[c * step : (c + 1) * step, 0:lines, :].reshape(count, DH)
        o_grad = rows_ref[c * step : (c + 1) * step, lines : 2 * lines, :].reshape(count, DH)
        end, live = line_limits(c * count, count, lines, rows, resp_len, prompt_end)
        dots = line_values(rows_ref, c * step, step, lines, PIECES)
        self_lse = line_values(rows_ref, c * step, step, lines, 0)
        tiles = range(c * count // DH, (c + 1) * count // DH)
        part_lse = [
            jnp.concatenate([ref[n : n + 1, :] for n in tiles], axis=1) for ref in lse_refs
        ]
        peak = functools.reduce(jnp.maximum, part_lse, self_lse)
        total = sum(jnp.exp(x - peak) for x in part_lse) + jnp.exp(self_lse - peak)
        lse = jnp.where(live, peak + jnp.log(total), DEAD_LSE)
        dq_t = jnp.zeros((DH, count), jnp.float32)
        for b in range(0, KVH, pair):
            blocks = range(b, b + pair)
            k = jnp.concatenate([kv_refs[j][0:tokens, :] for j in blocks], axis=0)
            v = jnp.concatenate([kv_refs[j][tokens:, :] for j in blocks], axis=0)
            scores = lax.dot_general(
                k, q, (((1,), (1,)), ((), ())), preferred_element_type=jnp.float32
            )
            offset = lax.broadcasted_iota(jnp.int32, (tokens, count), 0)
            visible = jnp.concatenate([offset < end - scalars[1 + j] for j in blocks], axis=0)
            prob = jnp.where(visible, jnp.exp(scores * SCALE - lse), 0.0)
            dprob = lax.dot_general(
                v, o_grad, (((1,), (1,)), ((), ())), preferred_element_type=jnp.float32
            )
            dscore = (prob * (dprob - dots)).astype(jnp.bfloat16)
            dv = jnp.dot(prob.astype(jnp.bfloat16), o_grad, preferred_element_type=jnp.float32)
            dk = jnp.dot(dscore, q, preferred_element_type=jnp.float32) * SCALE
            dq_t = dq_t + jnp.dot(k.T, dscore, preferred_element_type=jnp.float32)
            held = slice(b * tokens, (b + pair) * tokens)
            if c > 0:
                dk = dk + dk_acc[held, :]
                dv = dv + dv_acc[held, :]
            if c < sources // step - 1:
                dk_acc[held, :] = dk
                dv_acc[held, :] = dv
            else:
                for n, j in enumerate(blocks):
                    inner = slice(n * tokens, (n + 1) * tokens)
                    dkv_refs[j][0:tokens, :] = dk[inner].astype(jnp.bfloat16)
                    dkv_refs[j][tokens:, :] = dv[inner].astype(jnp.bfloat16)
        dq_ref[c * step : (c + 1) * step] = (
            (dq_t * SCALE).T.astype(jnp.bfloat16).reshape(step, lines, DH)
        )


def unpack_kernel(parts, groups, heads, scalars, dq_ref, *rest):
    dkv_refs, (out_q_ref, out_k_ref, out_v_ref) = rest[:KVH], rest[KVH:]
    lines = dq_ref.shape[1]
    tokens = out_k_ref.shape[0]
    for g in range(groups):
        total = dq_ref[g].astype(jnp.float32)
        for part in range(1, parts):
            total = total + dq_ref[part * groups + g].astype(jnp.float32)
        out_q_ref[g * lines : (g + 1) * lines, :] = total.astype(jnp.bfloat16)
    for j, ref in enumerate(dkv_refs):
        column = pl.multiple_of(group_of(scalars[0] ^ j, groups, heads) * DH, DH)
        out_k_ref[:, pl.ds(column, DH)] = ref[0:tokens, :]
        out_v_ref[:, pl.ds(column, DH)] = ref[tokens:, :]


def swap_with_peers(blocks):
    return [blocks[0]] + [
        lax.ppermute(blocks[j], ("group", "head"), [(i, i ^ j) for i in range(KVH)])
        for j in range(1, KVH)
    ]


def shards(parts, groups, heads, queries, grad_out, outputs, lse_self, keys, values, resp_len, prompt_end):
    rows = queries.shape[0]
    own_heads = queries.shape[1] // DH
    own_lines = rows * own_heads
    lines = own_lines // groups
    tokens = keys.shape[0]
    sources = parts * groups
    tiles = sources * lines // DH
    member = lax.axis_index("group") * heads + lax.axis_index("head")
    peers = member ^ jnp.arange(KVH, dtype=jnp.int32)
    starts = (lax.axis_index("part") * KVH + peers) * tokens
    scalars = jnp.concatenate([member.reshape(1), starts]).astype(jnp.int32)
    kv_shape = jax.ShapeDtypeStruct((2 * tokens, DH), jnp.bfloat16)

    def as_lines(x):
        return x.reshape(rows, own_heads, DH).transpose(1, 0, 2).reshape(own_lines, DH)

    kv_blocks = pl.pallas_call(
        functools.partial(pack_kv_kernel, groups, heads),
        in_specs=[SMEM, ANY, ANY],
        out_shape=[kv_shape] * KVH,
        scratch_shapes=[pltpu.SemaphoreType.DMA((2 * KVH,))],
        compiler_params=PARAMS,
    )(scalars, keys, values)
    kv_blocks = swap_with_peers(kv_blocks)
    row_block = pl.pallas_call(
        functools.partial(pack_rows_kernel, parts, groups),
        in_specs=[ANY] * 4,
        out_shape=jax.ShapeDtypeStruct((sources, 2 * lines + STAT_ROWS, DH), jnp.bfloat16),
        scratch_shapes=[pltpu.VMEM((own_lines, DH), jnp.bfloat16)] * 3
        + [pltpu.VMEM(lse_self.shape, jnp.float32), pltpu.SemaphoreType.DMA((4,))],
        compiler_params=PARAMS,
    )(as_lines(queries), as_lines(grad_out), as_lines(outputs), lse_self)
    row_block = lax.all_to_all(
        row_block, ("part", "group"), split_axis=0, concat_axis=0, tiled=True
    )

    part_lse = pl.pallas_call(
        functools.partial(stat_kernel, rows, tokens),
        in_specs=[SMEM] * 3 + [VMEM] * (1 + KVH),
        out_shape=jax.ShapeDtypeStruct((tiles, DH), jnp.float32),
        compiler_params=PARAMS,
    )(scalars, resp_len, prompt_end, row_block, *kv_blocks)
    every_lse = [part_lse] + [
        lax.ppermute(part_lse, "part", [(i, (i + j) % parts) for i in range(parts)])
        for j in range(1, parts)
    ]

    dq, *dkv_blocks = pl.pallas_call(
        functools.partial(grad_kernel, parts, rows, tokens),
        in_specs=[SMEM] * 3 + [VMEM] * (1 + KVH + parts),
        out_shape=[jax.ShapeDtypeStruct((sources, lines, DH), jnp.bfloat16)] + [kv_shape] * KVH,
        scratch_shapes=[pltpu.VMEM((KVH * tokens, DH), jnp.float32)] * 2,
        compiler_params=PARAMS,
    )(scalars, resp_len, prompt_end, row_block, *kv_blocks, *every_lse)
    dkv_blocks = swap_with_peers(dkv_blocks)
    dq = lax.all_to_all(dq, ("part", "group"), split_axis=0, concat_axis=0, tiled=True)
    out_q, out_k, out_v = pl.pallas_call(
        functools.partial(unpack_kernel, parts, groups, heads),
        in_specs=[SMEM] + [VMEM] * (1 + KVH),
        out_shape=[
            jax.ShapeDtypeStruct((own_lines, DH), jnp.bfloat16),
            jax.ShapeDtypeStruct(keys.shape, jnp.bfloat16),
            jax.ShapeDtypeStruct(values.shape, jnp.bfloat16),
        ],
        compiler_params=PARAMS,
    )(scalars, dq, *dkv_blocks)
    out_q = out_q.reshape(own_heads, rows, DH).transpose(1, 0, 2).reshape(rows, own_heads * DH)
    return out_q, out_k, out_v


def solution(mesh):
    ctx, heads = mesh.shape["ctx"], mesh.shape["head"]
    groups = KVH // heads
    parts = ctx // groups
    fine = Mesh(mesh.devices.reshape(parts, groups, heads), ("part", "group", "head"))
    rows = P(("part", "group"), "head")
    tokens = P(("part", "group", "head"), None)
    return jax.shard_map(
        functools.partial(shards, parts, groups, heads),
        mesh=fine,
        in_specs=(rows, rows, rows, rows, tokens, tokens, P(), P()),
        out_specs=(rows, tokens, tokens),
        check_vma=False,
    )
```

```python
import functools

import jax
import jax.numpy as jnp
from jax import lax
from jax.experimental import pallas as pl
from jax.experimental.pallas import tpu as pltpu
from jax.sharding import Mesh, PartitionSpec as P

DH = 128
KVH = 8
RESP_LEN = 64
SCALE = DH ** (-0.5)
MASKED_SCORE = -1e30
DEAD_LSE = 1e30
PIECES = 3
STAT_ROWS = 16
STEP_BLOCKS = 4
PARAMS = pltpu.CompilerParams(vmem_limit_bytes=48 * 1024 * 1024)
HBM = pl.BlockSpec(memory_space=pltpu.HBM)
SMEM = pl.BlockSpec(memory_space=pltpu.SMEM)
VMEM = pl.BlockSpec(memory_space=pltpu.VMEM)

NEAR = 2
KEEP = (0, 1, 4, 5)


def split_pieces(x):
    first = x.astype(jnp.bfloat16)
    rest = x - first.astype(jnp.float32)
    second = rest.astype(jnp.bfloat16)
    third = (rest - second.astype(jnp.float32)).astype(jnp.bfloat16)
    return first, second, third


def shift_of(n):
    assert n & (n - 1) == 0
    return n.bit_length() - 1


def column_of(member, groups, heads):
    head_index, group_index = member & (heads - 1), member >> shift_of(heads)
    return pl.multiple_of((head_index * groups + group_index) * DH, DH)


def pack_kernel(groups, heads, scalars, q_hbm, o_grad_hbm, o_hbm, lse_hbm, k_hbm, v_hbm, *rest):
    slab_refs, (keep_ref, send_ref, o_ref, lse_ref, sems) = rest[:groups], rest[groups:]
    rows, own_heads = lse_ref.shape
    lines = o_ref.shape[0] // groups
    tokens = k_hbm.shape[0]
    member = scalars[0]
    own_group = member >> shift_of(heads)
    copies = [(lse_hbm, lse_ref), (o_hbm, o_ref)]
    firsts = []
    for j in range(groups):
        firsts.append(pl.multiple_of((own_group ^ j) * lines, lines))
        held = pl.ds(firsts[j], lines)
        copies.append((q_hbm.at[held, :], slab_refs[j].at[0:lines, :]))
        copies.append((o_grad_hbm.at[held, :], slab_refs[j].at[lines : 2 * lines, :]))
    row_copies = len(copies)
    for i, j in enumerate(KEEP):
        for ref, peer in ((keep_ref, j), (send_ref, j ^ NEAR)):
            columns = pl.ds(column_of(member ^ peer, groups, heads), DH)
            copies.append((k_hbm.at[:, columns], ref.at[i, 0:tokens, :]))
            copies.append((v_hbm.at[:, columns], ref.at[i, tokens : 2 * tokens, :]))
    copies = [pltpu.make_async_copy(s, t, sems.at[n]) for n, (s, t) in enumerate(copies)]
    for copy in copies:
        copy.start()

    wide = 2 * lines
    shape = (own_heads, wide)
    head_ids = lax.broadcasted_iota(jnp.int32, shape, 0)
    line_heads = (lax.broadcasted_iota(jnp.int32, shape, 1) & (lines - 1)) >> shift_of(rows)
    chosen = [
        (head_ids == line_heads + (firsts[j] >> shift_of(rows))).astype(jnp.bfloat16)
        for j in range(groups)
    ]
    shape = (rows, wide)
    own_row = lax.broadcasted_iota(jnp.int32, shape, 0) == (
        lax.broadcasted_iota(jnp.int32, shape, 1) & (rows - 1)
    )
    for copy in copies[:row_copies]:
        copy.wait()
    pieces = split_pieces(lse_ref[...])
    for j in range(groups):
        stats = []
        for piece in pieces:
            spread = jnp.dot(piece, chosen[j], preferred_element_type=jnp.float32)
            stats.append(jnp.sum(jnp.where(own_row, spread, 0.0), axis=0, keepdims=True))
        o_grad = slab_refs[j][lines : 2 * lines, :].astype(jnp.float32)
        product = o_grad * o_ref[pl.ds(firsts[j], lines), :].astype(jnp.float32)
        dots = jnp.sum(jnp.concatenate([product, product], axis=0).T, axis=0, keepdims=True)
        stats += [piece.astype(jnp.float32) for piece in split_pieces(dots)]
        stats.append(jnp.zeros((STAT_ROWS - 2 * PIECES, wide), jnp.float32))
        slab_refs[j][wide:, :] = jnp.concatenate(stats, axis=0).astype(jnp.bfloat16)
    for copy in copies[row_copies:]:
        copy.wait()


def pair_starts(scalars, i, tokens):
    first = scalars[1] * KVH
    return [(first + (scalars[0] ^ KEEP[i] ^ other)) * tokens for other in (0, NEAR)]


def pair_keys(ref, tokens):
    return jnp.concatenate([ref[0, 0:tokens, :], ref[1, 0:tokens, :]], axis=0)


def pair_values(ref, tokens):
    return jnp.concatenate([ref[0, tokens : 2 * tokens, :], ref[1, tokens : 2 * tokens, :]], axis=0)


def response_of(scalars, b, groups, rows):
    return ((scalars[1] ^ b) * (groups * rows)) >> shift_of(RESP_LEN)


def lse_rows(groups, lines):
    return max(1, groups * lines // DH)


def stat_kernel(parts, groups, rows, tokens, scalars, prompt_end, *refs):
    row_refs, pair_refs, lse_ref = refs[:parts], refs[parts:-1], refs[-1]
    lines = (row_refs[0].shape[1] - STAT_ROWS) // 2
    count = groups * lines
    offset = lax.broadcasted_iota(jnp.int32, (tokens, count), 0)
    for b in range(parts):
        q = row_refs[b][:, 0:lines, :].reshape(count, DH)
        end = prompt_end[response_of(scalars, b, groups, rows)]
        scores = []
        for i, ref in enumerate(pair_refs):
            part = lax.dot_general(
                pair_keys(ref, tokens),
                q,
                (((1,), (1,)), ((), ())),
                preferred_element_type=jnp.float32,
            )
            visible = jnp.concatenate(
                [offset < end - start for start in pair_starts(scalars, i, tokens)], axis=0
            )
            scores.append(jnp.where(visible, part * SCALE, MASKED_SCORE))
        scores = jnp.concatenate(scores, axis=0)
        peak = jnp.max(scores, axis=0, keepdims=True)
        total = jnp.sum(jnp.exp(scores - peak), axis=0, keepdims=True)
        lse = peak + jnp.log(total)
        if count < DH:
            lse = jnp.concatenate([lse] * (DH // count), axis=1)
        held = lse_rows(groups, lines)
        for n in range(held):
            at = (scalars[1] ^ b) * held + n
            lse_ref[pl.ds(at, 1), :] = lse[:, n * DH : (n + 1) * DH]


def line_values(slabs, lines, first_piece):
    low = lax.broadcasted_iota(jnp.int32, (1, 2 * lines), 1) < lines
    out = []
    for n in range(0, len(slabs), 2):
        held = [
            ref[j, 2 * lines : 2 * lines + STAT_ROWS, :].astype(jnp.float32)
            for ref, j in slabs[n : n + 2]
        ]
        total = None
        for k in range(first_piece, first_piece + PIECES):
            piece = jnp.where(low, held[0][k : k + 1], held[1][k : k + 1])
            total = piece if total is None else total + piece
        out.append(total)
    return jnp.concatenate(out, axis=1)


def grad_kernel(parts, order, groups, heads, rows, tokens, scalars, resp_len, prompt_end, *refs):
    row_refs, refs = refs[:parts], refs[parts:]
    pair_refs, refs = refs[: len(KEEP)], refs[len(KEEP) :]
    lse_refs, refs = refs[:-6], refs[-6:]
    dq_keep_ref, dq_send_ref, dkv_keep_ref, dkv_send_ref, dk_acc, dv_acc = refs
    lines = (row_refs[0].shape[1] - STAT_ROWS) // 2
    block = groups * lines
    step = min(parts, STEP_BLOCKS)
    own_group = scalars[0] >> shift_of(heads)
    held = lse_rows(groups, lines)
    offset = lax.broadcasted_iota(jnp.int32, (tokens, step * block), 0)
    lane = lax.broadcasted_iota(jnp.int32, (1, 2 * lines), 1)
    for c in range(0, parts, step):
        blocks = range(c, c + step)
        slabs = [(b, j) for b in blocks for j in range(groups)]
        q = jnp.concatenate([row_refs[b][j, 0:lines, :] for b, j in slabs], axis=0)
        o_grad = jnp.concatenate([row_refs[b][j, lines : 2 * lines, :] for b, j in slabs], axis=0)
        values = [(row_refs[b], j) for b, j in slabs]
        self_lse, dots = line_values(values, lines, 0), line_values(values, lines, PIECES)
        live = []
        for n in range(0, len(slabs), 2):
            row, length = [], []
            for b, j in slabs[n : n + 2]:
                source = (scalars[1] ^ b) * groups + (own_group ^ j)
                row.append(source * rows & (RESP_LEN - 1))
                length.append(resp_len[response_of(scalars, b, groups, rows)])
            row = jnp.where(lane < lines, row[0], row[1]) + (lane & (rows - 1))
            live.append(row < jnp.where(lane < lines, length[0], length[1]))
        live = jnp.concatenate(live, axis=1)
        end = jnp.concatenate(
            [
                jnp.full((1, block), prompt_end[response_of(scalars, b, groups, rows)], jnp.int32)
                for b in blocks
            ],
            axis=1,
        )
        part_lse = []
        for ref in lse_refs:
            tiles = []
            for b in blocks:
                for n in range(held):
                    tile = ref[pl.ds((scalars[1] ^ b) * held + n, 1), :]
                    tiles.append(tile[:, : min(block, DH)])
            part_lse.append(jnp.concatenate(tiles, axis=1))
        peak = functools.reduce(jnp.maximum, part_lse, self_lse)
        total = sum(jnp.exp(x - peak) for x in part_lse) + jnp.exp(self_lse - peak)
        lse = jnp.where(live, peak + jnp.log(total), DEAD_LSE)
        dq_t = jnp.zeros((DH, step * block), jnp.float32)
        for i, ref in enumerate(pair_refs):
            k, v = pair_keys(ref, tokens), pair_values(ref, tokens)
            scores = lax.dot_general(
                k, q, (((1,), (1,)), ((), ())), preferred_element_type=jnp.float32
            )
            visible = jnp.concatenate(
                [offset < end - start for start in pair_starts(scalars, i, tokens)], axis=0
            )
            prob = jnp.where(visible, jnp.exp(scores * SCALE - lse), 0.0)
            dprob = lax.dot_general(
                v, o_grad, (((1,), (1,)), ((), ())), preferred_element_type=jnp.float32
            )
            dscore = (prob * (dprob - dots)).astype(jnp.bfloat16)
            dv = jnp.dot(prob.astype(jnp.bfloat16), o_grad, preferred_element_type=jnp.float32)
            dk = jnp.dot(dscore, q, preferred_element_type=jnp.float32) * SCALE
            dq_t = dq_t + jnp.dot(k.T, dscore, preferred_element_type=jnp.float32)
            if c > 0:
                dk = dk + dk_acc[i]
                dv = dv + dv_acc[i]
            if c + step < parts:
                dk_acc[i] = dk
                dv_acc[i] = dv
            else:
                for n, out in enumerate((dkv_keep_ref, dkv_send_ref)):
                    inner = slice(n * tokens, (n + 1) * tokens)
                    out[i, 0:tokens, :] = dk[inner].astype(jnp.bfloat16)
                    out[i, tokens : 2 * tokens, :] = dv[inner].astype(jnp.bfloat16)
        for n, b in enumerate(blocks):
            dq = (dq_t[:, n * block : (n + 1) * block] * SCALE).T.astype(jnp.bfloat16)
            place = order.index(b)
            if place < parts // 2:
                dq_keep_ref[place] = dq
            else:
                dq_send_ref[place - parts // 2] = dq


def unpack_kernel(groups, heads, scalars, *refs):
    slab_refs, pair_refs = refs[:groups], refs[groups : groups + len(KEEP)]
    out_q_ref, out_k_ref, out_v_ref = refs[groups + len(KEEP) :]
    lines = slab_refs[0].shape[0]
    tokens = out_k_ref.shape[0]
    own_group = scalars[0] >> shift_of(heads)
    for j, ref in enumerate(slab_refs):
        out_q_ref[pl.ds(pl.multiple_of((own_group ^ j) * lines, lines), lines), :] = ref[...]
    for i, ref in enumerate(pair_refs):
        for n, other in enumerate((0, NEAR)):
            columns = pl.ds(column_of(scalars[0] ^ KEEP[i] ^ other, groups, heads), DH)
            out_k_ref[:, columns] = ref[n, 0:tokens, :]
            out_v_ref[:, columns] = ref[n, tokens : 2 * tokens, :]


def swap(x, axis, distance, size):
    return lax.ppermute(x, axis, [(i, i ^ distance) for i in range(size)])


def swap_pairs(keep, send):
    members = ("group", "head")
    came = swap(send, members, NEAR, KVH)
    pairs = [jnp.stack([keep[i], came[i]]) for i in range(len(KEEP))]
    return [swap(x, members, j, KVH) if j else x for x, j in zip(pairs, KEEP)]


def add_lse(a, b):
    peak = jnp.maximum(a, b)
    return peak + jnp.log(jnp.exp(a - peak) + jnp.exp(b - peak))


def shards(parts, groups, heads, queries, grad_out, outputs, lse_self, keys, values, resp_len, prompt_end):
    rows = queries.shape[0]
    own_heads = queries.shape[1] // DH
    own_lines = rows * own_heads
    lines = own_lines // groups
    tokens = keys.shape[0]
    assert 2 * lines == DH and RESP_LEN % (groups * rows) == 0 and parts % 2 == 0
    member = lax.axis_index("group") * heads + lax.axis_index("head")
    scalars = jnp.stack([member, lax.axis_index("part")]).astype(jnp.int32)
    far = [1 << n for n in reversed(range(shift_of(parts)))]

    def as_lines(x):
        return x.reshape(rows, own_heads, DH).transpose(1, 0, 2).reshape(own_lines, DH)

    slab_shape = jax.ShapeDtypeStruct((2 * lines + STAT_ROWS, DH), jnp.bfloat16)
    half_shape = jax.ShapeDtypeStruct((len(KEEP), 2 * tokens, DH), jnp.bfloat16)
    *slabs, kv_keep, kv_send = pl.pallas_call(
        functools.partial(pack_kernel, groups, heads),
        in_specs=[SMEM] + [HBM] * 6,
        out_specs=[VMEM] * (groups + 2),
        out_shape=[slab_shape] * groups + [half_shape] * 2,
        scratch_shapes=[
            pltpu.VMEM((own_lines, DH), jnp.bfloat16),
            pltpu.VMEM(lse_self.shape, jnp.float32),
            pltpu.SemaphoreType.DMA((2 + 2 * groups + 4 * len(KEEP),)),
        ],
        compiler_params=PARAMS,
    )(scalars, as_lines(queries), as_lines(grad_out), as_lines(outputs), lse_self, keys, values)

    own_block = jnp.stack([swap(x, "group", j, groups) if j else x for j, x in enumerate(slabs)])
    order, blocks = [0], [own_block]
    for d in far:
        blocks = blocks + [swap(x, "part", d, parts) for x in blocks]
        order = order + [b ^ d for b in order]
    blocks = [blocks[order.index(b)] for b in range(parts)]
    pairs = swap_pairs(kv_keep, kv_send)

    lse = pl.pallas_call(
        functools.partial(stat_kernel, parts, groups, rows, tokens),
        in_specs=[SMEM] * 2 + [VMEM] * (parts + len(KEEP)),
        out_shape=jax.ShapeDtypeStruct((parts * lse_rows(groups, lines), DH), jnp.float32),
        compiler_params=PARAMS,
    )(scalars, prompt_end, *blocks, *pairs)
    for d in far[:0:-1]:
        lse = add_lse(lse, swap(lse, "part", d, parts))
    every_lse = [lse, swap(lse, "part", far[0], parts)]

    dq_shape = jax.ShapeDtypeStruct((parts // 2, groups * lines, DH), jnp.bfloat16)
    acc = pltpu.VMEM((len(KEEP), 2 * tokens, DH), jnp.float32)
    dq_keep, dq_send, dkv_keep, dkv_send = pl.pallas_call(
        functools.partial(grad_kernel, parts, order, groups, heads, rows, tokens),
        in_specs=[SMEM] * 3 + [VMEM] * (parts + len(KEEP) + len(every_lse)),
        out_shape=[dq_shape] * 2 + [half_shape] * 2,
        scratch_shapes=[acc] * 2,
        compiler_params=PARAMS,
    )(scalars, resp_len, prompt_end, *blocks, *pairs, *every_lse)

    for d in far[::-1]:
        came = swap(dq_send, "part", d, parts)
        total = dq_keep.astype(jnp.float32) + came.astype(jnp.float32)
        half = total.shape[0] // 2
        dq_keep, dq_send = total[:half], total[half:].astype(jnp.bfloat16)
    dq = total.astype(jnp.bfloat16).reshape(groups, lines, DH)
    slabs = [swap(dq[j], "group", j, groups) if j else dq[j] for j in range(groups)]
    pairs = swap_pairs(dkv_keep, dkv_send)
    out_q, out_k, out_v = pl.pallas_call(
        functools.partial(unpack_kernel, groups, heads),
        in_specs=[SMEM] + [VMEM] * (groups + len(KEEP)),
        out_shape=[
            jax.ShapeDtypeStruct((own_lines, DH), jnp.bfloat16),
            jax.ShapeDtypeStruct(keys.shape, jnp.bfloat16),
            jax.ShapeDtypeStruct(values.shape, jnp.bfloat16),
        ],
        compiler_params=PARAMS,
    )(scalars, *slabs, *pairs)
    out_q = out_q.reshape(own_heads, rows, DH).transpose(1, 0, 2).reshape(rows, own_heads * DH)
    return out_q, out_k, out_v


def solution(mesh):
    ctx, heads = mesh.shape["ctx"], mesh.shape["head"]
    groups = KVH // heads
    parts = ctx // groups
    fine = Mesh(mesh.devices.reshape(parts, groups, heads), ("part", "group", "head"))
    rows = P(("part", "group"), "head")
    tokens = P(("part", "group", "head"), None)
    return jax.shard_map(
        functools.partial(shards, parts, groups, heads),
        mesh=fine,
        in_specs=(rows, rows, rows, rows, tokens, tokens, P(), P()),
        out_specs=(rows, tokens, tokens),
        check_vma=False,
    )
```

```python
import functools

import jax
import jax.numpy as jnp
from jax import lax
from jax.experimental import pallas as pl
from jax.experimental.pallas import tpu as pltpu
from jax.sharding import Mesh, PartitionSpec as P

DH = 128
KVH = 8
RESP_LEN = 64
SCALE = DH ** (-0.5)
MASKED_SCORE = -1e30
DEAD_LSE = 1e30
PIECES = 3
STAT_ROWS = 16
STEP_LINES = 1024
PARAMS = pltpu.CompilerParams(vmem_limit_bytes=48 * 1024 * 1024)
HBM = pl.BlockSpec(memory_space=pltpu.HBM)
SMEM = pl.BlockSpec(memory_space=pltpu.SMEM)
VMEM = pl.BlockSpec(memory_space=pltpu.VMEM)

NEAR = 2
KEEP = (0, 1, 4, 5)


def split_pieces(x):
    first = x.astype(jnp.bfloat16)
    rest = x - first.astype(jnp.float32)
    second = rest.astype(jnp.bfloat16)
    third = (rest - second.astype(jnp.float32)).astype(jnp.bfloat16)
    return first, second, third


def shift_of(n):
    assert n & (n - 1) == 0
    return n.bit_length() - 1


def column_of(member, groups, heads):
    head_index, group_index = member & (heads - 1), member >> shift_of(heads)
    return pl.multiple_of((head_index * groups + group_index) * DH, DH)


def pack_kv_kernel(groups, heads, scalars, k_hbm, v_hbm, keep_ref, send_ref, sems):
    tokens = k_hbm.shape[0]
    copies = []
    for i, j in enumerate(KEEP):
        for ref, peer in ((send_ref, j ^ NEAR), (keep_ref, j)):
            columns = pl.ds(column_of(scalars[0] ^ peer, groups, heads), DH)
            copies.append((k_hbm.at[:, columns], ref.at[i, 0:tokens, :]))
            copies.append((v_hbm.at[:, columns], ref.at[i, tokens : 2 * tokens, :]))
    copies = [pltpu.make_async_copy(s, t, sems.at[n]) for n, (s, t) in enumerate(copies)]
    for copy in copies:
        copy.start()
    for copy in copies:
        copy.wait()


def pack_rows_kernel(parts, groups, q_hbm, o_grad_hbm, o_hbm, lse_hbm, rows_ref, o_ref, lse_ref, sems):
    rows, own_heads = lse_ref.shape
    lines = o_ref.shape[0] // groups
    copies = [(lse_hbm, lse_ref), (o_hbm, o_ref)]
    for g in range(groups):
        held = pl.ds(g * lines, lines)
        for part in range(parts):
            slab = rows_ref.at[part * groups + g]
            copies.append((q_hbm.at[held, :], slab.at[0:lines, :]))
            copies.append((o_grad_hbm.at[held, :], slab.at[lines : 2 * lines, :]))
    copies = [pltpu.make_async_copy(s, t, sems.at[n]) for n, (s, t) in enumerate(copies)]
    for copy in copies:
        copy.start()

    wide = 2 * lines
    shape = (own_heads, wide)
    head_ids = lax.broadcasted_iota(jnp.int32, shape, 0)
    line_heads = (lax.broadcasted_iota(jnp.int32, shape, 1) & (lines - 1)) >> shift_of(rows)
    group_heads = lines // rows
    chosen = [
        (head_ids == line_heads + g * group_heads).astype(jnp.bfloat16) for g in range(groups)
    ]
    shape = (rows, wide)
    own_row = lax.broadcasted_iota(jnp.int32, shape, 0) == (
        lax.broadcasted_iota(jnp.int32, shape, 1) & (rows - 1)
    )
    for copy in copies:
        copy.wait()
    pieces = split_pieces(lse_ref[...])
    for g in range(groups):
        stats = []
        for piece in pieces:
            spread = jnp.dot(piece, chosen[g], preferred_element_type=jnp.float32)
            stats.append(jnp.sum(jnp.where(own_row, spread, 0.0), axis=0, keepdims=True))
        o_grad = rows_ref[g, lines : 2 * lines, :].astype(jnp.float32)
        product = o_grad * o_ref[g * lines : (g + 1) * lines, :].astype(jnp.float32)
        dots = jnp.sum(jnp.concatenate([product, product], axis=0).T, axis=0, keepdims=True)
        stats += [piece.astype(jnp.float32) for piece in split_pieces(dots)]
        stats.append(jnp.zeros((STAT_ROWS - 2 * PIECES, wide), jnp.float32))
        stat_block = jnp.concatenate(stats, axis=0).astype(jnp.bfloat16)
        for part in range(parts):
            rows_ref[part * groups + g, wide:, :] = stat_block


def pair_starts(scalars, i, tokens):
    first = scalars[1] * KVH
    return [(first + (scalars[0] ^ KEEP[i] ^ other)) * tokens for other in (0, NEAR)]


def pair_keys(ref, tokens):
    return jnp.concatenate([ref[0, 0:tokens, :], ref[1, 0:tokens, :]], axis=0)


def pair_values(ref, tokens):
    return jnp.concatenate([ref[0, tokens : 2 * tokens, :], ref[1, tokens : 2 * tokens, :]], axis=0)


def response_of(source, rows):
    return source * rows // RESP_LEN


def stat_kernel(rows, tokens, scalars, prompt_end, rows_ref, *refs):
    pair_refs, lse_ref = refs[:-1], refs[-1]
    sources, lines = rows_ref.shape[0], (rows_ref.shape[1] - STAT_ROWS) // 2
    step = 256 // lines
    count = step * lines
    offset = lax.broadcasted_iota(jnp.int32, (tokens, count), 0)
    for c in range(0, sources, step):
        q = rows_ref[c : c + step, 0:lines, :].reshape(count, DH)
        end = prompt_end[response_of(c, rows)]
        scores = []
        for i, ref in enumerate(pair_refs):
            part = lax.dot_general(
                pair_keys(ref, tokens),
                q,
                (((1,), (1,)), ((), ())),
                preferred_element_type=jnp.float32,
            )
            visible = jnp.concatenate(
                [offset < end - start for start in pair_starts(scalars, i, tokens)], axis=0
            )
            scores.append(jnp.where(visible, part * SCALE, MASKED_SCORE))
        scores = jnp.concatenate(scores, axis=0)
        peak = jnp.max(scores, axis=0, keepdims=True)
        total = jnp.sum(jnp.exp(scores - peak), axis=0, keepdims=True)
        lse = peak + jnp.log(total)
        for n in range(count // DH):
            at = c * lines // DH + n
            lse_ref[at : at + 1, :] = lse[:, n * DH : (n + 1) * DH]


def line_values(rows_ref, sources, lines, first_piece):
    low = lax.broadcasted_iota(jnp.int32, (1, 2 * lines), 1) < lines
    out = []
    for n in sources[::2]:
        held = [
            rows_ref[s, 2 * lines : 2 * lines + STAT_ROWS, :].astype(jnp.float32)
            for s in (n, n + 1)
        ]
        total = None
        for k in range(first_piece, first_piece + PIECES):
            piece = jnp.where(low, held[0][k : k + 1], held[1][k : k + 1])
            total = piece if total is None else total + piece
        out.append(total)
    return jnp.concatenate(out, axis=1)


def grad_kernel(parts, rows, tokens, scalars, resp_len, prompt_end, rows_ref, *refs):
    pair_refs, refs = refs[: len(KEEP)], refs[len(KEEP) :]
    lse_refs, refs = refs[:parts], refs[parts:]
    dq_ref, dkv_keep_ref, dkv_send_ref, dk_acc, dv_acc = refs
    all_sources, lines = rows_ref.shape[0], (rows_ref.shape[1] - STAT_ROWS) // 2
    step = min(all_sources, STEP_LINES // lines)
    count = step * lines
    offset = lax.broadcasted_iota(jnp.int32, (tokens, count), 0)
    lane = lax.broadcasted_iota(jnp.int32, (1, 2 * lines), 1)
    for c in range(0, all_sources, step):
        sources = range(c, c + step)
        q = rows_ref[c : c + step, 0:lines, :].reshape(count, DH)
        o_grad = rows_ref[c : c + step, lines : 2 * lines, :].reshape(count, DH)
        self_lse = line_values(rows_ref, sources, lines, 0)
        dots = line_values(rows_ref, sources, lines, PIECES)
        live, end = [], []
        for s in sources[::2]:
            row = (s * rows + jnp.where(lane < lines, 0, rows) + (lane & (rows - 1))) & (RESP_LEN - 1)
            live.append(row < resp_len[response_of(s, rows)])
            end.append(jnp.full(lane.shape, prompt_end[response_of(s, rows)], jnp.int32))
        live = jnp.concatenate(live, axis=1)
        end = jnp.concatenate(end, axis=1)
        first = c * lines // DH
        part_lse = [
            jnp.concatenate([ref[n : n + 1, :] for n in range(first, first + count // DH)], axis=1)
            for ref in lse_refs
        ]
        peak = functools.reduce(jnp.maximum, part_lse, self_lse)
        total = sum(jnp.exp(x - peak) for x in part_lse) + jnp.exp(self_lse - peak)
        lse = jnp.where(live, peak + jnp.log(total), DEAD_LSE)
        dq_t = jnp.zeros((DH, count), jnp.float32)
        for i, ref in enumerate(pair_refs):
            k, v = pair_keys(ref, tokens), pair_values(ref, tokens)
            scores = lax.dot_general(
                k, q, (((1,), (1,)), ((), ())), preferred_element_type=jnp.float32
            )
            visible = jnp.concatenate(
                [offset < end - start for start in pair_starts(scalars, i, tokens)], axis=0
            )
            prob = jnp.where(visible, jnp.exp(scores * SCALE - lse), 0.0)
            dprob = lax.dot_general(
                v, o_grad, (((1,), (1,)), ((), ())), preferred_element_type=jnp.float32
            )
            dscore = (prob * (dprob - dots)).astype(jnp.bfloat16)
            dv = jnp.dot(prob.astype(jnp.bfloat16), o_grad, preferred_element_type=jnp.float32)
            dk = jnp.dot(dscore, q, preferred_element_type=jnp.float32) * SCALE
            dq_t = dq_t + jnp.dot(k.T, dscore, preferred_element_type=jnp.float32)
            if c > 0:
                dk = dk + dk_acc[i]
                dv = dv + dv_acc[i]
            if c + step < all_sources:
                dk_acc[i] = dk
                dv_acc[i] = dv
            else:
                for n, out in enumerate((dkv_keep_ref, dkv_send_ref)):
                    inner = slice(n * tokens, (n + 1) * tokens)
                    out[i, 0:tokens, :] = dk[inner].astype(jnp.bfloat16)
                    out[i, tokens : 2 * tokens, :] = dv[inner].astype(jnp.bfloat16)
        dq_ref[c : c + step] = (dq_t * SCALE).T.astype(jnp.bfloat16).reshape(step, lines, DH)


def unpack_kernel(parts, groups, heads, scalars, dq_ref, *refs):
    pair_refs, (out_q_ref, out_k_ref, out_v_ref) = refs[: len(KEEP)], refs[len(KEEP) :]
    lines = dq_ref.shape[1]
    tokens = out_k_ref.shape[0]
    for g in range(groups):
        total = dq_ref[g].astype(jnp.float32)
        for part in range(1, parts):
            total = total + dq_ref[part * groups + g].astype(jnp.float32)
        out_q_ref[g * lines : (g + 1) * lines, :] = total.astype(jnp.bfloat16)
    for i, ref in enumerate(pair_refs):
        for n, other in enumerate((0, NEAR)):
            columns = pl.ds(column_of(scalars[0] ^ KEEP[i] ^ other, groups, heads), DH)
            out_k_ref[:, columns] = ref[n, 0:tokens, :]
            out_v_ref[:, columns] = ref[n, tokens : 2 * tokens, :]


def swap(x, axis, distance, size):
    return lax.ppermute(x, axis, [(i, i ^ distance) for i in range(size)])


def swap_pairs(keep, send):
    members = ("group", "head")
    came = swap(send, members, NEAR, KVH)
    pairs = [jnp.stack([keep[i], came[i]]) for i in range(len(KEEP))]
    return [swap(x, members, j, KVH) if j else x for x, j in zip(pairs, KEEP)]


def exchange_rows(x, parts, groups, in_one_step):
    def one_step(x):
        return lax.all_to_all(x, ("part", "group"), split_axis=0, concat_axis=0, tiled=True)

    def two_steps(x):
        y = x.reshape(parts, groups, *x.shape[1:])
        y = lax.all_to_all(y, "group", split_axis=1, concat_axis=1, tiled=True)
        y = lax.all_to_all(y, "part", split_axis=0, concat_axis=0, tiled=True)
        return y.reshape(x.shape)

    return lax.cond(in_one_step, one_step, two_steps, x)


def shards(parts, groups, heads, queries, grad_out, outputs, lse_self, keys, values, resp_len, prompt_end):
    rows = queries.shape[0]
    own_heads = queries.shape[1] // DH
    own_lines = rows * own_heads
    lines = own_lines // groups
    tokens = keys.shape[0]
    sources = parts * groups
    assert 2 * lines == DH and RESP_LEN % (256 // lines * rows) == 0
    member = lax.axis_index("group") * heads + lax.axis_index("head")
    scalars = jnp.stack([member, lax.axis_index("part")]).astype(jnp.int32)
    in_one_step = prompt_end[0] > 0

    def as_lines(x):
        return x.reshape(rows, own_heads, DH).transpose(1, 0, 2).reshape(own_lines, DH)

    def in_hbm(x):
        return pltpu.with_memory_space_constraint(x, pltpu.HBM)

    half_shape = jax.ShapeDtypeStruct((len(KEEP), 2 * tokens, DH), jnp.bfloat16)
    kv_keep, kv_send = pl.pallas_call(
        functools.partial(pack_kv_kernel, groups, heads),
        in_specs=[SMEM] + [HBM] * 2,
        out_specs=[VMEM] * 2,
        out_shape=[half_shape] * 2,
        scratch_shapes=[pltpu.SemaphoreType.DMA((4 * len(KEEP),))],
        compiler_params=PARAMS,
    )(scalars, in_hbm(keys), in_hbm(values))
    row_block = pl.pallas_call(
        functools.partial(pack_rows_kernel, parts, groups),
        in_specs=[HBM] * 4,
        out_specs=VMEM,
        out_shape=jax.ShapeDtypeStruct((sources, 2 * lines + STAT_ROWS, DH), jnp.bfloat16),
        scratch_shapes=[
            pltpu.VMEM((own_lines, DH), jnp.bfloat16),
            pltpu.VMEM(lse_self.shape, jnp.float32),
            pltpu.SemaphoreType.DMA((2 + 2 * sources,)),
        ],
        compiler_params=PARAMS,
    )(in_hbm(as_lines(queries)), in_hbm(as_lines(grad_out)), in_hbm(as_lines(outputs)), in_hbm(lse_self))
    pairs = swap_pairs(kv_keep, kv_send)
    row_block = exchange_rows(row_block, parts, groups, in_one_step)

    lse = pl.pallas_call(
        functools.partial(stat_kernel, rows, tokens),
        in_specs=[SMEM] * 2 + [VMEM] * (1 + len(KEEP)),
        out_shape=jax.ShapeDtypeStruct((sources * lines // DH, DH), jnp.float32),
        compiler_params=PARAMS,
    )(scalars, prompt_end, row_block, *pairs)
    every_lse = [lse] + [swap(lse, "part", d, parts) for d in range(1, parts)]

    acc = pltpu.VMEM((len(KEEP), 2 * tokens, DH), jnp.float32)
    dq, dkv_keep, dkv_send = pl.pallas_call(
        functools.partial(grad_kernel, parts, rows, tokens),
        in_specs=[SMEM] * 3 + [VMEM] * (1 + len(KEEP) + parts),
        out_shape=[jax.ShapeDtypeStruct((sources, lines, DH), jnp.bfloat16)] + [half_shape] * 2,
        scratch_shapes=[acc] * 2,
        compiler_params=PARAMS,
    )(scalars, resp_len, prompt_end, row_block, *pairs, *every_lse)

    pairs = swap_pairs(dkv_keep, dkv_send)
    dq = exchange_rows(dq, parts, groups, in_one_step)
    out_q, out_k, out_v = pl.pallas_call(
        functools.partial(unpack_kernel, parts, groups, heads),
        in_specs=[SMEM] + [VMEM] * (1 + len(KEEP)),
        out_shape=[
            jax.ShapeDtypeStruct((own_lines, DH), jnp.bfloat16),
            jax.ShapeDtypeStruct(keys.shape, jnp.bfloat16),
            jax.ShapeDtypeStruct(values.shape, jnp.bfloat16),
        ],
        compiler_params=PARAMS,
    )(scalars, dq, *pairs)
    out_q = out_q.reshape(own_heads, rows, DH).transpose(1, 0, 2).reshape(rows, own_heads * DH)
    return out_q, out_k, out_v


def solution(mesh):
    ctx, heads = mesh.shape["ctx"], mesh.shape["head"]
    groups = KVH // heads
    parts = ctx // groups
    fine = Mesh(mesh.devices.reshape(parts, groups, heads), ("part", "group", "head"))
    rows = P(("part", "group"), "head")
    tokens = P(("part", "group", "head"), None)
    return jax.shard_map(
        functools.partial(shards, parts, groups, heads),
        mesh=fine,
        in_specs=(rows, rows, rows, rows, tokens, tokens, P(), P()),
        out_specs=(rows, tokens, tokens),
        check_vma=False,
    )
```

```python
import functools

import jax
import jax.numpy as jnp
from jax import lax
from jax.experimental import pallas as pl
from jax.experimental.pallas import tpu as pltpu
from jax.sharding import Mesh, PartitionSpec as P

DH = 128
KVH = 8
RESP_LEN = 64
SCALE = DH ** (-0.5)
MASKED_SCORE = -1e30
DEAD_LSE = 1e30
PIECES = 3
STAT_ROWS = 16
STEP_LINES = 512
PARAMS = pltpu.CompilerParams(vmem_limit_bytes=48 * 1024 * 1024)
HBM = pl.BlockSpec(memory_space=pltpu.HBM)
SMEM = pl.BlockSpec(memory_space=pltpu.SMEM)
VMEM = pl.BlockSpec(memory_space=pltpu.VMEM)

NEAR = 2
FIRST = 1
KEEP = (0, 2, 4, 6)


def split_pieces(x):
    first = x.astype(jnp.bfloat16)
    rest = x - first.astype(jnp.float32)
    second = rest.astype(jnp.bfloat16)
    third = (rest - second.astype(jnp.float32)).astype(jnp.bfloat16)
    return first, second, third


def shift_of(n):
    assert n & (n - 1) == 0
    return n.bit_length() - 1


def column_of(member, groups, heads):
    head_index, group_index = member & (heads - 1), member >> shift_of(heads)
    return pl.multiple_of((head_index * groups + group_index) * DH, DH)


def pack_kv_kernel(groups, heads, scalars, k_hbm, v_hbm, keep_ref, send_ref, sems):
    tokens = k_hbm.shape[0]
    copies = []
    for i, j in enumerate(KEEP):
        for ref, peer in ((send_ref, j ^ FIRST), (keep_ref, j)):
            columns = pl.ds(column_of(scalars[0] ^ peer, groups, heads), DH)
            copies.append((k_hbm.at[:, columns], ref.at[i, 0:tokens, :]))
            copies.append((v_hbm.at[:, columns], ref.at[i, tokens : 2 * tokens, :]))
    copies = [pltpu.make_async_copy(s, t, sems.at[n]) for n, (s, t) in enumerate(copies)]
    for copy in copies:
        copy.start()
    for copy in copies:
        copy.wait()


def pack_rows_kernel(far, groups, q_hbm, o_grad_hbm, o_hbm, lse_hbm, rows_ref, o_ref, lse_ref, sems):
    rows, own_heads = lse_ref.shape
    lines = o_ref.shape[0] // groups
    copies = [(lse_hbm, lse_ref), (o_hbm, o_ref)]
    for g in range(groups):
        held = pl.ds(g * lines, lines)
        for f in range(far):
            slab = rows_ref.at[f * groups + g]
            copies.append((q_hbm.at[held, :], slab.at[0:lines, :]))
            copies.append((o_grad_hbm.at[held, :], slab.at[lines : 2 * lines, :]))
    copies = [pltpu.make_async_copy(s, t, sems.at[n]) for n, (s, t) in enumerate(copies)]
    for copy in copies:
        copy.start()

    wide = 2 * lines
    shape = (own_heads, wide)
    head_ids = lax.broadcasted_iota(jnp.int32, shape, 0)
    line_heads = (lax.broadcasted_iota(jnp.int32, shape, 1) & (lines - 1)) >> shift_of(rows)
    group_heads = lines // rows
    chosen = [
        (head_ids == line_heads + g * group_heads).astype(jnp.bfloat16) for g in range(groups)
    ]
    shape = (rows, wide)
    own_row = lax.broadcasted_iota(jnp.int32, shape, 0) == (
        lax.broadcasted_iota(jnp.int32, shape, 1) & (rows - 1)
    )
    for copy in copies:
        copy.wait()
    pieces = split_pieces(lse_ref[...])
    for g in range(groups):
        stats = []
        for piece in pieces:
            spread = jnp.dot(piece, chosen[g], preferred_element_type=jnp.float32)
            stats.append(jnp.sum(jnp.where(own_row, spread, 0.0), axis=0, keepdims=True))
        o_grad = rows_ref[g, lines : 2 * lines, :].astype(jnp.float32)
        product = o_grad * o_ref[g * lines : (g + 1) * lines, :].astype(jnp.float32)
        dots = jnp.sum(jnp.concatenate([product, product], axis=0).T, axis=0, keepdims=True)
        stats += [piece.astype(jnp.float32) for piece in split_pieces(dots)]
        stats.append(jnp.zeros((STAT_ROWS - 2 * PIECES, wide), jnp.float32))
        stat_block = jnp.concatenate(stats, axis=0).astype(jnp.bfloat16)
        for f in range(far):
            rows_ref[f * groups + g, wide:, :] = stat_block


def pair_starts(scalars, i, groups, heads, tokens):
    starts = []
    for other in (0, FIRST):
        member = scalars[0] ^ KEEP[i] ^ other
        group_index, head_index = member >> shift_of(heads), member & (heads - 1)
        index = ((scalars[1] * groups + group_index) * NEAR + scalars[2]) * heads + head_index
        starts.append(index * tokens)
    return starts


def pair_keys(ref, tokens):
    return jnp.concatenate([ref[0, 0:tokens, :], ref[1, 0:tokens, :]], axis=0)


def pair_values(ref, tokens):
    return jnp.concatenate([ref[0, tokens : 2 * tokens, :], ref[1, tokens : 2 * tokens, :]], axis=0)


def response_of(source, rows):
    return source * NEAR * rows // RESP_LEN


def stat_kernel(groups, heads, rows, tokens, scalars, prompt_end, *refs):
    row_refs, pair_refs, lse_ref = refs[:NEAR], refs[NEAR:-1], refs[-1]
    sources, lines = row_refs[0].shape[0], (row_refs[0].shape[1] - STAT_ROWS) // 2
    step = 256 // lines
    count = step * lines
    offset = lax.broadcasted_iota(jnp.int32, (tokens, count), 0)
    for n, rows_ref in enumerate(row_refs):
        for c in range(0, sources, step):
            q = rows_ref[c : c + step, 0:lines, :].reshape(count, DH)
            end = prompt_end[response_of(c, rows)]
            scores = []
            for i, ref in enumerate(pair_refs):
                part = lax.dot_general(
                    pair_keys(ref, tokens),
                    q,
                    (((1,), (1,)), ((), ())),
                    preferred_element_type=jnp.float32,
                )
                starts = pair_starts(scalars, i, groups, heads, tokens)
                visible = jnp.concatenate([offset < end - start for start in starts], axis=0)
                scores.append(jnp.where(visible, part * SCALE, MASKED_SCORE))
            scores = jnp.concatenate(scores, axis=0)
            peak = jnp.max(scores, axis=0, keepdims=True)
            total = jnp.sum(jnp.exp(scores - peak), axis=0, keepdims=True)
            lse = peak + jnp.log(total)
            for k in range(count // DH):
                at = ((scalars[2] ^ n) * sources + c) * lines // DH + k
                lse_ref[pl.ds(at, 1), :] = lse[:, k * DH : (k + 1) * DH]


def line_values(rows_ref, sources, lines, first_piece):
    low = lax.broadcasted_iota(jnp.int32, (1, 2 * lines), 1) < lines
    out = []
    for n in sources[::2]:
        held = [
            rows_ref[s, 2 * lines : 2 * lines + STAT_ROWS, :].astype(jnp.float32)
            for s in (n, n + 1)
        ]
        total = None
        for k in range(first_piece, first_piece + PIECES):
            piece = jnp.where(low, held[0][k : k + 1], held[1][k : k + 1])
            total = piece if total is None else total + piece
        out.append(total)
    return jnp.concatenate(out, axis=1)


def grad_kernel(parts, groups, heads, rows, tokens, scalars, resp_len, prompt_end, *refs):
    row_refs, refs = refs[:NEAR], refs[NEAR:]
    pair_refs, refs = refs[: len(KEEP)], refs[len(KEEP) :]
    lse_refs, refs = refs[:parts], refs[parts:]
    dq_refs, (dkv_keep_ref, dkv_send_ref, dk_acc, dv_acc) = refs[:NEAR], refs[NEAR:]
    all_sources, lines = row_refs[0].shape[0], (row_refs[0].shape[1] - STAT_ROWS) // 2
    step = min(all_sources, STEP_LINES // lines)
    part_count = step * lines
    count = NEAR * part_count
    offset = lax.broadcasted_iota(jnp.int32, (tokens, count), 0)
    lane = lax.broadcasted_iota(jnp.int32, (1, 2 * lines), 1)
    for c in range(0, all_sources, step):
        sources = range(c, c + step)

        def both(part_of):
            return jnp.concatenate([part_of(n, ref) for n, ref in enumerate(row_refs)], axis=0)

        def both_lines(part_of):
            return jnp.concatenate([part_of(n, ref) for n, ref in enumerate(row_refs)], axis=1)

        def live_lines(n, _):
            live = []
            for s in sources[::2]:
                device = (s + jnp.where(lane < lines, 0, 1)) * NEAR + (scalars[2] ^ n)
                row = (device * rows + (lane & (rows - 1))) & (RESP_LEN - 1)
                live.append((row < resp_len[response_of(s, rows)]).astype(jnp.int32))
            return jnp.concatenate(live, axis=1)

        def end_lines(n, _):
            ends = [prompt_end[response_of(s, rows)] for s in sources[::2]]
            return jnp.concatenate([jnp.full(lane.shape, end, jnp.int32) for end in ends], axis=1)

        def lse_lines(ref):
            def part_of(n, _):
                first = ((scalars[2] ^ n) * all_sources + c) * lines // DH
                tiles = [ref[pl.ds(first + k, 1), :] for k in range(part_count // DH)]
                return jnp.concatenate(tiles, axis=1)

            return both_lines(part_of)

        q = both(lambda n, ref: ref[c : c + step, 0:lines, :].reshape(part_count, DH))
        o_grad = both(
            lambda n, ref: ref[c : c + step, lines : 2 * lines, :].reshape(part_count, DH)
        )
        self_lse = both_lines(lambda n, ref: line_values(ref, sources, lines, 0))
        dots = both_lines(lambda n, ref: line_values(ref, sources, lines, PIECES))
        live, end = both_lines(live_lines), both_lines(end_lines)
        part_lse = [lse_lines(ref) for ref in lse_refs]
        peak = functools.reduce(jnp.maximum, part_lse, self_lse)
        total = sum(jnp.exp(x - peak) for x in part_lse) + jnp.exp(self_lse - peak)
        lse = jnp.where(live > 0, peak + jnp.log(total), DEAD_LSE)
        dq_t = jnp.zeros((DH, count), jnp.float32)
        for i, ref in enumerate(pair_refs):
            k, v = pair_keys(ref, tokens), pair_values(ref, tokens)
            scores = lax.dot_general(
                k, q, (((1,), (1,)), ((), ())), preferred_element_type=jnp.float32
            )
            starts = pair_starts(scalars, i, groups, heads, tokens)
            visible = jnp.concatenate([offset < end - start for start in starts], axis=0)
            prob = jnp.where(visible, jnp.exp(scores * SCALE - lse), 0.0)
            dprob = lax.dot_general(
                v, o_grad, (((1,), (1,)), ((), ())), preferred_element_type=jnp.float32
            )
            dscore = (prob * (dprob - dots)).astype(jnp.bfloat16)
            dv = jnp.dot(prob.astype(jnp.bfloat16), o_grad, preferred_element_type=jnp.float32)
            dk = jnp.dot(dscore, q, preferred_element_type=jnp.float32) * SCALE
            dq_t = dq_t + jnp.dot(k.T, dscore, preferred_element_type=jnp.float32)
            if c > 0:
                dk = dk + dk_acc[i]
                dv = dv + dv_acc[i]
            if c + step < all_sources:
                dk_acc[i] = dk
                dv_acc[i] = dv
            else:
                for n, out in enumerate((dkv_keep_ref, dkv_send_ref)):
                    inner = slice(n * tokens, (n + 1) * tokens)
                    out[i, 0:tokens, :] = dk[inner].astype(jnp.bfloat16)
                    out[i, tokens : 2 * tokens, :] = dv[inner].astype(jnp.bfloat16)
        for n, ref in enumerate(dq_refs):
            dq = (dq_t[:, n * part_count : (n + 1) * part_count] * SCALE).T.astype(jnp.bfloat16)
            ref[c : c + step] = dq.reshape(step, lines, DH)


def write_query_kernel(far, groups, dq_ref, out_ref):
    lines = dq_ref.shape[1]
    for g in range(groups):
        total = dq_ref[g].astype(jnp.float32)
        for f in range(1, far):
            total = total + dq_ref[f * groups + g].astype(jnp.float32)
        out_ref[g * lines : (g + 1) * lines, :] = total.astype(jnp.bfloat16)


def write_kv_kernel(groups, heads, scalars, *refs):
    pair_refs, (out_k_ref, out_v_ref, sems) = refs[: len(KEEP)], refs[len(KEEP) :]
    tokens = out_k_ref.shape[0]
    copies = []
    for i, ref in enumerate(pair_refs):
        for n, other in enumerate((0, FIRST)):
            columns = pl.ds(column_of(scalars[0] ^ KEEP[i] ^ other, groups, heads), DH)
            copies.append((ref.at[n, 0:tokens, :], out_k_ref.at[:, columns]))
            copies.append((ref.at[n, tokens : 2 * tokens, :], out_v_ref.at[:, columns]))
    copies = [pltpu.make_async_copy(s, t, sems.at[n]) for n, (s, t) in enumerate(copies)]
    for copy in copies:
        copy.start()
    for copy in copies:
        copy.wait()


def swap(x, axis, distance, size):
    return lax.ppermute(x, axis, [(i, i ^ distance) for i in range(size)])


def swap_pairs(keep, send):
    members = ("group", "head")
    came = swap(send, members, FIRST, KVH)
    pairs = [jnp.stack([keep[i], came[i]]) for i in range(len(KEEP))]
    return [swap(x, members, j, KVH) if j else x for x, j in zip(pairs, KEEP)]


def exchange_slabs(x):
    return lax.all_to_all(x, ("far", "group"), split_axis=0, concat_axis=0, tiled=True)


def shards(far, groups, heads, queries, grad_out, outputs, lse_self, keys, values, resp_len, prompt_end):
    rows = queries.shape[0]
    own_heads = queries.shape[1] // DH
    own_lines = rows * own_heads
    lines = own_lines // groups
    tokens = keys.shape[0]
    sources = far * groups
    parts = far * NEAR
    assert 2 * lines == DH and RESP_LEN % (256 // lines * NEAR * rows) == 0
    member = lax.axis_index("group") * heads + lax.axis_index("head")
    scalars = jnp.stack([member, lax.axis_index("far"), lax.axis_index("near")]).astype(jnp.int32)

    def as_lines(x):
        return x.reshape(rows, own_heads, DH).transpose(1, 0, 2).reshape(own_lines, DH)

    def in_hbm(x):
        return pltpu.with_memory_space_constraint(x, pltpu.HBM)

    half_shape = jax.ShapeDtypeStruct((len(KEEP), 2 * tokens, DH), jnp.bfloat16)
    kv_keep, kv_send = pl.pallas_call(
        functools.partial(pack_kv_kernel, groups, heads),
        in_specs=[SMEM] + [HBM] * 2,
        out_specs=[VMEM] * 2,
        out_shape=[half_shape] * 2,
        scratch_shapes=[pltpu.SemaphoreType.DMA((4 * len(KEEP),))],
        compiler_params=PARAMS,
    )(scalars, in_hbm(keys), in_hbm(values))
    slabs = pl.pallas_call(
        functools.partial(pack_rows_kernel, far, groups),
        in_specs=[HBM] * 4,
        out_specs=VMEM,
        out_shape=jax.ShapeDtypeStruct((sources, 2 * lines + STAT_ROWS, DH), jnp.bfloat16),
        scratch_shapes=[
            pltpu.VMEM((own_lines, DH), jnp.bfloat16),
            pltpu.VMEM(lse_self.shape, jnp.float32),
            pltpu.SemaphoreType.DMA((2 + 2 * sources,)),
        ],
        compiler_params=PARAMS,
    )(in_hbm(as_lines(queries)), in_hbm(as_lines(grad_out)), in_hbm(as_lines(outputs)), in_hbm(lse_self))
    pairs = swap_pairs(kv_keep, kv_send)
    slabs = exchange_slabs(slabs)
    blocks = [slabs, swap(slabs, "near", 1, NEAR)]

    lse = pl.pallas_call(
        functools.partial(stat_kernel, groups, heads, rows, tokens),
        in_specs=[SMEM] * 2 + [VMEM] * (NEAR + len(KEEP)),
        out_shape=jax.ShapeDtypeStruct((NEAR * sources * lines // DH, DH), jnp.float32),
        compiler_params=PARAMS,
    )(scalars, prompt_end, *blocks, *pairs)
    every_lse = [lse] + [swap(lse, ("far", "near"), d, parts) for d in range(1, parts)]

    dq_shape = jax.ShapeDtypeStruct((sources, lines, DH), jnp.bfloat16)
    acc = pltpu.VMEM((len(KEEP), 2 * tokens, DH), jnp.float32)
    dq_keep, dq_send, dkv_keep, dkv_send = pl.pallas_call(
        functools.partial(grad_kernel, parts, groups, heads, rows, tokens),
        in_specs=[SMEM] * 3 + [VMEM] * (NEAR + len(KEEP) + parts),
        out_shape=[dq_shape] * NEAR + [half_shape] * 2,
        scratch_shapes=[acc] * 2,
        compiler_params=PARAMS,
    )(scalars, resp_len, prompt_end, *blocks, *pairs, *every_lse)

    pairs = swap_pairs(dkv_keep, dkv_send)
    came = swap(dq_send, "near", 1, NEAR)
    dq = (dq_keep.astype(jnp.float32) + came.astype(jnp.float32)).astype(jnp.bfloat16)
    dq = exchange_slabs(dq)
    out_q = pl.pallas_call(
        functools.partial(write_query_kernel, far, groups),
        in_specs=[VMEM],
        out_shape=jax.ShapeDtypeStruct((own_lines, DH), jnp.bfloat16),
        compiler_params=PARAMS,
    )(dq)
    out_k, out_v = pl.pallas_call(
        functools.partial(write_kv_kernel, groups, heads),
        in_specs=[SMEM] + [VMEM] * len(KEEP),
        out_specs=[HBM] * 2,
        out_shape=[
            jax.ShapeDtypeStruct(keys.shape, jnp.bfloat16),
            jax.ShapeDtypeStruct(values.shape, jnp.bfloat16),
        ],
        scratch_shapes=[pltpu.SemaphoreType.DMA((4 * len(KEEP),))],
        compiler_params=PARAMS,
    )(scalars, *pairs)
    out_q = out_q.reshape(own_heads, rows, DH).transpose(1, 0, 2).reshape(rows, own_heads * DH)
    return out_q, out_k, out_v


def solution(mesh):
    ctx, heads = mesh.shape["ctx"], mesh.shape["head"]
    groups = KVH // heads
    far = ctx // groups // NEAR
    fine = Mesh(mesh.devices.reshape(far, groups, NEAR, heads), ("far", "group", "near", "head"))
    rows = P(("far", "group", "near"), "head")
    tokens = P(("far", "group", "near", "head"), None)
    return jax.shard_map(
        functools.partial(shards, far, groups, heads),
        mesh=fine,
        in_specs=(rows, rows, rows, rows, tokens, tokens, P(), P()),
        out_specs=(rows, tokens, tokens),
        check_vma=False,
    )
```

```python
import functools

import jax
import jax.numpy as jnp
from jax import lax
from jax.experimental import pallas as pl
from jax.experimental.pallas import tpu as pltpu
from jax.sharding import Mesh, PartitionSpec as P

DH = 128
KVH = 8
RESP_LEN = 64
SCALE = DH ** (-0.5)
MASKED_SCORE = -1e30
DEAD_LSE = 1e30
PIECES = 3
STAT_ROWS = 16
STEP_LINES = 512
PARAMS = pltpu.CompilerParams(vmem_limit_bytes=48 * 1024 * 1024)
ANY = pl.BlockSpec(memory_space=pl.ANY)
HBM = pl.BlockSpec(memory_space=pltpu.HBM)
SMEM = pl.BlockSpec(memory_space=pltpu.SMEM)
VMEM = pl.BlockSpec(memory_space=pltpu.VMEM)

NEAR = 2
FIRST = 1
KEEP = (0, 2, 4, 6)


def split_pieces(x):
    first = x.astype(jnp.bfloat16)
    rest = x - first.astype(jnp.float32)
    second = rest.astype(jnp.bfloat16)
    third = (rest - second.astype(jnp.float32)).astype(jnp.bfloat16)
    return first, second, third


def shift_of(n):
    assert n & (n - 1) == 0
    return n.bit_length() - 1


def column_of(member, groups, heads):
    head_index, group_index = member & (heads - 1), member >> shift_of(heads)
    return pl.multiple_of((head_index * groups + group_index) * DH, DH)


def pack_kernel(far, groups, heads, scalars, q_hbm, o_grad_hbm, o_hbm, lse_hbm, k_hbm, v_hbm, *rest):
    rows_ref, keep_ref, send_ref, o_ref, lse_ref, sems = rest
    rows, own_heads = lse_ref.shape
    lines = o_ref.shape[0] // groups
    tokens = k_hbm.shape[0]
    copies = [(lse_hbm, lse_ref), (o_hbm, o_ref)]
    for g in range(groups):
        held = pl.ds(g * lines, lines)
        for f in range(far):
            slab = rows_ref.at[f * groups + g]
            copies.append((q_hbm.at[held, :], slab.at[0:lines, :]))
            copies.append((o_grad_hbm.at[held, :], slab.at[lines : 2 * lines, :]))
    row_copies = len(copies)
    for i, j in enumerate(KEEP):
        for ref, peer in ((send_ref, j ^ FIRST), (keep_ref, j)):
            columns = pl.ds(column_of(scalars[0] ^ peer, groups, heads), DH)
            copies.append((k_hbm.at[:, columns], ref.at[i, 0:tokens, :]))
            copies.append((v_hbm.at[:, columns], ref.at[i, tokens : 2 * tokens, :]))
    copies = [pltpu.make_async_copy(s, t, sems.at[n]) for n, (s, t) in enumerate(copies)]
    for copy in copies:
        copy.start()

    wide = 2 * lines
    shape = (own_heads, wide)
    head_ids = lax.broadcasted_iota(jnp.int32, shape, 0)
    line_heads = (lax.broadcasted_iota(jnp.int32, shape, 1) & (lines - 1)) >> shift_of(rows)
    group_heads = lines // rows
    chosen = [
        (head_ids == line_heads + g * group_heads).astype(jnp.bfloat16) for g in range(groups)
    ]
    shape = (rows, wide)
    own_row = lax.broadcasted_iota(jnp.int32, shape, 0) == (
        lax.broadcasted_iota(jnp.int32, shape, 1) & (rows - 1)
    )
    for copy in copies[:row_copies]:
        copy.wait()
    pieces = split_pieces(lse_ref[...])
    for g in range(groups):
        stats = []
        for piece in pieces:
            spread = jnp.dot(piece, chosen[g], preferred_element_type=jnp.float32)
            stats.append(jnp.sum(jnp.where(own_row, spread, 0.0), axis=0, keepdims=True))
        o_grad = rows_ref[g, lines : 2 * lines, :].astype(jnp.float32)
        product = o_grad * o_ref[g * lines : (g + 1) * lines, :].astype(jnp.float32)
        dots = jnp.sum(jnp.concatenate([product, product], axis=0).T, axis=0, keepdims=True)
        stats += [piece.astype(jnp.float32) for piece in split_pieces(dots)]
        stats.append(jnp.zeros((STAT_ROWS - 2 * PIECES, wide), jnp.float32))
        stat_block = jnp.concatenate(stats, axis=0).astype(jnp.bfloat16)
        for f in range(far):
            rows_ref[f * groups + g, wide:, :] = stat_block
    for copy in copies[row_copies:]:
        copy.wait()


def pair_starts(scalars, i, groups, heads, tokens):
    starts = []
    for other in (0, FIRST):
        member = scalars[0] ^ KEEP[i] ^ other
        group_index, head_index = member >> shift_of(heads), member & (heads - 1)
        index = ((scalars[1] * groups + group_index) * NEAR + scalars[2]) * heads + head_index
        starts.append(index * tokens)
    return starts


def pair_keys(ref, tokens):
    return jnp.concatenate([ref[0, 0:tokens, :], ref[1, 0:tokens, :]], axis=0)


def pair_values(ref, tokens):
    return jnp.concatenate([ref[0, tokens : 2 * tokens, :], ref[1, tokens : 2 * tokens, :]], axis=0)


def response_of(source, rows):
    return source * NEAR * rows // RESP_LEN


def stat_kernel(n, groups, heads, rows, tokens, scalars, prompt_end, rows_ref, *refs):
    pair_refs, before_refs, lse_ref = refs[: len(KEEP)], refs[len(KEEP) : -1], refs[-1]
    sources, lines = rows_ref.shape[0], (rows_ref.shape[1] - STAT_ROWS) // 2
    step = 256 // lines
    count = step * lines
    held = sources * lines // DH
    first = (scalars[2] ^ n) * held if before_refs else 0
    for ref in before_refs:
        for k in range(held):
            lse_ref[pl.ds((scalars[2] ^ 0) * held + k, 1), :] = ref[k : k + 1, :]
    offset = lax.broadcasted_iota(jnp.int32, (tokens, count), 0)
    for c in range(0, sources, step):
        q = rows_ref[c : c + step, 0:lines, :].reshape(count, DH)
        end = prompt_end[response_of(c, rows)]
        scores = []
        for i, ref in enumerate(pair_refs):
            part = lax.dot_general(
                pair_keys(ref, tokens),
                q,
                (((1,), (1,)), ((), ())),
                preferred_element_type=jnp.float32,
            )
            starts = pair_starts(scalars, i, groups, heads, tokens)
            visible = jnp.concatenate([offset < end - start for start in starts], axis=0)
            scores.append(jnp.where(visible, part * SCALE, MASKED_SCORE))
        scores = jnp.concatenate(scores, axis=0)
        peak = jnp.max(scores, axis=0, keepdims=True)
        total = jnp.sum(jnp.exp(scores - peak), axis=0, keepdims=True)
        lse = peak + jnp.log(total)
        for k in range(count // DH):
            at = first + c * lines // DH + k
            lse_ref[pl.ds(at, 1), :] = lse[:, k * DH : (k + 1) * DH]


def line_values(rows_ref, sources, lines, first_piece):
    low = lax.broadcasted_iota(jnp.int32, (1, 2 * lines), 1) < lines
    out = []
    for n in sources[::2]:
        held = [
            rows_ref[s, 2 * lines : 2 * lines + STAT_ROWS, :].astype(jnp.float32)
            for s in (n, n + 1)
        ]
        total = None
        for k in range(first_piece, first_piece + PIECES):
            piece = jnp.where(low, held[0][k : k + 1], held[1][k : k + 1])
            total = piece if total is None else total + piece
        out.append(total)
    return jnp.concatenate(out, axis=1)


def over_blocks(part_of, row_refs, axis):
    return jnp.concatenate([part_of(n, ref) for n, ref in enumerate(row_refs)], axis=axis)


def lse_lines(lse_ref, n, scalars, first_source, count, held, lines):
    first = (scalars[2] ^ n) * held + first_source * lines // DH
    return jnp.concatenate([lse_ref[pl.ds(first + k, 1), :] for k in range(count // DH)], axis=1)


def part_kernel(groups, heads, rows, tokens, scalars, prompt_end, *refs):
    row_refs, refs = refs[:NEAR], refs[NEAR:]
    pair_refs, (lse_ref, prob_ref, dscore_ref, *dq_refs) = refs[: len(KEEP)], refs[len(KEEP) :]
    all_sources, lines = row_refs[0].shape[0], (row_refs[0].shape[1] - STAT_ROWS) // 2
    held = all_sources * lines // DH
    step = min(all_sources, STEP_LINES // lines)
    part_count = step * lines
    count = NEAR * part_count
    offset = lax.broadcasted_iota(jnp.int32, (tokens, count), 0)
    for c in range(0, all_sources, step):
        sources = range(c, c + step)

        def end_lines(n, _):
            ends = [prompt_end[response_of(s, rows)] for s in sources]
            return jnp.concatenate([jnp.full((1, lines), end, jnp.int32) for end in ends], axis=1)

        q = over_blocks(
            lambda n, ref: ref[c : c + step, 0:lines, :].reshape(part_count, DH), row_refs, 0
        )
        o_grad = over_blocks(
            lambda n, ref: ref[c : c + step, lines : 2 * lines, :].reshape(part_count, DH),
            row_refs,
            0,
        )
        dots = over_blocks(
            lambda n, ref: line_values(ref, sources, lines, PIECES), row_refs, 1
        )
        lse = over_blocks(
            lambda n, ref: lse_lines(lse_ref, n, scalars, c, part_count, held, lines), row_refs, 1
        )
        end = over_blocks(end_lines, row_refs, 1)
        dq_t = jnp.zeros((DH, count), jnp.float32)
        lanes = slice(c * lines * NEAR, c * lines * NEAR + count)
        for i, ref in enumerate(pair_refs):
            k, v = pair_keys(ref, tokens), pair_values(ref, tokens)
            scores = lax.dot_general(
                k, q, (((1,), (1,)), ((), ())), preferred_element_type=jnp.float32
            )
            starts = pair_starts(scalars, i, groups, heads, tokens)
            visible = jnp.concatenate([offset < end - start for start in starts], axis=0)
            prob = jnp.where(visible, jnp.exp(scores * SCALE - lse), 0.0)
            dprob = lax.dot_general(
                v, o_grad, (((1,), (1,)), ((), ())), preferred_element_type=jnp.float32
            )
            dscore = (prob * (dprob - dots)).astype(jnp.bfloat16)
            prob_ref[i, :, lanes] = prob.astype(jnp.bfloat16)
            dscore_ref[i, :, lanes] = dscore
            dq_t = dq_t + jnp.dot(k.T, dscore, preferred_element_type=jnp.float32)
        for n, ref in enumerate(dq_refs):
            dq = dq_t[:, n * part_count : (n + 1) * part_count]
            ref[:, c * lines : c * lines + part_count] = dq.astype(jnp.bfloat16)


def token_kernel(parts, rows, tokens, scalars, resp_len, *refs):
    row_refs, refs = refs[:NEAR], refs[NEAR:]
    (prob_ref, dscore_ref), lse_refs, refs = refs[:2], refs[2 : 2 + parts], refs[2 + parts :]
    dkv_keep_ref, dkv_send_ref, weight_ref, dk_acc, dv_acc = refs
    all_sources, lines = row_refs[0].shape[0], (row_refs[0].shape[1] - STAT_ROWS) // 2
    held = all_sources * lines // DH
    step = min(all_sources, STEP_LINES // lines)
    part_count = step * lines
    count = NEAR * part_count
    lane = lax.broadcasted_iota(jnp.int32, (1, 2 * lines), 1)
    for c in range(0, all_sources, step):
        sources = range(c, c + step)

        def live_lines(n, _):
            live = []
            for s in sources[::2]:
                device = (s + jnp.where(lane < lines, 0, 1)) * NEAR + (scalars[2] ^ n)
                row = (device * rows + (lane & (rows - 1))) & (RESP_LEN - 1)
                live.append((row < resp_len[response_of(s, rows)]).astype(jnp.int32))
            return jnp.concatenate(live, axis=1)

        part_lse = [
            over_blocks(
                lambda n, ref: lse_lines(lse_ref, n, scalars, c, part_count, held, lines),
                row_refs,
                1,
            )
            for lse_ref in lse_refs
        ]
        self_lse = over_blocks(lambda n, ref: line_values(ref, sources, lines, 0), row_refs, 1)
        peak = functools.reduce(jnp.maximum, part_lse, self_lse)
        total = sum(jnp.exp(x - peak) for x in part_lse) + jnp.exp(self_lse - peak)
        live = over_blocks(live_lines, row_refs, 1)
        lse = jnp.where(live > 0, peak + jnp.log(total), DEAD_LSE)
        weights = [jnp.exp(x - lse) for x in part_lse[:NEAR]]
        for n, weight in enumerate(weights):
            weight_ref[n : n + 1, c * lines : c * lines + part_count] = weight[:, :part_count]
        weight = jnp.broadcast_to(weights[0], (DH, count)).T

        def scaled(first):
            x = over_blocks(
                lambda n, ref: ref[c : c + step, first : first + lines, :].reshape(part_count, DH),
                row_refs,
                0,
            )
            return (x.astype(jnp.float32) * weight).astype(jnp.bfloat16)

        q, o_grad = scaled(0), scaled(lines)
        lanes = slice(c * lines * NEAR, c * lines * NEAR + count)
        for i in range(len(KEEP)):
            dk = jnp.dot(dscore_ref[i, :, lanes], q, preferred_element_type=jnp.float32) * SCALE
            dv = jnp.dot(prob_ref[i, :, lanes], o_grad, preferred_element_type=jnp.float32)
            if c > 0:
                dk = dk + dk_acc[i]
                dv = dv + dv_acc[i]
            if c + step < all_sources:
                dk_acc[i] = dk
                dv_acc[i] = dv
            else:
                for n, out in enumerate((dkv_keep_ref, dkv_send_ref)):
                    inner = slice(n * tokens, (n + 1) * tokens)
                    out[i, 0:tokens, :] = dk[inner].astype(jnp.bfloat16)
                    out[i, tokens : 2 * tokens, :] = dv[inner].astype(jnp.bfloat16)


def add_query_kernel(own_ref, came_ref, weight_ref, out_ref):
    sources, lines, _ = out_ref.shape
    total = own_ref[...].astype(jnp.float32) * weight_ref[0:1, :]
    total = total + came_ref[...].astype(jnp.float32) * weight_ref[1:2, :]
    out_ref[...] = (total * SCALE).T.astype(jnp.bfloat16).reshape(sources, lines, DH)


def tie_kernel(*refs):
    pass


def write_query_kernel(far, groups, dq_ref, out_ref):
    lines = dq_ref.shape[1]
    for g in range(groups):
        total = dq_ref[g].astype(jnp.float32)
        for f in range(1, far):
            total = total + dq_ref[f * groups + g].astype(jnp.float32)
        out_ref[g * lines : (g + 1) * lines, :] = total.astype(jnp.bfloat16)


def write_kv_kernel(groups, heads, scalars, *refs):
    pair_refs, (out_k_ref, out_v_ref, sems) = refs[: len(KEEP)], refs[len(KEEP) :]
    tokens = out_k_ref.shape[0]
    copies = []
    for i, ref in enumerate(pair_refs):
        for n, other in enumerate((0, FIRST)):
            columns = pl.ds(column_of(scalars[0] ^ KEEP[i] ^ other, groups, heads), DH)
            copies.append((ref.at[n, 0:tokens, :], out_k_ref.at[:, columns]))
            copies.append((ref.at[n, tokens : 2 * tokens, :], out_v_ref.at[:, columns]))
    copies = [pltpu.make_async_copy(s, t, sems.at[n]) for n, (s, t) in enumerate(copies)]
    for copy in copies:
        copy.start()
    for copy in copies:
        copy.wait()


def swap(x, axis, distance, size):
    return lax.ppermute(x, axis, [(i, i ^ distance) for i in range(size)])


def swap_pairs(keep, send):
    members = ("group", "head")
    came = swap(send, members, FIRST, KVH)
    pairs = [jnp.stack([keep[i], came[i]]) for i in range(len(KEEP))]
    return [swap(x, members, j, KVH) if j else x for x, j in zip(pairs, KEEP)]


def exchange_slabs(x):
    return lax.all_to_all(x, ("far", "group"), split_axis=0, concat_axis=0, tiled=True)


def shards(far, groups, heads, queries, grad_out, outputs, lse_self, keys, values, resp_len, prompt_end):
    rows = queries.shape[0]
    own_heads = queries.shape[1] // DH
    own_lines = rows * own_heads
    lines = own_lines // groups
    tokens = keys.shape[0]
    sources = far * groups
    parts = far * NEAR
    assert 2 * lines == DH and RESP_LEN % (256 // lines * NEAR * rows) == 0
    member = lax.axis_index("group") * heads + lax.axis_index("head")
    scalars = jnp.stack([member, lax.axis_index("far"), lax.axis_index("near")]).astype(jnp.int32)

    def as_lines(x):
        return x.reshape(rows, own_heads, DH).transpose(1, 0, 2).reshape(own_lines, DH)

    def in_hbm(x):
        return pltpu.with_memory_space_constraint(x, pltpu.HBM)

    half_shape = jax.ShapeDtypeStruct((len(KEEP), 2 * tokens, DH), jnp.bfloat16)
    slabs, kv_keep, kv_send = pl.pallas_call(
        functools.partial(pack_kernel, far, groups, heads),
        in_specs=[SMEM] + [HBM] * 6,
        out_specs=[VMEM] * 3,
        out_shape=[
            jax.ShapeDtypeStruct((sources, 2 * lines + STAT_ROWS, DH), jnp.bfloat16),
            half_shape,
            half_shape,
        ],
        scratch_shapes=[
            pltpu.VMEM((own_lines, DH), jnp.bfloat16),
            pltpu.VMEM(lse_self.shape, jnp.float32),
            pltpu.SemaphoreType.DMA((2 + 2 * sources + 4 * len(KEEP),)),
        ],
        compiler_params=PARAMS,
    )(
        scalars,
        in_hbm(as_lines(queries)),
        in_hbm(as_lines(grad_out)),
        in_hbm(as_lines(outputs)),
        in_hbm(lse_self),
        in_hbm(keys),
        in_hbm(values),
    )
    pairs = swap_pairs(kv_keep, kv_send)
    slabs = exchange_slabs(slabs)
    slabs = pl.pallas_call(
        tie_kernel,
        in_specs=[ANY] * (1 + len(KEEP)),
        out_specs=ANY,
        out_shape=jax.ShapeDtypeStruct(slabs.shape, slabs.dtype),
        input_output_aliases={0: 0},
        compiler_params=PARAMS,
    )(slabs, *pairs)
    blocks = [slabs, swap(slabs, "near", 1, NEAR)]

    lse = []
    for n, block in enumerate(blocks):
        lse = [
            pl.pallas_call(
                functools.partial(stat_kernel, n, groups, heads, rows, tokens),
                in_specs=[SMEM] * 2 + [VMEM] * (1 + len(KEEP) + n),
                out_shape=jax.ShapeDtypeStruct(((n + 1) * sources * lines // DH, DH), jnp.float32),
                compiler_params=PARAMS,
            )(scalars, prompt_end, block, *pairs, *lse)
        ]
    every_lse = lse + [swap(lse[0], ("far", "near"), d, parts) for d in range(1, parts)]

    score_shape = jax.ShapeDtypeStruct(
        (len(KEEP), 2 * tokens, NEAR * sources * lines), jnp.bfloat16
    )
    dq_shape = jax.ShapeDtypeStruct((DH, sources * lines), jnp.bfloat16)
    prob, dscore, dq_keep, dq_send = pl.pallas_call(
        functools.partial(part_kernel, groups, heads, rows, tokens),
        in_specs=[SMEM] * 2 + [VMEM] * (NEAR + len(KEEP) + 1),
        out_specs=[VMEM] * 4,
        out_shape=[score_shape] * 2 + [dq_shape] * NEAR,
        compiler_params=PARAMS,
    )(scalars, prompt_end, *blocks, *pairs, *lse)
    came = swap(dq_send, "near", 1, NEAR)
    acc = pltpu.VMEM((len(KEEP), 2 * tokens, DH), jnp.float32)
    dkv_keep, dkv_send, weights = pl.pallas_call(
        functools.partial(token_kernel, parts, rows, tokens),
        in_specs=[SMEM] * 2 + [VMEM] * (NEAR + 2 + parts),
        out_shape=[half_shape] * 2 + [jax.ShapeDtypeStruct((NEAR, sources * lines), jnp.float32)],
        scratch_shapes=[acc] * 2,
        compiler_params=PARAMS,
    )(scalars, resp_len, *blocks, prob, dscore, *every_lse)
    pairs = swap_pairs(dkv_keep, dkv_send)
    dq = pl.pallas_call(
        add_query_kernel,
        in_specs=[VMEM] * 3,
        out_shape=jax.ShapeDtypeStruct((sources, lines, DH), jnp.bfloat16),
        compiler_params=PARAMS,
    )(dq_keep, came, weights)
    dq = exchange_slabs(dq)
    out_q = pl.pallas_call(
        functools.partial(write_query_kernel, far, groups),
        in_specs=[VMEM],
        out_shape=jax.ShapeDtypeStruct((own_lines, DH), jnp.bfloat16),
        compiler_params=PARAMS,
    )(dq)
    out_k, out_v = pl.pallas_call(
        functools.partial(write_kv_kernel, groups, heads),
        in_specs=[SMEM] + [VMEM] * len(KEEP),
        out_specs=[HBM] * 2,
        out_shape=[
            jax.ShapeDtypeStruct(keys.shape, jnp.bfloat16),
            jax.ShapeDtypeStruct(values.shape, jnp.bfloat16),
        ],
        scratch_shapes=[pltpu.SemaphoreType.DMA((4 * len(KEEP),))],
        compiler_params=PARAMS,
    )(scalars, *pairs)
    out_q = out_q.reshape(own_heads, rows, DH).transpose(1, 0, 2).reshape(rows, own_heads * DH)
    return out_q, out_k, out_v


def solution(mesh):
    ctx, heads = mesh.shape["ctx"], mesh.shape["head"]
    groups = KVH // heads
    far = ctx // groups // NEAR
    fine = Mesh(mesh.devices.reshape(far, groups, NEAR, heads), ("far", "group", "near", "head"))
    rows = P(("far", "group", "near"), "head")
    tokens = P(("far", "group", "near", "head"), None)
    return jax.shard_map(
        functools.partial(shards, far, groups, heads),
        mesh=fine,
        in_specs=(rows, rows, rows, rows, tokens, tokens, P(), P()),
        out_specs=(rows, tokens, tokens),
        check_vma=False,
    )
```

```python
import functools

import jax
import jax.numpy as jnp
from jax import lax
from jax.experimental import pallas as pl
from jax.experimental.pallas import tpu as pltpu
from jax.sharding import Mesh, PartitionSpec as P

DH = 128
KVH = 8
RESP_LEN = 64
SCALE = DH ** (-0.5)
MASKED_SCORE = -1e30
DEAD_LSE = 1e30
PIECES = 3
STAT_ROWS = 16
STEP_LINES = 1024
PARAMS = pltpu.CompilerParams(vmem_limit_bytes=24 * 1024 * 1024)
ANY = pl.BlockSpec(memory_space=pl.ANY)
HBM = pl.BlockSpec(memory_space=pltpu.HBM)
SMEM = pl.BlockSpec(memory_space=pltpu.SMEM)
VMEM = pl.BlockSpec(memory_space=pltpu.VMEM)

FIRST = 2
KEEP = (0, 1, 4, 5)


def split_pieces(x):
    first = x.astype(jnp.bfloat16)
    rest = x - first.astype(jnp.float32)
    second = rest.astype(jnp.bfloat16)
    third = (rest - second.astype(jnp.float32)).astype(jnp.bfloat16)
    return first, second, third


def shift_of(n):
    assert n & (n - 1) == 0
    return n.bit_length() - 1


def column_of(member, groups, heads):
    head_index, group_index = member & (heads - 1), member >> shift_of(heads)
    return pl.multiple_of((head_index * groups + group_index) * DH, DH)


def group_at(scalars, row_xor, near_xor, nears):
    return (scalars[1] ^ row_xor) * nears + (scalars[2] ^ near_xor)


def pack_kernel(row_count, nears, heads, scalars, q_hbm, o_grad_hbm, o_hbm, lse_hbm, k_hbm, v_hbm, *rest):
    slab_refs, (keep_ref, send_ref, o_ref, lse_ref, sems) = rest[:row_count], rest[row_count:]
    groups = row_count * nears
    rows, own_heads = lse_ref.shape
    lines = o_ref.shape[0] // groups
    tokens = k_hbm.shape[0]
    copies = [(lse_hbm, lse_ref), (o_hbm, o_ref)]
    slabs = []
    for j, ref in enumerate(slab_refs):
        for n in range(nears):
            first = pl.multiple_of(group_at(scalars, j, n, nears) * lines, lines)
            slabs.append((ref, n, first))
            copies.append((o_grad_hbm.at[pl.ds(first, lines), :], ref.at[n, lines : 2 * lines, :]))
    stat_copies = len(copies)
    for ref, n, first in slabs:
        copies.append((q_hbm.at[pl.ds(first, lines), :], ref.at[n, 0:lines, :]))
    for i, j in enumerate(KEEP):
        for ref, peer in ((send_ref, j ^ FIRST), (keep_ref, j)):
            columns = pl.ds(column_of(scalars[0] ^ peer, groups, heads), DH)
            copies.append((k_hbm.at[:, columns], ref.at[i, 0:tokens, :]))
            copies.append((v_hbm.at[:, columns], ref.at[i, tokens : 2 * tokens, :]))
    copies = [pltpu.make_async_copy(s, t, sems.at[n]) for n, (s, t) in enumerate(copies)]
    for copy in copies:
        copy.start()

    wide = 2 * lines
    shape = (own_heads, wide)
    head_ids = lax.broadcasted_iota(jnp.int32, shape, 0)
    line_heads = (lax.broadcasted_iota(jnp.int32, shape, 1) & (lines - 1)) >> shift_of(rows)
    chosen = jnp.concatenate(
        [(head_ids == line_heads + (first >> shift_of(rows))) for _, _, first in slabs], axis=1
    ).astype(jnp.bfloat16)
    shape = (STAT_ROWS, chosen.shape[1])
    own_row = (lax.broadcasted_iota(jnp.int32, shape, 0) & (rows - 1)) == (
        lax.broadcasted_iota(jnp.int32, shape, 1) & (rows - 1)
    )
    shape = (STAT_ROWS, STAT_ROWS)
    gather = lax.broadcasted_iota(jnp.int32, shape, 0) == (
        lax.broadcasted_iota(jnp.int32, shape, 1) >> shift_of(rows)
    )
    for copy in copies[:stat_copies]:
        copy.wait()
    pieces = [piece.astype(jnp.float32) for piece in split_pieces(lse_ref[...])]
    pieces.append(jnp.zeros((STAT_ROWS - PIECES * rows, own_heads), jnp.float32))
    pieces = jnp.concatenate(pieces, axis=0).astype(jnp.bfloat16)
    spread = jnp.dot(pieces, chosen, preferred_element_type=jnp.float32)
    spread = jnp.where(own_row, spread, 0.0).astype(jnp.bfloat16)
    lse_rows_all = jnp.dot(
        gather.astype(jnp.bfloat16), spread, preferred_element_type=jnp.float32
    )
    kind = lax.broadcasted_iota(jnp.int32, (STAT_ROWS, wide), 0)
    for m, (ref, n, first) in enumerate(slabs):
        o_grad = ref[n, lines:wide, :].astype(jnp.float32)
        product = o_grad * o_ref[pl.ds(first, lines), :].astype(jnp.float32)
        dots = jnp.sum(jnp.concatenate([product, product], axis=0).T, axis=0, keepdims=True)
        stats = lse_rows_all[:, m * wide : (m + 1) * wide]
        for k, piece in enumerate(split_pieces(dots)):
            stats = jnp.where(kind == PIECES + k, piece.astype(jnp.float32), stats)
        ref[n, wide:, :] = stats.astype(jnp.bfloat16)
    for copy in copies[stat_copies:]:
        copy.wait()


def pair_starts(scalars, i, tokens):
    first = scalars[3] * KVH
    return [(first + (scalars[0] ^ KEEP[i] ^ other)) * tokens for other in (0, FIRST)]


def pair_keys(ref, tokens):
    return jnp.concatenate([ref[0, 0:tokens, :], ref[1, 0:tokens, :]], axis=0)


def pair_values(ref, tokens):
    return jnp.concatenate([ref[0, tokens : 2 * tokens, :], ref[1, tokens : 2 * tokens, :]], axis=0)


def response_of(scalars, b, groups, rows):
    return ((scalars[3] ^ b) * (groups * rows)) >> shift_of(RESP_LEN)


def lse_rows(size):
    return max(1, size // DH)


def block_slabs(blocks, nears, row_refs):
    out = []
    for at in range(len(blocks)):
        refs = row_refs[at * nears : (at + 1) * nears]
        row_count = refs[0].shape[0] // nears
        out.append([(ref, j, n, j) for n, ref in enumerate(refs) for j in range(row_count)])
    return out


def lines_of(slabs, first, lines):
    return jnp.concatenate([ref[j, first : first + lines, :] for ref, j, _, _ in slabs], axis=0)


def stat_kernel(blocks, nears, rows, tokens, scalars, prompt_end, *refs):
    row_refs, refs = refs[: len(blocks) * nears], refs[len(blocks) * nears :]
    pair_refs, before_refs, lse_ref = refs[: len(KEEP)], refs[len(KEEP) : -1], refs[-1]
    lines = (row_refs[0].shape[1] - STAT_ROWS) // 2
    for ref in before_refs:
        lse_ref[...] = ref[...]
    for b, slabs in zip(blocks, block_slabs(blocks, nears, row_refs)):
        count = len(slabs) * lines
        offset = lax.broadcasted_iota(jnp.int32, (tokens, count), 0)
        q = lines_of(slabs, 0, lines)
        end = prompt_end[response_of(scalars, b, len(slabs), rows)]
        scores = []
        for i, ref in enumerate(pair_refs):
            part = lax.dot_general(
                pair_keys(ref, tokens),
                q,
                (((1,), (1,)), ((), ())),
                preferred_element_type=jnp.float32,
            )
            starts = pair_starts(scalars, i, tokens)
            visible = jnp.concatenate([offset < end - start for start in starts], axis=0)
            scores.append(jnp.where(visible, part * SCALE, MASKED_SCORE))
        scores = jnp.concatenate(scores, axis=0)
        peak = jnp.max(scores, axis=0, keepdims=True)
        total = jnp.sum(jnp.exp(scores - peak), axis=0, keepdims=True)
        lse = peak + jnp.log(total)
        if count < DH:
            lse = jnp.concatenate([lse] * (DH // count), axis=1)
        held = lse_rows(count)
        for k in range(held):
            lse_ref[pl.ds((scalars[3] ^ b) * held + k, 1), :] = lse[:, k * DH : (k + 1) * DH]


def line_values(slabs, lines, first_piece):
    low = lax.broadcasted_iota(jnp.int32, (1, 2 * lines), 1) < lines
    out = []
    for n in range(0, len(slabs), 2):
        held = [
            ref[j, 2 * lines : 2 * lines + STAT_ROWS, :].astype(jnp.float32)
            for ref, j, _, _ in slabs[n : n + 2]
        ]
        total = None
        for k in range(first_piece, first_piece + PIECES):
            piece = jnp.where(low, held[0][k : k + 1], held[1][k : k + 1])
            total = piece if total is None else total + piece
        out.append(total)
    return jnp.concatenate(out, axis=1)


def lse_lines(lse_ref, scalars, blocks, size):
    held = lse_rows(size)
    tiles = []
    for b in blocks:
        for k in range(held):
            tile = lse_ref[pl.ds((scalars[3] ^ b) * held + k, 1), :]
            tiles.append(tile[:, : min(size, DH)])
    return jnp.concatenate(tiles, axis=1)


def steps_of(blocks, all_slabs, lines):
    size = len(all_slabs[0]) * lines
    step = min(len(blocks), STEP_LINES // size)
    for c in range(0, len(blocks), step):
        slabs = [slab for held in all_slabs[c : c + step] for slab in held]
        yield c * size, step * size, blocks[c : c + step], slabs


def part_kernel(blocks, nears, rows, tokens, scalars, prompt_end, *refs):
    row_refs, refs = refs[: len(blocks) * nears], refs[len(blocks) * nears :]
    pair_refs, (lse_ref, prob_ref, dscore_ref, dq_ref) = refs[: len(KEEP)], refs[len(KEEP) :]
    lines = (row_refs[0].shape[1] - STAT_ROWS) // 2
    all_slabs = block_slabs(blocks, nears, row_refs)
    size = len(all_slabs[0]) * lines
    for first, count, held, slabs in steps_of(blocks, all_slabs, lines):
        offset = lax.broadcasted_iota(jnp.int32, (tokens, count), 0)
        q, o_grad = lines_of(slabs, 0, lines), lines_of(slabs, lines, lines)
        dots = line_values(slabs, lines, PIECES)
        lse = lse_lines(lse_ref, scalars, held, size)
        ends = [prompt_end[response_of(scalars, b, len(all_slabs[0]), rows)] for b in held]
        end = jnp.concatenate([jnp.full((1, size), x, jnp.int32) for x in ends], axis=1)
        dq_t = jnp.zeros((DH, count), jnp.float32)
        for i, ref in enumerate(pair_refs):
            k, v = pair_keys(ref, tokens), pair_values(ref, tokens)
            scores = lax.dot_general(
                k, q, (((1,), (1,)), ((), ())), preferred_element_type=jnp.float32
            )
            starts = pair_starts(scalars, i, tokens)
            visible = jnp.concatenate([offset < end - start for start in starts], axis=0)
            prob = jnp.where(visible, jnp.exp(scores * SCALE - lse), 0.0)
            dprob = lax.dot_general(
                v, o_grad, (((1,), (1,)), ((), ())), preferred_element_type=jnp.float32
            )
            dscore = (prob * (dprob - dots)).astype(jnp.bfloat16)
            prob_ref[i, :, first : first + count] = prob.astype(jnp.bfloat16)
            dscore_ref[i, :, first : first + count] = dscore
            dq_t = dq_t + jnp.dot(k.T, dscore, preferred_element_type=jnp.float32)
        dq_ref[:, first : first + count] = dq_t


def token_kernel(blocks, nears, rows, tokens, scalars, resp_len, *refs):
    row_refs, refs = refs[: len(blocks) * nears], refs[len(blocks) * nears :]
    (prob_ref, dscore_ref, dq_ref), refs = refs[:3], refs[3:]
    lse_refs, refs = refs[: len(blocks)], refs[len(blocks) :]
    dkv_refs, (*dq_refs, dk_acc, dv_acc) = refs[: len(KEEP)], refs[len(KEEP) :]
    lines = (row_refs[0].shape[1] - STAT_ROWS) // 2
    all_slabs = block_slabs(blocks, nears, row_refs)
    size = len(all_slabs[0]) * lines
    groups, row_count = len(all_slabs[0]), len(all_slabs[0]) // nears
    lane = lax.broadcasted_iota(jnp.int32, (1, 2 * lines), 1)
    for first, count, held, slabs in steps_of(blocks, all_slabs, lines):
        sources = [(b, slab) for b in held for slab in all_slabs[blocks.index(b)]]
        live = []
        for m in range(0, len(sources), 2):
            row, length = [], []
            for b, (_, _, n, j) in sources[m : m + 2]:
                device = (scalars[3] ^ b) * groups + group_at(scalars, j, n, nears)
                row.append(device * rows & (RESP_LEN - 1))
                length.append(resp_len[response_of(scalars, b, groups, rows)])
            row = jnp.where(lane < lines, row[0], row[1]) + (lane & (rows - 1))
            live.append((row < jnp.where(lane < lines, length[0], length[1])).astype(jnp.int32))
        live = jnp.concatenate(live, axis=1)
        part_lse = [lse_lines(ref, scalars, held, size) for ref in lse_refs]
        self_lse = line_values(slabs, lines, 0)
        peak = functools.reduce(jnp.maximum, part_lse, self_lse)
        total = sum(jnp.exp(x - peak) for x in part_lse) + jnp.exp(self_lse - peak)
        lse = jnp.where(live > 0, peak + jnp.log(total), DEAD_LSE)
        weight = jnp.exp(part_lse[0] - lse)
        weight_t = jnp.broadcast_to(weight, (DH, count)).T
        q, o_grad = (
            (lines_of(slabs, start, lines).astype(jnp.float32) * weight_t).astype(jnp.bfloat16)
            for start in (0, lines)
        )
        for i in range(len(KEEP)):
            dscore, prob = dscore_ref[i, :, first : first + count], prob_ref[i, :, first : first + count]
            dk = jnp.dot(dscore, q, preferred_element_type=jnp.float32) * SCALE
            dv = jnp.dot(prob, o_grad, preferred_element_type=jnp.float32)
            if first > 0:
                dk = dk + dk_acc[i]
                dv = dv + dv_acc[i]
            if first + count < len(blocks) * size:
                dk_acc[i] = dk
                dv_acc[i] = dv
            else:
                for n in range(2):
                    inner = slice(n * tokens, (n + 1) * tokens)
                    dkv_refs[i][n, 0:tokens, :] = dk[inner].astype(jnp.bfloat16)
                    dkv_refs[i][n, tokens : 2 * tokens, :] = dv[inner].astype(jnp.bfloat16)
        dq = (dq_ref[:, first : first + count] * (weight * SCALE)).T.astype(jnp.bfloat16)
        for m, (b, (_, _, n, j)) in enumerate(sources):
            dq_refs[n][blocks.index(b), j] = dq[m * lines : (m + 1) * lines]


def add_query_kernel(nears, *refs):
    own_refs, came_refs, out_refs = refs[:nears], refs[nears:-2], refs[-2:]
    row_count = own_refs[0].shape[0]
    for n in range(nears):
        for j in range(row_count):
            total = own_refs[n][j].astype(jnp.float32)
            for ref in came_refs:
                total = total + ref[n, j].astype(jnp.float32)
            out_refs[min(j, 1)][n] = total.astype(jnp.bfloat16)


def tie_kernel(*refs):
    pass


def write_query_kernel(nears, scalars, *refs):
    slab_refs, out_ref = refs[:-1], refs[-1]
    lines = slab_refs[0].shape[1]
    for j, ref in enumerate(slab_refs):
        for n in range(nears):
            first = pl.multiple_of(group_at(scalars, j, n, nears) * lines, lines)
            out_ref[pl.ds(first, lines), :] = ref[n]


def write_kv_kernel(groups, heads, scalars, *refs):
    pair_refs, (came_ref, out_k_ref, out_v_ref, sems) = refs[: len(KEEP)], refs[len(KEEP) :]
    tokens = out_k_ref.shape[0]
    copies = []
    for i, ref in enumerate(pair_refs):
        for source, other in ((ref.at[0], 0), (came_ref.at[i], FIRST)):
            columns = pl.ds(column_of(scalars[0] ^ KEEP[i] ^ other, groups, heads), DH)
            copies.append((source.at[0:tokens, :], out_k_ref.at[:, columns]))
            copies.append((source.at[tokens : 2 * tokens, :], out_v_ref.at[:, columns]))
    copies = [pltpu.make_async_copy(s, t, sems.at[n]) for n, (s, t) in enumerate(copies)]
    for copy in copies:
        copy.start()
    for copy in copies:
        copy.wait()


def swap(x, axis, distance, size):
    return lax.ppermute(x, axis, [(i, i ^ distance) for i in range(size)])


def swap_pairs(keep, send):
    members = ("row", "near", "head")
    came = swap(send, members, FIRST, KVH)
    pairs = [jnp.stack([keep[i], came[i]]) for i in range(len(KEEP))]
    return [swap(x, members, j, KVH) if j else x for x, j in zip(pairs, KEEP)]


def tie(x, others):
    return pl.pallas_call(
        tie_kernel,
        in_specs=[ANY] * (1 + len(others)),
        out_specs=ANY,
        out_shape=jax.ShapeDtypeStruct(x.shape, x.dtype),
        input_output_aliases={0: 0},
        compiler_params=PARAMS,
    )(x, *others)


def swap_back(pairs, others):
    members = ("row", "near", "head")
    pairs = [swap(x, members, j, KVH) if j else x for x, j in zip(pairs, KEEP)]
    return pairs, swap(tie(jnp.stack([x[1] for x in pairs]), others), members, FIRST, KVH)


def shards(parts, row_count, nears, heads, queries, grad_out, outputs, lse_self, keys, values, resp_len, prompt_end):
    rows = queries.shape[0]
    own_heads = queries.shape[1] // DH
    own_lines = rows * own_heads
    groups = row_count * nears
    lines = own_lines // groups
    tokens = keys.shape[0]
    assert 2 * lines == DH and RESP_LEN % (groups * rows) == 0 and row_count <= 2 and nears <= 2
    row, near = lax.axis_index("row"), lax.axis_index("near")
    member = (row * nears + near) * heads + lax.axis_index("head")
    scalars = jnp.stack([member, row, near, lax.axis_index("part")]).astype(jnp.int32)

    def as_lines(x):
        return x.reshape(rows, own_heads, DH).transpose(1, 0, 2).reshape(own_lines, DH)

    def in_hbm(x):
        return pltpu.with_memory_space_constraint(x, pltpu.HBM)

    half_shape = jax.ShapeDtypeStruct((len(KEEP), 2 * tokens, DH), jnp.bfloat16)
    slab_shape = jax.ShapeDtypeStruct((nears, 2 * lines + STAT_ROWS, DH), jnp.bfloat16)
    *slabs, kv_keep, kv_send = pl.pallas_call(
        functools.partial(pack_kernel, row_count, nears, heads),
        in_specs=[SMEM] + [HBM] * 6,
        out_specs=[VMEM] * (row_count + 2),
        out_shape=[slab_shape] * row_count + [half_shape] * 2,
        scratch_shapes=[
            pltpu.VMEM((own_lines, DH), jnp.bfloat16),
            pltpu.VMEM(lse_self.shape, jnp.float32),
            pltpu.SemaphoreType.DMA((2 + 2 * groups + 4 * len(KEEP),)),
        ],
        compiler_params=PARAMS,
    )(
        scalars,
        in_hbm(as_lines(queries)),
        in_hbm(as_lines(grad_out)),
        in_hbm(as_lines(outputs)),
        in_hbm(lse_self),
        in_hbm(keys),
        in_hbm(values),
    )
    slabs = [swap(x, "row", j, row_count) if j else x for j, x in enumerate(slabs)]
    own_block = jnp.stack([x[n] for n in range(nears) for x in slabs])
    pairs = swap_pairs(kv_keep, kv_send)
    far = [1 << n for n in reversed(range(shift_of(parts)))]
    order, came = [0], [own_block]
    for d in far:
        if d == 1:
            came = came[:1] + [tie(x, pairs[1:]) for x in came[1:]]
        came = came + [swap(x, "part", d, parts) for x in came]
        order = order + [b ^ d for b in order]
    blocks = order

    def row_refs_of(x):
        return [x, swap(x[row_count:], "near", 1, nears)] if nears > 1 else [x]

    def part_lse(held, refs, before):
        return pl.pallas_call(
            functools.partial(stat_kernel, held, nears, rows, tokens),
            in_specs=[SMEM] * 2 + [VMEM] * (len(refs) + len(KEEP) + len(before)),
            out_shape=jax.ShapeDtypeStruct((parts * lse_rows(groups * lines), DH), jnp.float32),
            compiler_params=PARAMS,
        )(scalars, prompt_end, *refs, *pairs, *before)

    row_refs = [ref for x in came[:-1] for ref in row_refs_of(x)]
    lse = [part_lse(blocks[:-1], row_refs, [])]
    last_refs = row_refs_of(tie(came[-1], lse))
    lse = [part_lse(blocks[-1:], last_refs, lse)]
    row_refs = row_refs + last_refs
    every_lse = lse + [swap(lse[0], "part", d, parts) for d in range(1, parts)]

    all_lines = parts * groups * lines
    score_shape = jax.ShapeDtypeStruct((len(KEEP), 2 * tokens, all_lines), jnp.bfloat16)
    prob, dscore, dq = pl.pallas_call(
        functools.partial(part_kernel, blocks, nears, rows, tokens),
        in_specs=[SMEM] * 2 + [VMEM] * (len(row_refs) + len(KEEP) + 1),
        out_specs=[VMEM] * 3,
        out_shape=[score_shape] * 2 + [jax.ShapeDtypeStruct((DH, all_lines), jnp.float32)],
        compiler_params=PARAMS,
    )(scalars, prompt_end, *row_refs, *pairs, *lse)
    dq_shape = jax.ShapeDtypeStruct((parts, row_count, lines, DH), jnp.bfloat16)
    acc = pltpu.VMEM((len(KEEP), 2 * tokens, DH), jnp.float32)
    pair_shape = jax.ShapeDtypeStruct((2, 2 * tokens, DH), jnp.bfloat16)
    outs = pl.pallas_call(
        functools.partial(token_kernel, blocks, nears, rows, tokens),
        in_specs=[SMEM] * 2 + [VMEM] * (len(row_refs) + 3 + parts),
        out_shape=[pair_shape] * len(KEEP) + [dq_shape] * nears,
        scratch_shapes=[acc] * 2,
        compiler_params=PARAMS,
    )(scalars, resp_len, *row_refs, prob, dscore, dq, *every_lse)
    dkv, dq = outs[: len(KEEP)], outs[len(KEEP) :]

    dq = [swap(x, "near", n, nears) if n else x for n, x in enumerate(dq)]
    came = [
        swap(jnp.stack([x[at] for x in dq]), "part", b, parts) for at, b in enumerate(blocks) if b
    ]
    sum_shape = jax.ShapeDtypeStruct((nears, lines, DH), jnp.bfloat16)
    own_sum, sent_sum = pl.pallas_call(
        functools.partial(add_query_kernel, nears),
        in_specs=[VMEM] * (nears + len(came)),
        out_shape=[sum_shape] * 2,
        compiler_params=PARAMS,
    )(*[x[0] for x in dq], *came)
    sums = [own_sum, swap(sent_sum, "row", 1, row_count)][:row_count]
    pairs, came = swap_back(dkv, came)
    out_q = pl.pallas_call(
        functools.partial(write_query_kernel, nears),
        in_specs=[SMEM] + [VMEM] * row_count,
        out_shape=jax.ShapeDtypeStruct((own_lines, DH), jnp.bfloat16),
        compiler_params=PARAMS,
    )(scalars, *sums)
    out_k, out_v = pl.pallas_call(
        functools.partial(write_kv_kernel, groups, heads),
        in_specs=[SMEM] + [VMEM] * (len(KEEP) + 1),
        out_specs=[HBM] * 2,
        out_shape=[
            jax.ShapeDtypeStruct(keys.shape, jnp.bfloat16),
            jax.ShapeDtypeStruct(values.shape, jnp.bfloat16),
        ],
        scratch_shapes=[pltpu.SemaphoreType.DMA((4 * len(KEEP),))],
        compiler_params=PARAMS,
    )(scalars, *pairs, came)
    out_q = out_q.reshape(own_heads, rows, DH).transpose(1, 0, 2).reshape(rows, own_heads * DH)
    return out_q, out_k, out_v


def solution(mesh):
    ctx, heads = mesh.shape["ctx"], mesh.shape["head"]
    groups = KVH // heads
    parts = ctx // groups
    nears = min(2, groups)
    row_count = groups // nears
    fine = Mesh(
        mesh.devices.reshape(parts, row_count, nears, heads), ("part", "row", "near", "head")
    )
    rows = P(("part", "row", "near"), "head")
    tokens = P(("part", "row", "near", "head"), None)
    return jax.shard_map(
        functools.partial(shards, parts, row_count, nears, heads),
        mesh=fine,
        in_specs=(rows, rows, rows, rows, tokens, tokens, P(), P()),
        out_specs=(rows, tokens, tokens),
        check_vma=False,
    )
```

```python
import functools

import jax
import jax.numpy as jnp
from jax import lax
from jax.experimental import pallas as pl
from jax.experimental.pallas import tpu as pltpu
from jax.sharding import Mesh, PartitionSpec as P

DH = 128
KVH = 8
RESP_LEN = 64
SCALE = DH ** (-0.5)
LOG2E = 1.4426950408889634
MASKED_SCORE = -1e30
DEAD_LSE = 1e30
PIECES = 3
STAT_ROWS = 16
STEP_LINES = 1024
PARAMS = pltpu.CompilerParams(vmem_limit_bytes=24 * 1024 * 1024)
ANY = pl.BlockSpec(memory_space=pl.ANY)
HBM = pl.BlockSpec(memory_space=pltpu.HBM)
SMEM = pl.BlockSpec(memory_space=pltpu.SMEM)
VMEM = pl.BlockSpec(memory_space=pltpu.VMEM)

FIRST = 2
KEEP = (0, 1, 4, 5)


def split_pieces(x):
    first = x.astype(jnp.bfloat16)
    rest = x - first.astype(jnp.float32)
    second = rest.astype(jnp.bfloat16)
    third = (rest - second.astype(jnp.float32)).astype(jnp.bfloat16)
    return first, second, third


def shift_of(n):
    assert n & (n - 1) == 0
    return n.bit_length() - 1


def column_of(member, groups, heads):
    head_index, group_index = member & (heads - 1), member >> shift_of(heads)
    return pl.multiple_of((head_index * groups + group_index) * DH, DH)


def group_at(scalars, row_xor, near_xor, nears):
    return (scalars[1] ^ row_xor) * nears + (scalars[2] ^ near_xor)


def pack_kernel(row_count, nears, heads, scalars, q_hbm, o_grad_hbm, o_hbm, lse_hbm, k_hbm, v_hbm, *rest):
    slab_refs, (keep_ref, send_ref, o_ref, lse_ref, sems) = rest[:row_count], rest[row_count:]
    groups = row_count * nears
    rows, own_heads = lse_ref.shape
    lines = o_ref.shape[0] // groups
    tokens = k_hbm.shape[0]
    copies = [(lse_hbm, lse_ref), (o_hbm, o_ref)]
    slabs = []
    for j, ref in enumerate(slab_refs):
        for n in range(nears):
            first = pl.multiple_of(group_at(scalars, j, n, nears) * lines, lines)
            slabs.append((ref, n, first))
            copies.append((o_grad_hbm.at[pl.ds(first, lines), :], ref.at[n, lines : 2 * lines, :]))
    stat_copies = len(copies)
    for ref, n, first in slabs:
        copies.append((q_hbm.at[pl.ds(first, lines), :], ref.at[n, 0:lines, :]))
    for i, j in enumerate(KEEP):
        for ref, peer in ((send_ref, j ^ FIRST), (keep_ref, j)):
            columns = pl.ds(column_of(scalars[0] ^ peer, groups, heads), DH)
            copies.append((k_hbm.at[:, columns], ref.at[i, 0:tokens, :]))
            copies.append((v_hbm.at[:, columns], ref.at[i, tokens : 2 * tokens, :]))
    copies = [pltpu.make_async_copy(s, t, sems.at[n]) for n, (s, t) in enumerate(copies)]
    for copy in copies:
        copy.start()

    wide = 2 * lines
    shape = (own_heads, wide)
    head_ids = lax.broadcasted_iota(jnp.int32, shape, 0)
    line_heads = (lax.broadcasted_iota(jnp.int32, shape, 1) & (lines - 1)) >> shift_of(rows)
    chosen = jnp.concatenate(
        [(head_ids == line_heads + (first >> shift_of(rows))) for _, _, first in slabs], axis=1
    ).astype(jnp.bfloat16)
    shape = (STAT_ROWS, chosen.shape[1])
    own_row = (lax.broadcasted_iota(jnp.int32, shape, 0) & (rows - 1)) == (
        lax.broadcasted_iota(jnp.int32, shape, 1) & (rows - 1)
    )
    shape = (STAT_ROWS, STAT_ROWS)
    gather = lax.broadcasted_iota(jnp.int32, shape, 0) == (
        lax.broadcasted_iota(jnp.int32, shape, 1) >> shift_of(rows)
    )
    for copy in copies[:stat_copies]:
        copy.wait()
    pieces = [piece.astype(jnp.float32) for piece in split_pieces(lse_ref[...])]
    pieces.append(jnp.zeros((STAT_ROWS - PIECES * rows, own_heads), jnp.float32))
    pieces = jnp.concatenate(pieces, axis=0).astype(jnp.bfloat16)
    spread = jnp.dot(pieces, chosen, preferred_element_type=jnp.float32)
    spread = jnp.where(own_row, spread, 0.0).astype(jnp.bfloat16)
    lse_rows_all = jnp.dot(
        gather.astype(jnp.bfloat16), spread, preferred_element_type=jnp.float32
    )
    kind = lax.broadcasted_iota(jnp.int32, (STAT_ROWS, wide), 0)
    for m, (ref, n, first) in enumerate(slabs):
        o_grad = ref[n, lines:wide, :].astype(jnp.float32)
        product = o_grad * o_ref[pl.ds(first, lines), :].astype(jnp.float32)
        dots = jnp.sum(jnp.concatenate([product, product], axis=0).T, axis=0, keepdims=True)
        stats = lse_rows_all[:, m * wide : (m + 1) * wide]
        for k, piece in enumerate(split_pieces(dots)):
            stats = jnp.where(kind == PIECES + k, piece.astype(jnp.float32), stats)
        ref[n, wide:, :] = stats.astype(jnp.bfloat16)
    for copy in copies[stat_copies:]:
        copy.wait()


def pair_starts(scalars, i, tokens):
    first = scalars[3] * KVH
    return [(first + (scalars[0] ^ KEEP[i] ^ other)) * tokens for other in (0, FIRST)]


def pair_keys(ref, tokens):
    return jnp.concatenate([ref[0, 0:tokens, :], ref[1, 0:tokens, :]], axis=0)


def pair_values(ref, tokens):
    return jnp.concatenate([ref[0, tokens : 2 * tokens, :], ref[1, tokens : 2 * tokens, :]], axis=0)


def response_of(scalars, b, groups, rows):
    return ((scalars[3] ^ b) * (groups * rows)) >> shift_of(RESP_LEN)


def prompt_end_of(scalars, response):
    return scalars[4 + response]


def resp_len_of(scalars, response):
    return scalars[4 + (scalars.shape[0] - 4) // 2 + response]


def all_visible(scalars, tokens):
    last = (scalars[3] + 1) * (KVH * tokens)
    seen = prompt_end_of(scalars, 0) >= last
    for response in range(1, (scalars.shape[0] - 4) // 2):
        seen = jnp.logical_and(seen, prompt_end_of(scalars, response) >= last)
    return seen


def in_branches(condition, body):
    pl.when(condition)(functools.partial(body, True))
    pl.when(jnp.logical_not(condition))(functools.partial(body, False))


def lse_rows(size):
    return max(1, size // DH)


def block_slabs(blocks, nears, row_refs):
    out = []
    for at in range(len(blocks)):
        refs = row_refs[at * nears : (at + 1) * nears]
        row_count = refs[0].shape[0] // nears
        out.append([(ref, j, n, j) for n, ref in enumerate(refs) for j in range(row_count)])
    return out


def lines_of(slabs, first, lines):
    return jnp.concatenate([ref[j, first : first + lines, :] for ref, j, _, _ in slabs], axis=0)


def stat_kernel(blocks, nears, rows, tokens, scalars, *refs):
    row_refs, refs = refs[: len(blocks) * nears], refs[len(blocks) * nears :]
    pair_refs, before_refs, lse_ref = refs[: len(KEEP)], refs[len(KEEP) : -1], refs[-1]
    lines = (row_refs[0].shape[1] - STAT_ROWS) // 2
    for ref in before_refs:
        lse_ref[...] = ref[...]

    def body(seen):
        for b, slabs in zip(blocks, block_slabs(blocks, nears, row_refs)):
            count = len(slabs) * lines
            q = lines_of(slabs, 0, lines)
            end = prompt_end_of(scalars, response_of(scalars, b, len(slabs), rows))
            scores = []
            for i, ref in enumerate(pair_refs):
                part = lax.dot_general(
                    pair_keys(ref, tokens),
                    q,
                    (((1,), (1,)), ((), ())),
                    preferred_element_type=jnp.float32,
                )
                if not seen:
                    offset = lax.broadcasted_iota(jnp.int32, (tokens, count), 0)
                    starts = pair_starts(scalars, i, tokens)
                    visible = jnp.concatenate([offset < end - x for x in starts], axis=0)
                    part = jnp.where(visible, part, MASKED_SCORE)
                scores.append(part)
            scores = jnp.concatenate(scores, axis=0)
            peak = jnp.max(scores, axis=0, keepdims=True)
            total = jnp.sum(jnp.exp2((scores - peak) * (SCALE * LOG2E)), axis=0, keepdims=True)
            lse = peak * SCALE + jnp.log(total)
            if count < DH:
                lse = jnp.concatenate([lse] * (DH // count), axis=1)
            held = lse_rows(count)
            for k in range(held):
                lse_ref[pl.ds((scalars[3] ^ b) * held + k, 1), :] = lse[:, k * DH : (k + 1) * DH]

    in_branches(all_visible(scalars, tokens), body)


def line_values(slabs, lines, first_piece):
    low = lax.broadcasted_iota(jnp.int32, (1, 2 * lines), 1) < lines
    out = []
    for n in range(0, len(slabs), 2):
        held = [
            ref[j, 2 * lines : 2 * lines + STAT_ROWS, :].astype(jnp.float32)
            for ref, j, _, _ in slabs[n : n + 2]
        ]
        total = None
        for k in range(first_piece, first_piece + PIECES):
            piece = jnp.where(low, held[0][k : k + 1], held[1][k : k + 1])
            total = piece if total is None else total + piece
        out.append(total)
    return jnp.concatenate(out, axis=1)


def lse_lines(lse_ref, scalars, blocks, size):
    held = lse_rows(size)
    tiles = []
    for b in blocks:
        for k in range(held):
            tile = lse_ref[pl.ds((scalars[3] ^ b) * held + k, 1), :]
            tiles.append(tile[:, : min(size, DH)])
    return jnp.concatenate(tiles, axis=1)


def steps_of(blocks, all_slabs, lines):
    size = len(all_slabs[0]) * lines
    step = min(len(blocks), STEP_LINES // size)
    for c in range(0, len(blocks), step):
        slabs = [slab for held in all_slabs[c : c + step] for slab in held]
        yield c * size, step * size, blocks[c : c + step], slabs


def part_kernel(blocks, nears, rows, tokens, scalars, *refs):
    row_refs, refs = refs[: len(blocks) * nears], refs[len(blocks) * nears :]
    pair_refs, (lse_ref, prob_ref, dscore_ref, dq_ref) = refs[: len(KEEP)], refs[len(KEEP) :]
    lines = (row_refs[0].shape[1] - STAT_ROWS) // 2
    all_slabs = block_slabs(blocks, nears, row_refs)
    size = len(all_slabs[0]) * lines

    def body(seen):
        for first, count, held, slabs in steps_of(blocks, all_slabs, lines):
            q, o_grad = lines_of(slabs, 0, lines), lines_of(slabs, lines, lines)
            dots = line_values(slabs, lines, PIECES)
            lse = lse_lines(lse_ref, scalars, held, size) * LOG2E
            dq_t = jnp.zeros((DH, count), jnp.float32)
            for i, ref in enumerate(pair_refs):
                k, v = pair_keys(ref, tokens), pair_values(ref, tokens)
                scores = lax.dot_general(
                    k, q, (((1,), (1,)), ((), ())), preferred_element_type=jnp.float32
                )
                prob = jnp.exp2(scores * (SCALE * LOG2E) - lse)
                if not seen:
                    responses = [response_of(scalars, b, len(all_slabs[0]), rows) for b in held]
                    end = jnp.concatenate(
                        [jnp.full((1, size), prompt_end_of(scalars, r), jnp.int32) for r in responses],
                        axis=1,
                    )
                    offset = lax.broadcasted_iota(jnp.int32, (tokens, count), 0)
                    starts = pair_starts(scalars, i, tokens)
                    visible = jnp.concatenate([offset < end - x for x in starts], axis=0)
                    prob = jnp.where(visible, prob, 0.0)
                dprob = lax.dot_general(
                    v, o_grad, (((1,), (1,)), ((), ())), preferred_element_type=jnp.float32
                )
                dscore = (prob * (dprob - dots)).astype(jnp.bfloat16)
                prob_ref[i, :, first : first + count] = prob.astype(jnp.bfloat16)
                dscore_ref[i, :, first : first + count] = dscore
                dq_t = dq_t + jnp.dot(k.T, dscore, preferred_element_type=jnp.float32)
            dq_ref[:, first : first + count] = dq_t

    in_branches(all_visible(scalars, tokens), body)


def weight_kernel(blocks, nears, rows, scalars, *refs):
    row_refs, refs = refs[: len(blocks) * nears], refs[len(blocks) * nears :]
    lse_refs, (dq_ref, weight_ref, *dq_refs) = refs[: len(blocks)], refs[len(blocks) :]
    lines = (row_refs[0].shape[1] - STAT_ROWS) // 2
    all_slabs = block_slabs(blocks, nears, row_refs)
    groups = len(all_slabs[0])
    size = groups * lines
    lane = lax.broadcasted_iota(jnp.int32, (1, 2 * lines), 1)
    for first, count, held, slabs in steps_of(blocks, all_slabs, lines):
        sources = [(b, slab) for b in held for slab in all_slabs[blocks.index(b)]]
        live = []
        for m in range(0, len(sources), 2):
            row, length = [], []
            for b, (_, _, n, j) in sources[m : m + 2]:
                device = (scalars[3] ^ b) * groups + group_at(scalars, j, n, nears)
                row.append(device * rows & (RESP_LEN - 1))
                length.append(resp_len_of(scalars, response_of(scalars, b, groups, rows)))
            row = jnp.where(lane < lines, row[0], row[1]) + (lane & (rows - 1))
            live.append((row < jnp.where(lane < lines, length[0], length[1])).astype(jnp.int32))
        live = jnp.concatenate(live, axis=1)
        part_lse = [lse_lines(ref, scalars, held, size) for ref in lse_refs]
        self_lse = line_values(slabs, lines, 0)
        peak = functools.reduce(jnp.maximum, part_lse, self_lse)
        total = sum(jnp.exp(x - peak) for x in part_lse) + jnp.exp(self_lse - peak)
        lse = jnp.where(live > 0, peak + jnp.log(total), DEAD_LSE)
        weight = jnp.exp(part_lse[0] - lse)
        weight_ref[:, first : first + count] = weight
        dq = (dq_ref[:, first : first + count] * (weight * SCALE)).T.astype(jnp.bfloat16)
        for m, (b, (_, _, n, j)) in enumerate(sources):
            source = (scalars[3] ^ b) * (groups // nears) + (scalars[1] ^ j)
            dq_refs[n][source] = dq[m * lines : (m + 1) * lines]


def token_kernel(blocks, nears, tokens, *refs):
    row_refs, refs = refs[: len(blocks) * nears], refs[len(blocks) * nears :]
    (prob_ref, dscore_ref, weight_ref), refs = refs[:3], refs[3:]
    *dkv_refs, dk_acc, dv_acc = refs
    lines = (row_refs[0].shape[1] - STAT_ROWS) // 2
    all_slabs = block_slabs(blocks, nears, row_refs)
    size = len(all_slabs[0]) * lines
    for first, count, held, slabs in steps_of(blocks, all_slabs, lines):
        weight = jnp.broadcast_to(weight_ref[:, first : first + count], (DH, count)).T
        q, o_grad = (
            (lines_of(slabs, start, lines).astype(jnp.float32) * weight).astype(jnp.bfloat16)
            for start in (0, lines)
        )
        for i in range(len(KEEP)):
            dscore, prob = dscore_ref[i, :, first : first + count], prob_ref[i, :, first : first + count]
            dk = jnp.dot(dscore, q, preferred_element_type=jnp.float32) * SCALE
            dv = jnp.dot(prob, o_grad, preferred_element_type=jnp.float32)
            if first > 0:
                dk = dk + dk_acc[i]
                dv = dv + dv_acc[i]
            if first + count < len(blocks) * size:
                dk_acc[i] = dk
                dv_acc[i] = dv
            else:
                for n, out in enumerate(dkv_refs):
                    inner = slice(n * tokens, (n + 1) * tokens)
                    out[i, 0:tokens, :] = dk[inner].astype(jnp.bfloat16)
                    out[i, tokens : 2 * tokens, :] = dv[inner].astype(jnp.bfloat16)


def tie_kernel(*refs):
    pass


def write_kernel(row_count, nears, heads, scalars, *refs):
    dq_ref, pair_refs, (out_q_ref, out_k_ref, out_v_ref, sum_ref, sems) = refs[0], refs[1:-5], refs[-5:]
    groups, lines, tokens = row_count * nears, dq_ref.shape[2], out_k_ref.shape[0]
    copies = []
    for i, ref in enumerate(pair_refs):
        for n, other in enumerate((0, FIRST)):
            columns = pl.ds(column_of(scalars[0] ^ KEEP[i] ^ other, groups, heads), DH)
            copies.append((ref.at[n, 0:tokens, :], out_k_ref.at[:, columns]))
            copies.append((ref.at[n, tokens : 2 * tokens, :], out_v_ref.at[:, columns]))
    for row in range(row_count):
        for n in range(nears):
            first = pl.multiple_of((row * nears + (scalars[2] ^ n)) * lines, lines)
            copies.append((sum_ref.at[row * nears + n], out_q_ref.at[pl.ds(first, lines), :]))
    copies = [pltpu.make_async_copy(s, t, sems.at[n]) for n, (s, t) in enumerate(copies)]
    for copy in copies[:-groups]:
        copy.start()
    for g in range(groups):
        total = dq_ref[g // nears, g % nears].astype(jnp.float32)
        for source in range(g // nears + row_count, dq_ref.shape[0], row_count):
            total = total + dq_ref[source, g % nears].astype(jnp.float32)
        sum_ref[g] = total.astype(jnp.bfloat16)
        copies[g - groups].start()
    for copy in copies:
        copy.wait()


def swap(x, axis, distance, size):
    return lax.ppermute(x, axis, [(i, i ^ distance) for i in range(size)])


def swap_pairs(keep, send):
    members = ("row", "near", "head")
    came = swap(send, members, FIRST, KVH)
    pairs = [jnp.stack([keep[i], came[i]]) for i in range(len(KEEP))]
    return [swap(x, members, j, KVH) if j else x for x, j in zip(pairs, KEEP)]


def tie(x, others, scalars):
    return pl.pallas_call(
        tie_kernel,
        in_specs=[SMEM] + [ANY] * (1 + len(others)),
        out_specs=ANY,
        out_shape=jax.ShapeDtypeStruct(x.shape, x.dtype),
        input_output_aliases={1: 0},
        compiler_params=PARAMS,
    )(scalars, x, *others)


def shards(parts, row_count, nears, heads, queries, grad_out, outputs, lse_self, keys, values, resp_len, prompt_end):
    rows = queries.shape[0]
    own_heads = queries.shape[1] // DH
    own_lines = rows * own_heads
    groups = row_count * nears
    lines = own_lines // groups
    tokens = keys.shape[0]
    assert 2 * lines == DH and RESP_LEN % (groups * rows) == 0 and row_count <= 2 and nears <= 2
    row, near = lax.axis_index("row"), lax.axis_index("near")
    member = (row * nears + near) * heads + lax.axis_index("head")
    place = jnp.stack([member, row, near, lax.axis_index("part")]).astype(jnp.int32)
    scalars = jnp.concatenate([place, prompt_end, resp_len])
    place, scalars = (pltpu.with_memory_space_constraint(x, pltpu.SMEM) for x in (place, scalars))

    def as_lines(x):
        return x.reshape(rows, own_heads, DH).transpose(1, 0, 2).reshape(own_lines, DH)

    def in_hbm(x):
        return pltpu.with_memory_space_constraint(x, pltpu.HBM)

    half_shape = jax.ShapeDtypeStruct((len(KEEP), 2 * tokens, DH), jnp.bfloat16)
    slab_shape = jax.ShapeDtypeStruct((nears, 2 * lines + STAT_ROWS, DH), jnp.bfloat16)
    *slabs, kv_keep, kv_send = pl.pallas_call(
        functools.partial(pack_kernel, row_count, nears, heads),
        in_specs=[SMEM] + [HBM] * 6,
        out_specs=[VMEM] * (row_count + 2),
        out_shape=[slab_shape] * row_count + [half_shape] * 2,
        scratch_shapes=[
            pltpu.VMEM((own_lines, DH), jnp.bfloat16),
            pltpu.VMEM(lse_self.shape, jnp.float32),
            pltpu.SemaphoreType.DMA((2 + 2 * groups + 4 * len(KEEP),)),
        ],
        compiler_params=PARAMS,
    )(
        place,
        in_hbm(as_lines(queries)),
        in_hbm(as_lines(grad_out)),
        in_hbm(as_lines(outputs)),
        in_hbm(lse_self),
        in_hbm(keys),
        in_hbm(values),
    )
    slabs = [swap(x, "row", j, row_count) if j else x for j, x in enumerate(slabs)]
    own_block = jnp.stack([x[n] for n in range(nears) for x in slabs])
    pairs = swap_pairs(kv_keep, kv_send)
    far = [1 << n for n in reversed(range(shift_of(parts)))]

    def row_refs_of(x):
        return [x, swap(x[row_count:], "near", 1, nears)] if nears > 1 else [x]

    row_refs = row_refs_of(own_block)
    blocks, came = [0], [own_block]
    for d in far:
        if d == 1:
            came = came[:1] + [tie(x, pairs[1:], scalars) for x in came[1:]]
        came = came + [swap(x, "part", d, parts) for x in came]
        blocks = blocks + [b ^ d for b in blocks]

    def part_lse(held, refs, before):
        return pl.pallas_call(
            functools.partial(stat_kernel, held, nears, rows, tokens),
            in_specs=[SMEM] + [VMEM] * (len(refs) + len(KEEP) + len(before)),
            out_shape=jax.ShapeDtypeStruct((parts * lse_rows(groups * lines), DH), jnp.float32),
            compiler_params=PARAMS,
        )(scalars, *refs, *pairs, *before)

    row_refs = row_refs + [ref for x in came[1:-1] for ref in row_refs_of(x)]
    lse = [part_lse(blocks[:-1], row_refs, [])]
    last_refs = row_refs_of(tie(came[-1], lse, scalars))
    lse = [part_lse(blocks[-1:], last_refs, lse)]
    row_refs = row_refs + last_refs
    every_lse = lse + [swap(lse[0], "part", d, parts) for d in range(1, parts)]

    all_lines = parts * groups * lines
    score_shape = jax.ShapeDtypeStruct((len(KEEP), 2 * tokens, all_lines), jnp.bfloat16)
    prob, dscore, dq = pl.pallas_call(
        functools.partial(part_kernel, blocks, nears, rows, tokens),
        in_specs=[SMEM] + [VMEM] * (len(row_refs) + len(KEEP) + 1),
        out_specs=[VMEM] * 3,
        out_shape=[score_shape] * 2 + [jax.ShapeDtypeStruct((DH, all_lines), jnp.float32)],
        compiler_params=PARAMS,
    )(scalars, *row_refs, *pairs, *lse)
    dq_shape = jax.ShapeDtypeStruct((parts * row_count, lines, DH), jnp.bfloat16)
    weight, *dq = pl.pallas_call(
        functools.partial(weight_kernel, blocks, nears, rows),
        in_specs=[SMEM] + [VMEM] * (len(row_refs) + parts + 1),
        out_shape=[jax.ShapeDtypeStruct((1, all_lines), jnp.float32)] + [dq_shape] * nears,
        compiler_params=PARAMS,
    )(scalars, *row_refs, *every_lse, dq)
    dq = [swap(x, "near", n, nears) if n else x for n, x in enumerate(dq)]
    acc = pltpu.VMEM((len(KEEP), 2 * tokens, DH), jnp.float32)
    dkv_keep, dkv_send = pl.pallas_call(
        functools.partial(token_kernel, blocks, nears, tokens),
        in_specs=[VMEM] * (len(row_refs) + 3),
        out_shape=[half_shape] * 2,
        scratch_shapes=[acc] * 2,
        compiler_params=PARAMS,
    )(*row_refs, prob, dscore, weight)
    dq = lax.all_to_all(
        jnp.stack(dq, axis=1), ("part", "row"), split_axis=0, concat_axis=0, tiled=True
    )
    pairs = swap_pairs(dkv_keep, dkv_send)
    out_q, out_k, out_v = pl.pallas_call(
        functools.partial(write_kernel, row_count, nears, heads),
        in_specs=[SMEM] + [VMEM] * (1 + len(KEEP)),
        out_specs=[HBM] * 3,
        out_shape=[
            jax.ShapeDtypeStruct((own_lines, DH), jnp.bfloat16),
            jax.ShapeDtypeStruct(keys.shape, jnp.bfloat16),
            jax.ShapeDtypeStruct(values.shape, jnp.bfloat16),
        ],
        scratch_shapes=[
            pltpu.VMEM((groups, lines, DH), jnp.bfloat16),
            pltpu.SemaphoreType.DMA((4 * len(KEEP) + groups,)),
        ],
        compiler_params=PARAMS,
    )(scalars, dq, *pairs)
    out_q = out_q.reshape(own_heads, rows, DH).transpose(1, 0, 2).reshape(rows, own_heads * DH)
    return out_q, out_k, out_v


def solution(mesh):
    ctx, heads = mesh.shape["ctx"], mesh.shape["head"]
    groups = KVH // heads
    parts = ctx // groups
    nears = min(2, groups)
    row_count = groups // nears
    fine = Mesh(
        mesh.devices.reshape(parts, row_count, nears, heads), ("part", "row", "near", "head")
    )
    rows = P(("part", "row", "near"), "head")
    tokens = P(("part", "row", "near", "head"), None)
    return jax.shard_map(
        functools.partial(shards, parts, row_count, nears, heads),
        mesh=fine,
        in_specs=(rows, rows, rows, rows, tokens, tokens, P(), P()),
        out_specs=(rows, tokens, tokens),
        check_vma=False,
    )
```

```python
import functools

import jax
import jax.numpy as jnp
from jax import lax
from jax.experimental import pallas as pl
from jax.experimental.pallas import tpu as pltpu
from jax.sharding import Mesh, PartitionSpec as P

DH = 128
KVH = 8
RESP_LEN = 64
SCALE = DH ** (-0.5)
LOG2E = 1.4426950408889634
MASKED_SCORE = -1e30
DEAD_LSE = 1e30
PIECES = 3
STAT_ROWS = 16
STEP_LINES = 1024
PARAMS = pltpu.CompilerParams(vmem_limit_bytes=24 * 1024 * 1024)
ANY = pl.BlockSpec(memory_space=pl.ANY)
HBM = pl.BlockSpec(memory_space=pltpu.HBM)
VMEM = pl.BlockSpec(memory_space=pltpu.VMEM)

FIRST = 2
KEEP = (0, 1, 4, 5)


def split_pieces(x):
    first = x.astype(jnp.bfloat16)
    rest = x - first.astype(jnp.float32)
    second = rest.astype(jnp.bfloat16)
    third = (rest - second.astype(jnp.float32)).astype(jnp.bfloat16)
    return first, second, third


def shift_of(n):
    assert n & (n - 1) == 0
    return n.bit_length() - 1


def column_of(member, groups, heads):
    head_index, group_index = member & (heads - 1), member >> shift_of(heads)
    return pl.multiple_of((head_index * groups + group_index) * DH, DH)


def place(nears, heads):
    row, near = lax.axis_index("row"), lax.axis_index("near")
    member = (row * nears + near) * heads + lax.axis_index("head")
    return member, row, near, lax.axis_index("part")


def group_at(at, row_xor, near_xor, nears):
    return (at[1] ^ row_xor) * nears + (at[2] ^ near_xor)


def pack_kernel(row_count, nears, heads, q_hbm, o_grad_hbm, o_hbm, lse_hbm, k_hbm, v_hbm, *rest):
    slab_refs, (keep_ref, send_ref, o_ref, lse_ref, sems) = rest[:row_count], rest[row_count:]
    at = place(nears, heads)
    groups = row_count * nears
    rows, own_heads = lse_ref.shape
    lines = o_ref.shape[0] // groups
    tokens = k_hbm.shape[0]
    copies = [(lse_hbm, lse_ref), (o_hbm, o_ref)]
    slabs = []
    for j, ref in enumerate(slab_refs):
        for n in range(nears):
            first = pl.multiple_of(group_at(at, j, n, nears) * lines, lines)
            slabs.append((ref, n, first))
            copies.append((o_grad_hbm.at[pl.ds(first, lines), :], ref.at[n, lines : 2 * lines, :]))
    stat_copies = len(copies)
    for ref, n, first in slabs:
        copies.append((q_hbm.at[pl.ds(first, lines), :], ref.at[n, 0:lines, :]))
    for i, j in enumerate(KEEP):
        for ref, peer in ((send_ref, j ^ FIRST), (keep_ref, j)):
            columns = pl.ds(column_of(at[0] ^ peer, groups, heads), DH)
            copies.append((k_hbm.at[:, columns], ref.at[i, 0:tokens, :]))
            copies.append((v_hbm.at[:, columns], ref.at[i, tokens : 2 * tokens, :]))
    copies = [pltpu.make_async_copy(s, t, sems.at[n]) for n, (s, t) in enumerate(copies)]
    for copy in copies:
        copy.start()

    wide = 2 * lines
    shape = (own_heads, wide)
    head_ids = lax.broadcasted_iota(jnp.int32, shape, 0)
    line_heads = (lax.broadcasted_iota(jnp.int32, shape, 1) & (lines - 1)) >> shift_of(rows)
    chosen = jnp.concatenate(
        [(head_ids == line_heads + (first >> shift_of(rows))) for _, _, first in slabs], axis=1
    ).astype(jnp.bfloat16)
    shape = (STAT_ROWS, chosen.shape[1])
    own_row = (lax.broadcasted_iota(jnp.int32, shape, 0) & (rows - 1)) == (
        lax.broadcasted_iota(jnp.int32, shape, 1) & (rows - 1)
    )
    shape = (STAT_ROWS, STAT_ROWS)
    gather = lax.broadcasted_iota(jnp.int32, shape, 0) == (
        lax.broadcasted_iota(jnp.int32, shape, 1) >> shift_of(rows)
    )
    for copy in copies[:stat_copies]:
        copy.wait()
    pieces = [piece.astype(jnp.float32) for piece in split_pieces(lse_ref[...])]
    pieces.append(jnp.zeros((STAT_ROWS - PIECES * rows, own_heads), jnp.float32))
    pieces = jnp.concatenate(pieces, axis=0).astype(jnp.bfloat16)
    spread = jnp.dot(pieces, chosen, preferred_element_type=jnp.float32)
    spread = jnp.where(own_row, spread, 0.0).astype(jnp.bfloat16)
    lse_rows_all = jnp.dot(
        gather.astype(jnp.bfloat16), spread, preferred_element_type=jnp.float32
    )
    kind = lax.broadcasted_iota(jnp.int32, (STAT_ROWS, wide), 0)
    for m, (ref, n, first) in enumerate(slabs):
        o_grad = ref[n, lines:wide, :].astype(jnp.float32)
        product = o_grad * o_ref[pl.ds(first, lines), :].astype(jnp.float32)
        dots = jnp.sum(jnp.concatenate([product, product], axis=0).T, axis=0, keepdims=True)
        stats = lse_rows_all[:, m * wide : (m + 1) * wide]
        for k, piece in enumerate(split_pieces(dots)):
            stats = jnp.where(kind == PIECES + k, piece.astype(jnp.float32), stats)
        ref[n, wide:, :] = stats.astype(jnp.bfloat16)
    for copy in copies[stat_copies:]:
        copy.wait()


def pair_starts(at, i, tokens):
    first = at[3] * KVH
    return [(first + (at[0] ^ KEEP[i] ^ other)) * tokens for other in (0, FIRST)]


def pair_keys(ref, tokens):
    return jnp.concatenate([ref[0, 0:tokens, :], ref[1, 0:tokens, :]], axis=0)


def pair_values(ref, tokens):
    return jnp.concatenate([ref[0, tokens : 2 * tokens, :], ref[1, tokens : 2 * tokens, :]], axis=0)


def all_visible(at, ends, tokens):
    last = (at[3] + 1) * (KVH * tokens)
    return jnp.min(ends.astype(jnp.float32)) >= last.astype(jnp.float32)


def hide(values, ends, at, i, tokens, hidden):
    offset = lax.broadcasted_iota(jnp.int32, (tokens, values.shape[1]), 0)
    starts = pair_starts(at, i, tokens)
    visible = jnp.concatenate([offset < ends - start for start in starts], axis=0)
    return jnp.where(visible, values, hidden)


def in_branches(condition, body):
    pl.when(condition)(functools.partial(body, True))
    pl.when(jnp.logical_not(condition))(functools.partial(body, False))


def lse_rows(size):
    return max(1, size // DH)


def block_slabs(blocks, nears, row_refs):
    out = []
    for at in range(len(blocks)):
        refs = row_refs[at * nears : (at + 1) * nears]
        row_count = refs[0].shape[0] // nears
        out.append([(ref, j, n, j) for n, ref in enumerate(refs) for j in range(row_count)])
    return out


def lines_of(slabs, first, lines):
    return jnp.concatenate([ref[j, first : first + lines, :] for ref, j, _, _ in slabs], axis=0)


def stat_kernel(blocks, first, nears, heads, tokens, ends_ref, *refs):
    at = place(nears, heads)
    row_refs, refs = refs[: len(blocks) * nears], refs[len(blocks) * nears :]
    pair_refs, before_refs, lse_ref = refs[: len(KEEP)], refs[len(KEEP) : -1], refs[-1]
    lines = (row_refs[0].shape[1] - STAT_ROWS) // 2
    for ref in before_refs:
        lse_ref[...] = ref[...]

    def body(seen):
        for m, (b, slabs) in enumerate(zip(blocks, block_slabs(blocks, nears, row_refs))):
            count = len(slabs) * lines
            q = lines_of(slabs, 0, lines)
            ends = ends_ref[:, first + m * count : first + (m + 1) * count]
            scores = []
            for i, ref in enumerate(pair_refs):
                part = lax.dot_general(
                    pair_keys(ref, tokens),
                    q,
                    (((1,), (1,)), ((), ())),
                    preferred_element_type=jnp.float32,
                )
                scores.append(part if seen else hide(part, ends, at, i, tokens, MASKED_SCORE))
            scores = jnp.concatenate(scores, axis=0)
            peak = jnp.max(scores, axis=0, keepdims=True)
            total = jnp.sum(jnp.exp2((scores - peak) * (SCALE * LOG2E)), axis=0, keepdims=True)
            lse = peak * SCALE + jnp.log(total)
            if count < DH:
                lse = jnp.concatenate([lse] * (DH // count), axis=1)
            held = lse_rows(count)
            for k in range(held):
                lse_ref[pl.ds((at[3] ^ b) * held + k, 1), :] = lse[:, k * DH : (k + 1) * DH]

    in_branches(all_visible(at, ends_ref[...], tokens), body)


def line_values(slabs, lines, first_piece):
    low = lax.broadcasted_iota(jnp.int32, (1, 2 * lines), 1) < lines
    out = []
    for n in range(0, len(slabs), 2):
        held = [
            ref[j, 2 * lines : 2 * lines + STAT_ROWS, :].astype(jnp.float32)
            for ref, j, _, _ in slabs[n : n + 2]
        ]
        total = None
        for k in range(first_piece, first_piece + PIECES):
            piece = jnp.where(low, held[0][k : k + 1], held[1][k : k + 1])
            total = piece if total is None else total + piece
        out.append(total)
    return jnp.concatenate(out, axis=1)


def lse_lines(lse_ref, at, blocks, size):
    held = lse_rows(size)
    tiles = []
    for b in blocks:
        for k in range(held):
            tile = lse_ref[pl.ds((at[3] ^ b) * held + k, 1), :]
            tiles.append(tile[:, : min(size, DH)])
    return jnp.concatenate(tiles, axis=1)


def steps_of(blocks, all_slabs, lines):
    size = len(all_slabs[0]) * lines
    step = min(len(blocks), STEP_LINES // size)
    for c in range(0, len(blocks), step):
        slabs = [slab for held in all_slabs[c : c + step] for slab in held]
        yield c * size, step * size, blocks[c : c + step], slabs


def part_kernel(blocks, nears, heads, tokens, ends_ref, *refs):
    at = place(nears, heads)
    row_refs, refs = refs[: len(blocks) * nears], refs[len(blocks) * nears :]
    pair_refs, (lse_ref, prob_ref, dscore_ref, dq_ref) = refs[: len(KEEP)], refs[len(KEEP) :]
    lines = (row_refs[0].shape[1] - STAT_ROWS) // 2
    all_slabs = block_slabs(blocks, nears, row_refs)
    size = len(all_slabs[0]) * lines

    def body(seen):
        for first, count, held, slabs in steps_of(blocks, all_slabs, lines):
            q, o_grad = lines_of(slabs, 0, lines), lines_of(slabs, lines, lines)
            dots = line_values(slabs, lines, PIECES)
            lse = lse_lines(lse_ref, at, held, size) * LOG2E
            lanes = slice(first, first + count)
            dq_t = jnp.zeros((DH, count), jnp.float32)
            for i, ref in enumerate(pair_refs):
                k, v = pair_keys(ref, tokens), pair_values(ref, tokens)
                scores = lax.dot_general(
                    k, q, (((1,), (1,)), ((), ())), preferred_element_type=jnp.float32
                )
                prob = jnp.exp2(scores * (SCALE * LOG2E) - lse)
                if not seen:
                    prob = hide(prob, ends_ref[:, lanes], at, i, tokens, 0.0)
                dprob = lax.dot_general(
                    v, o_grad, (((1,), (1,)), ((), ())), preferred_element_type=jnp.float32
                )
                dscore = (prob * (dprob - dots)).astype(jnp.bfloat16)
                prob_ref[i, :, lanes] = prob.astype(jnp.bfloat16)
                dscore_ref[i, :, lanes] = dscore
                dq_t = dq_t + jnp.dot(k.T, dscore, preferred_element_type=jnp.float32)
            dq_ref[:, lanes] = dq_t

    in_branches(all_visible(at, ends_ref[...], tokens), body)


def weight_kernel(blocks, nears, heads, live_ref, *refs):
    at = place(nears, heads)
    row_refs, refs = refs[: len(blocks) * nears], refs[len(blocks) * nears :]
    lse_refs, (dq_ref, weight_ref, *dq_refs) = refs[: len(blocks)], refs[len(blocks) :]
    lines = (row_refs[0].shape[1] - STAT_ROWS) // 2
    all_slabs = block_slabs(blocks, nears, row_refs)
    size = len(all_slabs[0]) * lines
    for first, count, held, slabs in steps_of(blocks, all_slabs, lines):
        lanes = slice(first, first + count)
        part_lse = [lse_lines(ref, at, held, size) for ref in lse_refs]
        self_lse = line_values(slabs, lines, 0)
        peak = functools.reduce(jnp.maximum, part_lse, self_lse)
        total = sum(jnp.exp(x - peak) for x in part_lse) + jnp.exp(self_lse - peak)
        lse = jnp.where(live_ref[:, lanes] > 0, peak + jnp.log(total), DEAD_LSE)
        weight = jnp.exp(part_lse[0] - lse)
        weight_ref[:, lanes] = weight
        dq = (dq_ref[:, lanes] * (weight * SCALE)).T.astype(jnp.bfloat16)
        sources = [(b, slab) for b in held for slab in all_slabs[blocks.index(b)]]
        for m, (b, (_, _, n, j)) in enumerate(sources):
            dq_refs[n][blocks.index(b), j] = dq[m * lines : (m + 1) * lines]


def token_kernel(blocks, nears, tokens, *refs):
    row_refs, refs = refs[: len(blocks) * nears], refs[len(blocks) * nears :]
    (prob_ref, dscore_ref, weight_ref), refs = refs[:3], refs[3:]
    dkv_refs, (dk_acc, dv_acc) = refs[: len(KEEP)], refs[len(KEEP) :]
    lines = (row_refs[0].shape[1] - STAT_ROWS) // 2
    all_slabs = block_slabs(blocks, nears, row_refs)
    size = len(all_slabs[0]) * lines
    for first, count, held, slabs in steps_of(blocks, all_slabs, lines):
        weight = jnp.broadcast_to(weight_ref[:, first : first + count], (DH, count)).T
        q, o_grad = (
            (lines_of(slabs, start, lines).astype(jnp.float32) * weight).astype(jnp.bfloat16)
            for start in (0, lines)
        )
        for i in range(len(KEEP)):
            dscore, prob = dscore_ref[i, :, first : first + count], prob_ref[i, :, first : first + count]
            dk = jnp.dot(dscore, q, preferred_element_type=jnp.float32) * SCALE
            dv = jnp.dot(prob, o_grad, preferred_element_type=jnp.float32)
            if first > 0:
                dk = dk + dk_acc[i]
                dv = dv + dv_acc[i]
            if first + count < len(blocks) * size:
                dk_acc[i] = dk
                dv_acc[i] = dv
            else:
                for n in range(2):
                    inner = slice(n * tokens, (n + 1) * tokens)
                    dkv_refs[i][n, 0:tokens, :] = dk[inner].astype(jnp.bfloat16)
                    dkv_refs[i][n, tokens : 2 * tokens, :] = dv[inner].astype(jnp.bfloat16)


def add_query_kernel(nears, *refs):
    own_refs, came_refs, out_refs = refs[:nears], refs[nears:-2], refs[-2:]
    for n in range(nears):
        for j in range(own_refs[0].shape[1]):
            total = own_refs[n][0, j].astype(jnp.float32)
            for ref in came_refs:
                total = total + ref[n, j].astype(jnp.float32)
            out_refs[min(j, 1)][n] = total.astype(jnp.bfloat16)


def tie_kernel(*refs):
    pass


def write_kernel(nears, heads, *refs):
    at = place(nears, heads)
    slab_refs, refs = refs[: -len(KEEP) - 5], refs[-len(KEEP) - 5 :]
    pair_refs, (came_ref, out_q_ref, out_k_ref, out_v_ref, sems) = refs[: len(KEEP)], refs[len(KEEP) :]
    groups, lines, tokens = len(slab_refs) * nears, slab_refs[0].shape[1], out_k_ref.shape[0]
    copies = []
    for i, ref in enumerate(pair_refs):
        for source, other in ((ref.at[0], 0), (came_ref.at[i], FIRST)):
            columns = pl.ds(column_of(at[0] ^ KEEP[i] ^ other, groups, heads), DH)
            copies.append((source.at[0:tokens, :], out_k_ref.at[:, columns]))
            copies.append((source.at[tokens : 2 * tokens, :], out_v_ref.at[:, columns]))
    for j, ref in enumerate(slab_refs):
        for n in range(nears):
            first = pl.multiple_of(group_at(at, j, n, nears) * lines, lines)
            copies.append((ref.at[n], out_q_ref.at[pl.ds(first, lines), :]))
    copies = [pltpu.make_async_copy(s, t, sems.at[n]) for n, (s, t) in enumerate(copies)]
    for copy in copies:
        copy.start()
    for copy in copies:
        copy.wait()


def swap(x, axis, distance, size):
    return lax.ppermute(x, axis, [(i, i ^ distance) for i in range(size)])


def swap_pairs(keep, send):
    members = ("row", "near", "head")
    came = swap(send, members, FIRST, KVH)
    pairs = [jnp.stack([keep[i], came[i]]) for i in range(len(KEEP))]
    return [swap(x, members, j, KVH) if j else x for x, j in zip(pairs, KEEP)]


def tie(x, others):
    return pl.pallas_call(
        tie_kernel,
        in_specs=[ANY] * (1 + len(others)),
        out_specs=ANY,
        out_shape=jax.ShapeDtypeStruct(x.shape, x.dtype),
        input_output_aliases={0: 0},
        compiler_params=PARAMS,
    )(x, *others)


def swap_back(pairs, after):
    members = ("row", "near", "head")
    pairs = [pairs[0]] + [
        tie(swap(x, members, j, KVH), after) for x, j in zip(pairs[1:], KEEP[1:])
    ]
    return [*pairs, swap(jnp.stack([x[1] for x in pairs]), members, FIRST, KVH)]


def line_limits(parts, row_count, nears, rows, lines, resp_len, prompt_end):
    line = lax.broadcasted_iota(jnp.int32, (1, parts * nears * row_count * lines), 1)
    slab = line >> shift_of(lines)
    row_xor = slab & (row_count - 1)
    near_xor = (slab >> shift_of(row_count)) & (nears - 1)
    place_of_block = slab >> shift_of(row_count * nears)
    block, bits = jnp.zeros_like(line), shift_of(parts)
    for k in range(bits):
        block = block | (((place_of_block >> k) & 1) << (bits - 1 - k))
    device = (lax.axis_index("part") ^ block) * row_count + (lax.axis_index("row") ^ row_xor)
    device = device * nears + (lax.axis_index("near") ^ near_xor)
    row = device * rows + (line & (rows - 1))
    ends, lengths = jnp.zeros_like(row), jnp.zeros_like(row)
    for r in range(resp_len.shape[0]):
        own = row >> shift_of(RESP_LEN) == r
        ends, lengths = jnp.where(own, prompt_end[r], ends), jnp.where(own, resp_len[r], lengths)
    return ends, ((row & (RESP_LEN - 1)) < lengths).astype(jnp.int32)


def shards(parts, row_count, nears, heads, queries, grad_out, outputs, lse_self, keys, values, resp_len, prompt_end):
    rows = queries.shape[0]
    own_heads = queries.shape[1] // DH
    own_lines = rows * own_heads
    groups = row_count * nears
    lines = own_lines // groups
    tokens = keys.shape[0]
    assert 2 * lines == DH and RESP_LEN % (groups * rows) == 0 and row_count <= 2 and nears <= 2

    def as_lines(x):
        return x.reshape(rows, own_heads, DH).transpose(1, 0, 2).reshape(own_lines, DH)

    def in_hbm(x):
        return pltpu.with_memory_space_constraint(x, pltpu.HBM)

    half_shape = jax.ShapeDtypeStruct((len(KEEP), 2 * tokens, DH), jnp.bfloat16)
    slab_shape = jax.ShapeDtypeStruct((nears, 2 * lines + STAT_ROWS, DH), jnp.bfloat16)
    *slabs, kv_keep, kv_send = pl.pallas_call(
        functools.partial(pack_kernel, row_count, nears, heads),
        in_specs=[HBM] * 6,
        out_specs=[VMEM] * (row_count + 2),
        out_shape=[slab_shape] * row_count + [half_shape] * 2,
        scratch_shapes=[
            pltpu.VMEM((own_lines, DH), jnp.bfloat16),
            pltpu.VMEM(lse_self.shape, jnp.float32),
            pltpu.SemaphoreType.DMA((2 + 2 * groups + 4 * len(KEEP),)),
        ],
        compiler_params=PARAMS,
    )(
        in_hbm(as_lines(queries)),
        in_hbm(as_lines(grad_out)),
        in_hbm(as_lines(outputs)),
        in_hbm(lse_self),
        in_hbm(keys),
        in_hbm(values),
    )
    slabs = [swap(x, "row", j, row_count) if j else x for j, x in enumerate(slabs)]
    own_block = jnp.stack([x[n] for n in range(nears) for x in slabs])
    pairs = swap_pairs(kv_keep, kv_send)
    far = [1 << n for n in reversed(range(shift_of(parts)))]

    def row_refs_of(x):
        return [x, swap(x[row_count:], "near", 1, nears)] if nears > 1 else [x]

    blocks, came = [0], [own_block]
    row_refs = row_refs_of(tie(own_block, pairs[1:2]))
    for d in far:
        if d == 1:
            came = came[:1] + [tie(x, pairs[1:] + row_refs[1:]) for x in came[1:]]
        came = came + [swap(x, "part", d, parts) for x in came]
        blocks = blocks + [b ^ d for b in blocks]
    ends, live = line_limits(parts, row_count, nears, rows, lines, resp_len, prompt_end)

    def part_lse(held, first, refs, before):
        return pl.pallas_call(
            functools.partial(stat_kernel, held, first, nears, heads, tokens),
            in_specs=[VMEM] * (1 + len(refs) + len(KEEP) + len(before)),
            out_shape=jax.ShapeDtypeStruct((parts * lse_rows(groups * lines), DH), jnp.float32),
            compiler_params=PARAMS,
        )(ends, *refs, *pairs, *before)

    row_refs = row_refs + [ref for x in came[1:-1] for ref in row_refs_of(x)]
    lse = [part_lse(blocks[:-1], 0, row_refs, [])]
    last_refs = row_refs_of(tie(came[-1], lse))
    lse = [part_lse(blocks[-1:], (parts - 1) * groups * lines, last_refs, lse)]
    row_refs = row_refs + last_refs
    every_lse = lse + [swap(lse[0], "part", d, parts) for d in range(1, parts)]

    all_lines = parts * groups * lines
    score_shape = jax.ShapeDtypeStruct((len(KEEP), 2 * tokens, all_lines), jnp.bfloat16)
    prob, dscore, dq = pl.pallas_call(
        functools.partial(part_kernel, blocks, nears, heads, tokens),
        in_specs=[VMEM] * (1 + len(row_refs) + len(KEEP) + 1),
        out_specs=[VMEM] * 3,
        out_shape=[score_shape] * 2 + [jax.ShapeDtypeStruct((DH, all_lines), jnp.float32)],
        compiler_params=PARAMS,
    )(ends, *row_refs, *pairs, *lse)
    dq_shape = jax.ShapeDtypeStruct((parts, row_count, lines, DH), jnp.bfloat16)
    weight, *dq = pl.pallas_call(
        functools.partial(weight_kernel, blocks, nears, heads),
        in_specs=[VMEM] * (1 + len(row_refs) + parts + 1),
        out_shape=[jax.ShapeDtypeStruct((1, all_lines), jnp.float32)] + [dq_shape] * nears,
        compiler_params=PARAMS,
    )(live, *row_refs, *every_lse, dq)
    dq = [swap(x, "near", n, nears) if n else x for n, x in enumerate(dq)]
    acc = pltpu.VMEM((len(KEEP), 2 * tokens, DH), jnp.float32)
    dkv = pl.pallas_call(
        functools.partial(token_kernel, blocks, nears, tokens),
        in_specs=[VMEM] * (len(row_refs) + 3),
        out_shape=[jax.ShapeDtypeStruct((2, 2 * tokens, DH), jnp.bfloat16)] * len(KEEP),
        scratch_shapes=[acc] * 2,
        compiler_params=PARAMS,
    )(*row_refs, prob, dscore, weight)
    from_parts = [
        swap(jnp.stack([x[at] for x in dq]), "part", b, parts) for at, b in enumerate(blocks) if b
    ]
    sum_shape = jax.ShapeDtypeStruct((nears, lines, DH), jnp.bfloat16)
    sums = pl.pallas_call(
        functools.partial(add_query_kernel, nears),
        in_specs=[VMEM] * (nears + len(from_parts)),
        out_shape=[sum_shape] * 2,
        compiler_params=PARAMS,
    )(*dq, *from_parts)
    pairs = swap_back(dkv, sums[:1])
    sums = [swap(x, "row", j, row_count) if j else x for j, x in enumerate(sums[:row_count])]
    out_q, out_k, out_v = pl.pallas_call(
        functools.partial(write_kernel, nears, heads),
        in_specs=[VMEM] * (row_count + len(pairs)),
        out_specs=[HBM] * 3,
        out_shape=[
            jax.ShapeDtypeStruct((own_lines, DH), jnp.bfloat16),
            jax.ShapeDtypeStruct(keys.shape, jnp.bfloat16),
            jax.ShapeDtypeStruct(values.shape, jnp.bfloat16),
        ],
        scratch_shapes=[pltpu.SemaphoreType.DMA((4 * len(KEEP) + groups,))],
        compiler_params=PARAMS,
    )(*sums, *pairs)
    out_q = out_q.reshape(own_heads, rows, DH).transpose(1, 0, 2).reshape(rows, own_heads * DH)
    return out_q, out_k, out_v


def solution(mesh):
    ctx, heads = mesh.shape["ctx"], mesh.shape["head"]
    groups = KVH // heads
    parts = ctx // groups
    nears = min(2, groups)
    row_count = groups // nears
    fine = Mesh(
        mesh.devices.reshape(parts, row_count, nears, heads), ("part", "row", "near", "head")
    )
    rows = P(("part", "row", "near"), "head")
    tokens = P(("part", "row", "near", "head"), None)
    return jax.shard_map(
        functools.partial(shards, parts, row_count, nears, heads),
        mesh=fine,
        in_specs=(rows, rows, rows, rows, tokens, tokens, P(), P()),
        out_specs=(rows, tokens, tokens),
        check_vma=False,
    )
```

```python
import functools

import jax
import jax.numpy as jnp
from jax import lax
from jax.experimental import pallas as pl
from jax.experimental.pallas import tpu as pltpu
from jax.sharding import Mesh, PartitionSpec as P

DH = 128
KVH = 8
RESP_LEN = 64
SCALE = DH ** (-0.5)
LOG2E = 1.4426950408889634
MASKED_SCORE = -1e30
DEAD_LSE = 1e30
PIECES = 3
STAT_ROWS = 16
STEP_LINES = 1024
PARAMS = pltpu.CompilerParams(vmem_limit_bytes=24 * 1024 * 1024)
ANY = pl.BlockSpec(memory_space=pl.ANY)
HBM = pl.BlockSpec(memory_space=pltpu.HBM)
VMEM = pl.BlockSpec(memory_space=pltpu.VMEM)

FIRST = 2
KEEP = (0, 1, 4, 5)


def split_pieces(x):
    first = x.astype(jnp.bfloat16)
    rest = x - first.astype(jnp.float32)
    second = rest.astype(jnp.bfloat16)
    third = (rest - second.astype(jnp.float32)).astype(jnp.bfloat16)
    return first, second, third


def shift_of(n):
    assert n & (n - 1) == 0
    return n.bit_length() - 1


def column_of(member, groups, heads):
    head_index, group_index = member & (heads - 1), member >> shift_of(heads)
    return pl.multiple_of((head_index * groups + group_index) * DH, DH)


def place(nears, heads):
    row, near = lax.axis_index("row"), lax.axis_index("near")
    member = (row * nears + near) * heads + lax.axis_index("head")
    return member, row, near, lax.axis_index("part")


def group_at(at, row_xor, near_xor, nears):
    return (at[1] ^ row_xor) * nears + (at[2] ^ near_xor)


def pack_kernel(row_count, nears, heads, q_hbm, o_grad_hbm, o_hbm, lse_hbm, k_hbm, v_hbm, *rest):
    slab_refs, (keep_ref, send_ref, o_ref, lse_ref, sems) = rest[:row_count], rest[row_count:]
    at = place(nears, heads)
    groups = row_count * nears
    rows, own_heads = lse_ref.shape
    lines = o_ref.shape[0] // groups
    tokens = k_hbm.shape[0]
    copies = [(lse_hbm, lse_ref), (o_hbm, o_ref)]
    slabs = []
    for j, ref in enumerate(slab_refs):
        for n in range(nears):
            first = pl.multiple_of(group_at(at, j, n, nears) * lines, lines)
            slabs.append((ref, n, first))
            copies.append((o_grad_hbm.at[pl.ds(first, lines), :], ref.at[n, lines : 2 * lines, :]))
    stat_copies = len(copies)
    for ref, n, first in slabs:
        copies.append((q_hbm.at[pl.ds(first, lines), :], ref.at[n, 0:lines, :]))
    for i, j in enumerate(KEEP):
        for ref, peer in ((send_ref, j ^ FIRST), (keep_ref, j)):
            columns = pl.ds(column_of(at[0] ^ peer, groups, heads), DH)
            copies.append((k_hbm.at[:, columns], ref.at[i, 0:tokens, :]))
            copies.append((v_hbm.at[:, columns], ref.at[i, tokens : 2 * tokens, :]))
    copies = [pltpu.make_async_copy(s, t, sems.at[n]) for n, (s, t) in enumerate(copies)]
    for copy in copies:
        copy.start()

    wide = 2 * lines
    shape = (own_heads, wide)
    head_ids = lax.broadcasted_iota(jnp.int32, shape, 0)
    line_heads = (lax.broadcasted_iota(jnp.int32, shape, 1) & (lines - 1)) >> shift_of(rows)
    chosen = jnp.concatenate(
        [(head_ids == line_heads + (first >> shift_of(rows))) for _, _, first in slabs], axis=1
    ).astype(jnp.bfloat16)
    shape = (STAT_ROWS, chosen.shape[1])
    own_row = (lax.broadcasted_iota(jnp.int32, shape, 0) & (rows - 1)) == (
        lax.broadcasted_iota(jnp.int32, shape, 1) & (rows - 1)
    )
    shape = (STAT_ROWS, STAT_ROWS)
    gather = lax.broadcasted_iota(jnp.int32, shape, 0) == (
        lax.broadcasted_iota(jnp.int32, shape, 1) >> shift_of(rows)
    )
    for copy in copies[:stat_copies]:
        copy.wait()
    pieces = [piece.astype(jnp.float32) for piece in split_pieces(lse_ref[...])]
    pieces.append(jnp.zeros((STAT_ROWS - PIECES * rows, own_heads), jnp.float32))
    pieces = jnp.concatenate(pieces, axis=0).astype(jnp.bfloat16)
    spread = jnp.dot(pieces, chosen, preferred_element_type=jnp.float32)
    spread = jnp.where(own_row, spread, 0.0).astype(jnp.bfloat16)
    lse_rows_all = jnp.dot(
        gather.astype(jnp.bfloat16), spread, preferred_element_type=jnp.float32
    )
    kind = lax.broadcasted_iota(jnp.int32, (STAT_ROWS, wide), 0)
    for m, (ref, n, first) in enumerate(slabs):
        o_grad = ref[n, lines:wide, :].astype(jnp.float32)
        product = o_grad * o_ref[pl.ds(first, lines), :].astype(jnp.float32)
        dots = jnp.sum(jnp.concatenate([product, product], axis=0).T, axis=0, keepdims=True)
        stats = lse_rows_all[:, m * wide : (m + 1) * wide]
        for k, piece in enumerate(split_pieces(dots)):
            stats = jnp.where(kind == PIECES + k, piece.astype(jnp.float32), stats)
        ref[n, wide:, :] = stats.astype(jnp.bfloat16)
    for copy in copies[stat_copies:]:
        copy.wait()


def pair_starts(at, i, tokens):
    first = at[3] * KVH
    return [(first + (at[0] ^ KEEP[i] ^ other)) * tokens for other in (0, FIRST)]


def pair_keys(ref, tokens):
    return jnp.concatenate([ref[0, 0:tokens, :], ref[1, 0:tokens, :]], axis=0)


def pair_values(ref, tokens):
    return jnp.concatenate([ref[0, tokens : 2 * tokens, :], ref[1, tokens : 2 * tokens, :]], axis=0)


def all_visible(at, ends, tokens):
    last = (at[3] + 1) * (KVH * tokens)
    return jnp.min(ends.astype(jnp.float32)) >= last.astype(jnp.float32)


def hide(values, ends, at, i, tokens, hidden):
    offset = lax.broadcasted_iota(jnp.int32, (tokens, values.shape[1]), 0)
    starts = pair_starts(at, i, tokens)
    visible = jnp.concatenate([offset < ends - start for start in starts], axis=0)
    return jnp.where(visible, values, hidden)


def in_branches(condition, body):
    pl.when(condition)(functools.partial(body, True))
    pl.when(jnp.logical_not(condition))(functools.partial(body, False))


def lse_rows(size):
    return max(1, size // DH)


def block_slabs(blocks, nears, row_refs):
    out = []
    for at in range(len(blocks)):
        refs = row_refs[at * nears : (at + 1) * nears]
        row_count = refs[0].shape[0] // nears
        out.append([(ref, j, n, j) for n, ref in enumerate(refs) for j in range(row_count)])
    return out


def lines_of(slabs, first, lines):
    return jnp.concatenate([ref[j, first : first + lines, :] for ref, j, _, _ in slabs], axis=0)


def stat_kernel(blocks, first, nears, heads, tokens, ends_ref, *refs):
    at = place(nears, heads)
    row_refs, refs = refs[: len(blocks) * nears], refs[len(blocks) * nears :]
    pair_refs, before_refs, lse_ref = refs[: len(KEEP)], refs[len(KEEP) : -1], refs[-1]
    lines = (row_refs[0].shape[1] - STAT_ROWS) // 2
    for ref in before_refs:
        lse_ref[...] = ref[...]

    def body(seen):
        for m, (b, slabs) in enumerate(zip(blocks, block_slabs(blocks, nears, row_refs))):
            count = len(slabs) * lines
            q = lines_of(slabs, 0, lines)
            ends = ends_ref[:, first + m * count : first + (m + 1) * count]
            scores = []
            for i, ref in enumerate(pair_refs):
                part = lax.dot_general(
                    pair_keys(ref, tokens),
                    q,
                    (((1,), (1,)), ((), ())),
                    preferred_element_type=jnp.float32,
                )
                scores.append(part if seen else hide(part, ends, at, i, tokens, MASKED_SCORE))
            scores = jnp.concatenate(scores, axis=0)
            peak = jnp.max(scores, axis=0, keepdims=True)
            total = jnp.sum(jnp.exp2((scores - peak) * (SCALE * LOG2E)), axis=0, keepdims=True)
            lse = peak * SCALE + jnp.log(total)
            if count < DH:
                lse = jnp.concatenate([lse] * (DH // count), axis=1)
            held = lse_rows(count)
            for k in range(held):
                lse_ref[pl.ds((at[3] ^ b) * held + k, 1), :] = lse[:, k * DH : (k + 1) * DH]

    in_branches(all_visible(at, ends_ref[...], tokens), body)


def line_values(slabs, lines, first_piece):
    low = lax.broadcasted_iota(jnp.int32, (1, 2 * lines), 1) < lines
    out = []
    for n in range(0, len(slabs), 2):
        held = [
            ref[j, 2 * lines : 2 * lines + STAT_ROWS, :].astype(jnp.float32)
            for ref, j, _, _ in slabs[n : n + 2]
        ]
        total = None
        for k in range(first_piece, first_piece + PIECES):
            piece = jnp.where(low, held[0][k : k + 1], held[1][k : k + 1])
            total = piece if total is None else total + piece
        out.append(total)
    return jnp.concatenate(out, axis=1)


def lse_lines(lse_ref, at, blocks, size):
    held = lse_rows(size)
    tiles = []
    for b in blocks:
        for k in range(held):
            tile = lse_ref[pl.ds((at[3] ^ b) * held + k, 1), :]
            tiles.append(tile[:, : min(size, DH)])
    return jnp.concatenate(tiles, axis=1)


def steps_of(blocks, all_slabs, lines):
    size = len(all_slabs[0]) * lines
    step = min(len(blocks), STEP_LINES // size)
    for c in range(0, len(blocks), step):
        slabs = [slab for held in all_slabs[c : c + step] for slab in held]
        yield c * size, step * size, blocks[c : c + step], slabs


def part_kernel(blocks, nears, heads, tokens, ends_ref, *refs):
    at = place(nears, heads)
    row_refs, refs = refs[: len(blocks) * nears], refs[len(blocks) * nears :]
    pair_refs, (lse_ref, prob_ref, dscore_ref, dq_ref) = refs[: len(KEEP)], refs[len(KEEP) :]
    lines = (row_refs[0].shape[1] - STAT_ROWS) // 2
    all_slabs = block_slabs(blocks, nears, row_refs)
    size = len(all_slabs[0]) * lines

    def body(seen):
        for first, count, held, slabs in steps_of(blocks, all_slabs, lines):
            q, o_grad = lines_of(slabs, 0, lines), lines_of(slabs, lines, lines)
            dots = line_values(slabs, lines, PIECES)
            lse = lse_lines(lse_ref, at, held, size) * LOG2E
            lanes = slice(first, first + count)
            dq_t = jnp.zeros((DH, count), jnp.float32)
            for i, ref in enumerate(pair_refs):
                k, v = pair_keys(ref, tokens), pair_values(ref, tokens)
                scores = lax.dot_general(
                    k, q, (((1,), (1,)), ((), ())), preferred_element_type=jnp.float32
                )
                prob = jnp.exp2(scores * (SCALE * LOG2E) - lse)
                if not seen:
                    prob = hide(prob, ends_ref[:, lanes], at, i, tokens, 0.0)
                dprob = lax.dot_general(
                    v, o_grad, (((1,), (1,)), ((), ())), preferred_element_type=jnp.float32
                )
                dscore = (prob * (dprob - dots)).astype(jnp.bfloat16)
                prob_ref[i, :, lanes] = prob.astype(jnp.bfloat16)
                dscore_ref[i, :, lanes] = dscore
                dq_t = dq_t + jnp.dot(k.T, dscore, preferred_element_type=jnp.float32)
            dq_ref[:, lanes] = dq_t

    in_branches(all_visible(at, ends_ref[...], tokens), body)


def token_kernel(blocks, nears, heads, tokens, live_ref, *refs):
    at = place(nears, heads)
    row_refs, refs = refs[: len(blocks) * nears], refs[len(blocks) * nears :]
    (prob_ref, dscore_ref, dq_ref), refs = refs[:3], refs[3:]
    lse_refs, refs = refs[: len(blocks)], refs[len(blocks) :]
    dkv_refs, (*dq_refs, dk_acc, dv_acc) = refs[: len(KEEP)], refs[len(KEEP) :]
    lines = (row_refs[0].shape[1] - STAT_ROWS) // 2
    all_slabs = block_slabs(blocks, nears, row_refs)
    size = len(all_slabs[0]) * lines
    for first, count, held, slabs in steps_of(blocks, all_slabs, lines):
        lanes = slice(first, first + count)
        part_lse = [lse_lines(ref, at, held, size) for ref in lse_refs]
        self_lse = line_values(slabs, lines, 0)
        peak = functools.reduce(jnp.maximum, part_lse, self_lse)
        total = sum(jnp.exp(x - peak) for x in part_lse) + jnp.exp(self_lse - peak)
        lse = jnp.where(live_ref[:, lanes] > 0, peak + jnp.log(total), DEAD_LSE)
        weight = jnp.exp(part_lse[0] - lse)
        dq = (dq_ref[:, lanes] * (weight * SCALE)).T.astype(jnp.bfloat16)
        sources = [(b, slab) for b in held for slab in all_slabs[blocks.index(b)]]
        for m, (b, (_, _, n, j)) in enumerate(sources):
            dq_refs[n][blocks.index(b), j] = dq[m * lines : (m + 1) * lines]
        weight_t = jnp.broadcast_to(weight, (DH, count)).T
        q, o_grad = (
            (lines_of(slabs, start, lines).astype(jnp.float32) * weight_t).astype(jnp.bfloat16)
            for start in (0, lines)
        )
        for i in range(len(KEEP)):
            dk = jnp.dot(dscore_ref[i, :, lanes], q, preferred_element_type=jnp.float32) * SCALE
            dv = jnp.dot(prob_ref[i, :, lanes], o_grad, preferred_element_type=jnp.float32)
            if first > 0:
                dk = dk + dk_acc[i]
                dv = dv + dv_acc[i]
            if first + count < len(blocks) * size:
                dk_acc[i] = dk
                dv_acc[i] = dv
            else:
                for n in range(2):
                    inner = slice(n * tokens, (n + 1) * tokens)
                    dkv_refs[i][n, 0:tokens, :] = dk[inner].astype(jnp.bfloat16)
                    dkv_refs[i][n, tokens : 2 * tokens, :] = dv[inner].astype(jnp.bfloat16)


def add_query_kernel(nears, *refs):
    own_refs, came_refs, out_refs = refs[:nears], refs[nears:-2], refs[-2:]
    for n in range(nears):
        for j in range(own_refs[0].shape[1]):
            total = own_refs[n][0, j].astype(jnp.float32)
            for ref in came_refs:
                total = total + ref[n, j].astype(jnp.float32)
            out_refs[min(j, 1)][n] = total.astype(jnp.bfloat16)


def tie_kernel(*refs):
    pass


def write_kernel(nears, heads, *refs):
    at = place(nears, heads)
    slab_refs, refs = refs[: -len(KEEP) - 5], refs[-len(KEEP) - 5 :]
    pair_refs, (came_ref, out_q_ref, out_k_ref, out_v_ref, sems) = refs[: len(KEEP)], refs[len(KEEP) :]
    groups, lines, tokens = len(slab_refs) * nears, slab_refs[0].shape[1], out_k_ref.shape[0]
    copies = []
    for i, ref in enumerate(pair_refs):
        for source, other in ((ref.at[0], 0), (came_ref.at[i], FIRST)):
            columns = pl.ds(column_of(at[0] ^ KEEP[i] ^ other, groups, heads), DH)
            copies.append((source.at[0:tokens, :], out_k_ref.at[:, columns]))
            copies.append((source.at[tokens : 2 * tokens, :], out_v_ref.at[:, columns]))
    for j, ref in enumerate(slab_refs):
        for n in range(nears):
            first = pl.multiple_of(group_at(at, j, n, nears) * lines, lines)
            copies.append((ref.at[n], out_q_ref.at[pl.ds(first, lines), :]))
    copies = [pltpu.make_async_copy(s, t, sems.at[n]) for n, (s, t) in enumerate(copies)]
    for copy in copies:
        copy.start()
    for copy in copies:
        copy.wait()


def swap(x, axis, distance, size):
    return lax.ppermute(x, axis, [(i, i ^ distance) for i in range(size)])


def swap_pairs(keep, send):
    members = ("row", "near", "head")
    came = swap(send, members, FIRST, KVH)
    pairs = [jnp.stack([keep[i], came[i]]) for i in range(len(KEEP))]
    return [swap(x, members, j, KVH) if j else x for x, j in zip(pairs, KEEP)]


def tie(x, others):
    return pl.pallas_call(
        tie_kernel,
        in_specs=[ANY] * (1 + len(others)),
        out_specs=ANY,
        out_shape=jax.ShapeDtypeStruct(x.shape, x.dtype),
        input_output_aliases={0: 0},
        compiler_params=PARAMS,
    )(x, *others)


def swap_back(pairs, after):
    members = ("row", "near", "head")
    pairs = [swap(x, members, j, KVH) if j else x for x, j in zip(pairs, KEEP)]
    beyond = tie(jnp.stack([x[1] for x in pairs]), after)
    return [*pairs, swap(beyond, members, FIRST, KVH)]


def line_limits(parts, row_count, nears, rows, lines, resp_len, prompt_end):
    line = lax.broadcasted_iota(jnp.int32, (1, parts * nears * row_count * lines), 1)
    slab = line >> shift_of(lines)
    row_xor = slab & (row_count - 1)
    near_xor = (slab >> shift_of(row_count)) & (nears - 1)
    place_of_block = slab >> shift_of(row_count * nears)
    block, bits = jnp.zeros_like(line), shift_of(parts)
    for k in range(bits):
        block = block | (((place_of_block >> k) & 1) << (bits - 1 - k))
    device = (lax.axis_index("part") ^ block) * row_count + (lax.axis_index("row") ^ row_xor)
    device = device * nears + (lax.axis_index("near") ^ near_xor)
    row = device * rows + (line & (rows - 1))
    ends, lengths = jnp.zeros_like(row), jnp.zeros_like(row)
    for r in range(resp_len.shape[0]):
        own = row >> shift_of(RESP_LEN) == r
        ends, lengths = jnp.where(own, prompt_end[r], ends), jnp.where(own, resp_len[r], lengths)
    return ends, ((row & (RESP_LEN - 1)) < lengths).astype(jnp.int32)


def shards(parts, row_count, nears, heads, queries, grad_out, outputs, lse_self, keys, values, resp_len, prompt_end):
    rows = queries.shape[0]
    own_heads = queries.shape[1] // DH
    own_lines = rows * own_heads
    groups = row_count * nears
    lines = own_lines // groups
    tokens = keys.shape[0]
    assert 2 * lines == DH and RESP_LEN % (groups * rows) == 0 and row_count <= 2 and nears <= 2

    def as_lines(x):
        return x.reshape(rows, own_heads, DH).transpose(1, 0, 2).reshape(own_lines, DH)

    def in_hbm(x):
        return pltpu.with_memory_space_constraint(x, pltpu.HBM)

    half_shape = jax.ShapeDtypeStruct((len(KEEP), 2 * tokens, DH), jnp.bfloat16)
    slab_shape = jax.ShapeDtypeStruct((nears, 2 * lines + STAT_ROWS, DH), jnp.bfloat16)
    *slabs, kv_keep, kv_send = pl.pallas_call(
        functools.partial(pack_kernel, row_count, nears, heads),
        in_specs=[HBM] * 6,
        out_specs=[VMEM] * (row_count + 2),
        out_shape=[slab_shape] * row_count + [half_shape] * 2,
        scratch_shapes=[
            pltpu.VMEM((own_lines, DH), jnp.bfloat16),
            pltpu.VMEM(lse_self.shape, jnp.float32),
            pltpu.SemaphoreType.DMA((2 + 2 * groups + 4 * len(KEEP),)),
        ],
        compiler_params=PARAMS,
    )(
        in_hbm(as_lines(queries)),
        in_hbm(as_lines(grad_out)),
        in_hbm(as_lines(outputs)),
        in_hbm(lse_self),
        in_hbm(keys),
        in_hbm(values),
    )
    slabs = [swap(x, "row", j, row_count) if j else x for j, x in enumerate(slabs)]
    own_block = jnp.stack([x[n] for n in range(nears) for x in slabs])
    pairs = swap_pairs(kv_keep, kv_send)
    far = [1 << n for n in reversed(range(shift_of(parts)))]

    def row_refs_of(x):
        return [x, swap(x[row_count:], "near", 1, nears)] if nears > 1 else [x]

    blocks, came = [0], [own_block]
    row_refs = row_refs_of(own_block)
    for d in far:
        if d == 1:
            came = came[:1] + [tie(x, pairs[1:]) for x in came[1:]]
        came = came + [swap(x, "part", d, parts) for x in came]
        blocks = blocks + [b ^ d for b in blocks]
    ends, live = line_limits(parts, row_count, nears, rows, lines, resp_len, prompt_end)

    def part_lse(held, first, refs, before):
        return pl.pallas_call(
            functools.partial(stat_kernel, held, first, nears, heads, tokens),
            in_specs=[VMEM] * (1 + len(refs) + len(KEEP) + len(before)),
            out_shape=jax.ShapeDtypeStruct((parts * lse_rows(groups * lines), DH), jnp.float32),
            compiler_params=PARAMS,
        )(ends, *refs, *pairs, *before)

    row_refs = row_refs + [ref for x in came[1:-1] for ref in row_refs_of(x)]
    lse = [part_lse(blocks[:-1], 0, row_refs, [])]
    last_refs = row_refs_of(tie(came[-1], lse))
    lse = [part_lse(blocks[-1:], (parts - 1) * groups * lines, last_refs, lse)]
    row_refs = row_refs + last_refs
    every_lse = lse + [swap(lse[0], "part", d, parts) for d in range(1, parts)]

    all_lines = parts * groups * lines
    score_shape = jax.ShapeDtypeStruct((len(KEEP), 2 * tokens, all_lines), jnp.bfloat16)
    prob, dscore, dq = pl.pallas_call(
        functools.partial(part_kernel, blocks, nears, heads, tokens),
        in_specs=[VMEM] * (1 + len(row_refs) + len(KEEP) + 1),
        out_specs=[VMEM] * 3,
        out_shape=[score_shape] * 2 + [jax.ShapeDtypeStruct((DH, all_lines), jnp.float32)],
        compiler_params=PARAMS,
    )(ends, *row_refs, *pairs, *lse)
    dq_shape = jax.ShapeDtypeStruct((parts, row_count, lines, DH), jnp.bfloat16)
    acc = pltpu.VMEM((len(KEEP), 2 * tokens, DH), jnp.float32)
    outs = pl.pallas_call(
        functools.partial(token_kernel, blocks, nears, heads, tokens),
        in_specs=[VMEM] * (1 + len(row_refs) + 3 + parts),
        out_shape=[jax.ShapeDtypeStruct((2, 2 * tokens, DH), jnp.bfloat16)] * len(KEEP)
        + [dq_shape] * nears,
        scratch_shapes=[acc] * 2,
        compiler_params=PARAMS,
    )(live, *row_refs, prob, dscore, dq, *every_lse)
    dkv, dq = outs[: len(KEEP)], outs[len(KEEP) :]
    dq = [swap(x, "near", n, nears) if n else x for n, x in enumerate(dq)]
    from_parts = [
        swap(jnp.stack([x[at] for x in dq]), "part", b, parts) for at, b in enumerate(blocks) if b
    ]
    sum_shape = jax.ShapeDtypeStruct((nears, lines, DH), jnp.bfloat16)
    sums = pl.pallas_call(
        functools.partial(add_query_kernel, nears),
        in_specs=[VMEM] * (nears + len(from_parts)),
        out_shape=[sum_shape] * 2,
        compiler_params=PARAMS,
    )(*dq, *from_parts)
    pairs = swap_back(dkv, from_parts)
    sums = [swap(x, "row", j, row_count) if j else x for j, x in enumerate(sums[:row_count])]
    out_q, out_k, out_v = pl.pallas_call(
        functools.partial(write_kernel, nears, heads),
        in_specs=[VMEM] * (row_count + len(pairs)),
        out_specs=[HBM] * 3,
        out_shape=[
            jax.ShapeDtypeStruct((own_lines, DH), jnp.bfloat16),
            jax.ShapeDtypeStruct(keys.shape, jnp.bfloat16),
            jax.ShapeDtypeStruct(values.shape, jnp.bfloat16),
        ],
        scratch_shapes=[pltpu.SemaphoreType.DMA((4 * len(KEEP) + groups,))],
        compiler_params=PARAMS,
    )(*sums, *pairs)
    out_q = out_q.reshape(own_heads, rows, DH).transpose(1, 0, 2).reshape(rows, own_heads * DH)
    return out_q, out_k, out_v


def solution(mesh):
    ctx, heads = mesh.shape["ctx"], mesh.shape["head"]
    groups = KVH // heads
    parts = ctx // groups
    nears = min(2, groups)
    row_count = groups // nears
    fine = Mesh(
        mesh.devices.reshape(parts, row_count, nears, heads), ("part", "row", "near", "head")
    )
    rows = P(("part", "row", "near"), "head")
    tokens = P(("part", "row", "near", "head"), None)
    return jax.shard_map(
        functools.partial(shards, parts, row_count, nears, heads),
        mesh=fine,
        in_specs=(rows, rows, rows, rows, tokens, tokens, P(), P()),
        out_specs=(rows, tokens, tokens),
        check_vma=False,
    )
```

```python
import functools

import jax
import jax.numpy as jnp
from jax import lax
from jax.experimental import pallas as pl
from jax.experimental.pallas import tpu as pltpu
from jax.sharding import Mesh, PartitionSpec as P

DH = 128
KVH = 8
RESP_LEN = 64
SCALE = DH ** (-0.5)
LOG2E = 1.4426950408889634
MASKED_SCORE = -1e30
DEAD_LSE = 1e30
PIECES = 3
STAT_ROWS = 16
STEP_LINES = 1024
PARAMS = pltpu.CompilerParams(vmem_limit_bytes=24 * 1024 * 1024)
ANY = pl.BlockSpec(memory_space=pl.ANY)
HBM = pl.BlockSpec(memory_space=pltpu.HBM)
VMEM = pl.BlockSpec(memory_space=pltpu.VMEM)

FIRST = 2
KEEP = (0, 1, 4, 5)


def split_pieces(x):
    first = x.astype(jnp.bfloat16)
    rest = x - first.astype(jnp.float32)
    second = rest.astype(jnp.bfloat16)
    third = (rest - second.astype(jnp.float32)).astype(jnp.bfloat16)
    return first, second, third


def shift_of(n):
    assert n & (n - 1) == 0
    return n.bit_length() - 1


def column_of(member, groups, heads):
    head_index, group_index = member & (heads - 1), member >> shift_of(heads)
    return pl.multiple_of((head_index * groups + group_index) * DH, DH)


def place(nears, heads):
    row, near = lax.axis_index("row"), lax.axis_index("near")
    member = (row * nears + near) * heads + lax.axis_index("head")
    return member, row, near, lax.axis_index("part")


def group_at(at, row_xor, near_xor, nears):
    return (at[1] ^ row_xor) * nears + (at[2] ^ near_xor)


def pack_kernel(row_count, nears, heads, q_hbm, o_grad_hbm, o_hbm, lse_hbm, k_hbm, v_hbm, *rest):
    slab_refs, (keep_ref, send_ref, o_ref, lse_ref, sems) = rest[:row_count], rest[row_count:]
    at = place(nears, heads)
    groups = row_count * nears
    rows, own_heads = lse_ref.shape
    lines = o_ref.shape[0] // groups
    tokens = k_hbm.shape[0]
    copies = [(lse_hbm, lse_ref), (o_hbm, o_ref)]
    slabs = []
    for j, ref in enumerate(slab_refs):
        for n in range(nears):
            first = pl.multiple_of(group_at(at, j, n, nears) * lines, lines)
            slabs.append((ref, n, first))
            copies.append((o_grad_hbm.at[pl.ds(first, lines), :], ref.at[n, lines : 2 * lines, :]))
    stat_copies = len(copies)
    for ref, n, first in slabs:
        copies.append((q_hbm.at[pl.ds(first, lines), :], ref.at[n, 0:lines, :]))
    for i, j in enumerate(KEEP):
        for ref, peer in ((send_ref, j ^ FIRST), (keep_ref, j)):
            columns = pl.ds(column_of(at[0] ^ peer, groups, heads), DH)
            copies.append((k_hbm.at[:, columns], ref.at[i, 0:tokens, :]))
            copies.append((v_hbm.at[:, columns], ref.at[i, tokens : 2 * tokens, :]))
    copies = [pltpu.make_async_copy(s, t, sems.at[n]) for n, (s, t) in enumerate(copies)]
    for copy in copies:
        copy.start()

    wide = 2 * lines
    shape = (own_heads, wide)
    head_ids = lax.broadcasted_iota(jnp.int32, shape, 0)
    line_heads = (lax.broadcasted_iota(jnp.int32, shape, 1) & (lines - 1)) >> shift_of(rows)
    chosen = jnp.concatenate(
        [(head_ids == line_heads + (first >> shift_of(rows))) for _, _, first in slabs], axis=1
    ).astype(jnp.bfloat16)
    shape = (STAT_ROWS, chosen.shape[1])
    own_row = (lax.broadcasted_iota(jnp.int32, shape, 0) & (rows - 1)) == (
        lax.broadcasted_iota(jnp.int32, shape, 1) & (rows - 1)
    )
    shape = (STAT_ROWS, STAT_ROWS)
    gather = lax.broadcasted_iota(jnp.int32, shape, 0) == (
        lax.broadcasted_iota(jnp.int32, shape, 1) >> shift_of(rows)
    )
    for copy in copies[:stat_copies]:
        copy.wait()
    pieces = [piece.astype(jnp.float32) for piece in split_pieces(lse_ref[...])]
    pieces.append(jnp.zeros((STAT_ROWS - PIECES * rows, own_heads), jnp.float32))
    pieces = jnp.concatenate(pieces, axis=0).astype(jnp.bfloat16)
    spread = jnp.dot(pieces, chosen, preferred_element_type=jnp.float32)
    spread = jnp.where(own_row, spread, 0.0).astype(jnp.bfloat16)
    lse_rows_all = jnp.dot(
        gather.astype(jnp.bfloat16), spread, preferred_element_type=jnp.float32
    )
    kind = lax.broadcasted_iota(jnp.int32, (STAT_ROWS, wide), 0)
    for m, (ref, n, first) in enumerate(slabs):
        o_grad = ref[n, lines:wide, :].astype(jnp.float32)
        product = o_grad * o_ref[pl.ds(first, lines), :].astype(jnp.float32)
        dots = jnp.sum(jnp.concatenate([product, product], axis=0).T, axis=0, keepdims=True)
        stats = lse_rows_all[:, m * wide : (m + 1) * wide]
        for k, piece in enumerate(split_pieces(dots)):
            stats = jnp.where(kind == PIECES + k, piece.astype(jnp.float32), stats)
        ref[n, wide:, :] = stats.astype(jnp.bfloat16)
    for copy in copies[stat_copies:]:
        copy.wait()


def pair_starts(at, i, tokens):
    first = at[3] * KVH
    return [(first + (at[0] ^ KEEP[i] ^ other)) * tokens for other in (0, FIRST)]


def pair_keys(ref, tokens):
    return jnp.concatenate([ref[0, 0:tokens, :], ref[1, 0:tokens, :]], axis=0)


def pair_values(ref, tokens):
    return jnp.concatenate([ref[0, tokens : 2 * tokens, :], ref[1, tokens : 2 * tokens, :]], axis=0)


def all_visible(at, ends, tokens):
    last = (at[3] + 1) * (KVH * tokens)
    return jnp.min(ends.astype(jnp.float32)) >= last.astype(jnp.float32)


def hide(values, ends, at, i, tokens, hidden):
    offset = lax.broadcasted_iota(jnp.int32, (tokens, values.shape[1]), 0)
    starts = pair_starts(at, i, tokens)
    visible = jnp.concatenate([offset < ends - start for start in starts], axis=0)
    return jnp.where(visible, values, hidden)


def in_branches(condition, body):
    pl.when(condition)(functools.partial(body, True))
    pl.when(jnp.logical_not(condition))(functools.partial(body, False))


def lse_rows(size):
    return max(1, size // DH)


def block_slabs(blocks, nears, row_refs):
    out = []
    for at in range(len(blocks)):
        refs = row_refs[at * nears : (at + 1) * nears]
        row_count = refs[0].shape[0] // nears
        out.append([(ref, j, n, j) for n, ref in enumerate(refs) for j in range(row_count)])
    return out


def lines_of(slabs, first, lines):
    return jnp.concatenate([ref[j, first : first + lines, :] for ref, j, _, _ in slabs], axis=0)


def stat_kernel(blocks, first, nears, heads, tokens, ends_ref, *refs):
    at = place(nears, heads)
    row_refs, refs = refs[: len(blocks) * nears], refs[len(blocks) * nears :]
    pair_refs, before_refs, lse_ref = refs[: len(KEEP)], refs[len(KEEP) : -1], refs[-1]
    lines = (row_refs[0].shape[1] - STAT_ROWS) // 2
    for ref in before_refs:
        lse_ref[...] = ref[...]

    def body(seen):
        for m, (b, slabs) in enumerate(zip(blocks, block_slabs(blocks, nears, row_refs))):
            count = len(slabs) * lines
            q = lines_of(slabs, 0, lines)
            ends = ends_ref[:, first + m * count : first + (m + 1) * count]
            scores = []
            for i, ref in enumerate(pair_refs):
                part = lax.dot_general(
                    pair_keys(ref, tokens),
                    q,
                    (((1,), (1,)), ((), ())),
                    preferred_element_type=jnp.float32,
                )
                scores.append(part if seen else hide(part, ends, at, i, tokens, MASKED_SCORE))
            scores = jnp.concatenate(scores, axis=0)
            peak = jnp.max(scores, axis=0, keepdims=True)
            total = jnp.sum(jnp.exp2((scores - peak) * (SCALE * LOG2E)), axis=0, keepdims=True)
            lse = peak * SCALE + jnp.log(total)
            if count < DH:
                lse = jnp.concatenate([lse] * (DH // count), axis=1)
            held = lse_rows(count)
            for k in range(held):
                lse_ref[pl.ds((at[3] ^ b) * held + k, 1), :] = lse[:, k * DH : (k + 1) * DH]

    in_branches(all_visible(at, ends_ref[...], tokens), body)


def line_values(slabs, lines, first_piece):
    low = lax.broadcasted_iota(jnp.int32, (1, 2 * lines), 1) < lines
    out = []
    for n in range(0, len(slabs), 2):
        held = [
            ref[j, 2 * lines : 2 * lines + STAT_ROWS, :].astype(jnp.float32)
            for ref, j, _, _ in slabs[n : n + 2]
        ]
        total = None
        for k in range(first_piece, first_piece + PIECES):
            piece = jnp.where(low, held[0][k : k + 1], held[1][k : k + 1])
            total = piece if total is None else total + piece
        out.append(total)
    return jnp.concatenate(out, axis=1)


def lse_lines(lse_ref, at, blocks, size):
    held = lse_rows(size)
    tiles = []
    for b in blocks:
        for k in range(held):
            tile = lse_ref[pl.ds((at[3] ^ b) * held + k, 1), :]
            tiles.append(tile[:, : min(size, DH)])
    return jnp.concatenate(tiles, axis=1)


def steps_of(blocks, all_slabs, lines):
    size = len(all_slabs[0]) * lines
    step = min(len(blocks), STEP_LINES // size)
    for c in range(0, len(blocks), step):
        slabs = [slab for held in all_slabs[c : c + step] for slab in held]
        yield c * size, step * size, blocks[c : c + step], slabs


def part_kernel(blocks, nears, heads, tokens, ends_ref, *refs):
    at = place(nears, heads)
    row_refs, refs = refs[: len(blocks) * nears], refs[len(blocks) * nears :]
    pair_refs, (lse_ref, prob_ref, dscore_ref, dq_ref) = refs[: len(KEEP)], refs[len(KEEP) :]
    lines = (row_refs[0].shape[1] - STAT_ROWS) // 2
    all_slabs = block_slabs(blocks, nears, row_refs)
    size = len(all_slabs[0]) * lines

    def body(seen):
        for first, count, held, slabs in steps_of(blocks, all_slabs, lines):
            q, o_grad = lines_of(slabs, 0, lines), lines_of(slabs, lines, lines)
            dots = line_values(slabs, lines, PIECES)
            lse = lse_lines(lse_ref, at, held, size) * LOG2E
            lanes = slice(first, first + count)
            dq_t = jnp.zeros((DH, count), jnp.float32)
            for i, ref in enumerate(pair_refs):
                k, v = pair_keys(ref, tokens), pair_values(ref, tokens)
                scores = lax.dot_general(
                    k, q, (((1,), (1,)), ((), ())), preferred_element_type=jnp.float32
                )
                prob = jnp.exp2(scores * (SCALE * LOG2E) - lse)
                if not seen:
                    prob = hide(prob, ends_ref[:, lanes], at, i, tokens, 0.0)
                dprob = lax.dot_general(
                    v, o_grad, (((1,), (1,)), ((), ())), preferred_element_type=jnp.float32
                )
                dscore = (prob * (dprob - dots)).astype(jnp.bfloat16)
                prob_ref[i, :, lanes] = prob.astype(jnp.bfloat16)
                dscore_ref[i, :, lanes] = dscore
                dq_t = dq_t + jnp.dot(k.T, dscore, preferred_element_type=jnp.float32)
            dq_ref[:, lanes] = dq_t

    in_branches(all_visible(at, ends_ref[...], tokens), body)


def token_kernel(blocks, nears, heads, tokens, live_ref, *refs):
    at = place(nears, heads)
    row_refs, refs = refs[: len(blocks) * nears], refs[len(blocks) * nears :]
    (prob_ref, dscore_ref, dq_ref), refs = refs[:3], refs[3:]
    lse_refs, refs = refs[: len(blocks)], refs[len(blocks) :]
    dkv_refs, (*dq_refs, dk_acc, dv_acc) = refs[: len(KEEP)], refs[len(KEEP) :]
    lines = (row_refs[0].shape[1] - STAT_ROWS) // 2
    all_slabs = block_slabs(blocks, nears, row_refs)
    groups = len(all_slabs[0])
    size = groups * lines
    for first, count, held, slabs in steps_of(blocks, all_slabs, lines):
        lanes = slice(first, first + count)
        part_lse = [lse_lines(ref, at, held, size) for ref in lse_refs]
        self_lse = line_values(slabs, lines, 0)
        peak = functools.reduce(jnp.maximum, part_lse, self_lse)
        total = sum(jnp.exp(x - peak) for x in part_lse) + jnp.exp(self_lse - peak)
        lse = jnp.where(live_ref[:, lanes] > 0, peak + jnp.log(total), DEAD_LSE)
        weight = jnp.exp(part_lse[0] - lse)
        dq = (dq_ref[:, lanes] * (weight * SCALE)).T.astype(jnp.bfloat16)
        sources = [(b, slab) for b in held for slab in all_slabs[blocks.index(b)]]
        for m, (b, (_, _, n, j)) in enumerate(sources):
            source = (at[3] ^ b) * (groups // nears) + (at[1] ^ j)
            dq_refs[n][source] = dq[m * lines : (m + 1) * lines]
        weight_t = jnp.broadcast_to(weight, (DH, count)).T
        q, o_grad = (
            (lines_of(slabs, start, lines).astype(jnp.float32) * weight_t).astype(jnp.bfloat16)
            for start in (0, lines)
        )
        for i in range(len(KEEP)):
            dk = jnp.dot(dscore_ref[i, :, lanes], q, preferred_element_type=jnp.float32) * SCALE
            dv = jnp.dot(prob_ref[i, :, lanes], o_grad, preferred_element_type=jnp.float32)
            if first > 0:
                dk = dk + dk_acc[i]
                dv = dv + dv_acc[i]
            if first + count < len(blocks) * size:
                dk_acc[i] = dk
                dv_acc[i] = dv
            else:
                for n in range(2):
                    inner = slice(n * tokens, (n + 1) * tokens)
                    dkv_refs[i][n, 0:tokens, :] = dk[inner].astype(jnp.bfloat16)
                    dkv_refs[i][n, tokens : 2 * tokens, :] = dv[inner].astype(jnp.bfloat16)


def join_kernel(*refs):
    for n, ref in enumerate(refs[:-1]):
        refs[-1][:, n] = ref[...]


def tie_kernel(*refs):
    pass


def write_kernel(row_count, nears, heads, *refs):
    at = place(nears, heads)
    dq_ref, pair_refs, refs = refs[0], refs[1 : 1 + len(KEEP)], refs[1 + len(KEEP) :]
    came_ref, out_q_ref, out_k_ref, out_v_ref, sum_ref, sems = refs
    groups, lines, tokens = row_count * nears, dq_ref.shape[2], out_k_ref.shape[0]
    copies = []
    for i, ref in enumerate(pair_refs):
        for source, other in ((ref.at[0], 0), (came_ref.at[i], FIRST)):
            columns = pl.ds(column_of(at[0] ^ KEEP[i] ^ other, groups, heads), DH)
            copies.append((source.at[0:tokens, :], out_k_ref.at[:, columns]))
            copies.append((source.at[tokens : 2 * tokens, :], out_v_ref.at[:, columns]))
    for row in range(row_count):
        for n in range(nears):
            first = pl.multiple_of((row * nears + (at[2] ^ n)) * lines, lines)
            copies.append((sum_ref.at[row * nears + n], out_q_ref.at[pl.ds(first, lines), :]))
    copies = [pltpu.make_async_copy(s, t, sems.at[n]) for n, (s, t) in enumerate(copies)]
    for copy in copies[:-groups]:
        copy.start()
    for g in range(groups):
        total = dq_ref[g // nears, g % nears].astype(jnp.float32)
        for source in range(g // nears + row_count, dq_ref.shape[0], row_count):
            total = total + dq_ref[source, g % nears].astype(jnp.float32)
        sum_ref[g] = total.astype(jnp.bfloat16)
        copies[g - groups].start()
    for copy in copies:
        copy.wait()


def swap(x, axis, distance, size):
    return lax.ppermute(x, axis, [(i, i ^ distance) for i in range(size)])


def swap_pairs(keep, send):
    members = ("row", "near", "head")
    came = swap(send, members, FIRST, KVH)
    pairs = [jnp.stack([keep[i], came[i]]) for i in range(len(KEEP))]
    return [swap(x, members, j, KVH) if j else x for x, j in zip(pairs, KEEP)]


def tie(x, others):
    return pl.pallas_call(
        tie_kernel,
        in_specs=[ANY] * (1 + len(others)),
        out_specs=ANY,
        out_shape=jax.ShapeDtypeStruct(x.shape, x.dtype),
        input_output_aliases={0: 0},
        compiler_params=PARAMS,
    )(x, *others)


def swap_back(pairs, after):
    members = ("row", "near", "head")
    pairs = [tie(swap(x, members, j, KVH), after) if j else x for x, j in zip(pairs, KEEP)]
    return [*pairs, swap(jnp.stack([x[1] for x in pairs]), members, FIRST, KVH)]


def line_limits(parts, row_count, nears, rows, lines, resp_len, prompt_end):
    line = lax.broadcasted_iota(jnp.int32, (1, parts * nears * row_count * lines), 1)
    slab = line >> shift_of(lines)
    row_xor = slab & (row_count - 1)
    near_xor = (slab >> shift_of(row_count)) & (nears - 1)
    place_of_block = slab >> shift_of(row_count * nears)
    block, bits = jnp.zeros_like(line), shift_of(parts)
    for k in range(bits):
        block = block | (((place_of_block >> k) & 1) << (bits - 1 - k))
    device = (lax.axis_index("part") ^ block) * row_count + (lax.axis_index("row") ^ row_xor)
    device = device * nears + (lax.axis_index("near") ^ near_xor)
    row = device * rows + (line & (rows - 1))
    ends, lengths = jnp.zeros_like(row), jnp.zeros_like(row)
    for r in range(resp_len.shape[0]):
        own = row >> shift_of(RESP_LEN) == r
        ends, lengths = jnp.where(own, prompt_end[r], ends), jnp.where(own, resp_len[r], lengths)
    return ends, ((row & (RESP_LEN - 1)) < lengths).astype(jnp.int32)


def shards(parts, row_count, nears, heads, queries, grad_out, outputs, lse_self, keys, values, resp_len, prompt_end):
    rows = queries.shape[0]
    own_heads = queries.shape[1] // DH
    own_lines = rows * own_heads
    groups = row_count * nears
    lines = own_lines // groups
    tokens = keys.shape[0]
    assert 2 * lines == DH and RESP_LEN % (groups * rows) == 0 and row_count <= 2 and nears <= 2

    def as_lines(x):
        return x.reshape(rows, own_heads, DH).transpose(1, 0, 2).reshape(own_lines, DH)

    def in_hbm(x):
        return pltpu.with_memory_space_constraint(x, pltpu.HBM)

    half_shape = jax.ShapeDtypeStruct((len(KEEP), 2 * tokens, DH), jnp.bfloat16)
    slab_shape = jax.ShapeDtypeStruct((nears, 2 * lines + STAT_ROWS, DH), jnp.bfloat16)
    *slabs, kv_keep, kv_send = pl.pallas_call(
        functools.partial(pack_kernel, row_count, nears, heads),
        in_specs=[HBM] * 6,
        out_specs=[VMEM] * (row_count + 2),
        out_shape=[slab_shape] * row_count + [half_shape] * 2,
        scratch_shapes=[
            pltpu.VMEM((own_lines, DH), jnp.bfloat16),
            pltpu.VMEM(lse_self.shape, jnp.float32),
            pltpu.SemaphoreType.DMA((2 + 2 * groups + 4 * len(KEEP),)),
        ],
        compiler_params=PARAMS,
    )(
        in_hbm(as_lines(queries)),
        in_hbm(as_lines(grad_out)),
        in_hbm(as_lines(outputs)),
        in_hbm(lse_self),
        in_hbm(keys),
        in_hbm(values),
    )
    slabs = [swap(x, "row", j, row_count) if j else x for j, x in enumerate(slabs)]
    own_block = jnp.stack([x[n] for n in range(nears) for x in slabs])
    pairs = swap_pairs(kv_keep, kv_send)
    far = [1 << n for n in reversed(range(shift_of(parts)))]

    def row_refs_of(x):
        return [x, swap(x[row_count:], "near", 1, nears)] if nears > 1 else [x]

    blocks, came = [0], [own_block]
    row_refs = row_refs_of(own_block)
    for d in far:
        if d == 1:
            came = came[:1] + [tie(x, pairs[1:]) for x in came[1:]]
        came = came + [swap(x, "part", d, parts) for x in came]
        blocks = blocks + [b ^ d for b in blocks]
    ends, live = line_limits(parts, row_count, nears, rows, lines, resp_len, prompt_end)

    def part_lse(held, first, refs, before):
        return pl.pallas_call(
            functools.partial(stat_kernel, held, first, nears, heads, tokens),
            in_specs=[VMEM] * (1 + len(refs) + len(KEEP) + len(before)),
            out_shape=jax.ShapeDtypeStruct((parts * lse_rows(groups * lines), DH), jnp.float32),
            compiler_params=PARAMS,
        )(ends, *refs, *pairs, *before)

    row_refs = row_refs + [ref for x in came[1:-1] for ref in row_refs_of(x)]
    lse = [part_lse(blocks[:-1], 0, row_refs, [])]
    last_refs = row_refs_of(tie(came[-1], lse))
    lse = [part_lse(blocks[-1:], (parts - 1) * groups * lines, last_refs, lse)]
    row_refs = row_refs + last_refs
    every_lse = lse + [swap(lse[0], "part", d, parts) for d in range(1, parts)]

    all_lines = parts * groups * lines
    score_shape = jax.ShapeDtypeStruct((len(KEEP), 2 * tokens, all_lines), jnp.bfloat16)
    prob, dscore, dq = pl.pallas_call(
        functools.partial(part_kernel, blocks, nears, heads, tokens),
        in_specs=[VMEM] * (1 + len(row_refs) + len(KEEP) + 1),
        out_specs=[VMEM] * 3,
        out_shape=[score_shape] * 2 + [jax.ShapeDtypeStruct((DH, all_lines), jnp.float32)],
        compiler_params=PARAMS,
    )(ends, *row_refs, *pairs, *lse)
    dq_shape = jax.ShapeDtypeStruct((parts * row_count, lines, DH), jnp.bfloat16)
    acc = pltpu.VMEM((len(KEEP), 2 * tokens, DH), jnp.float32)
    outs = pl.pallas_call(
        functools.partial(token_kernel, blocks, nears, heads, tokens),
        in_specs=[VMEM] * (1 + len(row_refs) + 3 + parts),
        out_shape=[jax.ShapeDtypeStruct((2, 2 * tokens, DH), jnp.bfloat16)] * len(KEEP)
        + [dq_shape] * nears,
        scratch_shapes=[acc] * 2,
        compiler_params=PARAMS,
    )(live, *row_refs, prob, dscore, dq, *every_lse)
    dkv, dq = outs[: len(KEEP)], outs[len(KEEP) :]
    dq = [swap(x, "near", n, nears) if n else x for n, x in enumerate(dq)]
    dq = pl.pallas_call(
        join_kernel,
        in_specs=[VMEM] * nears,
        out_shape=jax.ShapeDtypeStruct((parts * row_count, nears, lines, DH), jnp.bfloat16),
        compiler_params=PARAMS,
    )(*dq)
    pairs = swap_back(dkv, [dq])
    dq = lax.all_to_all(dq, ("part", "row"), split_axis=0, concat_axis=0, tiled=True)
    out_q, out_k, out_v = pl.pallas_call(
        functools.partial(write_kernel, row_count, nears, heads),
        in_specs=[VMEM] * (1 + len(pairs)),
        out_specs=[HBM] * 3,
        out_shape=[
            jax.ShapeDtypeStruct((own_lines, DH), jnp.bfloat16),
            jax.ShapeDtypeStruct(keys.shape, jnp.bfloat16),
            jax.ShapeDtypeStruct(values.shape, jnp.bfloat16),
        ],
        scratch_shapes=[
            pltpu.VMEM((groups, lines, DH), jnp.bfloat16),
            pltpu.SemaphoreType.DMA((4 * len(KEEP) + groups,)),
        ],
        compiler_params=PARAMS,
    )(dq, *pairs)
    out_q = out_q.reshape(own_heads, rows, DH).transpose(1, 0, 2).reshape(rows, own_heads * DH)
    return out_q, out_k, out_v


def solution(mesh):
    ctx, heads = mesh.shape["ctx"], mesh.shape["head"]
    groups = KVH // heads
    parts = ctx // groups
    nears = min(2, groups)
    row_count = groups // nears
    fine = Mesh(
        mesh.devices.reshape(parts, row_count, nears, heads), ("part", "row", "near", "head")
    )
    rows = P(("part", "row", "near"), "head")
    tokens = P(("part", "row", "near", "head"), None)
    return jax.shard_map(
        functools.partial(shards, parts, row_count, nears, heads),
        mesh=fine,
        in_specs=(rows, rows, rows, rows, tokens, tokens, P(), P()),
        out_specs=(rows, tokens, tokens),
        check_vma=False,
    )
```

```python
import functools

import jax
import jax.numpy as jnp
from jax import lax
from jax.experimental import pallas as pl
from jax.experimental.pallas import tpu as pltpu
from jax.sharding import Mesh, PartitionSpec as P

DH = 128
KVH = 8
RESP_LEN = 64
SCALE = DH ** (-0.5)
LOG2E = 1.4426950408889634
MASKED_SCORE = -1e30
DEAD_LSE = 1e30
PIECES = 3
STAT_ROWS = 16
STEP_LINES = 1024
PARAMS = pltpu.CompilerParams(vmem_limit_bytes=24 * 1024 * 1024)
ANY = pl.BlockSpec(memory_space=pl.ANY)
HBM = pl.BlockSpec(memory_space=pltpu.HBM)
VMEM = pl.BlockSpec(memory_space=pltpu.VMEM)

FIRST = 2
KEEP = (0, 1, 4, 5)


def split_pieces(x):
    first = x.astype(jnp.bfloat16)
    rest = x - first.astype(jnp.float32)
    second = rest.astype(jnp.bfloat16)
    third = (rest - second.astype(jnp.float32)).astype(jnp.bfloat16)
    return first, second, third


def shift_of(n):
    assert n & (n - 1) == 0
    return n.bit_length() - 1


def column_of(member, groups, heads):
    head_index, group_index = member & (heads - 1), member >> shift_of(heads)
    return pl.multiple_of((head_index * groups + group_index) * DH, DH)


def place(nears, heads):
    row, near = lax.axis_index("row"), lax.axis_index("near")
    member = (row * nears + near) * heads + lax.axis_index("head")
    return member, row, near, lax.axis_index("part")


def group_at(at, row_xor, near_xor, nears):
    return (at[1] ^ row_xor) * nears + (at[2] ^ near_xor)


def pack_kernel(row_count, nears, heads, q_hbm, o_grad_hbm, o_hbm, lse_hbm, k_hbm, v_hbm, *rest):
    groups = row_count * nears
    slab_refs, (keep_ref, send_ref, o_ref, lse_ref, sems) = rest[:groups], rest[groups:]
    at = place(nears, heads)
    rows, own_heads = lse_ref.shape
    lines = o_ref.shape[0] // groups
    tokens = k_hbm.shape[0]
    copies = [(lse_hbm, lse_ref), (o_hbm, o_ref)]
    slabs = []
    for m, ref in enumerate(slab_refs):
        first = pl.multiple_of(group_at(at, m // nears, m % nears, nears) * lines, lines)
        slabs.append((ref, first))
        copies.append((o_grad_hbm.at[pl.ds(first, lines), :], ref.at[lines : 2 * lines, :]))
    stat_copies = len(copies)
    for ref, first in slabs:
        copies.append((q_hbm.at[pl.ds(first, lines), :], ref.at[0:lines, :]))
    for i, j in enumerate(KEEP):
        for ref, peer in ((send_ref, j ^ FIRST), (keep_ref, j)):
            columns = pl.ds(column_of(at[0] ^ peer, groups, heads), DH)
            copies.append((k_hbm.at[:, columns], ref.at[i, 0:tokens, :]))
            copies.append((v_hbm.at[:, columns], ref.at[i, tokens : 2 * tokens, :]))
    copies = [pltpu.make_async_copy(s, t, sems.at[n]) for n, (s, t) in enumerate(copies)]
    for copy in copies:
        copy.start()

    wide = 2 * lines
    shape = (own_heads, wide)
    head_ids = lax.broadcasted_iota(jnp.int32, shape, 0)
    line_heads = (lax.broadcasted_iota(jnp.int32, shape, 1) & (lines - 1)) >> shift_of(rows)
    chosen = jnp.concatenate(
        [(head_ids == line_heads + (first >> shift_of(rows))) for _, first in slabs], axis=1
    ).astype(jnp.bfloat16)
    shape = (STAT_ROWS, chosen.shape[1])
    own_row = (lax.broadcasted_iota(jnp.int32, shape, 0) & (rows - 1)) == (
        lax.broadcasted_iota(jnp.int32, shape, 1) & (rows - 1)
    )
    shape = (STAT_ROWS, STAT_ROWS)
    gather = lax.broadcasted_iota(jnp.int32, shape, 0) == (
        lax.broadcasted_iota(jnp.int32, shape, 1) >> shift_of(rows)
    )
    for copy in copies[:stat_copies]:
        copy.wait()
    pieces = [piece.astype(jnp.float32) for piece in split_pieces(lse_ref[...])]
    pieces.append(jnp.zeros((STAT_ROWS - PIECES * rows, own_heads), jnp.float32))
    pieces = jnp.concatenate(pieces, axis=0).astype(jnp.bfloat16)
    spread = jnp.dot(pieces, chosen, preferred_element_type=jnp.float32)
    spread = jnp.where(own_row, spread, 0.0).astype(jnp.bfloat16)
    lse_rows_all = jnp.dot(
        gather.astype(jnp.bfloat16), spread, preferred_element_type=jnp.float32
    )
    kind = lax.broadcasted_iota(jnp.int32, (STAT_ROWS, wide), 0)
    for m, (ref, first) in enumerate(slabs):
        o_grad = ref[lines:wide, :].astype(jnp.float32)
        product = o_grad * o_ref[pl.ds(first, lines), :].astype(jnp.float32)
        dots = jnp.sum(jnp.concatenate([product, product], axis=0).T, axis=0, keepdims=True)
        stats = lse_rows_all[:, m * wide : (m + 1) * wide]
        for k, piece in enumerate(split_pieces(dots)):
            stats = jnp.where(kind == PIECES + k, piece.astype(jnp.float32), stats)
        ref[wide:, :] = stats.astype(jnp.bfloat16)
    for copy in copies[stat_copies:]:
        copy.wait()


def pair_starts(at, i, tokens):
    first = at[3] * KVH
    return [(first + (at[0] ^ KEEP[i] ^ other)) * tokens for other in (0, FIRST)]


def pair_keys(ref, tokens):
    return jnp.concatenate([ref[0, 0:tokens, :], ref[1, 0:tokens, :]], axis=0)


def pair_values(ref, tokens):
    return jnp.concatenate([ref[0, tokens : 2 * tokens, :], ref[1, tokens : 2 * tokens, :]], axis=0)


def all_visible(at, ends, tokens):
    last = (at[3] + 1) * (KVH * tokens)
    return jnp.min(ends.astype(jnp.float32)) >= last.astype(jnp.float32)


def hide(values, ends, at, i, tokens, hidden):
    offset = lax.broadcasted_iota(jnp.int32, (tokens, values.shape[1]), 0)
    starts = pair_starts(at, i, tokens)
    visible = jnp.concatenate([offset < ends - start for start in starts], axis=0)
    return jnp.where(visible, values, hidden)


def in_branches(condition, body):
    pl.when(condition)(functools.partial(body, True))
    pl.when(jnp.logical_not(condition))(functools.partial(body, False))


def lse_rows(size):
    return max(1, size // DH)


def slabs_of(row_refs):
    return [[(ref, m) for m in range(ref.shape[0])] for ref in row_refs]


def lines_of(slabs, first, lines):
    return jnp.concatenate([ref[j, first : first + lines, :] for ref, j in slabs], axis=0)


def stat_kernel(blocks, first, nears, heads, tokens, ends_ref, *refs):
    at = place(nears, heads)
    row_refs, refs = refs[: len(blocks)], refs[len(blocks) :]
    pair_refs, before_refs, lse_ref = refs[: len(KEEP)], refs[len(KEEP) : -1], refs[-1]
    lines = (row_refs[0].shape[1] - STAT_ROWS) // 2
    for ref in before_refs:
        lse_ref[...] = ref[...]

    def body(seen):
        for m, (b, slabs) in enumerate(zip(blocks, slabs_of(row_refs))):
            count = len(slabs) * lines
            q = lines_of(slabs, 0, lines)
            ends = ends_ref[:, first + m * count : first + (m + 1) * count]
            scores = []
            for i, ref in enumerate(pair_refs):
                part = lax.dot_general(
                    pair_keys(ref, tokens),
                    q,
                    (((1,), (1,)), ((), ())),
                    preferred_element_type=jnp.float32,
                )
                scores.append(part if seen else hide(part, ends, at, i, tokens, MASKED_SCORE))
            scores = jnp.concatenate(scores, axis=0)
            peak = jnp.max(scores, axis=0, keepdims=True)
            total = jnp.sum(jnp.exp2((scores - peak) * (SCALE * LOG2E)), axis=0, keepdims=True)
            lse = peak * SCALE + jnp.log(total)
            if count < DH:
                lse = jnp.concatenate([lse] * (DH // count), axis=1)
            held = lse_rows(count)
            for k in range(held):
                lse_ref[pl.ds((at[3] ^ b) * held + k, 1), :] = lse[:, k * DH : (k + 1) * DH]

    in_branches(all_visible(at, ends_ref[...], tokens), body)


def line_values(slabs, lines, first_piece):
    low = lax.broadcasted_iota(jnp.int32, (1, 2 * lines), 1) < lines
    out = []
    for n in range(0, len(slabs), 2):
        held = [
            ref[j, 2 * lines : 2 * lines + STAT_ROWS, :].astype(jnp.float32)
            for ref, j in slabs[n : n + 2]
        ]
        total = None
        for k in range(first_piece, first_piece + PIECES):
            piece = jnp.where(low, held[0][k : k + 1], held[1][k : k + 1])
            total = piece if total is None else total + piece
        out.append(total)
    return jnp.concatenate(out, axis=1)


def lse_lines(lse_ref, at, blocks, size):
    held = lse_rows(size)
    tiles = []
    for b in blocks:
        for k in range(held):
            tile = lse_ref[pl.ds((at[3] ^ b) * held + k, 1), :]
            tiles.append(tile[:, : min(size, DH)])
    return jnp.concatenate(tiles, axis=1)


def steps_of(blocks, all_slabs, lines):
    size = len(all_slabs[0]) * lines
    step = min(len(blocks), STEP_LINES // size)
    for c in range(0, len(blocks), step):
        slabs = [slab for held in all_slabs[c : c + step] for slab in held]
        yield c * size, step * size, blocks[c : c + step], slabs


def part_kernel(blocks, nears, heads, tokens, ends_ref, *refs):
    at = place(nears, heads)
    row_refs, refs = refs[: len(blocks)], refs[len(blocks) :]
    pair_refs, (lse_ref, prob_ref, dscore_ref, dq_ref) = refs[: len(KEEP)], refs[len(KEEP) :]
    lines = (row_refs[0].shape[1] - STAT_ROWS) // 2
    all_slabs = slabs_of(row_refs)
    size = len(all_slabs[0]) * lines

    def body(seen):
        for first, count, held, slabs in steps_of(blocks, all_slabs, lines):
            q, o_grad = lines_of(slabs, 0, lines), lines_of(slabs, lines, lines)
            dots = line_values(slabs, lines, PIECES)
            lse = lse_lines(lse_ref, at, held, size) * LOG2E
            lanes = slice(first, first + count)
            dq_t = jnp.zeros((DH, count), jnp.float32)
            for i, ref in enumerate(pair_refs):
                k, v = pair_keys(ref, tokens), pair_values(ref, tokens)
                scores = lax.dot_general(
                    k, q, (((1,), (1,)), ((), ())), preferred_element_type=jnp.float32
                )
                prob = jnp.exp2(scores * (SCALE * LOG2E) - lse)
                if not seen:
                    prob = hide(prob, ends_ref[:, lanes], at, i, tokens, 0.0)
                dprob = lax.dot_general(
                    v, o_grad, (((1,), (1,)), ((), ())), preferred_element_type=jnp.float32
                )
                dscore = (prob * (dprob - dots)).astype(jnp.bfloat16)
                prob_ref[i, :, lanes] = prob.astype(jnp.bfloat16)
                dscore_ref[i, :, lanes] = dscore
                dq_t = dq_t + jnp.dot(k.T, dscore, preferred_element_type=jnp.float32)
            dq_ref[:, lanes] = dq_t

    in_branches(all_visible(at, ends_ref[...], tokens), body)


def token_kernel(blocks, nears, heads, tokens, live_ref, *refs):
    at = place(nears, heads)
    row_refs, refs = refs[: len(blocks)], refs[len(blocks) :]
    (prob_ref, dscore_ref, dq_ref), refs = refs[:3], refs[3:]
    lse_refs, refs = refs[: len(blocks)], refs[len(blocks) :]
    dkv_refs, (*dq_refs, dk_acc, dv_acc) = refs[: len(KEEP)], refs[len(KEEP) :]
    lines = (row_refs[0].shape[1] - STAT_ROWS) // 2
    all_slabs = slabs_of(row_refs)
    size = len(all_slabs[0]) * lines
    for first, count, held, slabs in steps_of(blocks, all_slabs, lines):
        lanes = slice(first, first + count)
        part_lse = [lse_lines(ref, at, held, size) for ref in lse_refs]
        self_lse = line_values(slabs, lines, 0)
        peak = functools.reduce(jnp.maximum, part_lse, self_lse)
        total = sum(jnp.exp(x - peak) for x in part_lse) + jnp.exp(self_lse - peak)
        lse = jnp.where(live_ref[:, lanes] > 0, peak + jnp.log(total), DEAD_LSE)
        weight = jnp.exp(part_lse[0] - lse)
        dq = (dq_ref[:, lanes] * (weight * SCALE)).T.astype(jnp.bfloat16)
        groups = len(dq_refs)
        for m in range(len(slabs)):
            block = first // size + m // groups
            dq_refs[m % groups][block] = dq[m * lines : (m + 1) * lines]
        weight_t = jnp.broadcast_to(weight, (DH, count)).T
        q, o_grad = (
            (lines_of(slabs, start, lines).astype(jnp.float32) * weight_t).astype(jnp.bfloat16)
            for start in (0, lines)
        )
        for i in range(len(KEEP)):
            dk = jnp.dot(dscore_ref[i, :, lanes], q, preferred_element_type=jnp.float32) * SCALE
            dv = jnp.dot(prob_ref[i, :, lanes], o_grad, preferred_element_type=jnp.float32)
            if first > 0:
                dk = dk + dk_acc[i]
                dv = dv + dv_acc[i]
            if first + count < len(blocks) * size:
                dk_acc[i] = dk
                dv_acc[i] = dv
            else:
                for n in range(2):
                    inner = slice(n * tokens, (n + 1) * tokens)
                    dkv_refs[i][n, 0:tokens, :] = dk[inner].astype(jnp.bfloat16)
                    dkv_refs[i][n, tokens : 2 * tokens, :] = dv[inner].astype(jnp.bfloat16)


def tie_kernel(*refs):
    pass


def write_kernel(nears, heads, *refs):
    at = place(nears, heads)
    out_q_ref, out_k_ref, out_v_ref, sum_ref, sems = refs[-5:]
    pair_refs, came_ref, refs = refs[: len(KEEP)], refs[len(KEEP)], refs[len(KEEP) + 1 : -5]
    groups, lines, _ = sum_ref.shape
    own_refs, part_refs = refs[:groups], refs[groups:]
    tokens = out_k_ref.shape[0]
    copies = []
    for i, ref in enumerate(pair_refs):
        for source, other in ((ref.at[0], 0), (came_ref.at[i], FIRST)):
            columns = pl.ds(column_of(at[0] ^ KEEP[i] ^ other, groups, heads), DH)
            copies.append((source.at[0:tokens, :], out_k_ref.at[:, columns]))
            copies.append((source.at[tokens : 2 * tokens, :], out_v_ref.at[:, columns]))
    for m in range(groups):
        first = pl.multiple_of(group_at(at, m // nears, m % nears, nears) * lines, lines)
        copies.append((sum_ref.at[m], out_q_ref.at[pl.ds(first, lines), :]))
    copies = [pltpu.make_async_copy(s, t, sems.at[n]) for n, (s, t) in enumerate(copies)]
    for copy in copies[:-groups]:
        copy.start()
    for m in range(groups):
        total = own_refs[m][0].astype(jnp.float32)
        for ref in part_refs:
            total = total + ref[m].astype(jnp.float32)
        sum_ref[m] = total.astype(jnp.bfloat16)
        copies[m - groups].start()
    for copy in copies:
        copy.wait()


def swap(x, axis, distance, size):
    return lax.ppermute(x, axis, [(i, i ^ distance) for i in range(size)])


def swap_pairs(keep, send):
    members = ("row", "near", "head")
    came = swap(send, members, FIRST, KVH)
    pairs = [jnp.stack([keep[i], came[i]]) for i in range(len(KEEP))]
    return [swap(x, members, j, KVH) if j else x for x, j in zip(pairs, KEEP)]


def tie(x, others):
    return pl.pallas_call(
        tie_kernel,
        in_specs=[ANY] * (1 + len(others)),
        out_specs=ANY,
        out_shape=jax.ShapeDtypeStruct(x.shape, x.dtype),
        input_output_aliases={0: 0},
        compiler_params=PARAMS,
    )(x, *others)


def swap_back(pairs, after):
    members = ("row", "near", "head")
    pairs = [swap(x, members, j, KVH) if j else x for x, j in zip(pairs, KEEP)]
    beyond = tie(jnp.stack([x[1] for x in pairs]), after)
    return [*pairs, swap(beyond, members, FIRST, KVH)]


def swap_slabs(slabs, groups):
    return [swap(x, ("row", "near"), m, groups) if m else x for m, x in enumerate(slabs)]


def line_limits(parts, row_count, nears, rows, lines, resp_len, prompt_end):
    line = lax.broadcasted_iota(jnp.int32, (1, parts * nears * row_count * lines), 1)
    slab = line >> shift_of(lines)
    near_xor = slab & (nears - 1)
    row_xor = (slab >> shift_of(nears)) & (row_count - 1)
    place_of_block = slab >> shift_of(row_count * nears)
    block, bits = jnp.zeros_like(line), shift_of(parts)
    for k in range(bits):
        block = block | (((place_of_block >> k) & 1) << (bits - 1 - k))
    device = (lax.axis_index("part") ^ block) * row_count + (lax.axis_index("row") ^ row_xor)
    device = device * nears + (lax.axis_index("near") ^ near_xor)
    row = device * rows + (line & (rows - 1))
    ends, lengths = jnp.zeros_like(row), jnp.zeros_like(row)
    for r in range(resp_len.shape[0]):
        own = row >> shift_of(RESP_LEN) == r
        ends, lengths = jnp.where(own, prompt_end[r], ends), jnp.where(own, resp_len[r], lengths)
    return ends, ((row & (RESP_LEN - 1)) < lengths).astype(jnp.int32)


def shards(parts, row_count, nears, heads, queries, grad_out, outputs, lse_self, keys, values, resp_len, prompt_end):
    rows = queries.shape[0]
    own_heads = queries.shape[1] // DH
    own_lines = rows * own_heads
    groups = row_count * nears
    lines = own_lines // groups
    tokens = keys.shape[0]
    assert 2 * lines == DH and RESP_LEN % (groups * rows) == 0 and row_count <= 2 and nears <= 2

    def as_lines(x):
        return x.reshape(rows, own_heads, DH).transpose(1, 0, 2).reshape(own_lines, DH)

    def in_hbm(x):
        return pltpu.with_memory_space_constraint(x, pltpu.HBM)

    half_shape = jax.ShapeDtypeStruct((len(KEEP), 2 * tokens, DH), jnp.bfloat16)
    slab_shape = jax.ShapeDtypeStruct((2 * lines + STAT_ROWS, DH), jnp.bfloat16)
    *slabs, kv_keep, kv_send = pl.pallas_call(
        functools.partial(pack_kernel, row_count, nears, heads),
        in_specs=[HBM] * 6,
        out_specs=[VMEM] * (groups + 2),
        out_shape=[slab_shape] * groups + [half_shape] * 2,
        scratch_shapes=[
            pltpu.VMEM((own_lines, DH), jnp.bfloat16),
            pltpu.VMEM(lse_self.shape, jnp.float32),
            pltpu.SemaphoreType.DMA((2 + 2 * groups + 4 * len(KEEP),)),
        ],
        compiler_params=PARAMS,
    )(
        in_hbm(as_lines(queries)),
        in_hbm(as_lines(grad_out)),
        in_hbm(as_lines(outputs)),
        in_hbm(lse_self),
        in_hbm(keys),
        in_hbm(values),
    )
    own_block = jnp.stack(swap_slabs(slabs, groups))
    pairs = swap_pairs(kv_keep, kv_send)
    far = [1 << n for n in reversed(range(shift_of(parts)))]

    blocks, came = [0], [own_block]
    for d in far:
        if d == 1:
            came = came[:1] + [tie(x, pairs[1:]) for x in came[1:]]
        came = came + [swap(x, "part", d, parts) for x in came]
        blocks = blocks + [b ^ d for b in blocks]
    ends, live = line_limits(parts, row_count, nears, rows, lines, resp_len, prompt_end)

    def part_lse(held, first, refs, before):
        return pl.pallas_call(
            functools.partial(stat_kernel, held, first, nears, heads, tokens),
            in_specs=[VMEM] * (1 + len(refs) + len(KEEP) + len(before)),
            out_shape=jax.ShapeDtypeStruct((parts * lse_rows(groups * lines), DH), jnp.float32),
            compiler_params=PARAMS,
        )(ends, *refs, *pairs, *before)

    lse = [part_lse(blocks[:-1], 0, came[:-1], [])]
    row_refs = [*came[:-1], tie(came[-1], lse)]
    lse = [part_lse(blocks[-1:], (parts - 1) * groups * lines, row_refs[-1:], lse)]
    every_lse = lse + [swap(lse[0], "part", d, parts) for d in range(1, parts)]

    all_lines = parts * groups * lines
    score_shape = jax.ShapeDtypeStruct((len(KEEP), 2 * tokens, all_lines), jnp.bfloat16)
    prob, dscore, dq = pl.pallas_call(
        functools.partial(part_kernel, blocks, nears, heads, tokens),
        in_specs=[VMEM] * (1 + len(row_refs) + len(KEEP) + 1),
        out_specs=[VMEM] * 3,
        out_shape=[score_shape] * 2 + [jax.ShapeDtypeStruct((DH, all_lines), jnp.float32)],
        compiler_params=PARAMS,
    )(ends, *row_refs, *pairs, *lse)
    dq_shape = jax.ShapeDtypeStruct((parts, lines, DH), jnp.bfloat16)
    acc = pltpu.VMEM((len(KEEP), 2 * tokens, DH), jnp.float32)
    outs = pl.pallas_call(
        functools.partial(token_kernel, blocks, nears, heads, tokens),
        in_specs=[VMEM] * (1 + len(row_refs) + 3 + parts),
        out_shape=[jax.ShapeDtypeStruct((2, 2 * tokens, DH), jnp.bfloat16)] * len(KEEP)
        + [dq_shape] * groups,
        scratch_shapes=[acc] * 2,
        compiler_params=PARAMS,
    )(live, *row_refs, prob, dscore, dq, *every_lse)
    dkv, dq = outs[: len(KEEP)], outs[len(KEEP) :]
    dq = swap_slabs(dq, groups)
    from_parts = [
        swap(jnp.stack([x[at] for x in dq]), "part", b, parts) for at, b in enumerate(blocks) if b
    ]
    pairs = swap_back(dkv, from_parts)
    out_q, out_k, out_v = pl.pallas_call(
        functools.partial(write_kernel, nears, heads),
        in_specs=[VMEM] * (len(pairs) + groups + parts - 1),
        out_specs=[HBM] * 3,
        out_shape=[
            jax.ShapeDtypeStruct((own_lines, DH), jnp.bfloat16),
            jax.ShapeDtypeStruct(keys.shape, jnp.bfloat16),
            jax.ShapeDtypeStruct(values.shape, jnp.bfloat16),
        ],
        scratch_shapes=[
            pltpu.VMEM((groups, lines, DH), jnp.bfloat16),
            pltpu.SemaphoreType.DMA((4 * len(KEEP) + groups,)),
        ],
        compiler_params=PARAMS,
    )(*pairs, *dq, *from_parts)
    out_q = out_q.reshape(own_heads, rows, DH).transpose(1, 0, 2).reshape(rows, own_heads * DH)
    return out_q, out_k, out_v


def solution(mesh):
    ctx, heads = mesh.shape["ctx"], mesh.shape["head"]
    groups = KVH // heads
    parts = ctx // groups
    nears = min(2, groups)
    row_count = groups // nears
    fine = Mesh(
        mesh.devices.reshape(parts, row_count, nears, heads), ("part", "row", "near", "head")
    )
    rows = P(("part", "row", "near"), "head")
    tokens = P(("part", "row", "near", "head"), None)
    return jax.shard_map(
        functools.partial(shards, parts, row_count, nears, heads),
        mesh=fine,
        in_specs=(rows, rows, rows, rows, tokens, tokens, P(), P()),
        out_specs=(rows, tokens, tokens),
        check_vma=False,
    )
```

```python
import functools

import jax
import jax.numpy as jnp
from jax import lax
from jax.experimental import pallas as pl
from jax.experimental.pallas import tpu as pltpu
from jax.sharding import Mesh, PartitionSpec as P

DH = 128
KVH = 8
RESP_LEN = 64
SCALE = DH ** (-0.5)
LOG2E = 1.4426950408889634
MASKED_SCORE = -1e30
DEAD_LSE = 1e30
PIECES = 3
STAT_ROWS = 16
STEP_LINES = 1024
PARAMS = pltpu.CompilerParams(vmem_limit_bytes=24 * 1024 * 1024)
ANY = pl.BlockSpec(memory_space=pl.ANY)
HBM = pl.BlockSpec(memory_space=pltpu.HBM)
VMEM = pl.BlockSpec(memory_space=pltpu.VMEM)

FIRST = 2
KEEP = (0, 1, 4, 5)


def split_pieces(x):
    first = x.astype(jnp.bfloat16)
    rest = x - first.astype(jnp.float32)
    second = rest.astype(jnp.bfloat16)
    third = (rest - second.astype(jnp.float32)).astype(jnp.bfloat16)
    return first, second, third


def shift_of(n):
    assert n & (n - 1) == 0
    return n.bit_length() - 1


def column_of(member, groups, heads):
    head_index, group_index = member & (heads - 1), member >> shift_of(heads)
    return pl.multiple_of((head_index * groups + group_index) * DH, DH)


def place(nears, heads):
    row, near = lax.axis_index("row"), lax.axis_index("near")
    member = (row * nears + near) * heads + lax.axis_index("head")
    return member, row, near, lax.axis_index("part")


def group_at(at, row_xor, near_xor, nears):
    return (at[1] ^ row_xor) * nears + (at[2] ^ near_xor)


def pack_kernel(row_count, nears, heads, q_hbm, o_grad_hbm, o_hbm, lse_hbm, k_hbm, v_hbm, *rest):
    groups = row_count * nears
    slab_refs, (keep_ref, send_ref, o_ref, lse_ref, sems) = rest[:groups], rest[groups:]
    at = place(nears, heads)
    rows, own_heads = lse_ref.shape
    lines = o_ref.shape[0] // groups
    tokens = k_hbm.shape[0]
    copies = [(lse_hbm, lse_ref), (o_hbm, o_ref)]
    slabs = []
    for m, ref in enumerate(slab_refs):
        first = pl.multiple_of(group_at(at, m // nears, m % nears, nears) * lines, lines)
        slabs.append((ref, first))
        copies.append((o_grad_hbm.at[pl.ds(first, lines), :], ref.at[lines : 2 * lines, :]))
    stat_copies = len(copies)
    for ref, first in slabs:
        copies.append((q_hbm.at[pl.ds(first, lines), :], ref.at[0:lines, :]))
    for i, j in enumerate(KEEP):
        for ref, peer in ((send_ref, j ^ FIRST), (keep_ref, j)):
            columns = pl.ds(column_of(at[0] ^ peer, groups, heads), DH)
            copies.append((k_hbm.at[:, columns], ref.at[i, 0:tokens, :]))
            copies.append((v_hbm.at[:, columns], ref.at[i, tokens : 2 * tokens, :]))
    copies = [pltpu.make_async_copy(s, t, sems.at[n]) for n, (s, t) in enumerate(copies)]
    for copy in copies:
        copy.start()

    wide = 2 * lines
    shape = (own_heads, wide)
    head_ids = lax.broadcasted_iota(jnp.int32, shape, 0)
    line_heads = (lax.broadcasted_iota(jnp.int32, shape, 1) & (lines - 1)) >> shift_of(rows)
    chosen = jnp.concatenate(
        [(head_ids == line_heads + (first >> shift_of(rows))) for _, first in slabs], axis=1
    ).astype(jnp.bfloat16)
    shape = (STAT_ROWS, chosen.shape[1])
    own_row = (lax.broadcasted_iota(jnp.int32, shape, 0) & (rows - 1)) == (
        lax.broadcasted_iota(jnp.int32, shape, 1) & (rows - 1)
    )
    shape = (STAT_ROWS, STAT_ROWS)
    gather = lax.broadcasted_iota(jnp.int32, shape, 0) == (
        lax.broadcasted_iota(jnp.int32, shape, 1) >> shift_of(rows)
    )
    for copy in copies[:stat_copies]:
        copy.wait()
    pieces = [piece.astype(jnp.float32) for piece in split_pieces(lse_ref[...])]
    pieces.append(jnp.zeros((STAT_ROWS - PIECES * rows, own_heads), jnp.float32))
    pieces = jnp.concatenate(pieces, axis=0).astype(jnp.bfloat16)
    spread = jnp.dot(pieces, chosen, preferred_element_type=jnp.float32)
    spread = jnp.where(own_row, spread, 0.0).astype(jnp.bfloat16)
    lse_rows_all = jnp.dot(
        gather.astype(jnp.bfloat16), spread, preferred_element_type=jnp.float32
    )
    kind = lax.broadcasted_iota(jnp.int32, (STAT_ROWS, wide), 0)
    for m, (ref, first) in enumerate(slabs):
        o_grad = ref[lines:wide, :].astype(jnp.float32)
        product = o_grad * o_ref[pl.ds(first, lines), :].astype(jnp.float32)
        dots = jnp.sum(jnp.concatenate([product, product], axis=0).T, axis=0, keepdims=True)
        stats = lse_rows_all[:, m * wide : (m + 1) * wide]
        for k, piece in enumerate(split_pieces(dots)):
            stats = jnp.where(kind == PIECES + k, piece.astype(jnp.float32), stats)
        ref[wide:, :] = stats.astype(jnp.bfloat16)
    for copy in copies[stat_copies:]:
        copy.wait()


def pair_starts(at, i, tokens):
    first = at[3] * KVH
    return [(first + (at[0] ^ KEEP[i] ^ other)) * tokens for other in (0, FIRST)]


def pair_keys(ref, tokens):
    return jnp.concatenate([ref[0, 0:tokens, :], ref[1, 0:tokens, :]], axis=0)


def pair_values(ref, tokens):
    return jnp.concatenate([ref[0, tokens : 2 * tokens, :], ref[1, tokens : 2 * tokens, :]], axis=0)


def all_visible(at, ends, tokens):
    last = (at[3] + 1) * (KVH * tokens)
    return jnp.min(ends.astype(jnp.float32)) >= last.astype(jnp.float32)


def hide(values, ends, at, i, tokens, hidden):
    offset = lax.broadcasted_iota(jnp.int32, (tokens, values.shape[1]), 0)
    starts = pair_starts(at, i, tokens)
    visible = jnp.concatenate([offset < ends - start for start in starts], axis=0)
    return jnp.where(visible, values, hidden)


def in_branches(condition, body):
    pl.when(condition)(functools.partial(body, True))
    pl.when(jnp.logical_not(condition))(functools.partial(body, False))


def lse_rows(size):
    return max(1, size // DH)


def slabs_of(row_refs):
    return [[(ref, m) for m in range(ref.shape[0])] for ref in row_refs]


def lines_of(slabs, first, lines):
    return jnp.concatenate([ref[j, first : first + lines, :] for ref, j in slabs], axis=0)


def stat_kernel(blocks, first, nears, heads, tokens, ends_ref, *refs):
    at = place(nears, heads)
    row_refs, refs = refs[: len(blocks)], refs[len(blocks) :]
    pair_refs, before_refs, lse_ref = refs[: len(KEEP)], refs[len(KEEP) : -1], refs[-1]
    lines = (row_refs[0].shape[1] - STAT_ROWS) // 2
    for ref in before_refs:
        lse_ref[...] = ref[...]

    def body(seen):
        for m, (b, slabs) in enumerate(zip(blocks, slabs_of(row_refs))):
            count = len(slabs) * lines
            q = lines_of(slabs, 0, lines)
            ends = ends_ref[:, first + m * count : first + (m + 1) * count]
            scores = []
            for i, ref in enumerate(pair_refs):
                part = lax.dot_general(
                    pair_keys(ref, tokens),
                    q,
                    (((1,), (1,)), ((), ())),
                    preferred_element_type=jnp.float32,
                )
                scores.append(part if seen else hide(part, ends, at, i, tokens, MASKED_SCORE))
            scores = jnp.concatenate(scores, axis=0)
            peak = jnp.max(scores, axis=0, keepdims=True)
            total = jnp.sum(jnp.exp2((scores - peak) * (SCALE * LOG2E)), axis=0, keepdims=True)
            lse = peak * SCALE + jnp.log(total)
            if count < DH:
                lse = jnp.concatenate([lse] * (DH // count), axis=1)
            held = lse_rows(count)
            for k in range(held):
                lse_ref[pl.ds((at[3] ^ b) * held + k, 1), :] = lse[:, k * DH : (k + 1) * DH]

    in_branches(all_visible(at, ends_ref[...], tokens), body)


def line_values(slabs, lines, first_piece):
    low = lax.broadcasted_iota(jnp.int32, (1, 2 * lines), 1) < lines
    out = []
    for n in range(0, len(slabs), 2):
        held = [
            ref[j, 2 * lines : 2 * lines + STAT_ROWS, :].astype(jnp.float32)
            for ref, j in slabs[n : n + 2]
        ]
        total = None
        for k in range(first_piece, first_piece + PIECES):
            piece = jnp.where(low, held[0][k : k + 1], held[1][k : k + 1])
            total = piece if total is None else total + piece
        out.append(total)
    return jnp.concatenate(out, axis=1)


def lse_lines(lse_ref, at, blocks, size):
    held = lse_rows(size)
    tiles = []
    for b in blocks:
        for k in range(held):
            tile = lse_ref[pl.ds((at[3] ^ b) * held + k, 1), :]
            tiles.append(tile[:, : min(size, DH)])
    return jnp.concatenate(tiles, axis=1)


def steps_of(blocks, all_slabs, lines):
    size = len(all_slabs[0]) * lines
    step = min(len(blocks), STEP_LINES // size)
    for c in range(0, len(blocks), step):
        slabs = [slab for held in all_slabs[c : c + step] for slab in held]
        yield c * size, step * size, blocks[c : c + step], slabs


def part_kernel(blocks, nears, heads, tokens, ends_ref, *refs):
    at = place(nears, heads)
    row_refs, refs = refs[: len(blocks)], refs[len(blocks) :]
    pair_refs, (lse_ref, prob_ref, dscore_ref, dq_ref) = refs[: len(KEEP)], refs[len(KEEP) :]
    lines = (row_refs[0].shape[1] - STAT_ROWS) // 2
    all_slabs = slabs_of(row_refs)
    size = len(all_slabs[0]) * lines

    def body(seen):
        for first, count, held, slabs in steps_of(blocks, all_slabs, lines):
            q, o_grad = lines_of(slabs, 0, lines), lines_of(slabs, lines, lines)
            dots = line_values(slabs, lines, PIECES)
            lse = lse_lines(lse_ref, at, held, size) * LOG2E
            lanes = slice(first, first + count)
            dq_t = jnp.zeros((DH, count), jnp.float32)
            for i, ref in enumerate(pair_refs):
                k, v = pair_keys(ref, tokens), pair_values(ref, tokens)
                scores = lax.dot_general(
                    k, q, (((1,), (1,)), ((), ())), preferred_element_type=jnp.float32
                )
                prob = jnp.exp2(scores * (SCALE * LOG2E) - lse)
                if not seen:
                    prob = hide(prob, ends_ref[:, lanes], at, i, tokens, 0.0)
                dprob = lax.dot_general(
                    v, o_grad, (((1,), (1,)), ((), ())), preferred_element_type=jnp.float32
                )
                dscore = (prob * (dprob - dots)).astype(jnp.bfloat16)
                prob_ref[i, :, lanes] = prob.astype(jnp.bfloat16)
                dscore_ref[i, :, lanes] = dscore
                dq_t = dq_t + jnp.dot(k.T, dscore, preferred_element_type=jnp.float32)
            dq_ref[:, lanes] = dq_t

    in_branches(all_visible(at, ends_ref[...], tokens), body)


def token_kernel(blocks, nears, heads, tokens, live_ref, *refs):
    at = place(nears, heads)
    row_refs, refs = refs[: len(blocks)], refs[len(blocks) :]
    (prob_ref, dscore_ref, dq_ref), refs = refs[:3], refs[3:]
    lse_refs, refs = refs[: len(blocks)], refs[len(blocks) :]
    dkv_refs, (*dq_refs, dk_acc, dv_acc) = refs[: len(KEEP)], refs[len(KEEP) :]
    lines = (row_refs[0].shape[1] - STAT_ROWS) // 2
    all_slabs = slabs_of(row_refs)
    size = len(all_slabs[0]) * lines
    for first, count, held, slabs in steps_of(blocks, all_slabs, lines):
        lanes = slice(first, first + count)
        part_lse = [lse_lines(ref, at, held, size) for ref in lse_refs]
        self_lse = line_values(slabs, lines, 0)
        peak = functools.reduce(jnp.maximum, part_lse, self_lse)
        total = sum(jnp.exp(x - peak) for x in part_lse) + jnp.exp(self_lse - peak)
        lse = jnp.where(live_ref[:, lanes] > 0, peak + jnp.log(total), DEAD_LSE)
        weight = jnp.exp(part_lse[0] - lse)
        dq = (dq_ref[:, lanes] * (weight * SCALE)).T.astype(jnp.bfloat16)
        groups = len(all_slabs[0])
        for m in range(len(slabs)):
            block, j, n = first // size + m // groups, m % groups // nears, m % nears
            dq_refs[n][block, j] = dq[m * lines : (m + 1) * lines]
        weight_t = jnp.broadcast_to(weight, (DH, count)).T
        q, o_grad = (
            (lines_of(slabs, start, lines).astype(jnp.float32) * weight_t).astype(jnp.bfloat16)
            for start in (0, lines)
        )
        for i in range(len(KEEP)):
            dk = jnp.dot(dscore_ref[i, :, lanes], q, preferred_element_type=jnp.float32) * SCALE
            dv = jnp.dot(prob_ref[i, :, lanes], o_grad, preferred_element_type=jnp.float32)
            if first > 0:
                dk = dk + dk_acc[i]
                dv = dv + dv_acc[i]
            if first + count < len(blocks) * size:
                dk_acc[i] = dk
                dv_acc[i] = dv
            else:
                for n in range(2):
                    inner = slice(n * tokens, (n + 1) * tokens)
                    dkv_refs[i][n, 0:tokens, :] = dk[inner].astype(jnp.bfloat16)
                    dkv_refs[i][n, tokens : 2 * tokens, :] = dv[inner].astype(jnp.bfloat16)


def add_query_kernel(nears, *refs):
    own_refs, came_refs, out_refs = refs[:nears], refs[nears:-2], refs[-2:]
    for n in range(nears):
        for j in range(own_refs[0].shape[1]):
            total = own_refs[n][0, j].astype(jnp.float32)
            for ref in came_refs:
                total = total + ref[n, j].astype(jnp.float32)
            out_refs[min(j, 1)][n] = total.astype(jnp.bfloat16)


def tie_kernel(*refs):
    pass


def write_kernel(nears, heads, *refs):
    at = place(nears, heads)
    pair_refs, came_ref, refs = refs[: len(KEEP)], refs[len(KEEP)], refs[len(KEEP) + 1 :]
    slab_refs, (out_q_ref, out_k_ref, out_v_ref, sems) = refs[:-4], refs[-4:]
    groups, lines, tokens = len(slab_refs) * nears, slab_refs[0].shape[1], out_k_ref.shape[0]
    copies = []
    for i, ref in enumerate(pair_refs):
        for source, other in ((ref.at[0], 0), (came_ref.at[i], FIRST)):
            columns = pl.ds(column_of(at[0] ^ KEEP[i] ^ other, groups, heads), DH)
            copies.append((source.at[0:tokens, :], out_k_ref.at[:, columns]))
            copies.append((source.at[tokens : 2 * tokens, :], out_v_ref.at[:, columns]))
    for j, ref in enumerate(slab_refs):
        for n in range(nears):
            first = pl.multiple_of(group_at(at, j, n, nears) * lines, lines)
            copies.append((ref.at[n], out_q_ref.at[pl.ds(first, lines), :]))
    copies = [pltpu.make_async_copy(s, t, sems.at[n]) for n, (s, t) in enumerate(copies)]
    for copy in copies:
        copy.start()
    for copy in copies:
        copy.wait()


def swap(x, axis, distance, size):
    return lax.ppermute(x, axis, [(i, i ^ distance) for i in range(size)])


def swap_pairs(keep, send):
    members = ("row", "near", "head")
    came = swap(send, members, FIRST, KVH)
    pairs = [jnp.stack([keep[i], came[i]]) for i in range(len(KEEP))]
    return [swap(x, members, j, KVH) if j else x for x, j in zip(pairs, KEEP)]


def tie(x, others):
    return pl.pallas_call(
        tie_kernel,
        in_specs=[ANY] * (1 + len(others)),
        out_specs=ANY,
        out_shape=jax.ShapeDtypeStruct(x.shape, x.dtype),
        input_output_aliases={0: 0},
        compiler_params=PARAMS,
    )(x, *others)


def swap_back(pairs, after):
    members = ("row", "near", "head")
    pairs = [swap(x, members, j, KVH) if j else x for x, j in zip(pairs, KEEP)]
    beyond = tie(jnp.stack([x[1] for x in pairs]), after)
    return [*pairs, swap(beyond, members, FIRST, KVH)]


def swap_slabs(slabs, groups):
    return [swap(x, ("row", "near"), m, groups) if m else x for m, x in enumerate(slabs)]


def line_limits(parts, row_count, nears, rows, lines, resp_len, prompt_end):
    line = lax.broadcasted_iota(jnp.int32, (1, parts * nears * row_count * lines), 1)
    slab = line >> shift_of(lines)
    near_xor = slab & (nears - 1)
    row_xor = (slab >> shift_of(nears)) & (row_count - 1)
    place_of_block = slab >> shift_of(row_count * nears)
    block, bits = jnp.zeros_like(line), shift_of(parts)
    for k in range(bits):
        block = block | (((place_of_block >> k) & 1) << (bits - 1 - k))
    device = (lax.axis_index("part") ^ block) * row_count + (lax.axis_index("row") ^ row_xor)
    device = device * nears + (lax.axis_index("near") ^ near_xor)
    row = device * rows + (line & (rows - 1))
    ends, lengths = jnp.zeros_like(row), jnp.zeros_like(row)
    for r in range(resp_len.shape[0]):
        own = row >> shift_of(RESP_LEN) == r
        ends, lengths = jnp.where(own, prompt_end[r], ends), jnp.where(own, resp_len[r], lengths)
    return ends, ((row & (RESP_LEN - 1)) < lengths).astype(jnp.int32)


def shards(parts, row_count, nears, heads, queries, grad_out, outputs, lse_self, keys, values, resp_len, prompt_end):
    rows = queries.shape[0]
    own_heads = queries.shape[1] // DH
    own_lines = rows * own_heads
    groups = row_count * nears
    lines = own_lines // groups
    tokens = keys.shape[0]
    assert 2 * lines == DH and RESP_LEN % (groups * rows) == 0 and row_count <= 2 and nears <= 2

    def as_lines(x):
        return x.reshape(rows, own_heads, DH).transpose(1, 0, 2).reshape(own_lines, DH)

    def in_hbm(x):
        return pltpu.with_memory_space_constraint(x, pltpu.HBM)

    half_shape = jax.ShapeDtypeStruct((len(KEEP), 2 * tokens, DH), jnp.bfloat16)
    slab_shape = jax.ShapeDtypeStruct((2 * lines + STAT_ROWS, DH), jnp.bfloat16)
    *slabs, kv_keep, kv_send = pl.pallas_call(
        functools.partial(pack_kernel, row_count, nears, heads),
        in_specs=[HBM] * 6,
        out_specs=[VMEM] * (groups + 2),
        out_shape=[slab_shape] * groups + [half_shape] * 2,
        scratch_shapes=[
            pltpu.VMEM((own_lines, DH), jnp.bfloat16),
            pltpu.VMEM(lse_self.shape, jnp.float32),
            pltpu.SemaphoreType.DMA((2 + 2 * groups + 4 * len(KEEP),)),
        ],
        compiler_params=PARAMS,
    )(
        in_hbm(as_lines(queries)),
        in_hbm(as_lines(grad_out)),
        in_hbm(as_lines(outputs)),
        in_hbm(lse_self),
        in_hbm(keys),
        in_hbm(values),
    )
    own_block = jnp.stack(swap_slabs(slabs, groups))
    pairs = swap_pairs(kv_keep, kv_send)
    far = [1 << n for n in reversed(range(shift_of(parts)))]

    blocks, came = [0], [own_block]
    for d in far:
        if d == 1:
            came = came[:1] + [tie(x, pairs[1:]) for x in came[1:]]
        came = came + [swap(x, "part", d, parts) for x in came]
        blocks = blocks + [b ^ d for b in blocks]
    ends, live = line_limits(parts, row_count, nears, rows, lines, resp_len, prompt_end)

    def part_lse(held, first, refs, before):
        return pl.pallas_call(
            functools.partial(stat_kernel, held, first, nears, heads, tokens),
            in_specs=[VMEM] * (1 + len(refs) + len(KEEP) + len(before)),
            out_shape=jax.ShapeDtypeStruct((parts * lse_rows(groups * lines), DH), jnp.float32),
            compiler_params=PARAMS,
        )(ends, *refs, *pairs, *before)

    lse = [part_lse(blocks[:-1], 0, came[:-1], [])]
    row_refs = [*came[:-1], tie(came[-1], lse)]
    lse = [part_lse(blocks[-1:], (parts - 1) * groups * lines, row_refs[-1:], lse)]
    every_lse = lse + [swap(lse[0], "part", d, parts) for d in range(1, parts)]

    all_lines = parts * groups * lines
    score_shape = jax.ShapeDtypeStruct((len(KEEP), 2 * tokens, all_lines), jnp.bfloat16)
    prob, dscore, dq = pl.pallas_call(
        functools.partial(part_kernel, blocks, nears, heads, tokens),
        in_specs=[VMEM] * (1 + len(row_refs) + len(KEEP) + 1),
        out_specs=[VMEM] * 3,
        out_shape=[score_shape] * 2 + [jax.ShapeDtypeStruct((DH, all_lines), jnp.float32)],
        compiler_params=PARAMS,
    )(ends, *row_refs, *pairs, *lse)
    dq_shape = jax.ShapeDtypeStruct((parts, row_count, lines, DH), jnp.bfloat16)
    acc = pltpu.VMEM((len(KEEP), 2 * tokens, DH), jnp.float32)
    outs = pl.pallas_call(
        functools.partial(token_kernel, blocks, nears, heads, tokens),
        in_specs=[VMEM] * (1 + len(row_refs) + 3 + parts),
        out_shape=[jax.ShapeDtypeStruct((2, 2 * tokens, DH), jnp.bfloat16)] * len(KEEP)
        + [dq_shape] * nears,
        scratch_shapes=[acc] * 2,
        compiler_params=PARAMS,
    )(live, *row_refs, prob, dscore, dq, *every_lse)
    dkv, dq = outs[: len(KEEP)], outs[len(KEEP) :]
    dq = [swap(x, "near", n, nears) if n else x for n, x in enumerate(dq)]
    from_parts = [
        swap(jnp.stack([x[at] for x in dq]), "part", b, parts) for at, b in enumerate(blocks) if b
    ]
    sum_shape = jax.ShapeDtypeStruct((nears, lines, DH), jnp.bfloat16)
    sums = pl.pallas_call(
        functools.partial(add_query_kernel, nears),
        in_specs=[VMEM] * (nears + len(from_parts)),
        out_shape=[sum_shape] * 2,
        compiler_params=PARAMS,
    )(*dq, *from_parts)
    sums = [swap(x, "row", j, row_count) if j else x for j, x in enumerate(sums[:row_count])]
    pairs = swap_back(dkv, sums[:1])
    out_q, out_k, out_v = pl.pallas_call(
        functools.partial(write_kernel, nears, heads),
        in_specs=[VMEM] * (row_count + len(pairs)),
        out_specs=[HBM] * 3,
        out_shape=[
            jax.ShapeDtypeStruct((own_lines, DH), jnp.bfloat16),
            jax.ShapeDtypeStruct(keys.shape, jnp.bfloat16),
            jax.ShapeDtypeStruct(values.shape, jnp.bfloat16),
        ],
        scratch_shapes=[pltpu.SemaphoreType.DMA((4 * len(KEEP) + groups,))],
        compiler_params=PARAMS,
    )(*pairs, *sums)
    out_q = out_q.reshape(own_heads, rows, DH).transpose(1, 0, 2).reshape(rows, own_heads * DH)
    return out_q, out_k, out_v


def solution(mesh):
    ctx, heads = mesh.shape["ctx"], mesh.shape["head"]
    groups = KVH // heads
    parts = ctx // groups
    nears = min(2, groups)
    row_count = groups // nears
    fine = Mesh(
        mesh.devices.reshape(parts, row_count, nears, heads), ("part", "row", "near", "head")
    )
    rows = P(("part", "row", "near"), "head")
    tokens = P(("part", "row", "near", "head"), None)
    return jax.shard_map(
        functools.partial(shards, parts, row_count, nears, heads),
        mesh=fine,
        in_specs=(rows, rows, rows, rows, tokens, tokens, P(), P()),
        out_specs=(rows, tokens, tokens),
        check_vma=False,
    )
```

```python
import functools

import jax
import jax.numpy as jnp
from jax import lax
from jax.experimental import pallas as pl
from jax.experimental.pallas import tpu as pltpu
from jax.sharding import Mesh, PartitionSpec as P

DH = 128
KVH = 8
RESP_LEN = 64
SCALE = DH ** (-0.5)
LOG2E = 1.4426950408889634
MASKED_SCORE = -1e30
DEAD_LSE = 1e30
PIECES = 3
STAT_ROWS = 16
STEP_LINES = 1024
PARAMS = pltpu.CompilerParams(vmem_limit_bytes=24 * 1024 * 1024)
ANY = pl.BlockSpec(memory_space=pl.ANY)
HBM = pl.BlockSpec(memory_space=pltpu.HBM)
VMEM = pl.BlockSpec(memory_space=pltpu.VMEM)

FIRST = 2
KEEP = (0, 1, 4, 5)


def split_pieces(x):
    first = x.astype(jnp.bfloat16)
    rest = x - first.astype(jnp.float32)
    second = rest.astype(jnp.bfloat16)
    third = (rest - second.astype(jnp.float32)).astype(jnp.bfloat16)
    return first, second, third


def shift_of(n):
    assert n & (n - 1) == 0
    return n.bit_length() - 1


def column_of(member, groups, heads):
    head_index, group_index = member & (heads - 1), member >> shift_of(heads)
    return pl.multiple_of((head_index * groups + group_index) * DH, DH)


def place(nears, heads):
    row, near = lax.axis_index("row"), lax.axis_index("near")
    member = (row * nears + near) * heads + lax.axis_index("head")
    return member, row, near, lax.axis_index("part")


def group_at(at, row_xor, near_xor, nears):
    return (at[1] ^ row_xor) * nears + (at[2] ^ near_xor)


def pack_kernel(row_count, nears, heads, q_hbm, o_grad_hbm, o_hbm, lse_hbm, k_hbm, v_hbm, *rest):
    groups = row_count * nears
    slab_refs, (keep_ref, send_ref, o_ref, lse_ref, sems) = rest[:groups], rest[groups:]
    at = place(nears, heads)
    rows, own_heads = lse_ref.shape
    lines = o_ref.shape[0] // groups
    tokens = k_hbm.shape[0]
    copies = [(lse_hbm, lse_ref), (o_hbm, o_ref)]
    slabs = []
    for m, ref in enumerate(slab_refs):
        first = pl.multiple_of(group_at(at, m // nears, m % nears, nears) * lines, lines)
        slabs.append((ref, first))
        copies.append((o_grad_hbm.at[pl.ds(first, lines), :], ref.at[lines : 2 * lines, :]))
    stat_copies = len(copies)
    for ref, first in slabs:
        copies.append((q_hbm.at[pl.ds(first, lines), :], ref.at[0:lines, :]))
    for i, j in enumerate(KEEP):
        for ref, peer in ((send_ref, j ^ FIRST), (keep_ref, j)):
            columns = pl.ds(column_of(at[0] ^ peer, groups, heads), DH)
            copies.append((k_hbm.at[:, columns], ref.at[i, 0:tokens, :]))
            copies.append((v_hbm.at[:, columns], ref.at[i, tokens : 2 * tokens, :]))
    copies = [pltpu.make_async_copy(s, t, sems.at[n]) for n, (s, t) in enumerate(copies)]
    for copy in copies:
        copy.start()

    wide = 2 * lines
    shape = (own_heads, wide)
    head_ids = lax.broadcasted_iota(jnp.int32, shape, 0)
    line_heads = (lax.broadcasted_iota(jnp.int32, shape, 1) & (lines - 1)) >> shift_of(rows)
    chosen = jnp.concatenate(
        [(head_ids == line_heads + (first >> shift_of(rows))) for _, first in slabs], axis=1
    ).astype(jnp.bfloat16)
    shape = (STAT_ROWS, chosen.shape[1])
    own_row = (lax.broadcasted_iota(jnp.int32, shape, 0) & (rows - 1)) == (
        lax.broadcasted_iota(jnp.int32, shape, 1) & (rows - 1)
    )
    shape = (STAT_ROWS, STAT_ROWS)
    gather = lax.broadcasted_iota(jnp.int32, shape, 0) == (
        lax.broadcasted_iota(jnp.int32, shape, 1) >> shift_of(rows)
    )
    for copy in copies[:stat_copies]:
        copy.wait()
    pieces = [piece.astype(jnp.float32) for piece in split_pieces(lse_ref[...])]
    pieces.append(jnp.zeros((STAT_ROWS - PIECES * rows, own_heads), jnp.float32))
    pieces = jnp.concatenate(pieces, axis=0).astype(jnp.bfloat16)
    spread = jnp.dot(pieces, chosen, preferred_element_type=jnp.float32)
    spread = jnp.where(own_row, spread, 0.0).astype(jnp.bfloat16)
    lse_rows_all = jnp.dot(
        gather.astype(jnp.bfloat16), spread, preferred_element_type=jnp.float32
    )
    kind = lax.broadcasted_iota(jnp.int32, (STAT_ROWS, wide), 0)
    for m, (ref, first) in enumerate(slabs):
        o_grad = ref[lines:wide, :].astype(jnp.float32)
        product = o_grad * o_ref[pl.ds(first, lines), :].astype(jnp.float32)
        dots = jnp.sum(jnp.concatenate([product, product], axis=0).T, axis=0, keepdims=True)
        stats = lse_rows_all[:, m * wide : (m + 1) * wide]
        for k, piece in enumerate(split_pieces(dots)):
            stats = jnp.where(kind == PIECES + k, piece.astype(jnp.float32), stats)
        ref[wide:, :] = stats.astype(jnp.bfloat16)
    for copy in copies[stat_copies:]:
        copy.wait()


def pair_starts(at, i, tokens):
    first = at[3] * KVH
    return [(first + (at[0] ^ KEEP[i] ^ other)) * tokens for other in (0, FIRST)]


def pair_keys(ref, tokens):
    return jnp.concatenate([ref[0, 0:tokens, :], ref[1, 0:tokens, :]], axis=0)


def pair_values(ref, tokens):
    return jnp.concatenate([ref[0, tokens : 2 * tokens, :], ref[1, tokens : 2 * tokens, :]], axis=0)


def all_visible(at, ends, tokens):
    last = (at[3] + 1) * (KVH * tokens)
    return jnp.min(ends.astype(jnp.float32)) >= last.astype(jnp.float32)


def hide(values, ends, at, i, tokens, hidden):
    offset = lax.broadcasted_iota(jnp.int32, (tokens, values.shape[1]), 0)
    starts = pair_starts(at, i, tokens)
    visible = jnp.concatenate([offset < ends - start for start in starts], axis=0)
    return jnp.where(visible, values, hidden)


def in_branches(condition, body):
    pl.when(condition)(functools.partial(body, True))
    pl.when(jnp.logical_not(condition))(functools.partial(body, False))


def lse_rows(size):
    return max(1, size // DH)


def block_kernel(*refs):
    slab_refs, out_ref = refs[:-1], refs[-1]
    low = lax.broadcasted_iota(jnp.int32, (STAT_ROWS, DH), 1) < DH // 2
    stats = []
    for m, ref in enumerate(slab_refs):
        out_ref[m * DH : (m + 1) * DH, :] = ref[0:DH, :]
        stats.append(ref[DH : DH + STAT_ROWS, :].astype(jnp.float32))
    if len(stats) > 1:
        pairs = [
            jnp.where(low, stats[m], stats[m + 1])[: 2 * PIECES] for m in range(0, len(stats), 2)
        ]
        rest = STAT_ROWS - len(pairs) * 2 * PIECES
        stats = [jnp.concatenate([*pairs, jnp.zeros((rest, DH), jnp.float32)], axis=0)]
    out_ref[len(slab_refs) * DH :, :] = stats[0].astype(jnp.bfloat16)


def slabs_of(row_refs):
    return [[(ref, m) for m in range(ref.shape[0] // DH)] for ref in row_refs]


def lines_of(slabs, first, lines):
    return jnp.concatenate(
        [ref[m * DH + first : m * DH + first + lines, :] for ref, m in slabs], axis=0
    )


def stat_kernel(blocks, first, nears, heads, tokens, ends_ref, *refs):
    at = place(nears, heads)
    row_refs, refs = refs[: len(blocks)], refs[len(blocks) :]
    pair_refs, before_refs, lse_ref = refs[: len(KEEP)], refs[len(KEEP) : -1], refs[-1]
    lines = DH // 2
    for ref in before_refs:
        lse_ref[...] = ref[...]

    def body(seen):
        for m, (b, slabs) in enumerate(zip(blocks, slabs_of(row_refs))):
            count = len(slabs) * lines
            q = lines_of(slabs, 0, lines)
            ends = ends_ref[:, first + m * count : first + (m + 1) * count]
            scores = []
            for i, ref in enumerate(pair_refs):
                part = lax.dot_general(
                    pair_keys(ref, tokens),
                    q,
                    (((1,), (1,)), ((), ())),
                    preferred_element_type=jnp.float32,
                )
                scores.append(part if seen else hide(part, ends, at, i, tokens, MASKED_SCORE))
            scores = jnp.concatenate(scores, axis=0)
            peak = jnp.max(scores, axis=0, keepdims=True)
            total = jnp.sum(jnp.exp2((scores - peak) * (SCALE * LOG2E)), axis=0, keepdims=True)
            lse = peak * SCALE + jnp.log(total)
            if count < DH:
                lse = jnp.concatenate([lse] * (DH // count), axis=1)
            held = lse_rows(count)
            for k in range(held):
                lse_ref[pl.ds((at[3] ^ b) * held + k, 1), :] = lse[:, k * DH : (k + 1) * DH]

    in_branches(all_visible(at, ends_ref[...], tokens), body)


def line_values(slabs, lines, first_piece):
    low = lax.broadcasted_iota(jnp.int32, (1, 2 * lines), 1) < lines

    def stats_of(ref):
        first = ref.shape[0] - STAT_ROWS
        return ref[first : first + STAT_ROWS, :].astype(jnp.float32)

    out = []
    for n in range(0, len(slabs), 2):
        ref, m = slabs[n]
        total = None
        for k in range(first_piece, first_piece + PIECES):
            if ref.shape[0] > DH + STAT_ROWS:
                k = m // 2 * (2 * PIECES) + k
                piece = stats_of(ref)[k : k + 1]
            else:
                piece = jnp.where(low, stats_of(ref)[k : k + 1], stats_of(slabs[n + 1][0])[k : k + 1])
            total = piece if total is None else total + piece
        out.append(total)
    return jnp.concatenate(out, axis=1)


def lse_lines(lse_ref, at, blocks, size):
    held = lse_rows(size)
    tiles = []
    for b in blocks:
        for k in range(held):
            tile = lse_ref[pl.ds((at[3] ^ b) * held + k, 1), :]
            tiles.append(tile[:, : min(size, DH)])
    return jnp.concatenate(tiles, axis=1)


def steps_of(blocks, all_slabs, lines):
    size = len(all_slabs[0]) * lines
    step = min(len(blocks), STEP_LINES // size)
    for c in range(0, len(blocks), step):
        slabs = [slab for held in all_slabs[c : c + step] for slab in held]
        yield c * size, step * size, blocks[c : c + step], slabs


def part_kernel(blocks, nears, heads, tokens, ends_ref, *refs):
    at = place(nears, heads)
    row_refs, refs = refs[: len(blocks)], refs[len(blocks) :]
    pair_refs, (lse_ref, prob_ref, dscore_ref, dq_ref) = refs[: len(KEEP)], refs[len(KEEP) :]
    lines = DH // 2
    all_slabs = slabs_of(row_refs)
    size = len(all_slabs[0]) * lines

    def body(seen):
        for first, count, held, slabs in steps_of(blocks, all_slabs, lines):
            q, o_grad = lines_of(slabs, 0, lines), lines_of(slabs, lines, lines)
            dots = line_values(slabs, lines, PIECES)
            lse = lse_lines(lse_ref, at, held, size) * LOG2E
            lanes = slice(first, first + count)
            dq_t = jnp.zeros((DH, count), jnp.float32)
            for i, ref in enumerate(pair_refs):
                k, v = pair_keys(ref, tokens), pair_values(ref, tokens)
                scores = lax.dot_general(
                    k, q, (((1,), (1,)), ((), ())), preferred_element_type=jnp.float32
                )
                prob = jnp.exp2(scores * (SCALE * LOG2E) - lse)
                if not seen:
                    prob = hide(prob, ends_ref[:, lanes], at, i, tokens, 0.0)
                dprob = lax.dot_general(
                    v, o_grad, (((1,), (1,)), ((), ())), preferred_element_type=jnp.float32
                )
                dscore = (prob * (dprob - dots)).astype(jnp.bfloat16)
                prob_ref[i, :, lanes] = prob.astype(jnp.bfloat16)
                dscore_ref[i, :, lanes] = dscore
                dq_t = dq_t + jnp.dot(k.T, dscore, preferred_element_type=jnp.float32)
            dq_ref[:, lanes] = dq_t

    in_branches(all_visible(at, ends_ref[...], tokens), body)


def token_kernel(blocks, nears, heads, tokens, live_ref, *refs):
    at = place(nears, heads)
    row_refs, refs = refs[: len(blocks)], refs[len(blocks) :]
    (prob_ref, dscore_ref, dq_ref), refs = refs[:3], refs[3:]
    lse_refs, refs = refs[: len(blocks)], refs[len(blocks) :]
    dkv_refs, (*dq_refs, dk_acc, dv_acc) = refs[: len(KEEP)], refs[len(KEEP) :]
    lines = DH // 2
    all_slabs = slabs_of(row_refs)
    size = len(all_slabs[0]) * lines
    for first, count, held, slabs in steps_of(blocks, all_slabs, lines):
        lanes = slice(first, first + count)
        part_lse = [lse_lines(ref, at, held, size) for ref in lse_refs]
        self_lse = line_values(slabs, lines, 0)
        peak = functools.reduce(jnp.maximum, part_lse, self_lse)
        total = sum(jnp.exp(x - peak) for x in part_lse) + jnp.exp(self_lse - peak)
        lse = jnp.where(live_ref[:, lanes] > 0, peak + jnp.log(total), DEAD_LSE)
        weight = jnp.exp(part_lse[0] - lse)
        dq = (dq_ref[:, lanes] * (weight * SCALE)).T.astype(jnp.bfloat16)
        groups = len(all_slabs[0])
        for m in range(len(slabs)):
            block, j, n = first // size + m // groups, m % groups // nears, m % nears
            dq_refs[n][block, j] = dq[m * lines : (m + 1) * lines]
        weight_t = jnp.broadcast_to(weight, (DH, count)).T
        q, o_grad = (
            (lines_of(slabs, start, lines).astype(jnp.float32) * weight_t).astype(jnp.bfloat16)
            for start in (0, lines)
        )
        for i in range(len(KEEP)):
            dk = jnp.dot(dscore_ref[i, :, lanes], q, preferred_element_type=jnp.float32) * SCALE
            dv = jnp.dot(prob_ref[i, :, lanes], o_grad, preferred_element_type=jnp.float32)
            if first > 0:
                dk = dk + dk_acc[i]
                dv = dv + dv_acc[i]
            if first + count < len(blocks) * size:
                dk_acc[i] = dk
                dv_acc[i] = dv
            else:
                for n in range(2):
                    inner = slice(n * tokens, (n + 1) * tokens)
                    dkv_refs[i][n, 0:tokens, :] = dk[inner].astype(jnp.bfloat16)
                    dkv_refs[i][n, tokens : 2 * tokens, :] = dv[inner].astype(jnp.bfloat16)


def add_query_kernel(nears, *refs):
    own_refs, came_refs, out_refs = refs[:nears], refs[nears:-2], refs[-2:]
    for n in range(nears):
        for j in range(own_refs[0].shape[1]):
            total = own_refs[n][0, j].astype(jnp.float32)
            for ref in came_refs:
                total = total + ref[n, j].astype(jnp.float32)
            out_refs[min(j, 1)][n] = total.astype(jnp.bfloat16)


def tie_kernel(*refs):
    pass


def write_kernel(nears, heads, *refs):
    at = place(nears, heads)
    slab_refs, refs = refs[: -len(KEEP) - 5], refs[-len(KEEP) - 5 :]
    pair_refs, (came_ref, out_q_ref, out_k_ref, out_v_ref, sems) = refs[: len(KEEP)], refs[len(KEEP) :]
    groups, lines, tokens = len(slab_refs) * nears, slab_refs[0].shape[1], out_k_ref.shape[0]
    copies = []
    for i, ref in enumerate(pair_refs):
        for source, other in ((ref.at[0], 0), (came_ref.at[i], FIRST)):
            columns = pl.ds(column_of(at[0] ^ KEEP[i] ^ other, groups, heads), DH)
            copies.append((source.at[0:tokens, :], out_k_ref.at[:, columns]))
            copies.append((source.at[tokens : 2 * tokens, :], out_v_ref.at[:, columns]))
    for j, ref in enumerate(slab_refs):
        for n in range(nears):
            first = pl.multiple_of(group_at(at, j, n, nears) * lines, lines)
            copies.append((ref.at[n], out_q_ref.at[pl.ds(first, lines), :]))
    copies = [pltpu.make_async_copy(s, t, sems.at[n]) for n, (s, t) in enumerate(copies)]
    for copy in copies:
        copy.start()
    for copy in copies:
        copy.wait()


def swap(x, axis, distance, size):
    return lax.ppermute(x, axis, [(i, i ^ distance) for i in range(size)])


def swap_pairs(keep, send):
    members = ("row", "near", "head")
    came = swap(send, members, FIRST, KVH)
    pairs = [jnp.stack([keep[i], came[i]]) for i in range(len(KEEP))]
    return [swap(x, members, j, KVH) if j else x for x, j in zip(pairs, KEEP)]


def tie(x, others):
    return pl.pallas_call(
        tie_kernel,
        in_specs=[ANY] * (1 + len(others)),
        out_specs=ANY,
        out_shape=jax.ShapeDtypeStruct(x.shape, x.dtype),
        input_output_aliases={0: 0},
        compiler_params=PARAMS,
    )(x, *others)


def swap_back(pairs, after):
    members = ("row", "near", "head")
    pairs = [swap(x, members, j, KVH) if j else x for x, j in zip(pairs, KEEP)]
    beyond = tie(jnp.stack([x[1] for x in pairs]), after)
    return [*pairs, swap(beyond, members, FIRST, KVH)]


def swap_slabs(slabs, groups):
    return [swap(x, ("row", "near"), m, groups) if m else x for m, x in enumerate(slabs)]


def line_limits(parts, row_count, nears, rows, lines, resp_len, prompt_end):
    line = lax.broadcasted_iota(jnp.int32, (1, parts * nears * row_count * lines), 1)
    slab = line >> shift_of(lines)
    near_xor = slab & (nears - 1)
    row_xor = (slab >> shift_of(nears)) & (row_count - 1)
    place_of_block = slab >> shift_of(row_count * nears)
    block, bits = jnp.zeros_like(line), shift_of(parts)
    for k in range(bits):
        block = block | (((place_of_block >> k) & 1) << (bits - 1 - k))
    device = (lax.axis_index("part") ^ block) * row_count + (lax.axis_index("row") ^ row_xor)
    device = device * nears + (lax.axis_index("near") ^ near_xor)
    row = device * rows + (line & (rows - 1))
    ends, lengths = jnp.zeros_like(row), jnp.zeros_like(row)
    for r in range(resp_len.shape[0]):
        own = row >> shift_of(RESP_LEN) == r
        ends, lengths = jnp.where(own, prompt_end[r], ends), jnp.where(own, resp_len[r], lengths)
    return ends, ((row & (RESP_LEN - 1)) < lengths).astype(jnp.int32)


def shards(parts, row_count, nears, heads, queries, grad_out, outputs, lse_self, keys, values, resp_len, prompt_end):
    rows = queries.shape[0]
    own_heads = queries.shape[1] // DH
    own_lines = rows * own_heads
    groups = row_count * nears
    lines = own_lines // groups
    tokens = keys.shape[0]
    assert 2 * lines == DH and RESP_LEN % (groups * rows) == 0 and row_count <= 2 and nears <= 2

    def as_lines(x):
        return x.reshape(rows, own_heads, DH).transpose(1, 0, 2).reshape(own_lines, DH)

    def in_hbm(x):
        return pltpu.with_memory_space_constraint(x, pltpu.HBM)

    half_shape = jax.ShapeDtypeStruct((len(KEEP), 2 * tokens, DH), jnp.bfloat16)
    slab_shape = jax.ShapeDtypeStruct((2 * lines + STAT_ROWS, DH), jnp.bfloat16)
    *slabs, kv_keep, kv_send = pl.pallas_call(
        functools.partial(pack_kernel, row_count, nears, heads),
        in_specs=[HBM] * 6,
        out_specs=[VMEM] * (groups + 2),
        out_shape=[slab_shape] * groups + [half_shape] * 2,
        scratch_shapes=[
            pltpu.VMEM((own_lines, DH), jnp.bfloat16),
            pltpu.VMEM(lse_self.shape, jnp.float32),
            pltpu.SemaphoreType.DMA((2 + 2 * groups + 4 * len(KEEP),)),
        ],
        compiler_params=PARAMS,
    )(
        in_hbm(as_lines(queries)),
        in_hbm(as_lines(grad_out)),
        in_hbm(as_lines(outputs)),
        in_hbm(lse_self),
        in_hbm(keys),
        in_hbm(values),
    )
    own_block = pl.pallas_call(
        block_kernel,
        in_specs=[VMEM] * groups,
        out_specs=VMEM,
        out_shape=jax.ShapeDtypeStruct((groups * DH + STAT_ROWS, DH), jnp.bfloat16),
        compiler_params=PARAMS,
    )(*swap_slabs(slabs, groups))
    pairs = swap_pairs(kv_keep, kv_send)
    far = [1 << n for n in reversed(range(shift_of(parts)))]

    blocks, came = [0], [own_block]
    for d in far:
        if d == 1:
            came = came[:1] + [tie(x, pairs[1:]) for x in came[1:]]
        came = came + [swap(x, "part", d, parts) for x in came]
        blocks = blocks + [b ^ d for b in blocks]
    ends, live = line_limits(parts, row_count, nears, rows, lines, resp_len, prompt_end)

    def part_lse(held, first, refs, before):
        return pl.pallas_call(
            functools.partial(stat_kernel, held, first, nears, heads, tokens),
            in_specs=[VMEM] * (1 + len(refs) + len(KEEP) + len(before)),
            out_shape=jax.ShapeDtypeStruct((parts * lse_rows(groups * lines), DH), jnp.float32),
            compiler_params=PARAMS,
        )(ends, *refs, *pairs, *before)

    lse = [part_lse(blocks[:-1], 0, came[:-1], [])]
    row_refs = [*came[:-1], tie(came[-1], lse)]
    lse = [part_lse(blocks[-1:], (parts - 1) * groups * lines, row_refs[-1:], lse)]
    every_lse = lse + [swap(lse[0], "part", d, parts) for d in range(1, parts)]

    all_lines = parts * groups * lines
    score_shape = jax.ShapeDtypeStruct((len(KEEP), 2 * tokens, all_lines), jnp.bfloat16)
    prob, dscore, dq = pl.pallas_call(
        functools.partial(part_kernel, blocks, nears, heads, tokens),
        in_specs=[VMEM] * (1 + len(row_refs) + len(KEEP) + 1),
        out_specs=[VMEM] * 3,
        out_shape=[score_shape] * 2 + [jax.ShapeDtypeStruct((DH, all_lines), jnp.float32)],
        compiler_params=PARAMS,
    )(ends, *row_refs, *pairs, *lse)
    dq_shape = jax.ShapeDtypeStruct((parts, row_count, lines, DH), jnp.bfloat16)
    acc = pltpu.VMEM((len(KEEP), 2 * tokens, DH), jnp.float32)
    outs = pl.pallas_call(
        functools.partial(token_kernel, blocks, nears, heads, tokens),
        in_specs=[VMEM] * (1 + len(row_refs) + 3 + parts),
        out_shape=[jax.ShapeDtypeStruct((2, 2 * tokens, DH), jnp.bfloat16)] * len(KEEP)
        + [dq_shape] * nears,
        scratch_shapes=[acc] * 2,
        compiler_params=PARAMS,
    )(live, *row_refs, prob, dscore, dq, *every_lse)
    dkv, dq = outs[: len(KEEP)], outs[len(KEEP) :]
    dq = [swap(x, "near", n, nears) if n else x for n, x in enumerate(dq)]
    from_parts = [
        swap(jnp.stack([x[at] for x in dq]), "part", b, parts) for at, b in enumerate(blocks) if b
    ]
    sum_shape = jax.ShapeDtypeStruct((nears, lines, DH), jnp.bfloat16)
    sums = pl.pallas_call(
        functools.partial(add_query_kernel, nears),
        in_specs=[VMEM] * (nears + len(from_parts)),
        out_shape=[sum_shape] * 2,
        compiler_params=PARAMS,
    )(*dq, *from_parts)
    pairs = swap_back(dkv, from_parts)
    sums = [swap(x, "row", j, row_count) if j else x for j, x in enumerate(sums[:row_count])]
    out_q, out_k, out_v = pl.pallas_call(
        functools.partial(write_kernel, nears, heads),
        in_specs=[VMEM] * (row_count + len(pairs)),
        out_specs=[HBM] * 3,
        out_shape=[
            jax.ShapeDtypeStruct((own_lines, DH), jnp.bfloat16),
            jax.ShapeDtypeStruct(keys.shape, jnp.bfloat16),
            jax.ShapeDtypeStruct(values.shape, jnp.bfloat16),
        ],
        scratch_shapes=[pltpu.SemaphoreType.DMA((4 * len(KEEP) + groups,))],
        compiler_params=PARAMS,
    )(*sums, *pairs)
    out_q = out_q.reshape(own_heads, rows, DH).transpose(1, 0, 2).reshape(rows, own_heads * DH)
    return out_q, out_k, out_v


def solution(mesh):
    ctx, heads = mesh.shape["ctx"], mesh.shape["head"]
    groups = KVH // heads
    parts = ctx // groups
    nears = min(2, groups)
    row_count = groups // nears
    fine = Mesh(
        mesh.devices.reshape(parts, row_count, nears, heads), ("part", "row", "near", "head")
    )
    rows = P(("part", "row", "near"), "head")
    tokens = P(("part", "row", "near", "head"), None)
    return jax.shard_map(
        functools.partial(shards, parts, row_count, nears, heads),
        mesh=fine,
        in_specs=(rows, rows, rows, rows, tokens, tokens, P(), P()),
        out_specs=(rows, tokens, tokens),
        check_vma=False,
    )
```

```python
import functools

import jax
import jax.numpy as jnp
from jax import lax
from jax.experimental import pallas as pl
from jax.experimental.pallas import tpu as pltpu
from jax.sharding import Mesh, PartitionSpec as P

DH = 128
KVH = 8
RESP_LEN = 64
SCALE = DH ** (-0.5)
LOG2E = 1.4426950408889634
MASKED_SCORE = -1e30
DEAD_LSE = 1e30
PIECES = 3
STAT_ROWS = 16
STEP_LINES = 1024
PARAMS = pltpu.CompilerParams(vmem_limit_bytes=24 * 1024 * 1024)
ANY = pl.BlockSpec(memory_space=pl.ANY)
HBM = pl.BlockSpec(memory_space=pltpu.HBM)
VMEM = pl.BlockSpec(memory_space=pltpu.VMEM)

FIRST = 2
KEEP = (0, 1, 4, 5)


def split_pieces(x):
    first = x.astype(jnp.bfloat16)
    rest = x - first.astype(jnp.float32)
    second = rest.astype(jnp.bfloat16)
    third = (rest - second.astype(jnp.float32)).astype(jnp.bfloat16)
    return first, second, third


def shift_of(n):
    assert n & (n - 1) == 0
    return n.bit_length() - 1


def column_of(member, groups, heads):
    head_index, group_index = member & (heads - 1), member >> shift_of(heads)
    return pl.multiple_of((head_index * groups + group_index) * DH, DH)


def place(nears, heads):
    row, near = lax.axis_index("row"), lax.axis_index("near")
    member = (row * nears + near) * heads + lax.axis_index("head")
    return member, row, near, lax.axis_index("part")


def group_at(at, row_xor, near_xor, nears):
    return (at[1] ^ row_xor) * nears + (at[2] ^ near_xor)


def pack_kernel(row_count, nears, heads, q_hbm, o_grad_hbm, o_hbm, lse_hbm, k_hbm, v_hbm, *rest):
    groups = row_count * nears
    slab_refs, (keep_ref, send_ref, o_ref, lse_ref, sems) = rest[:groups], rest[groups:]
    at = place(nears, heads)
    rows, own_heads = lse_ref.shape
    lines = o_ref.shape[0] // groups
    tokens = k_hbm.shape[0]
    copies = [(lse_hbm, lse_ref), (o_hbm, o_ref)]
    slabs = []
    for m, ref in enumerate(slab_refs):
        first = pl.multiple_of(group_at(at, m // nears, m % nears, nears) * lines, lines)
        slabs.append((ref, first))
        copies.append((o_grad_hbm.at[pl.ds(first, lines), :], ref.at[lines : 2 * lines, :]))
    stat_copies = len(copies)
    for ref, first in slabs:
        copies.append((q_hbm.at[pl.ds(first, lines), :], ref.at[0:lines, :]))
    for i, j in enumerate(KEEP):
        for ref, peer in ((send_ref, j ^ FIRST), (keep_ref, j)):
            columns = pl.ds(column_of(at[0] ^ peer, groups, heads), DH)
            copies.append((k_hbm.at[:, columns], ref.at[i, 0:tokens, :]))
            copies.append((v_hbm.at[:, columns], ref.at[i, tokens : 2 * tokens, :]))
    copies = [pltpu.make_async_copy(s, t, sems.at[n]) for n, (s, t) in enumerate(copies)]
    for copy in copies:
        copy.start()

    wide = 2 * lines
    shape = (own_heads, wide)
    head_ids = lax.broadcasted_iota(jnp.int32, shape, 0)
    line_heads = (lax.broadcasted_iota(jnp.int32, shape, 1) & (lines - 1)) >> shift_of(rows)
    chosen = jnp.concatenate(
        [(head_ids == line_heads + (first >> shift_of(rows))) for _, first in slabs], axis=1
    ).astype(jnp.bfloat16)
    shape = (STAT_ROWS, chosen.shape[1])
    own_row = (lax.broadcasted_iota(jnp.int32, shape, 0) & (rows - 1)) == (
        lax.broadcasted_iota(jnp.int32, shape, 1) & (rows - 1)
    )
    shape = (STAT_ROWS, STAT_ROWS)
    piece_of = lax.broadcasted_iota(jnp.int32, shape, 1) >> shift_of(rows)
    stat_row = lax.broadcasted_iota(jnp.int32, shape, 0)
    for copy in copies[:stat_copies]:
        copy.wait()
    pieces = [piece.astype(jnp.float32) for piece in split_pieces(lse_ref[...])]
    pieces.append(jnp.zeros((STAT_ROWS - PIECES * rows, own_heads), jnp.float32))
    pieces = jnp.concatenate(pieces, axis=0).astype(jnp.bfloat16)
    spread = jnp.dot(pieces, chosen, preferred_element_type=jnp.float32)
    spread = jnp.where(own_row, spread, 0.0).astype(jnp.bfloat16)
    kind = lax.broadcasted_iota(jnp.int32, (STAT_ROWS, wide), 0)
    half = lax.broadcasted_iota(jnp.int32, (STAT_ROWS, wide), 1) >> shift_of(lines)
    for m, (ref, first) in enumerate(slabs):
        top = m // 2 * (2 * PIECES)
        gather = (stat_row - top == piece_of).astype(jnp.bfloat16)
        own = spread[:, m * wide : (m + 1) * wide]
        stats = jnp.dot(gather, own, preferred_element_type=jnp.float32)
        o_grad = ref[lines:wide, :].astype(jnp.float32)
        product = o_grad * o_ref[pl.ds(first, lines), :].astype(jnp.float32)
        dots = jnp.sum(jnp.concatenate([product, product], axis=0).T, axis=0, keepdims=True)
        for k, piece in enumerate(split_pieces(dots)):
            stats = jnp.where(kind == top + PIECES + k, piece.astype(jnp.float32), stats)
        if len(slabs) > 1:
            stats = jnp.where(half == m % 2, stats, 0.0)
        ref[wide:, :] = stats.astype(jnp.bfloat16)
    for copy in copies[stat_copies:]:
        copy.wait()


def pair_starts(at, i, tokens):
    first = at[3] * KVH
    return [(first + (at[0] ^ KEEP[i] ^ other)) * tokens for other in (0, FIRST)]


def pair_keys(ref, tokens):
    return jnp.concatenate([ref[0, 0:tokens, :], ref[1, 0:tokens, :]], axis=0)


def pair_values(ref, tokens):
    return jnp.concatenate([ref[0, tokens : 2 * tokens, :], ref[1, tokens : 2 * tokens, :]], axis=0)


def all_visible(at, ends, tokens):
    last = (at[3] + 1) * (KVH * tokens)
    return jnp.min(ends.astype(jnp.float32)) >= last.astype(jnp.float32)


def hide(values, ends, at, i, tokens, hidden):
    offset = lax.broadcasted_iota(jnp.int32, (tokens, values.shape[1]), 0)
    starts = pair_starts(at, i, tokens)
    visible = jnp.concatenate([offset < ends - start for start in starts], axis=0)
    return jnp.where(visible, values, hidden)


def in_branches(condition, body):
    pl.when(condition)(functools.partial(body, True))
    pl.when(jnp.logical_not(condition))(functools.partial(body, False))


def lse_rows(size):
    return max(1, size // DH)


def slabs_of(row_refs):
    return [[(ref, m) for m in range(ref.shape[0] // DH)] for ref in row_refs]


def lines_of(slabs, first, lines):
    return jnp.concatenate(
        [ref[m * DH + first : m * DH + first + lines, :] for ref, m in slabs], axis=0
    )


def stat_kernel(blocks, first, nears, heads, tokens, ends_ref, *refs):
    at = place(nears, heads)
    row_refs, refs = refs[: len(blocks)], refs[len(blocks) :]
    pair_refs, before_refs, lse_ref = refs[: len(KEEP)], refs[len(KEEP) : -1], refs[-1]
    lines = DH // 2
    for ref in before_refs:
        lse_ref[...] = ref[...]

    def body(seen):
        for m, (b, slabs) in enumerate(zip(blocks, slabs_of(row_refs))):
            count = len(slabs) * lines
            q = lines_of(slabs, 0, lines)
            ends = ends_ref[:, first + m * count : first + (m + 1) * count]
            scores = []
            for i, ref in enumerate(pair_refs):
                part = lax.dot_general(
                    pair_keys(ref, tokens),
                    q,
                    (((1,), (1,)), ((), ())),
                    preferred_element_type=jnp.float32,
                )
                scores.append(part if seen else hide(part, ends, at, i, tokens, MASKED_SCORE))
            scores = jnp.concatenate(scores, axis=0)
            peak = jnp.max(scores, axis=0, keepdims=True)
            total = jnp.sum(jnp.exp2((scores - peak) * (SCALE * LOG2E)), axis=0, keepdims=True)
            lse = peak * SCALE + jnp.log(total)
            if count < DH:
                lse = jnp.concatenate([lse] * (DH // count), axis=1)
            held = lse_rows(count)
            for k in range(held):
                lse_ref[pl.ds((at[3] ^ b) * held + k, 1), :] = lse[:, k * DH : (k + 1) * DH]

    in_branches(all_visible(at, ends_ref[...], tokens), body)


def line_values(slabs, lines, first_piece):
    low = lax.broadcasted_iota(jnp.int32, (1, 2 * lines), 1) < lines

    def stats_of(ref):
        first = ref.shape[0] - STAT_ROWS
        return ref[first : first + STAT_ROWS, :].astype(jnp.float32)

    out = []
    for n in range(0, len(slabs), 2):
        ref, m = slabs[n]
        total = None
        for k in range(first_piece, first_piece + PIECES):
            if ref.shape[0] > DH + STAT_ROWS:
                k = m // 2 * (2 * PIECES) + k
                piece = stats_of(ref)[k : k + 1]
            else:
                piece = jnp.where(low, stats_of(ref)[k : k + 1], stats_of(slabs[n + 1][0])[k : k + 1])
            total = piece if total is None else total + piece
        out.append(total)
    return jnp.concatenate(out, axis=1)


def lse_lines(lse_ref, at, blocks, size):
    held = lse_rows(size)
    tiles = []
    for b in blocks:
        for k in range(held):
            tile = lse_ref[pl.ds((at[3] ^ b) * held + k, 1), :]
            tiles.append(tile[:, : min(size, DH)])
    return jnp.concatenate(tiles, axis=1)


def steps_of(blocks, all_slabs, lines):
    size = len(all_slabs[0]) * lines
    step = min(len(blocks), STEP_LINES // size)
    for c in range(0, len(blocks), step):
        slabs = [slab for held in all_slabs[c : c + step] for slab in held]
        yield c * size, step * size, blocks[c : c + step], slabs


def part_kernel(blocks, nears, heads, tokens, ends_ref, *refs):
    at = place(nears, heads)
    row_refs, refs = refs[: len(blocks)], refs[len(blocks) :]
    pair_refs, (lse_ref, prob_ref, dscore_ref, dq_ref) = refs[: len(KEEP)], refs[len(KEEP) :]
    lines = DH // 2
    all_slabs = slabs_of(row_refs)
    size = len(all_slabs[0]) * lines

    def body(seen):
        for first, count, held, slabs in steps_of(blocks, all_slabs, lines):
            q, o_grad = lines_of(slabs, 0, lines), lines_of(slabs, lines, lines)
            dots = line_values(slabs, lines, PIECES)
            lse = lse_lines(lse_ref, at, held, size) * LOG2E
            lanes = slice(first, first + count)
            dq_t = jnp.zeros((DH, count), jnp.float32)
            for i, ref in enumerate(pair_refs):
                k, v = pair_keys(ref, tokens), pair_values(ref, tokens)
                scores = lax.dot_general(
                    k, q, (((1,), (1,)), ((), ())), preferred_element_type=jnp.float32
                )
                prob = jnp.exp2(scores * (SCALE * LOG2E) - lse)
                if not seen:
                    prob = hide(prob, ends_ref[:, lanes], at, i, tokens, 0.0)
                dprob = lax.dot_general(
                    v, o_grad, (((1,), (1,)), ((), ())), preferred_element_type=jnp.float32
                )
                dscore = (prob * (dprob - dots)).astype(jnp.bfloat16)
                prob_ref[i, :, lanes] = prob.astype(jnp.bfloat16)
                dscore_ref[i, :, lanes] = dscore
                dq_t = dq_t + jnp.dot(k.T, dscore, preferred_element_type=jnp.float32)
            dq_ref[:, lanes] = dq_t

    in_branches(all_visible(at, ends_ref[...], tokens), body)


def token_kernel(blocks, nears, heads, tokens, live_ref, *refs):
    at = place(nears, heads)
    row_refs, refs = refs[: len(blocks)], refs[len(blocks) :]
    (prob_ref, dscore_ref, dq_ref), refs = refs[:3], refs[3:]
    lse_refs, refs = refs[: len(blocks)], refs[len(blocks) :]
    dkv_refs, (*dq_refs, dk_acc, dv_acc) = refs[: len(KEEP)], refs[len(KEEP) :]
    lines = DH // 2
    all_slabs = slabs_of(row_refs)
    size = len(all_slabs[0]) * lines
    for first, count, held, slabs in steps_of(blocks, all_slabs, lines):
        lanes = slice(first, first + count)
        part_lse = [lse_lines(ref, at, held, size) for ref in lse_refs]
        self_lse = line_values(slabs, lines, 0)
        peak = functools.reduce(jnp.maximum, part_lse, self_lse)
        total = sum(jnp.exp(x - peak) for x in part_lse) + jnp.exp(self_lse - peak)
        lse = jnp.where(live_ref[:, lanes] > 0, peak + jnp.log(total), DEAD_LSE)
        weight = jnp.exp(part_lse[0] - lse)
        dq = (dq_ref[:, lanes] * (weight * SCALE)).T.astype(jnp.bfloat16)
        groups = len(all_slabs[0])
        for m in range(len(slabs)):
            block, j, n = first // size + m // groups, m % groups // nears, m % nears
            dq_refs[n][block, j] = dq[m * lines : (m + 1) * lines]
        weight_t = jnp.broadcast_to(weight, (DH, count)).T
        q, o_grad = (
            (lines_of(slabs, start, lines).astype(jnp.float32) * weight_t).astype(jnp.bfloat16)
            for start in (0, lines)
        )
        for i in range(len(KEEP)):
            dk = jnp.dot(dscore_ref[i, :, lanes], q, preferred_element_type=jnp.float32) * SCALE
            dv = jnp.dot(prob_ref[i, :, lanes], o_grad, preferred_element_type=jnp.float32)
            if first > 0:
                dk = dk + dk_acc[i]
                dv = dv + dv_acc[i]
            if first + count < len(blocks) * size:
                dk_acc[i] = dk
                dv_acc[i] = dv
            else:
                for n in range(2):
                    inner = slice(n * tokens, (n + 1) * tokens)
                    dkv_refs[i][n, 0:tokens, :] = dk[inner].astype(jnp.bfloat16)
                    dkv_refs[i][n, tokens : 2 * tokens, :] = dv[inner].astype(jnp.bfloat16)


def add_query_kernel(nears, *refs):
    own_refs, came_refs, out_refs = refs[:nears], refs[nears:-2], refs[-2:]
    for n in range(nears):
        for j in range(own_refs[0].shape[1]):
            total = own_refs[n][0, j].astype(jnp.float32)
            for ref in came_refs:
                total = total + ref[n, j].astype(jnp.float32)
            out_refs[min(j, 1)][n] = total.astype(jnp.bfloat16)


def tie_kernel(*refs):
    pass


def write_kernel(nears, heads, *refs):
    at = place(nears, heads)
    slab_refs, refs = refs[: -len(KEEP) - 5], refs[-len(KEEP) - 5 :]
    pair_refs, (came_ref, out_q_ref, out_k_ref, out_v_ref, sems) = refs[: len(KEEP)], refs[len(KEEP) :]
    groups, lines, tokens = len(slab_refs) * nears, slab_refs[0].shape[1], out_k_ref.shape[0]
    copies = []
    for i, ref in enumerate(pair_refs):
        for source, other in ((ref.at[0], 0), (came_ref.at[i], FIRST)):
            columns = pl.ds(column_of(at[0] ^ KEEP[i] ^ other, groups, heads), DH)
            copies.append((source.at[0:tokens, :], out_k_ref.at[:, columns]))
            copies.append((source.at[tokens : 2 * tokens, :], out_v_ref.at[:, columns]))
    for j, ref in enumerate(slab_refs):
        for n in range(nears):
            first = pl.multiple_of(group_at(at, j, n, nears) * lines, lines)
            copies.append((ref.at[n], out_q_ref.at[pl.ds(first, lines), :]))
    copies = [pltpu.make_async_copy(s, t, sems.at[n]) for n, (s, t) in enumerate(copies)]
    for copy in copies:
        copy.start()
    for copy in copies:
        copy.wait()


def swap(x, axis, distance, size):
    return lax.ppermute(x, axis, [(i, i ^ distance) for i in range(size)])


def swap_pairs(keep, send):
    members = ("row", "near", "head")
    came = swap(send, members, FIRST, KVH)
    pairs = [jnp.stack([keep[i], came[i]]) for i in range(len(KEEP))]
    return [swap(x, members, j, KVH) if j else x for x, j in zip(pairs, KEEP)]


def tie(x, others):
    return pl.pallas_call(
        tie_kernel,
        in_specs=[ANY] * (1 + len(others)),
        out_specs=ANY,
        out_shape=jax.ShapeDtypeStruct(x.shape, x.dtype),
        input_output_aliases={0: 0},
        compiler_params=PARAMS,
    )(x, *others)


def swap_back(pairs, after):
    members = ("row", "near", "head")
    pairs = [swap(x, members, j, KVH) if j else x for x, j in zip(pairs, KEEP)]
    beyond = tie(jnp.stack([x[1] for x in pairs]), after)
    return [*pairs, swap(beyond, members, FIRST, KVH)]


def swap_slabs(slabs, groups):
    return [swap(x, ("row", "near"), m, groups) if m else x for m, x in enumerate(slabs)]


def line_limits(parts, row_count, nears, rows, lines, resp_len, prompt_end):
    line = lax.broadcasted_iota(jnp.int32, (1, parts * nears * row_count * lines), 1)
    slab = line >> shift_of(lines)
    near_xor = slab & (nears - 1)
    row_xor = (slab >> shift_of(nears)) & (row_count - 1)
    place_of_block = slab >> shift_of(row_count * nears)
    block, bits = jnp.zeros_like(line), shift_of(parts)
    for k in range(bits):
        block = block | (((place_of_block >> k) & 1) << (bits - 1 - k))
    device = (lax.axis_index("part") ^ block) * row_count + (lax.axis_index("row") ^ row_xor)
    device = device * nears + (lax.axis_index("near") ^ near_xor)
    row = device * rows + (line & (rows - 1))
    ends, lengths = jnp.zeros_like(row), jnp.zeros_like(row)
    for r in range(resp_len.shape[0]):
        own = row >> shift_of(RESP_LEN) == r
        ends, lengths = jnp.where(own, prompt_end[r], ends), jnp.where(own, resp_len[r], lengths)
    return ends, ((row & (RESP_LEN - 1)) < lengths).astype(jnp.int32)


def shards(parts, row_count, nears, heads, queries, grad_out, outputs, lse_self, keys, values, resp_len, prompt_end):
    rows = queries.shape[0]
    own_heads = queries.shape[1] // DH
    own_lines = rows * own_heads
    groups = row_count * nears
    lines = own_lines // groups
    tokens = keys.shape[0]
    assert 2 * lines == DH and RESP_LEN % (groups * rows) == 0 and row_count <= 2 and nears <= 2

    def as_lines(x):
        return x.reshape(rows, own_heads, DH).transpose(1, 0, 2).reshape(own_lines, DH)

    def in_hbm(x):
        return pltpu.with_memory_space_constraint(x, pltpu.HBM)

    half_shape = jax.ShapeDtypeStruct((len(KEEP), 2 * tokens, DH), jnp.bfloat16)
    slab_shape = jax.ShapeDtypeStruct((2 * lines + STAT_ROWS, DH), jnp.bfloat16)
    *slabs, kv_keep, kv_send = pl.pallas_call(
        functools.partial(pack_kernel, row_count, nears, heads),
        in_specs=[HBM] * 6,
        out_specs=[VMEM] * (groups + 2),
        out_shape=[slab_shape] * groups + [half_shape] * 2,
        scratch_shapes=[
            pltpu.VMEM((own_lines, DH), jnp.bfloat16),
            pltpu.VMEM(lse_self.shape, jnp.float32),
            pltpu.SemaphoreType.DMA((2 + 2 * groups + 4 * len(KEEP),)),
        ],
        compiler_params=PARAMS,
    )(
        in_hbm(as_lines(queries)),
        in_hbm(as_lines(grad_out)),
        in_hbm(as_lines(outputs)),
        in_hbm(lse_self),
        in_hbm(keys),
        in_hbm(values),
    )
    slabs = swap_slabs(slabs, groups)
    own_block = jnp.concatenate([x[:DH] for x in slabs] + [sum(x[DH:] for x in slabs)], axis=0)
    pairs = swap_pairs(kv_keep, kv_send)
    far = [1 << n for n in reversed(range(shift_of(parts)))]

    blocks, came = [0], [own_block]
    for d in far:
        if d == 1:
            came = came[:1] + [tie(x, pairs[1:3]) for x in came[1:]]
        came = came + [swap(x, "part", d, parts) for x in came]
        blocks = blocks + [b ^ d for b in blocks]
    ends, live = line_limits(parts, row_count, nears, rows, lines, resp_len, prompt_end)

    def part_lse(held, first, refs, before):
        return pl.pallas_call(
            functools.partial(stat_kernel, held, first, nears, heads, tokens),
            in_specs=[VMEM] * (1 + len(refs) + len(KEEP) + len(before)),
            out_shape=jax.ShapeDtypeStruct((parts * lse_rows(groups * lines), DH), jnp.float32),
            compiler_params=PARAMS,
        )(ends, *refs, *pairs, *before)

    lse = [part_lse(blocks[:-1], 0, came[:-1], [])]
    row_refs = [*came[:-1], tie(came[-1], lse)]
    lse = [part_lse(blocks[-1:], (parts - 1) * groups * lines, row_refs[-1:], lse)]
    every_lse = lse + [swap(lse[0], "part", d, parts) for d in range(1, parts)]

    all_lines = parts * groups * lines
    score_shape = jax.ShapeDtypeStruct((len(KEEP), 2 * tokens, all_lines), jnp.bfloat16)
    prob, dscore, dq = pl.pallas_call(
        functools.partial(part_kernel, blocks, nears, heads, tokens),
        in_specs=[VMEM] * (1 + len(row_refs) + len(KEEP) + 1),
        out_specs=[VMEM] * 3,
        out_shape=[score_shape] * 2 + [jax.ShapeDtypeStruct((DH, all_lines), jnp.float32)],
        compiler_params=PARAMS,
    )(ends, *row_refs, *pairs, *lse)
    dq_shape = jax.ShapeDtypeStruct((parts, row_count, lines, DH), jnp.bfloat16)
    acc = pltpu.VMEM((len(KEEP), 2 * tokens, DH), jnp.float32)
    outs = pl.pallas_call(
        functools.partial(token_kernel, blocks, nears, heads, tokens),
        in_specs=[VMEM] * (1 + len(row_refs) + 3 + parts),
        out_shape=[jax.ShapeDtypeStruct((2, 2 * tokens, DH), jnp.bfloat16)] * len(KEEP)
        + [dq_shape] * nears,
        scratch_shapes=[acc] * 2,
        compiler_params=PARAMS,
    )(live, *row_refs, prob, dscore, dq, *every_lse)
    dkv, dq = outs[: len(KEEP)], outs[len(KEEP) :]
    dq = [swap(x, "near", n, nears) if n else x for n, x in enumerate(dq)]
    from_parts = [
        swap(jnp.stack([x[at] for x in dq]), "part", b, parts) for at, b in enumerate(blocks) if b
    ]
    sum_shape = jax.ShapeDtypeStruct((nears, lines, DH), jnp.bfloat16)
    sums = pl.pallas_call(
        functools.partial(add_query_kernel, nears),
        in_specs=[VMEM] * (nears + len(from_parts)),
        out_shape=[sum_shape] * 2,
        compiler_params=PARAMS,
    )(*dq, *from_parts)
    pairs = swap_back(dkv, from_parts)
    sums = [swap(x, "row", j, row_count) if j else x for j, x in enumerate(sums[:row_count])]
    out_q, out_k, out_v = pl.pallas_call(
        functools.partial(write_kernel, nears, heads),
        in_specs=[VMEM] * (row_count + len(pairs)),
        out_specs=[HBM] * 3,
        out_shape=[
            jax.ShapeDtypeStruct((own_lines, DH), jnp.bfloat16),
            jax.ShapeDtypeStruct(keys.shape, jnp.bfloat16),
            jax.ShapeDtypeStruct(values.shape, jnp.bfloat16),
        ],
        scratch_shapes=[pltpu.SemaphoreType.DMA((4 * len(KEEP) + groups,))],
        compiler_params=PARAMS,
    )(*sums, *pairs)
    out_q = out_q.reshape(own_heads, rows, DH).transpose(1, 0, 2).reshape(rows, own_heads * DH)
    return out_q, out_k, out_v


def solution(mesh):
    ctx, heads = mesh.shape["ctx"], mesh.shape["head"]
    groups = KVH // heads
    parts = ctx // groups
    nears = min(2, groups)
    row_count = groups // nears
    fine = Mesh(
        mesh.devices.reshape(parts, row_count, nears, heads), ("part", "row", "near", "head")
    )
    rows = P(("part", "row", "near"), "head")
    tokens = P(("part", "row", "near", "head"), None)
    return jax.shard_map(
        functools.partial(shards, parts, row_count, nears, heads),
        mesh=fine,
        in_specs=(rows, rows, rows, rows, tokens, tokens, P(), P()),
        out_specs=(rows, tokens, tokens),
        check_vma=False,
    )
```

```python
import functools

import jax
import jax.numpy as jnp
from jax import lax
from jax.experimental import pallas as pl
from jax.experimental.pallas import tpu as pltpu
from jax.sharding import Mesh, PartitionSpec as P

DH = 128
KVH = 8
RESP_LEN = 64
SCALE = DH ** (-0.5)
LOG2E = 1.4426950408889634
MASKED_SCORE = -1e30
DEAD_LSE = 1e30
PIECES = 3
STAT_ROWS = 16
STEP_LINES = 1024
PARAMS = pltpu.CompilerParams(vmem_limit_bytes=24 * 1024 * 1024)
ANY = pl.BlockSpec(memory_space=pl.ANY)
HBM = pl.BlockSpec(memory_space=pltpu.HBM)
VMEM = pl.BlockSpec(memory_space=pltpu.VMEM)

FIRST = 2
KEEP = (0, 1, 4, 5)


def split_pieces(x):
    first = x.astype(jnp.bfloat16)
    rest = x - first.astype(jnp.float32)
    second = rest.astype(jnp.bfloat16)
    third = (rest - second.astype(jnp.float32)).astype(jnp.bfloat16)
    return first, second, third


def shift_of(n):
    assert n & (n - 1) == 0
    return n.bit_length() - 1


def column_of(member, groups, heads):
    head_index, group_index = member & (heads - 1), member >> shift_of(heads)
    return pl.multiple_of((head_index * groups + group_index) * DH, DH)


def place(nears, heads):
    row, near = lax.axis_index("row"), lax.axis_index("near")
    member = (row * nears + near) * heads + lax.axis_index("head")
    return member, row, near, lax.axis_index("part")


def group_at(at, row_xor, near_xor, nears):
    return (at[1] ^ row_xor) * nears + (at[2] ^ near_xor)


def pack_kernel(row_count, nears, heads, q_hbm, o_grad_hbm, o_hbm, lse_hbm, k_hbm, v_hbm, *rest):
    groups = row_count * nears
    slab_refs, (keep_ref, send_ref, o_ref, lse_ref, sems) = rest[:groups], rest[groups:]
    at = place(nears, heads)
    rows, own_heads = lse_ref.shape
    lines = o_ref.shape[0] // groups
    tokens = k_hbm.shape[0]
    copies = [(lse_hbm, lse_ref), (o_hbm, o_ref)]
    slabs = []
    for m, ref in enumerate(slab_refs):
        first = pl.multiple_of(group_at(at, m // nears, m % nears, nears) * lines, lines)
        slabs.append((ref, first))
        copies.append((o_grad_hbm.at[pl.ds(first, lines), :], ref.at[lines : 2 * lines, :]))
    stat_copies = len(copies)
    for ref, first in slabs:
        copies.append((q_hbm.at[pl.ds(first, lines), :], ref.at[0:lines, :]))
    for i, j in enumerate(KEEP):
        for ref, peer in ((send_ref, j ^ FIRST), (keep_ref, j)):
            columns = pl.ds(column_of(at[0] ^ peer, groups, heads), DH)
            copies.append((k_hbm.at[:, columns], ref.at[i, 0:tokens, :]))
            copies.append((v_hbm.at[:, columns], ref.at[i, tokens : 2 * tokens, :]))
    copies = [pltpu.make_async_copy(s, t, sems.at[n]) for n, (s, t) in enumerate(copies)]
    for copy in copies:
        copy.start()

    wide = 2 * lines
    shape = (own_heads, wide)
    head_ids = lax.broadcasted_iota(jnp.int32, shape, 0)
    line_heads = (lax.broadcasted_iota(jnp.int32, shape, 1) & (lines - 1)) >> shift_of(rows)
    chosen = jnp.concatenate(
        [(head_ids == line_heads + (first >> shift_of(rows))) for _, first in slabs], axis=1
    ).astype(jnp.bfloat16)
    shape = (STAT_ROWS, chosen.shape[1])
    own_row = (lax.broadcasted_iota(jnp.int32, shape, 0) & (rows - 1)) == (
        lax.broadcasted_iota(jnp.int32, shape, 1) & (rows - 1)
    )
    shape = (STAT_ROWS, STAT_ROWS)
    piece_of = lax.broadcasted_iota(jnp.int32, shape, 1) >> shift_of(rows)
    stat_row = lax.broadcasted_iota(jnp.int32, shape, 0)
    for copy in copies[:stat_copies]:
        copy.wait()
    pieces = [piece.astype(jnp.float32) for piece in split_pieces(lse_ref[...])]
    pieces.append(jnp.zeros((STAT_ROWS - PIECES * rows, own_heads), jnp.float32))
    pieces = jnp.concatenate(pieces, axis=0).astype(jnp.bfloat16)
    spread = jnp.dot(pieces, chosen, preferred_element_type=jnp.float32)
    spread = jnp.where(own_row, spread, 0.0).astype(jnp.bfloat16)
    kind = lax.broadcasted_iota(jnp.int32, (STAT_ROWS, wide), 0)
    half = lax.broadcasted_iota(jnp.int32, (STAT_ROWS, wide), 1) >> shift_of(lines)
    for m, (ref, first) in enumerate(slabs):
        top = m // 2 * (2 * PIECES)
        gather = (stat_row - top == piece_of).astype(jnp.bfloat16)
        own = spread[:, m * wide : (m + 1) * wide]
        stats = jnp.dot(gather, own, preferred_element_type=jnp.float32)
        o_grad = ref[lines:wide, :].astype(jnp.float32)
        product = o_grad * o_ref[pl.ds(first, lines), :].astype(jnp.float32)
        dots = jnp.sum(jnp.concatenate([product, product], axis=0).T, axis=0, keepdims=True)
        for k, piece in enumerate(split_pieces(dots)):
            stats = jnp.where(kind == top + PIECES + k, piece.astype(jnp.float32), stats)
        if len(slabs) > 1:
            stats = jnp.where(half == m % 2, stats, 0.0)
        ref[wide:, :] = stats.astype(jnp.bfloat16)
    for copy in copies[stat_copies:]:
        copy.wait()


def pair_starts(at, i, tokens):
    first = at[3] * KVH
    return [(first + (at[0] ^ KEEP[i] ^ other)) * tokens for other in (0, FIRST)]


def pair_keys(ref, tokens):
    return jnp.concatenate([ref[0, 0:tokens, :], ref[1, 0:tokens, :]], axis=0)


def pair_values(ref, tokens):
    return jnp.concatenate([ref[0, tokens : 2 * tokens, :], ref[1, tokens : 2 * tokens, :]], axis=0)


def all_visible(at, ends, tokens):
    last = (at[3] + 1) * (KVH * tokens)
    return jnp.min(ends.astype(jnp.float32)) >= last.astype(jnp.float32)


def hide(values, ends, at, i, tokens, hidden):
    offset = lax.broadcasted_iota(jnp.int32, (tokens, values.shape[1]), 0)
    starts = pair_starts(at, i, tokens)
    visible = jnp.concatenate([offset < ends - start for start in starts], axis=0)
    return jnp.where(visible, values, hidden)


def in_branches(condition, body):
    pl.when(condition)(functools.partial(body, True))
    pl.when(jnp.logical_not(condition))(functools.partial(body, False))


def lse_rows(size):
    return max(1, size // DH)


def slabs_of(row_refs):
    return [[(ref, m) for m in range(ref.shape[0] // DH)] for ref in row_refs]


def lines_of(slabs, first, lines):
    return jnp.concatenate(
        [ref[m * DH + first : m * DH + first + lines, :] for ref, m in slabs], axis=0
    )


def stat_kernel(blocks, first, nears, heads, tokens, ends_ref, *refs):
    at = place(nears, heads)
    row_refs, refs = refs[: len(blocks)], refs[len(blocks) :]
    pair_refs, before_refs, lse_ref = refs[: len(KEEP)], refs[len(KEEP) : -1], refs[-1]
    lines = DH // 2
    for ref in before_refs:
        lse_ref[...] = ref[...]

    def body(seen):
        for m, (b, slabs) in enumerate(zip(blocks, slabs_of(row_refs))):
            count = len(slabs) * lines
            q = lines_of(slabs, 0, lines)
            ends = ends_ref[:, first + m * count : first + (m + 1) * count]
            scores = []
            for i, ref in enumerate(pair_refs):
                part = lax.dot_general(
                    pair_keys(ref, tokens),
                    q,
                    (((1,), (1,)), ((), ())),
                    preferred_element_type=jnp.float32,
                )
                scores.append(part if seen else hide(part, ends, at, i, tokens, MASKED_SCORE))
            scores = jnp.concatenate(scores, axis=0)
            peak = jnp.max(scores, axis=0, keepdims=True)
            total = jnp.sum(jnp.exp2((scores - peak) * (SCALE * LOG2E)), axis=0, keepdims=True)
            lse = peak * SCALE + jnp.log(total)
            if count < DH:
                lse = jnp.concatenate([lse] * (DH // count), axis=1)
            held = lse_rows(count)
            for k in range(held):
                lse_ref[pl.ds((at[3] ^ b) * held + k, 1), :] = lse[:, k * DH : (k + 1) * DH]

    in_branches(all_visible(at, ends_ref[...], tokens), body)


def line_values(slabs, lines, first_piece):
    low = lax.broadcasted_iota(jnp.int32, (1, 2 * lines), 1) < lines

    def stats_of(ref):
        first = ref.shape[0] - STAT_ROWS
        return ref[first : first + STAT_ROWS, :].astype(jnp.float32)

    out = []
    for n in range(0, len(slabs), 2):
        ref, m = slabs[n]
        total = None
        for k in range(first_piece, first_piece + PIECES):
            if ref.shape[0] > DH + STAT_ROWS:
                k = m // 2 * (2 * PIECES) + k
                piece = stats_of(ref)[k : k + 1]
            else:
                piece = jnp.where(low, stats_of(ref)[k : k + 1], stats_of(slabs[n + 1][0])[k : k + 1])
            total = piece if total is None else total + piece
        out.append(total)
    return jnp.concatenate(out, axis=1)


def lse_lines(lse_ref, at, blocks, size):
    held = lse_rows(size)
    tiles = []
    for b in blocks:
        for k in range(held):
            tile = lse_ref[pl.ds((at[3] ^ b) * held + k, 1), :]
            tiles.append(tile[:, : min(size, DH)])
    return jnp.concatenate(tiles, axis=1)


def steps_of(blocks, all_slabs, lines):
    size = len(all_slabs[0]) * lines
    step = min(len(blocks), STEP_LINES // size)
    for c in range(0, len(blocks), step):
        slabs = [slab for held in all_slabs[c : c + step] for slab in held]
        yield c * size, step * size, blocks[c : c + step], slabs


def part_kernel(blocks, nears, heads, tokens, ends_ref, *refs):
    at = place(nears, heads)
    row_refs, refs = refs[: len(blocks)], refs[len(blocks) :]
    pair_refs, (lse_ref, prob_ref, dscore_ref, dq_ref) = refs[: len(KEEP)], refs[len(KEEP) :]
    lines = DH // 2
    all_slabs = slabs_of(row_refs)
    size = len(all_slabs[0]) * lines

    def body(seen):
        for first, count, held, slabs in steps_of(blocks, all_slabs, lines):
            q, o_grad = lines_of(slabs, 0, lines), lines_of(slabs, lines, lines)
            dots = line_values(slabs, lines, PIECES)
            lse = lse_lines(lse_ref, at, held, size) * LOG2E
            lanes = slice(first, first + count)
            dq_t = jnp.zeros((DH, count), jnp.float32)
            for i, ref in enumerate(pair_refs):
                k, v = pair_keys(ref, tokens), pair_values(ref, tokens)
                scores = lax.dot_general(
                    k, q, (((1,), (1,)), ((), ())), preferred_element_type=jnp.float32
                )
                prob = jnp.exp2(scores * (SCALE * LOG2E) - lse)
                if not seen:
                    prob = hide(prob, ends_ref[:, lanes], at, i, tokens, 0.0)
                dprob = lax.dot_general(
                    v, o_grad, (((1,), (1,)), ((), ())), preferred_element_type=jnp.float32
                )
                dscore = (prob * (dprob - dots)).astype(jnp.bfloat16)
                prob_ref[i, :, lanes] = prob.astype(jnp.bfloat16)
                dscore_ref[i, :, lanes] = dscore
                dq_t = dq_t + jnp.dot(k.T, dscore, preferred_element_type=jnp.float32)
            dq_ref[:, lanes] = dq_t

    in_branches(all_visible(at, ends_ref[...], tokens), body)


def token_kernel(blocks, nears, heads, tokens, live_ref, *refs):
    at = place(nears, heads)
    row_refs, refs = refs[: len(blocks)], refs[len(blocks) :]
    (prob_ref, dscore_ref, dq_ref), refs = refs[:3], refs[3:]
    lse_refs, refs = refs[: len(blocks)], refs[len(blocks) :]
    dkv_refs, (*dq_refs, dk_acc, dv_acc) = refs[: len(KEEP)], refs[len(KEEP) :]
    lines = DH // 2
    all_slabs = slabs_of(row_refs)
    size = len(all_slabs[0]) * lines
    for first, count, held, slabs in steps_of(blocks, all_slabs, lines):
        lanes = slice(first, first + count)
        part_lse = [lse_lines(ref, at, held, size) for ref in lse_refs]
        self_lse = line_values(slabs, lines, 0)
        peak = functools.reduce(jnp.maximum, part_lse, self_lse)
        total = sum(jnp.exp(x - peak) for x in part_lse) + jnp.exp(self_lse - peak)
        lse = jnp.where(live_ref[:, lanes] > 0, peak + jnp.log(total), DEAD_LSE)
        weight = jnp.exp(part_lse[0] - lse)
        dq = (dq_ref[:, lanes] * (weight * SCALE)).T.astype(jnp.bfloat16)
        groups = len(all_slabs[0])
        for m in range(len(slabs)):
            block, j, n = first // size + m // groups, m % groups // nears, m % nears
            dq_refs[n][block, j] = dq[m * lines : (m + 1) * lines]
        weight_t = jnp.broadcast_to(weight, (DH, count)).T
        q, o_grad = (
            (lines_of(slabs, start, lines).astype(jnp.float32) * weight_t).astype(jnp.bfloat16)
            for start in (0, lines)
        )
        for i in range(len(KEEP)):
            dk = jnp.dot(dscore_ref[i, :, lanes], q, preferred_element_type=jnp.float32) * SCALE
            dv = jnp.dot(prob_ref[i, :, lanes], o_grad, preferred_element_type=jnp.float32)
            if first > 0:
                dk = dk + dk_acc[i]
                dv = dv + dv_acc[i]
            if first + count < len(blocks) * size:
                dk_acc[i] = dk
                dv_acc[i] = dv
            else:
                for n in range(2):
                    inner = slice(n * tokens, (n + 1) * tokens)
                    dkv_refs[i][n, 0:tokens, :] = dk[inner].astype(jnp.bfloat16)
                    dkv_refs[i][n, tokens : 2 * tokens, :] = dv[inner].astype(jnp.bfloat16)


def add_query_kernel(nears, *refs):
    own_refs, came_refs, out_refs = refs[:nears], refs[nears:-2], refs[-2:]
    for n in range(nears):
        for j in range(own_refs[0].shape[1]):
            total = own_refs[n][0, j].astype(jnp.float32)
            for ref in came_refs:
                total = total + ref[n, j].astype(jnp.float32)
            out_refs[min(j, 1)][n] = total.astype(jnp.bfloat16)


def tie_kernel(*refs):
    pass


def write_kernel(nears, heads, *refs):
    at = place(nears, heads)
    slab_refs, refs = refs[: -len(KEEP) - 5], refs[-len(KEEP) - 5 :]
    pair_refs, (came_ref, out_q_ref, out_k_ref, out_v_ref, sems) = refs[: len(KEEP)], refs[len(KEEP) :]
    groups, lines, tokens = len(slab_refs) * nears, slab_refs[0].shape[1], out_k_ref.shape[0]
    copies = []
    for i, ref in enumerate(pair_refs):
        for source, other in ((ref.at[0], 0), (came_ref.at[i], FIRST)):
            columns = pl.ds(column_of(at[0] ^ KEEP[i] ^ other, groups, heads), DH)
            copies.append((source.at[0:tokens, :], out_k_ref.at[:, columns]))
            copies.append((source.at[tokens : 2 * tokens, :], out_v_ref.at[:, columns]))
    for j, ref in enumerate(slab_refs):
        for n in range(nears):
            first = pl.multiple_of(group_at(at, j, n, nears) * lines, lines)
            copies.append((ref.at[n], out_q_ref.at[pl.ds(first, lines), :]))
    copies = [pltpu.make_async_copy(s, t, sems.at[n]) for n, (s, t) in enumerate(copies)]
    for copy in copies:
        copy.start()
    for copy in copies:
        copy.wait()


def swap(x, axis, distance, size):
    return lax.ppermute(x, axis, [(i, i ^ distance) for i in range(size)])


def swap_pairs(keep, send):
    members = ("row", "near", "head")
    came = swap(send, members, FIRST, KVH)
    pairs = [jnp.stack([keep[i], came[i]]) for i in range(len(KEEP))]
    return [swap(x, members, j, KVH) if j else x for x, j in zip(pairs, KEEP)]


def tie(x, others):
    return pl.pallas_call(
        tie_kernel,
        in_specs=[ANY] * (1 + len(others)),
        out_specs=ANY,
        out_shape=jax.ShapeDtypeStruct(x.shape, x.dtype),
        input_output_aliases={0: 0},
        compiler_params=PARAMS,
    )(x, *others)


def swap_back(pairs, after):
    members = ("row", "near", "head")
    pairs = [swap(x, members, j, KVH) if j else x for x, j in zip(pairs, KEEP)]
    beyond = tie(jnp.stack([x[1] for x in pairs]), after)
    return [*pairs, swap(beyond, members, FIRST, KVH)]


def swap_slabs(slabs, groups):
    return [swap(x, ("row", "near"), m, groups) if m else x for m, x in enumerate(slabs)]


def line_limits(parts, row_count, nears, rows, lines, resp_len, prompt_end):
    line = lax.broadcasted_iota(jnp.int32, (1, parts * nears * row_count * lines), 1)
    slab = line >> shift_of(lines)
    near_xor = slab & (nears - 1)
    row_xor = (slab >> shift_of(nears)) & (row_count - 1)
    place_of_block = slab >> shift_of(row_count * nears)
    block, bits = jnp.zeros_like(line), shift_of(parts)
    for k in range(bits):
        block = block | (((place_of_block >> k) & 1) << (bits - 1 - k))
    device = (lax.axis_index("part") ^ block) * row_count + (lax.axis_index("row") ^ row_xor)
    device = device * nears + (lax.axis_index("near") ^ near_xor)
    row = device * rows + (line & (rows - 1))
    ends, lengths = jnp.zeros_like(row), jnp.zeros_like(row)
    for r in range(resp_len.shape[0]):
        own = row >> shift_of(RESP_LEN) == r
        ends, lengths = jnp.where(own, prompt_end[r], ends), jnp.where(own, resp_len[r], lengths)
    return ends, ((row & (RESP_LEN - 1)) < lengths).astype(jnp.int32)


def shards(parts, row_count, nears, heads, queries, grad_out, outputs, lse_self, keys, values, resp_len, prompt_end):
    rows = queries.shape[0]
    own_heads = queries.shape[1] // DH
    own_lines = rows * own_heads
    groups = row_count * nears
    lines = own_lines // groups
    tokens = keys.shape[0]
    assert 2 * lines == DH and RESP_LEN % (groups * rows) == 0 and row_count <= 2 and nears <= 2

    def as_lines(x):
        return x.reshape(rows, own_heads, DH).transpose(1, 0, 2).reshape(own_lines, DH)

    def in_hbm(x):
        return pltpu.with_memory_space_constraint(x, pltpu.HBM)

    half_shape = jax.ShapeDtypeStruct((len(KEEP), 2 * tokens, DH), jnp.bfloat16)
    slab_shape = jax.ShapeDtypeStruct((2 * lines + STAT_ROWS, DH), jnp.bfloat16)
    *slabs, kv_keep, kv_send = pl.pallas_call(
        functools.partial(pack_kernel, row_count, nears, heads),
        in_specs=[HBM] * 6,
        out_specs=[VMEM] * (groups + 2),
        out_shape=[slab_shape] * groups + [half_shape] * 2,
        scratch_shapes=[
            pltpu.VMEM((own_lines, DH), jnp.bfloat16),
            pltpu.VMEM(lse_self.shape, jnp.float32),
            pltpu.SemaphoreType.DMA((2 + 2 * groups + 4 * len(KEEP),)),
        ],
        compiler_params=PARAMS,
    )(
        in_hbm(as_lines(queries)),
        in_hbm(as_lines(grad_out)),
        in_hbm(as_lines(outputs)),
        in_hbm(lse_self),
        in_hbm(keys),
        in_hbm(values),
    )
    slabs = swap_slabs(slabs, groups)
    own_block = jnp.concatenate([x[:DH] for x in slabs] + [sum(x[DH:] for x in slabs)], axis=0)
    pairs = swap_pairs(kv_keep, kv_send)
    blocks = [0]
    for d in [1 << n for n in reversed(range(shift_of(parts)))]:
        blocks = blocks + [b ^ d for b in blocks]
    came = [swap(own_block, "part", b, parts) if b else own_block for b in blocks]
    ends, live = line_limits(parts, row_count, nears, rows, lines, resp_len, prompt_end)

    def part_lse(held, first, refs, before):
        return pl.pallas_call(
            functools.partial(stat_kernel, held, first, nears, heads, tokens),
            in_specs=[VMEM] * (1 + len(refs) + len(KEEP) + len(before)),
            out_shape=jax.ShapeDtypeStruct((parts * lse_rows(groups * lines), DH), jnp.float32),
            compiler_params=PARAMS,
        )(ends, *refs, *pairs, *before)

    lse = [part_lse(blocks[:-1], 0, came[:-1], [])]
    row_refs = [*came[:-1], tie(came[-1], lse)]
    lse = [part_lse(blocks[-1:], (parts - 1) * groups * lines, row_refs[-1:], lse)]
    every_lse = lse + [swap(lse[0], "part", d, parts) for d in range(1, parts)]

    all_lines = parts * groups * lines
    score_shape = jax.ShapeDtypeStruct((len(KEEP), 2 * tokens, all_lines), jnp.bfloat16)
    prob, dscore, dq = pl.pallas_call(
        functools.partial(part_kernel, blocks, nears, heads, tokens),
        in_specs=[VMEM] * (1 + len(row_refs) + len(KEEP) + 1),
        out_specs=[VMEM] * 3,
        out_shape=[score_shape] * 2 + [jax.ShapeDtypeStruct((DH, all_lines), jnp.float32)],
        compiler_params=PARAMS,
    )(ends, *row_refs, *pairs, *lse)
    dq_shape = jax.ShapeDtypeStruct((parts, row_count, lines, DH), jnp.bfloat16)
    acc = pltpu.VMEM((len(KEEP), 2 * tokens, DH), jnp.float32)
    outs = pl.pallas_call(
        functools.partial(token_kernel, blocks, nears, heads, tokens),
        in_specs=[VMEM] * (1 + len(row_refs) + 3 + parts),
        out_shape=[jax.ShapeDtypeStruct((2, 2 * tokens, DH), jnp.bfloat16)] * len(KEEP)
        + [dq_shape] * nears,
        scratch_shapes=[acc] * 2,
        compiler_params=PARAMS,
    )(live, *row_refs, prob, dscore, dq, *every_lse)
    dkv, dq = outs[: len(KEEP)], outs[len(KEEP) :]
    dq = [swap(x, "near", n, nears) if n else x for n, x in enumerate(dq)]
    from_parts = [
        swap(jnp.stack([x[at] for x in dq]), "part", b, parts) for at, b in enumerate(blocks) if b
    ]
    sum_shape = jax.ShapeDtypeStruct((nears, lines, DH), jnp.bfloat16)
    sums = pl.pallas_call(
        functools.partial(add_query_kernel, nears),
        in_specs=[VMEM] * (nears + len(from_parts)),
        out_shape=[sum_shape] * 2,
        compiler_params=PARAMS,
    )(*dq, *from_parts)
    pairs = swap_back(dkv, from_parts)
    sums = [swap(x, "row", j, row_count) if j else x for j, x in enumerate(sums[:row_count])]
    out_q, out_k, out_v = pl.pallas_call(
        functools.partial(write_kernel, nears, heads),
        in_specs=[VMEM] * (row_count + len(pairs)),
        out_specs=[HBM] * 3,
        out_shape=[
            jax.ShapeDtypeStruct((own_lines, DH), jnp.bfloat16),
            jax.ShapeDtypeStruct(keys.shape, jnp.bfloat16),
            jax.ShapeDtypeStruct(values.shape, jnp.bfloat16),
        ],
        scratch_shapes=[pltpu.SemaphoreType.DMA((4 * len(KEEP) + groups,))],
        compiler_params=PARAMS,
    )(*sums, *pairs)
    out_q = out_q.reshape(own_heads, rows, DH).transpose(1, 0, 2).reshape(rows, own_heads * DH)
    return out_q, out_k, out_v


def solution(mesh):
    ctx, heads = mesh.shape["ctx"], mesh.shape["head"]
    groups = KVH // heads
    parts = ctx // groups
    nears = min(2, groups)
    row_count = groups // nears
    fine = Mesh(
        mesh.devices.reshape(parts, row_count, nears, heads), ("part", "row", "near", "head")
    )
    rows = P(("part", "row", "near"), "head")
    tokens = P(("part", "row", "near", "head"), None)
    return jax.shard_map(
        functools.partial(shards, parts, row_count, nears, heads),
        mesh=fine,
        in_specs=(rows, rows, rows, rows, tokens, tokens, P(), P()),
        out_specs=(rows, tokens, tokens),
        check_vma=False,
    )
```

```python
import functools

import jax
import jax.numpy as jnp
from jax import lax
from jax.experimental import pallas as pl
from jax.experimental.pallas import tpu as pltpu
from jax.sharding import Mesh, PartitionSpec as P

DH = 128
KVH = 8
RESP_LEN = 64
SCALE = DH ** (-0.5)
LOG2E = 1.4426950408889634
MASKED_SCORE = -1e30
DEAD_LSE = 1e30
PIECES = 3
STAT_ROWS = 16
STEP_LINES = 1024
PARAMS = pltpu.CompilerParams(vmem_limit_bytes=24 * 1024 * 1024)
ANY = pl.BlockSpec(memory_space=pl.ANY)
HBM = pl.BlockSpec(memory_space=pltpu.HBM)
VMEM = pl.BlockSpec(memory_space=pltpu.VMEM)

FIRST = 2
KEEP = (0, 1, 4, 5)


def split_pieces(x):
    first = x.astype(jnp.bfloat16)
    rest = x - first.astype(jnp.float32)
    second = rest.astype(jnp.bfloat16)
    third = (rest - second.astype(jnp.float32)).astype(jnp.bfloat16)
    return first, second, third


def shift_of(n):
    assert n & (n - 1) == 0
    return n.bit_length() - 1


def column_of(member, groups, heads):
    head_index, group_index = member & (heads - 1), member >> shift_of(heads)
    return pl.multiple_of((head_index * groups + group_index) * DH, DH)


def place(nears, heads):
    row, near = lax.axis_index("row"), lax.axis_index("near")
    member = (row * nears + near) * heads + lax.axis_index("head")
    return member, row, near, lax.axis_index("part")


def group_at(at, row_xor, near_xor, nears):
    return (at[1] ^ row_xor) * nears + (at[2] ^ near_xor)


def pack_kernel(row_count, nears, heads, q_hbm, o_grad_hbm, o_hbm, lse_hbm, k_hbm, v_hbm, *rest):
    groups = row_count * nears
    slab_refs, (keep_ref, send_ref, o_ref, lse_ref, sems) = rest[:groups], rest[groups:]
    at = place(nears, heads)
    rows, own_heads = lse_ref.shape
    lines = o_ref.shape[0] // groups
    tokens = k_hbm.shape[0]
    copies = [(lse_hbm, lse_ref), (o_hbm, o_ref)]
    slabs = []
    for m, ref in enumerate(slab_refs):
        first = pl.multiple_of(group_at(at, m // nears, m % nears, nears) * lines, lines)
        slabs.append((ref, first))
        copies.append((o_grad_hbm.at[pl.ds(first, lines), :], ref.at[lines : 2 * lines, :]))
    stat_copies = len(copies)
    for ref, first in slabs:
        copies.append((q_hbm.at[pl.ds(first, lines), :], ref.at[0:lines, :]))
    for i, j in enumerate(KEEP):
        for ref, peer in ((send_ref, j ^ FIRST), (keep_ref, j)):
            columns = pl.ds(column_of(at[0] ^ peer, groups, heads), DH)
            copies.append((k_hbm.at[:, columns], ref.at[i, 0:tokens, :]))
            copies.append((v_hbm.at[:, columns], ref.at[i, tokens : 2 * tokens, :]))
    copies = [pltpu.make_async_copy(s, t, sems.at[n]) for n, (s, t) in enumerate(copies)]
    for copy in copies:
        copy.start()

    wide = 2 * lines
    shape = (own_heads, wide)
    head_ids = lax.broadcasted_iota(jnp.int32, shape, 0)
    line_heads = (lax.broadcasted_iota(jnp.int32, shape, 1) & (lines - 1)) >> shift_of(rows)
    chosen = jnp.concatenate(
        [(head_ids == line_heads + (first >> shift_of(rows))) for _, first in slabs], axis=1
    ).astype(jnp.bfloat16)
    shape = (STAT_ROWS, chosen.shape[1])
    own_row = (lax.broadcasted_iota(jnp.int32, shape, 0) & (rows - 1)) == (
        lax.broadcasted_iota(jnp.int32, shape, 1) & (rows - 1)
    )
    shape = (STAT_ROWS, STAT_ROWS)
    piece_of = lax.broadcasted_iota(jnp.int32, shape, 1) >> shift_of(rows)
    stat_row = lax.broadcasted_iota(jnp.int32, shape, 0)
    for copy in copies[:stat_copies]:
        copy.wait()
    pieces = [piece.astype(jnp.float32) for piece in split_pieces(lse_ref[...])]
    pieces.append(jnp.zeros((STAT_ROWS - PIECES * rows, own_heads), jnp.float32))
    pieces = jnp.concatenate(pieces, axis=0).astype(jnp.bfloat16)
    spread = jnp.dot(pieces, chosen, preferred_element_type=jnp.float32)
    spread = jnp.where(own_row, spread, 0.0).astype(jnp.bfloat16)
    kind = lax.broadcasted_iota(jnp.int32, (STAT_ROWS, wide), 0)
    half = lax.broadcasted_iota(jnp.int32, (STAT_ROWS, wide), 1) >> shift_of(lines)
    for m, (ref, first) in enumerate(slabs):
        top = m // 2 * (2 * PIECES)
        gather = (stat_row - top == piece_of).astype(jnp.bfloat16)
        own = spread[:, m * wide : (m + 1) * wide]
        stats = jnp.dot(gather, own, preferred_element_type=jnp.float32)
        o_grad = ref[lines:wide, :].astype(jnp.float32)
        product = o_grad * o_ref[pl.ds(first, lines), :].astype(jnp.float32)
        dots = jnp.sum(jnp.concatenate([product, product], axis=0).T, axis=0, keepdims=True)
        for k, piece in enumerate(split_pieces(dots)):
            stats = jnp.where(kind == top + PIECES + k, piece.astype(jnp.float32), stats)
        if len(slabs) > 1:
            stats = jnp.where(half == m % 2, stats, 0.0)
        ref[wide:, :] = stats.astype(jnp.bfloat16)
    for copy in copies[stat_copies:]:
        copy.wait()


def pair_starts(at, i, tokens):
    first = at[3] * KVH
    return [(first + (at[0] ^ KEEP[i] ^ other)) * tokens for other in (0, FIRST)]


def pair_keys(ref, tokens):
    return jnp.concatenate([ref[0, 0:tokens, :], ref[1, 0:tokens, :]], axis=0)


def pair_values(ref, tokens):
    return jnp.concatenate([ref[0, tokens : 2 * tokens, :], ref[1, tokens : 2 * tokens, :]], axis=0)


def all_visible(at, ends, tokens):
    last = (at[3] + 1) * (KVH * tokens)
    return jnp.min(ends.astype(jnp.float32)) >= last.astype(jnp.float32)


def hide(values, ends, at, i, tokens, hidden):
    offset = lax.broadcasted_iota(jnp.int32, (tokens, values.shape[1]), 0)
    starts = pair_starts(at, i, tokens)
    visible = jnp.concatenate([offset < ends - start for start in starts], axis=0)
    return jnp.where(visible, values, hidden)


def in_branches(condition, body):
    pl.when(condition)(functools.partial(body, True))
    pl.when(jnp.logical_not(condition))(functools.partial(body, False))


def lse_rows(size):
    return max(1, size // DH)


def slabs_of(row_refs):
    return [[(ref, m) for m in range(ref.shape[0] // DH)] for ref in row_refs]


def lines_of(slabs, first, lines):
    return jnp.concatenate(
        [ref[m * DH + first : m * DH + first + lines, :] for ref, m in slabs], axis=0
    )


def stat_kernel(blocks, first, nears, heads, tokens, ends_ref, *refs):
    at = place(nears, heads)
    row_refs, refs = refs[: len(blocks)], refs[len(blocks) :]
    pair_refs, before_refs, lse_ref = refs[: len(KEEP)], refs[len(KEEP) : -1], refs[-1]
    lines = DH // 2
    for ref in before_refs:
        lse_ref[...] = ref[...]

    def body(seen):
        for m, (b, slabs) in enumerate(zip(blocks, slabs_of(row_refs))):
            count = len(slabs) * lines
            q = lines_of(slabs, 0, lines)
            ends = ends_ref[:, first + m * count : first + (m + 1) * count]
            scores = []
            for i, ref in enumerate(pair_refs):
                part = lax.dot_general(
                    pair_keys(ref, tokens),
                    q,
                    (((1,), (1,)), ((), ())),
                    preferred_element_type=jnp.float32,
                )
                scores.append(part if seen else hide(part, ends, at, i, tokens, MASKED_SCORE))
            scores = jnp.concatenate(scores, axis=0)
            peak = jnp.max(scores, axis=0, keepdims=True)
            total = jnp.sum(jnp.exp2((scores - peak) * (SCALE * LOG2E)), axis=0, keepdims=True)
            lse = peak * SCALE + jnp.log(total)
            if count < DH:
                lse = jnp.concatenate([lse] * (DH // count), axis=1)
            held = lse_rows(count)
            for k in range(held):
                lse_ref[pl.ds((at[3] ^ b) * held + k, 1), :] = lse[:, k * DH : (k + 1) * DH]

    in_branches(all_visible(at, ends_ref[...], tokens), body)


def line_values(slabs, lines, first_piece):
    low = lax.broadcasted_iota(jnp.int32, (1, 2 * lines), 1) < lines

    def stats_of(ref):
        first = ref.shape[0] - STAT_ROWS
        return ref[first : first + STAT_ROWS, :].astype(jnp.float32)

    out = []
    for n in range(0, len(slabs), 2):
        ref, m = slabs[n]
        total = None
        for k in range(first_piece, first_piece + PIECES):
            if ref.shape[0] > DH + STAT_ROWS:
                k = m // 2 * (2 * PIECES) + k
                piece = stats_of(ref)[k : k + 1]
            else:
                piece = jnp.where(low, stats_of(ref)[k : k + 1], stats_of(slabs[n + 1][0])[k : k + 1])
            total = piece if total is None else total + piece
        out.append(total)
    return jnp.concatenate(out, axis=1)


def lse_lines(lse_ref, at, blocks, size):
    held = lse_rows(size)
    tiles = []
    for b in blocks:
        for k in range(held):
            tile = lse_ref[pl.ds((at[3] ^ b) * held + k, 1), :]
            tiles.append(tile[:, : min(size, DH)])
    return jnp.concatenate(tiles, axis=1)


def steps_of(blocks, all_slabs, lines):
    size = len(all_slabs[0]) * lines
    step = min(len(blocks), STEP_LINES // size)
    for c in range(0, len(blocks), step):
        slabs = [slab for held in all_slabs[c : c + step] for slab in held]
        yield c * size, step * size, blocks[c : c + step], slabs


def part_kernel(blocks, nears, heads, tokens, ends_ref, *refs):
    at = place(nears, heads)
    row_refs, refs = refs[: len(blocks)], refs[len(blocks) :]
    pair_refs, (lse_ref, prob_ref, dscore_ref, dq_ref) = refs[: len(KEEP)], refs[len(KEEP) :]
    lines = DH // 2
    all_slabs = slabs_of(row_refs)
    size = len(all_slabs[0]) * lines

    def body(seen):
        for first, count, held, slabs in steps_of(blocks, all_slabs, lines):
            q, o_grad = lines_of(slabs, 0, lines), lines_of(slabs, lines, lines)
            dots = line_values(slabs, lines, PIECES)
            lse = lse_lines(lse_ref, at, held, size) * LOG2E
            lanes = slice(first, first + count)
            dq_t = jnp.zeros((DH, count), jnp.float32)
            for i, ref in enumerate(pair_refs):
                k, v = pair_keys(ref, tokens), pair_values(ref, tokens)
                scores = lax.dot_general(
                    k, q, (((1,), (1,)), ((), ())), preferred_element_type=jnp.float32
                )
                prob = jnp.exp2(scores * (SCALE * LOG2E) - lse)
                if not seen:
                    prob = hide(prob, ends_ref[:, lanes], at, i, tokens, 0.0)
                dprob = lax.dot_general(
                    v, o_grad, (((1,), (1,)), ((), ())), preferred_element_type=jnp.float32
                )
                dscore = (prob * (dprob - dots)).astype(jnp.bfloat16)
                prob_ref[i, :, lanes] = prob.astype(jnp.bfloat16)
                dscore_ref[i, :, lanes] = dscore
                dq_t = dq_t + jnp.dot(k.T, dscore, preferred_element_type=jnp.float32)
            dq_ref[:, lanes] = dq_t

    in_branches(all_visible(at, ends_ref[...], tokens), body)


def token_kernel(blocks, nears, heads, tokens, live_ref, *refs):
    at = place(nears, heads)
    row_refs, refs = refs[: len(blocks)], refs[len(blocks) :]
    (prob_ref, dscore_ref, dq_ref), refs = refs[:3], refs[3:]
    lse_refs, refs = refs[: len(blocks)], refs[len(blocks) :]
    dkv_refs, (*dq_refs, dk_acc, dv_acc) = refs[: len(KEEP)], refs[len(KEEP) :]
    lines = DH // 2
    all_slabs = slabs_of(row_refs)
    size = len(all_slabs[0]) * lines
    for first, count, held, slabs in steps_of(blocks, all_slabs, lines):
        lanes = slice(first, first + count)
        part_lse = [lse_lines(ref, at, held, size) for ref in lse_refs]
        self_lse = line_values(slabs, lines, 0)
        peak = functools.reduce(jnp.maximum, part_lse, self_lse)
        total = sum(jnp.exp(x - peak) for x in part_lse) + jnp.exp(self_lse - peak)
        lse = jnp.where(live_ref[:, lanes] > 0, peak + jnp.log(total), DEAD_LSE)
        weight = jnp.exp(part_lse[0] - lse)
        dq = (dq_ref[:, lanes] * (weight * SCALE)).T.astype(jnp.bfloat16)
        groups = len(all_slabs[0])
        for m in range(len(slabs)):
            block, j, n = first // size + m // groups, m % groups // nears, m % nears
            dq_refs[n][block, j] = dq[m * lines : (m + 1) * lines]
        weight_t = jnp.broadcast_to(weight, (DH, count)).T
        q, o_grad = (
            (lines_of(slabs, start, lines).astype(jnp.float32) * weight_t).astype(jnp.bfloat16)
            for start in (0, lines)
        )
        for i in range(len(KEEP)):
            dk = jnp.dot(dscore_ref[i, :, lanes], q, preferred_element_type=jnp.float32) * SCALE
            dv = jnp.dot(prob_ref[i, :, lanes], o_grad, preferred_element_type=jnp.float32)
            if first > 0:
                dk = dk + dk_acc[i]
                dv = dv + dv_acc[i]
            if first + count < len(blocks) * size:
                dk_acc[i] = dk
                dv_acc[i] = dv
            else:
                for n in range(2):
                    inner = slice(n * tokens, (n + 1) * tokens)
                    dkv_refs[i][n, 0:tokens, :] = dk[inner].astype(jnp.bfloat16)
                    dkv_refs[i][n, tokens : 2 * tokens, :] = dv[inner].astype(jnp.bfloat16)


def add_query_kernel(nears, *refs):
    own_refs, came_refs, out_refs = refs[:nears], refs[nears:-2], refs[-2:]
    for n in range(nears):
        for j in range(own_refs[0].shape[1]):
            total = own_refs[n][0, j].astype(jnp.float32)
            for ref in came_refs:
                total = total + ref[n, j].astype(jnp.float32)
            out_refs[min(j, 1)][n] = total.astype(jnp.bfloat16)


def tie_kernel(*refs):
    pass


def write_kernel(nears, heads, *refs):
    at = place(nears, heads)
    slab_refs, refs = refs[: -len(KEEP) - 5], refs[-len(KEEP) - 5 :]
    pair_refs, (came_ref, out_q_ref, out_k_ref, out_v_ref, sems) = refs[: len(KEEP)], refs[len(KEEP) :]
    groups, lines, tokens = len(slab_refs) * nears, slab_refs[0].shape[1], out_k_ref.shape[0]
    copies = []
    for i, ref in enumerate(pair_refs):
        for source, other in ((ref.at[0], 0), (came_ref.at[i], FIRST)):
            columns = pl.ds(column_of(at[0] ^ KEEP[i] ^ other, groups, heads), DH)
            copies.append((source.at[0:tokens, :], out_k_ref.at[:, columns]))
            copies.append((source.at[tokens : 2 * tokens, :], out_v_ref.at[:, columns]))
    for j, ref in enumerate(slab_refs):
        for n in range(nears):
            first = pl.multiple_of(group_at(at, j, n, nears) * lines, lines)
            copies.append((ref.at[n], out_q_ref.at[pl.ds(first, lines), :]))
    copies = [pltpu.make_async_copy(s, t, sems.at[n]) for n, (s, t) in enumerate(copies)]
    for copy in copies:
        copy.start()
    for copy in copies:
        copy.wait()


def swap(x, axis, distance, size):
    return lax.ppermute(x, axis, [(i, i ^ distance) for i in range(size)])


def swap_pairs(keep, send):
    members = ("row", "near", "head")
    came = swap(send, members, FIRST, KVH)
    pairs = [jnp.stack([keep[i], came[i]]) for i in range(len(KEEP))]
    return [swap(x, members, j, KVH) if j else x for x, j in zip(pairs, KEEP)]


def tie(x, others):
    return pl.pallas_call(
        tie_kernel,
        in_specs=[ANY] * (1 + len(others)),
        out_specs=ANY,
        out_shape=jax.ShapeDtypeStruct(x.shape, x.dtype),
        input_output_aliases={0: 0},
        compiler_params=PARAMS,
    )(x, *others)


def swap_back(pairs, after):
    members = ("row", "near", "head")
    pairs = [swap(x, members, j, KVH) if j else x for x, j in zip(pairs, KEEP)]
    beyond = tie(jnp.stack([x[1] for x in pairs]), after)
    return [*pairs, swap(beyond, members, FIRST, KVH)]


def swap_slabs(slabs, groups):
    return [swap(x, ("row", "near"), m, groups) if m else x for m, x in enumerate(slabs)]


def line_limits(parts, row_count, nears, rows, lines, resp_len, prompt_end):
    line = lax.broadcasted_iota(jnp.int32, (1, parts * nears * row_count * lines), 1)
    slab = line >> shift_of(lines)
    near_xor = slab & (nears - 1)
    row_xor = (slab >> shift_of(nears)) & (row_count - 1)
    place_of_block = slab >> shift_of(row_count * nears)
    block, bits = jnp.zeros_like(line), shift_of(parts)
    for k in range(bits):
        block = block | (((place_of_block >> k) & 1) << (bits - 1 - k))
    device = (lax.axis_index("part") ^ block) * row_count + (lax.axis_index("row") ^ row_xor)
    device = device * nears + (lax.axis_index("near") ^ near_xor)
    row = device * rows + (line & (rows - 1))
    ends, lengths = jnp.zeros_like(row), jnp.zeros_like(row)
    for r in range(resp_len.shape[0]):
        own = row >> shift_of(RESP_LEN) == r
        ends, lengths = jnp.where(own, prompt_end[r], ends), jnp.where(own, resp_len[r], lengths)
    return ends, ((row & (RESP_LEN - 1)) < lengths).astype(jnp.int32)


def shards(parts, row_count, nears, heads, queries, grad_out, outputs, lse_self, keys, values, resp_len, prompt_end):
    rows = queries.shape[0]
    own_heads = queries.shape[1] // DH
    own_lines = rows * own_heads
    groups = row_count * nears
    lines = own_lines // groups
    tokens = keys.shape[0]
    assert 2 * lines == DH and RESP_LEN % (groups * rows) == 0 and row_count <= 2 and nears <= 2

    def as_lines(x):
        return x.reshape(rows, own_heads, DH).transpose(1, 0, 2).reshape(own_lines, DH)

    def in_hbm(x):
        return pltpu.with_memory_space_constraint(x, pltpu.HBM)

    half_shape = jax.ShapeDtypeStruct((len(KEEP), 2 * tokens, DH), jnp.bfloat16)
    slab_shape = jax.ShapeDtypeStruct((2 * lines + STAT_ROWS, DH), jnp.bfloat16)
    *slabs, kv_keep, kv_send = pl.pallas_call(
        functools.partial(pack_kernel, row_count, nears, heads),
        in_specs=[HBM] * 6,
        out_specs=[VMEM] * (groups + 2),
        out_shape=[slab_shape] * groups + [half_shape] * 2,
        scratch_shapes=[
            pltpu.VMEM((own_lines, DH), jnp.bfloat16),
            pltpu.VMEM(lse_self.shape, jnp.float32),
            pltpu.SemaphoreType.DMA((2 + 2 * groups + 4 * len(KEEP),)),
        ],
        compiler_params=PARAMS,
    )(
        in_hbm(as_lines(queries)),
        in_hbm(as_lines(grad_out)),
        in_hbm(as_lines(outputs)),
        in_hbm(lse_self),
        in_hbm(keys),
        in_hbm(values),
    )
    slabs = swap_slabs(slabs, groups)
    own_block = jnp.concatenate([x[:DH] for x in slabs] + [sum(x[DH:] for x in slabs)], axis=0)
    pairs = swap_pairs(kv_keep, kv_send)
    far = [1 << n for n in reversed(range(shift_of(parts)))]

    blocks, came = [0], [own_block]
    for d in far:
        if d == 1:
            came = came[:1] + [tie(x, pairs[1:3]) for x in came[1:]]
        came = came + [swap(x, "part", d, parts) for x in came]
        blocks = blocks + [b ^ d for b in blocks]
    ends, live = line_limits(parts, row_count, nears, rows, lines, resp_len, prompt_end)

    def part_lse(held, first, refs, before):
        return pl.pallas_call(
            functools.partial(stat_kernel, held, first, nears, heads, tokens),
            in_specs=[VMEM] * (1 + len(refs) + len(KEEP) + len(before)),
            out_shape=jax.ShapeDtypeStruct((parts * lse_rows(groups * lines), DH), jnp.float32),
            compiler_params=PARAMS,
        )(ends, *refs, *pairs, *before)

    lse = [part_lse(blocks[:-1], 0, came[:-1], [])]
    row_refs = [*came[:-1], tie(came[-1], lse)]
    lse = [part_lse(blocks[-1:], (parts - 1) * groups * lines, row_refs[-1:], lse)]
    every_lse = lse + [swap(lse[0], "part", d, parts) for d in range(1, parts)]

    all_lines = parts * groups * lines
    score_shape = jax.ShapeDtypeStruct((len(KEEP), 2 * tokens, all_lines), jnp.bfloat16)
    prob, dscore, dq = pl.pallas_call(
        functools.partial(part_kernel, blocks, nears, heads, tokens),
        in_specs=[VMEM] * (1 + len(row_refs) + len(KEEP) + 1),
        out_specs=[VMEM] * 3,
        out_shape=[score_shape] * 2 + [jax.ShapeDtypeStruct((DH, all_lines), jnp.float32)],
        compiler_params=PARAMS,
    )(ends, *row_refs, *pairs, *lse)
    dq_shape = jax.ShapeDtypeStruct((parts, row_count, lines, DH), jnp.bfloat16)
    acc = pltpu.VMEM((len(KEEP), 2 * tokens, DH), jnp.float32)
    outs = pl.pallas_call(
        functools.partial(token_kernel, blocks, nears, heads, tokens),
        in_specs=[VMEM] * (1 + len(row_refs) + 3 + parts),
        out_shape=[jax.ShapeDtypeStruct((2, 2 * tokens, DH), jnp.bfloat16)] * len(KEEP)
        + [dq_shape] * nears,
        scratch_shapes=[acc] * 2,
        compiler_params=PARAMS,
    )(live, *row_refs, prob, dscore, dq, *every_lse)
    dkv, dq = outs[: len(KEEP)], outs[len(KEEP) :]
    dq = [swap(x, "near", n, nears) if n else x for n, x in enumerate(dq)]
    from_parts = [
        swap(jnp.stack([x[blocks.index(b)] for x in dq]), "part", b, parts)
        for b in range(parts - 1, 0, -1)
    ]
    sum_shape = jax.ShapeDtypeStruct((nears, lines, DH), jnp.bfloat16)
    sums = pl.pallas_call(
        functools.partial(add_query_kernel, nears),
        in_specs=[VMEM] * (nears + len(from_parts)),
        out_shape=[sum_shape] * 2,
        compiler_params=PARAMS,
    )(*dq, *from_parts)
    pairs = swap_back(dkv, from_parts)
    sums = [swap(x, "row", j, row_count) if j else x for j, x in enumerate(sums[:row_count])]
    out_q, out_k, out_v = pl.pallas_call(
        functools.partial(write_kernel, nears, heads),
        in_specs=[VMEM] * (row_count + len(pairs)),
        out_specs=[HBM] * 3,
        out_shape=[
            jax.ShapeDtypeStruct((own_lines, DH), jnp.bfloat16),
            jax.ShapeDtypeStruct(keys.shape, jnp.bfloat16),
            jax.ShapeDtypeStruct(values.shape, jnp.bfloat16),
        ],
        scratch_shapes=[pltpu.SemaphoreType.DMA((4 * len(KEEP) + groups,))],
        compiler_params=PARAMS,
    )(*sums, *pairs)
    out_q = out_q.reshape(own_heads, rows, DH).transpose(1, 0, 2).reshape(rows, own_heads * DH)
    return out_q, out_k, out_v


def solution(mesh):
    ctx, heads = mesh.shape["ctx"], mesh.shape["head"]
    groups = KVH // heads
    parts = ctx // groups
    nears = min(2, groups)
    row_count = groups // nears
    fine = Mesh(
        mesh.devices.reshape(parts, row_count, nears, heads), ("part", "row", "near", "head")
    )
    rows = P(("part", "row", "near"), "head")
    tokens = P(("part", "row", "near", "head"), None)
    return jax.shard_map(
        functools.partial(shards, parts, row_count, nears, heads),
        mesh=fine,
        in_specs=(rows, rows, rows, rows, tokens, tokens, P(), P()),
        out_specs=(rows, tokens, tokens),
        check_vma=False,
    )
```

```python
import functools

import jax
import jax.numpy as jnp
from jax import lax
from jax.experimental import pallas as pl
from jax.experimental.pallas import tpu as pltpu
from jax.sharding import Mesh, PartitionSpec as P

DH = 128
KVH = 8
RESP_LEN = 64
SCALE = DH ** (-0.5)
LOG2E = 1.4426950408889634
MASKED_SCORE = -1e30
DEAD_LSE = 1e30
PIECES = 3
STAT_ROWS = 16
STEP_LINES = 1024
PARAMS = pltpu.CompilerParams(vmem_limit_bytes=24 * 1024 * 1024)
ANY = pl.BlockSpec(memory_space=pl.ANY)
HBM = pl.BlockSpec(memory_space=pltpu.HBM)
VMEM = pl.BlockSpec(memory_space=pltpu.VMEM)

FIRST = 2
KEEP = (0, 1, 4, 5)


def split_pieces(x):
    first = x.astype(jnp.bfloat16)
    rest = x - first.astype(jnp.float32)
    second = rest.astype(jnp.bfloat16)
    third = (rest - second.astype(jnp.float32)).astype(jnp.bfloat16)
    return first, second, third


def shift_of(n):
    assert n & (n - 1) == 0
    return n.bit_length() - 1


def column_of(member, groups, heads):
    head_index, group_index = member & (heads - 1), member >> shift_of(heads)
    return pl.multiple_of((head_index * groups + group_index) * DH, DH)


def place(nears, heads):
    row, near = lax.axis_index("row"), lax.axis_index("near")
    member = (row * nears + near) * heads + lax.axis_index("head")
    return member, row, near, lax.axis_index("part")


def group_at(at, row_xor, near_xor, nears):
    return (at[1] ^ row_xor) * nears + (at[2] ^ near_xor)


def pack_kernel(row_count, nears, heads, q_hbm, o_grad_hbm, o_hbm, lse_hbm, k_hbm, v_hbm, *rest):
    groups = row_count * nears
    slab_refs, (keep_ref, send_ref, o_ref, lse_ref, sems) = rest[:groups], rest[groups:]
    at = place(nears, heads)
    rows, own_heads = lse_ref.shape
    lines = o_ref.shape[0] // groups
    tokens = k_hbm.shape[0]
    copies = [(lse_hbm, lse_ref), (o_hbm, o_ref)]
    slabs = []
    for m, ref in enumerate(slab_refs):
        first = pl.multiple_of(group_at(at, m // nears, m % nears, nears) * lines, lines)
        slabs.append((ref, first))
        copies.append((o_grad_hbm.at[pl.ds(first, lines), :], ref.at[lines : 2 * lines, :]))
    stat_copies = len(copies)
    for ref, first in slabs:
        copies.append((q_hbm.at[pl.ds(first, lines), :], ref.at[0:lines, :]))
    for i, j in enumerate(KEEP):
        for ref, peer in ((send_ref, j ^ FIRST), (keep_ref, j)):
            columns = pl.ds(column_of(at[0] ^ peer, groups, heads), DH)
            copies.append((k_hbm.at[:, columns], ref.at[i, 0:tokens, :]))
            copies.append((v_hbm.at[:, columns], ref.at[i, tokens : 2 * tokens, :]))
    copies = [pltpu.make_async_copy(s, t, sems.at[n]) for n, (s, t) in enumerate(copies)]
    for copy in copies:
        copy.start()

    wide = 2 * lines
    shape = (own_heads, wide)
    head_ids = lax.broadcasted_iota(jnp.int32, shape, 0)
    line_heads = (lax.broadcasted_iota(jnp.int32, shape, 1) & (lines - 1)) >> shift_of(rows)
    chosen = jnp.concatenate(
        [(head_ids == line_heads + (first >> shift_of(rows))) for _, first in slabs], axis=1
    ).astype(jnp.bfloat16)
    shape = (STAT_ROWS, chosen.shape[1])
    own_row = (lax.broadcasted_iota(jnp.int32, shape, 0) & (rows - 1)) == (
        lax.broadcasted_iota(jnp.int32, shape, 1) & (rows - 1)
    )
    shape = (STAT_ROWS, STAT_ROWS)
    piece_of = lax.broadcasted_iota(jnp.int32, shape, 1) >> shift_of(rows)
    stat_row = lax.broadcasted_iota(jnp.int32, shape, 0)
    for copy in copies[:stat_copies]:
        copy.wait()
    pieces = [piece.astype(jnp.float32) for piece in split_pieces(lse_ref[...])]
    pieces.append(jnp.zeros((STAT_ROWS - PIECES * rows, own_heads), jnp.float32))
    pieces = jnp.concatenate(pieces, axis=0).astype(jnp.bfloat16)
    spread = jnp.dot(pieces, chosen, preferred_element_type=jnp.float32)
    spread = jnp.where(own_row, spread, 0.0).astype(jnp.bfloat16)
    kind = lax.broadcasted_iota(jnp.int32, (STAT_ROWS, wide), 0)
    half = lax.broadcasted_iota(jnp.int32, (STAT_ROWS, wide), 1) >> shift_of(lines)
    for m, (ref, first) in enumerate(slabs):
        top = m // 2 * (2 * PIECES)
        gather = (stat_row - top == piece_of).astype(jnp.bfloat16)
        own = spread[:, m * wide : (m + 1) * wide]
        stats = jnp.dot(gather, own, preferred_element_type=jnp.float32)
        o_grad = ref[lines:wide, :].astype(jnp.float32)
        product = o_grad * o_ref[pl.ds(first, lines), :].astype(jnp.float32)
        dots = jnp.sum(jnp.concatenate([product, product], axis=0).T, axis=0, keepdims=True)
        for k, piece in enumerate(split_pieces(dots)):
            stats = jnp.where(kind == top + PIECES + k, piece.astype(jnp.float32), stats)
        if len(slabs) > 1:
            stats = jnp.where(half == m % 2, stats, 0.0)
        ref[wide:, :] = stats.astype(jnp.bfloat16)
    for copy in copies[stat_copies:]:
        copy.wait()


def pair_starts(at, i, tokens):
    first = at[3] * KVH
    return [(first + (at[0] ^ KEEP[i] ^ other)) * tokens for other in (0, FIRST)]


def pair_keys(ref, tokens):
    return jnp.concatenate([ref[0, 0:tokens, :], ref[1, 0:tokens, :]], axis=0)


def pair_values(ref, tokens):
    return jnp.concatenate([ref[0, tokens : 2 * tokens, :], ref[1, tokens : 2 * tokens, :]], axis=0)


def all_visible(at, ends, tokens):
    last = (at[3] + 1) * (KVH * tokens)
    return jnp.min(ends.astype(jnp.float32)) >= last.astype(jnp.float32)


def hide(values, ends, at, i, tokens, hidden):
    offset = lax.broadcasted_iota(jnp.int32, (tokens, values.shape[1]), 0)
    starts = pair_starts(at, i, tokens)
    visible = jnp.concatenate([offset < ends - start for start in starts], axis=0)
    return jnp.where(visible, values, hidden)


def in_branches(condition, body):
    pl.when(condition)(functools.partial(body, True))
    pl.when(jnp.logical_not(condition))(functools.partial(body, False))


def lse_rows(size):
    return max(1, size // DH)


def slabs_of(row_refs):
    return [[(ref, m) for m in range(ref.shape[0] // DH)] for ref in row_refs]


def lines_of(slabs, first, lines):
    return jnp.concatenate(
        [ref[m * DH + first : m * DH + first + lines, :] for ref, m in slabs], axis=0
    )


def stat_kernel(blocks, first, nears, heads, tokens, ends_ref, *refs):
    at = place(nears, heads)
    row_refs, refs = refs[: len(blocks)], refs[len(blocks) :]
    pair_refs, before_refs, lse_ref = refs[: len(KEEP)], refs[len(KEEP) : -1], refs[-1]
    lines = DH // 2
    for ref in before_refs:
        lse_ref[...] = ref[...]

    def body(seen):
        for m, (b, slabs) in enumerate(zip(blocks, slabs_of(row_refs))):
            count = len(slabs) * lines
            q = lines_of(slabs, 0, lines)
            ends = ends_ref[:, first + m * count : first + (m + 1) * count]
            scores = []
            for i, ref in enumerate(pair_refs):
                part = lax.dot_general(
                    pair_keys(ref, tokens),
                    q,
                    (((1,), (1,)), ((), ())),
                    preferred_element_type=jnp.float32,
                )
                scores.append(part if seen else hide(part, ends, at, i, tokens, MASKED_SCORE))
            scores = jnp.concatenate(scores, axis=0)
            peak = jnp.max(scores, axis=0, keepdims=True)
            total = jnp.sum(jnp.exp2((scores - peak) * (SCALE * LOG2E)), axis=0, keepdims=True)
            lse = peak * SCALE + jnp.log(total)
            if count < DH:
                lse = jnp.concatenate([lse] * (DH // count), axis=1)
            held = lse_rows(count)
            for k in range(held):
                lse_ref[pl.ds((at[3] ^ b) * held + k, 1), :] = lse[:, k * DH : (k + 1) * DH]

    in_branches(all_visible(at, ends_ref[...], tokens), body)


def line_values(slabs, lines, first_piece):
    low = lax.broadcasted_iota(jnp.int32, (1, 2 * lines), 1) < lines

    def stats_of(ref):
        first = ref.shape[0] - STAT_ROWS
        return ref[first : first + STAT_ROWS, :].astype(jnp.float32)

    out = []
    for n in range(0, len(slabs), 2):
        ref, m = slabs[n]
        total = None
        for k in range(first_piece, first_piece + PIECES):
            if ref.shape[0] > DH + STAT_ROWS:
                k = m // 2 * (2 * PIECES) + k
                piece = stats_of(ref)[k : k + 1]
            else:
                piece = jnp.where(low, stats_of(ref)[k : k + 1], stats_of(slabs[n + 1][0])[k : k + 1])
            total = piece if total is None else total + piece
        out.append(total)
    return jnp.concatenate(out, axis=1)


def lse_lines(lse_ref, at, blocks, size):
    held = lse_rows(size)
    tiles = []
    for b in blocks:
        for k in range(held):
            tile = lse_ref[pl.ds((at[3] ^ b) * held + k, 1), :]
            tiles.append(tile[:, : min(size, DH)])
    return jnp.concatenate(tiles, axis=1)


def steps_of(blocks, all_slabs, lines):
    size = len(all_slabs[0]) * lines
    step = min(len(blocks), STEP_LINES // size)
    for c in range(0, len(blocks), step):
        slabs = [slab for held in all_slabs[c : c + step] for slab in held]
        yield c * size, step * size, blocks[c : c + step], slabs


def part_kernel(blocks, nears, heads, tokens, ends_ref, *refs):
    at = place(nears, heads)
    row_refs, refs = refs[: len(blocks)], refs[len(blocks) :]
    pair_refs, (lse_ref, prob_ref, dscore_ref, dq_ref) = refs[: len(KEEP)], refs[len(KEEP) :]
    lines = DH // 2
    all_slabs = slabs_of(row_refs)
    size = len(all_slabs[0]) * lines

    def body(seen):
        for first, count, held, slabs in steps_of(blocks, all_slabs, lines):
            q, o_grad = lines_of(slabs, 0, lines), lines_of(slabs, lines, lines)
            dots = line_values(slabs, lines, PIECES)
            lse = lse_lines(lse_ref, at, held, size) * LOG2E
            lanes = slice(first, first + count)
            dq_t = jnp.zeros((DH, count), jnp.float32)
            for i, ref in enumerate(pair_refs):
                k, v = pair_keys(ref, tokens), pair_values(ref, tokens)
                scores = lax.dot_general(
                    k, q, (((1,), (1,)), ((), ())), preferred_element_type=jnp.float32
                )
                prob = jnp.exp2(scores * (SCALE * LOG2E) - lse)
                if not seen:
                    prob = hide(prob, ends_ref[:, lanes], at, i, tokens, 0.0)
                dprob = lax.dot_general(
                    v, o_grad, (((1,), (1,)), ((), ())), preferred_element_type=jnp.float32
                )
                dscore = (prob * (dprob - dots)).astype(jnp.bfloat16)
                prob_ref[i, :, lanes] = prob.astype(jnp.bfloat16)
                dscore_ref[i, :, lanes] = dscore
                dq_t = dq_t + jnp.dot(k.T, dscore, preferred_element_type=jnp.float32)
            dq_ref[:, lanes] = dq_t

    in_branches(all_visible(at, ends_ref[...], tokens), body)


def token_kernel(blocks, nears, heads, tokens, live_ref, *refs):
    at = place(nears, heads)
    row_refs, refs = refs[: len(blocks)], refs[len(blocks) :]
    (prob_ref, dscore_ref, dq_ref), refs = refs[:3], refs[3:]
    lse_refs, refs = refs[: len(blocks)], refs[len(blocks) :]
    dkv_refs, (*dq_refs, dk_acc, dv_acc) = refs[: len(KEEP)], refs[len(KEEP) :]
    lines = DH // 2
    all_slabs = slabs_of(row_refs)
    size = len(all_slabs[0]) * lines
    for first, count, held, slabs in steps_of(blocks, all_slabs, lines):
        lanes = slice(first, first + count)
        part_lse = [lse_lines(ref, at, held, size) for ref in lse_refs]
        self_lse = line_values(slabs, lines, 0)
        peak = functools.reduce(jnp.maximum, part_lse, self_lse)
        total = sum(jnp.exp(x - peak) for x in part_lse) + jnp.exp(self_lse - peak)
        lse = jnp.where(live_ref[:, lanes] > 0, peak + jnp.log(total), DEAD_LSE)
        weight = jnp.exp(part_lse[0] - lse)
        dq = (dq_ref[:, lanes] * (weight * SCALE)).T.astype(jnp.bfloat16)
        groups = len(all_slabs[0])
        for m in range(len(slabs)):
            block, j, n = first // size + m // groups, m % groups // nears, m % nears
            dq_refs[n][block, j] = dq[m * lines : (m + 1) * lines]
        weight_t = jnp.broadcast_to(weight, (DH, count)).T
        q, o_grad = (
            (lines_of(slabs, start, lines).astype(jnp.float32) * weight_t).astype(jnp.bfloat16)
            for start in (0, lines)
        )
        for i in range(len(KEEP)):
            dk = jnp.dot(dscore_ref[i, :, lanes], q, preferred_element_type=jnp.float32) * SCALE
            dv = jnp.dot(prob_ref[i, :, lanes], o_grad, preferred_element_type=jnp.float32)
            if first > 0:
                dk = dk + dk_acc[i]
                dv = dv + dv_acc[i]
            if first + count < len(blocks) * size:
                dk_acc[i] = dk
                dv_acc[i] = dv
            else:
                for n in range(2):
                    inner = slice(n * tokens, (n + 1) * tokens)
                    dkv_refs[i][n, 0:tokens, :] = dk[inner].astype(jnp.bfloat16)
                    dkv_refs[i][n, tokens : 2 * tokens, :] = dv[inner].astype(jnp.bfloat16)


def add_query_kernel(nears, *refs):
    own_refs, came_refs, out_refs = refs[:nears], refs[nears:-2], refs[-2:]
    for n in range(nears):
        for j in range(own_refs[0].shape[1]):
            total = own_refs[n][0, j].astype(jnp.float32)
            for ref in came_refs:
                total = total + ref[n, j].astype(jnp.float32)
            out_refs[min(j, 1)][n] = total.astype(jnp.bfloat16)


def tie_kernel(*refs):
    pass


def write_kernel(nears, heads, *refs):
    at = place(nears, heads)
    slab_refs, refs = refs[: -len(KEEP) - 5], refs[-len(KEEP) - 5 :]
    pair_refs, (came_ref, out_q_ref, out_k_ref, out_v_ref, sems) = refs[: len(KEEP)], refs[len(KEEP) :]
    groups, lines, tokens = len(slab_refs) * nears, slab_refs[0].shape[1], out_k_ref.shape[0]
    copies = []
    for i, ref in enumerate(pair_refs):
        for source, other in ((ref.at[0], 0), (came_ref.at[i], FIRST)):
            columns = pl.ds(column_of(at[0] ^ KEEP[i] ^ other, groups, heads), DH)
            copies.append((source.at[0:tokens, :], out_k_ref.at[:, columns]))
            copies.append((source.at[tokens : 2 * tokens, :], out_v_ref.at[:, columns]))
    for j, ref in enumerate(slab_refs):
        for n in range(nears):
            first = pl.multiple_of(group_at(at, j, n, nears) * lines, lines)
            copies.append((ref.at[n], out_q_ref.at[pl.ds(first, lines), :]))
    copies = [pltpu.make_async_copy(s, t, sems.at[n]) for n, (s, t) in enumerate(copies)]
    for copy in copies:
        copy.start()
    for copy in copies:
        copy.wait()


def swap(x, axis, distance, size):
    return lax.ppermute(x, axis, [(i, i ^ distance) for i in range(size)])


def swap_pairs(keep, send):
    members = ("row", "near", "head")
    came = swap(send, members, FIRST, KVH)
    pairs = [jnp.stack([keep[i], came[i]]) for i in range(len(KEEP))]
    return [swap(x, members, j, KVH) if j else x for x, j in zip(pairs, KEEP)]


def tie(x, others):
    return pl.pallas_call(
        tie_kernel,
        in_specs=[ANY] * (1 + len(others)),
        out_specs=ANY,
        out_shape=jax.ShapeDtypeStruct(x.shape, x.dtype),
        input_output_aliases={0: 0},
        compiler_params=PARAMS,
    )(x, *others)


def swap_back(pairs, after):
    members = ("row", "near", "head")
    pairs = [swap(x, members, j, KVH) if j else x for x, j in zip(pairs, KEEP)]
    beyond = tie(jnp.stack([x[1] for x in pairs]), after)
    return [*pairs, swap(beyond, members, FIRST, KVH)]


def swap_slabs(slabs, groups):
    came = [swap(slabs[m], ("row", "near"), m, groups) for m in range(groups - 1, 0, -1)]
    return [slabs[0], *came[::-1]]


def line_limits(parts, row_count, nears, rows, lines, resp_len, prompt_end):
    line = lax.broadcasted_iota(jnp.int32, (1, parts * nears * row_count * lines), 1)
    slab = line >> shift_of(lines)
    near_xor = slab & (nears - 1)
    row_xor = (slab >> shift_of(nears)) & (row_count - 1)
    place_of_block = slab >> shift_of(row_count * nears)
    block, bits = jnp.zeros_like(line), shift_of(parts)
    for k in range(bits):
        block = block | (((place_of_block >> k) & 1) << (bits - 1 - k))
    device = (lax.axis_index("part") ^ block) * row_count + (lax.axis_index("row") ^ row_xor)
    device = device * nears + (lax.axis_index("near") ^ near_xor)
    row = device * rows + (line & (rows - 1))
    ends, lengths = jnp.zeros_like(row), jnp.zeros_like(row)
    for r in range(resp_len.shape[0]):
        own = row >> shift_of(RESP_LEN) == r
        ends, lengths = jnp.where(own, prompt_end[r], ends), jnp.where(own, resp_len[r], lengths)
    return ends, ((row & (RESP_LEN - 1)) < lengths).astype(jnp.int32)


def shards(parts, row_count, nears, heads, queries, grad_out, outputs, lse_self, keys, values, resp_len, prompt_end):
    rows = queries.shape[0]
    own_heads = queries.shape[1] // DH
    own_lines = rows * own_heads
    groups = row_count * nears
    lines = own_lines // groups
    tokens = keys.shape[0]
    assert 2 * lines == DH and RESP_LEN % (groups * rows) == 0 and row_count <= 2 and nears <= 2

    def as_lines(x):
        return x.reshape(rows, own_heads, DH).transpose(1, 0, 2).reshape(own_lines, DH)

    def in_hbm(x):
        return pltpu.with_memory_space_constraint(x, pltpu.HBM)

    half_shape = jax.ShapeDtypeStruct((len(KEEP), 2 * tokens, DH), jnp.bfloat16)
    slab_shape = jax.ShapeDtypeStruct((2 * lines + STAT_ROWS, DH), jnp.bfloat16)
    *slabs, kv_keep, kv_send = pl.pallas_call(
        functools.partial(pack_kernel, row_count, nears, heads),
        in_specs=[HBM] * 6,
        out_specs=[VMEM] * (groups + 2),
        out_shape=[slab_shape] * groups + [half_shape] * 2,
        scratch_shapes=[
            pltpu.VMEM((own_lines, DH), jnp.bfloat16),
            pltpu.VMEM(lse_self.shape, jnp.float32),
            pltpu.SemaphoreType.DMA((2 + 2 * groups + 4 * len(KEEP),)),
        ],
        compiler_params=PARAMS,
    )(
        in_hbm(as_lines(queries)),
        in_hbm(as_lines(grad_out)),
        in_hbm(as_lines(outputs)),
        in_hbm(lse_self),
        in_hbm(keys),
        in_hbm(values),
    )
    slabs = swap_slabs(slabs, groups)
    own_block = jnp.concatenate([x[:DH] for x in slabs] + [sum(x[DH:] for x in slabs)], axis=0)
    pairs = swap_pairs(kv_keep, kv_send)
    far = [1 << n for n in reversed(range(shift_of(parts)))]

    blocks, came = [0], [own_block]
    for d in far:
        if d == 1:
            came = came[:1] + [tie(x, pairs[1:3]) for x in came[1:]]
        came = came + [swap(x, "part", d, parts) for x in came]
        blocks = blocks + [b ^ d for b in blocks]
    ends, live = line_limits(parts, row_count, nears, rows, lines, resp_len, prompt_end)

    def part_lse(held, first, refs, before):
        return pl.pallas_call(
            functools.partial(stat_kernel, held, first, nears, heads, tokens),
            in_specs=[VMEM] * (1 + len(refs) + len(KEEP) + len(before)),
            out_shape=jax.ShapeDtypeStruct((parts * lse_rows(groups * lines), DH), jnp.float32),
            compiler_params=PARAMS,
        )(ends, *refs, *pairs, *before)

    lse = [part_lse(blocks[:-1], 0, came[:-1], [])]
    row_refs = [*came[:-1], tie(came[-1], lse)]
    lse = [part_lse(blocks[-1:], (parts - 1) * groups * lines, row_refs[-1:], lse)]
    every_lse = lse + [swap(lse[0], "part", d, parts) for d in range(1, parts)]

    all_lines = parts * groups * lines
    score_shape = jax.ShapeDtypeStruct((len(KEEP), 2 * tokens, all_lines), jnp.bfloat16)
    prob, dscore, dq = pl.pallas_call(
        functools.partial(part_kernel, blocks, nears, heads, tokens),
        in_specs=[VMEM] * (1 + len(row_refs) + len(KEEP) + 1),
        out_specs=[VMEM] * 3,
        out_shape=[score_shape] * 2 + [jax.ShapeDtypeStruct((DH, all_lines), jnp.float32)],
        compiler_params=PARAMS,
    )(ends, *row_refs, *pairs, *lse)
    dq_shape = jax.ShapeDtypeStruct((parts, row_count, lines, DH), jnp.bfloat16)
    acc = pltpu.VMEM((len(KEEP), 2 * tokens, DH), jnp.float32)
    outs = pl.pallas_call(
        functools.partial(token_kernel, blocks, nears, heads, tokens),
        in_specs=[VMEM] * (1 + len(row_refs) + 3 + parts),
        out_shape=[jax.ShapeDtypeStruct((2, 2 * tokens, DH), jnp.bfloat16)] * len(KEEP)
        + [dq_shape] * nears,
        scratch_shapes=[acc] * 2,
        compiler_params=PARAMS,
    )(live, *row_refs, prob, dscore, dq, *every_lse)
    dkv, dq = outs[: len(KEEP)], outs[len(KEEP) :]
    dq = [swap(x, "near", n, nears) if n else x for n, x in enumerate(dq)]
    from_parts = [
        swap(jnp.stack([x[blocks.index(b)] for x in dq]), "part", b, parts)
        for b in range(parts - 1, 0, -1)
    ]
    sum_shape = jax.ShapeDtypeStruct((nears, lines, DH), jnp.bfloat16)
    sums = pl.pallas_call(
        functools.partial(add_query_kernel, nears),
        in_specs=[VMEM] * (nears + len(from_parts)),
        out_shape=[sum_shape] * 2,
        compiler_params=PARAMS,
    )(*dq, *from_parts)
    pairs = swap_back(dkv, from_parts)
    sums = [swap(x, "row", j, row_count) if j else x for j, x in enumerate(sums[:row_count])]
    out_q, out_k, out_v = pl.pallas_call(
        functools.partial(write_kernel, nears, heads),
        in_specs=[VMEM] * (row_count + len(pairs)),
        out_specs=[HBM] * 3,
        out_shape=[
            jax.ShapeDtypeStruct((own_lines, DH), jnp.bfloat16),
            jax.ShapeDtypeStruct(keys.shape, jnp.bfloat16),
            jax.ShapeDtypeStruct(values.shape, jnp.bfloat16),
        ],
        scratch_shapes=[pltpu.SemaphoreType.DMA((4 * len(KEEP) + groups,))],
        compiler_params=PARAMS,
    )(*sums, *pairs)
    out_q = out_q.reshape(own_heads, rows, DH).transpose(1, 0, 2).reshape(rows, own_heads * DH)
    return out_q, out_k, out_v


def solution(mesh):
    ctx, heads = mesh.shape["ctx"], mesh.shape["head"]
    groups = KVH // heads
    parts = ctx // groups
    nears = min(2, groups)
    row_count = groups // nears
    fine = Mesh(
        mesh.devices.reshape(parts, row_count, nears, heads), ("part", "row", "near", "head")
    )
    rows = P(("part", "row", "near"), "head")
    tokens = P(("part", "row", "near", "head"), None)
    return jax.shard_map(
        functools.partial(shards, parts, row_count, nears, heads),
        mesh=fine,
        in_specs=(rows, rows, rows, rows, tokens, tokens, P(), P()),
        out_specs=(rows, tokens, tokens),
        check_vma=False,
    )
```

```python
import functools

import jax
import jax.numpy as jnp
from jax import lax
from jax.experimental import pallas as pl
from jax.experimental.pallas import tpu as pltpu
from jax.sharding import Mesh, PartitionSpec as P

DH = 128
KVH = 8
RESP_LEN = 64
SCALE = DH ** (-0.5)
LOG2E = 1.4426950408889634
MASKED_SCORE = -1e30
DEAD_LSE = 1e30
PIECES = 3
STAT_ROWS = 16
STEP_LINES = 1024
PARAMS = pltpu.CompilerParams(vmem_limit_bytes=24 * 1024 * 1024)
ANY = pl.BlockSpec(memory_space=pl.ANY)
HBM = pl.BlockSpec(memory_space=pltpu.HBM)
VMEM = pl.BlockSpec(memory_space=pltpu.VMEM)

FIRST = 2
KEEP = (0, 5, 1, 4)


def split_pieces(x):
    first = x.astype(jnp.bfloat16)
    rest = x - first.astype(jnp.float32)
    second = rest.astype(jnp.bfloat16)
    third = (rest - second.astype(jnp.float32)).astype(jnp.bfloat16)
    return first, second, third


def shift_of(n):
    assert n & (n - 1) == 0
    return n.bit_length() - 1


def column_of(member, groups, heads):
    head_index, group_index = member & (heads - 1), member >> shift_of(heads)
    return pl.multiple_of((head_index * groups + group_index) * DH, DH)


def place(nears, heads):
    row, near = lax.axis_index("row"), lax.axis_index("near")
    member = (row * nears + near) * heads + lax.axis_index("head")
    return member, row, near, lax.axis_index("part")


def group_at(at, row_xor, near_xor, nears):
    return (at[1] ^ row_xor) * nears + (at[2] ^ near_xor)


def pack_kernel(row_count, nears, heads, q_hbm, o_grad_hbm, o_hbm, lse_hbm, k_hbm, v_hbm, *rest):
    groups = row_count * nears
    slab_refs, (keep_ref, send_ref, o_ref, lse_ref, sems) = rest[:groups], rest[groups:]
    at = place(nears, heads)
    rows, own_heads = lse_ref.shape
    lines = o_ref.shape[0] // groups
    tokens = k_hbm.shape[0]
    copies = [(lse_hbm, lse_ref), (o_hbm, o_ref)]
    slabs = []
    for m, ref in enumerate(slab_refs):
        first = pl.multiple_of(group_at(at, m // nears, m % nears, nears) * lines, lines)
        slabs.append((ref, first))
        copies.append((o_grad_hbm.at[pl.ds(first, lines), :], ref.at[lines : 2 * lines, :]))
    stat_copies = len(copies)
    for ref, first in slabs:
        copies.append((q_hbm.at[pl.ds(first, lines), :], ref.at[0:lines, :]))
    for i, j in enumerate(KEEP):
        for ref, peer in ((send_ref, j ^ FIRST), (keep_ref, j)):
            columns = pl.ds(column_of(at[0] ^ peer, groups, heads), DH)
            copies.append((k_hbm.at[:, columns], ref.at[i, 0:tokens, :]))
            copies.append((v_hbm.at[:, columns], ref.at[i, tokens : 2 * tokens, :]))
    copies = [pltpu.make_async_copy(s, t, sems.at[n]) for n, (s, t) in enumerate(copies)]
    for copy in copies:
        copy.start()

    wide = 2 * lines
    shape = (own_heads, wide)
    head_ids = lax.broadcasted_iota(jnp.int32, shape, 0)
    line_heads = (lax.broadcasted_iota(jnp.int32, shape, 1) & (lines - 1)) >> shift_of(rows)
    chosen = jnp.concatenate(
        [(head_ids == line_heads + (first >> shift_of(rows))) for _, first in slabs], axis=1
    ).astype(jnp.bfloat16)
    shape = (STAT_ROWS, chosen.shape[1])
    own_row = (lax.broadcasted_iota(jnp.int32, shape, 0) & (rows - 1)) == (
        lax.broadcasted_iota(jnp.int32, shape, 1) & (rows - 1)
    )
    shape = (STAT_ROWS, STAT_ROWS)
    piece_of = lax.broadcasted_iota(jnp.int32, shape, 1) >> shift_of(rows)
    stat_row = lax.broadcasted_iota(jnp.int32, shape, 0)
    for copy in copies[:stat_copies]:
        copy.wait()
    pieces = [piece.astype(jnp.float32) for piece in split_pieces(lse_ref[...])]
    pieces.append(jnp.zeros((STAT_ROWS - PIECES * rows, own_heads), jnp.float32))
    pieces = jnp.concatenate(pieces, axis=0).astype(jnp.bfloat16)
    spread = jnp.dot(pieces, chosen, preferred_element_type=jnp.float32)
    spread = jnp.where(own_row, spread, 0.0).astype(jnp.bfloat16)
    kind = lax.broadcasted_iota(jnp.int32, (STAT_ROWS, wide), 0)
    half = lax.broadcasted_iota(jnp.int32, (STAT_ROWS, wide), 1) >> shift_of(lines)
    for m, (ref, first) in enumerate(slabs):
        top = m // 2 * (2 * PIECES)
        gather = (stat_row - top == piece_of).astype(jnp.bfloat16)
        own = spread[:, m * wide : (m + 1) * wide]
        stats = jnp.dot(gather, own, preferred_element_type=jnp.float32)
        o_grad = ref[lines:wide, :].astype(jnp.float32)
        product = o_grad * o_ref[pl.ds(first, lines), :].astype(jnp.float32)
        dots = jnp.sum(jnp.concatenate([product, product], axis=0).T, axis=0, keepdims=True)
        for k, piece in enumerate(split_pieces(dots)):
            stats = jnp.where(kind == top + PIECES + k, piece.astype(jnp.float32), stats)
        if len(slabs) > 1:
            stats = jnp.where(half == m % 2, stats, 0.0)
        ref[wide:, :] = stats.astype(jnp.bfloat16)
    for copy in copies[stat_copies:]:
        copy.wait()


def pair_starts(at, i, tokens):
    first = at[3] * KVH
    return [(first + (at[0] ^ KEEP[i] ^ other)) * tokens for other in (0, FIRST)]


def pair_keys(ref, tokens):
    return jnp.concatenate([ref[0, 0:tokens, :], ref[1, 0:tokens, :]], axis=0)


def pair_values(ref, tokens):
    return jnp.concatenate([ref[0, tokens : 2 * tokens, :], ref[1, tokens : 2 * tokens, :]], axis=0)


def all_visible(at, ends, tokens):
    last = (at[3] + 1) * (KVH * tokens)
    return jnp.min(ends.astype(jnp.float32)) >= last.astype(jnp.float32)


def hide(values, ends, at, i, tokens, hidden):
    offset = lax.broadcasted_iota(jnp.int32, (tokens, values.shape[1]), 0)
    starts = pair_starts(at, i, tokens)
    visible = jnp.concatenate([offset < ends - start for start in starts], axis=0)
    return jnp.where(visible, values, hidden)


def in_branches(condition, body):
    pl.when(condition)(functools.partial(body, True))
    pl.when(jnp.logical_not(condition))(functools.partial(body, False))


def lse_rows(size):
    return max(1, size // DH)


def slabs_of(row_refs):
    return [[(ref, m) for m in range(ref.shape[0] // DH)] for ref in row_refs]


def lines_of(slabs, first, lines):
    return jnp.concatenate(
        [ref[m * DH + first : m * DH + first + lines, :] for ref, m in slabs], axis=0
    )


def stat_kernel(blocks, first, nears, heads, tokens, ends_ref, *refs):
    at = place(nears, heads)
    row_refs, refs = refs[: len(blocks)], refs[len(blocks) :]
    pair_refs, before_refs, lse_ref = refs[: len(KEEP)], refs[len(KEEP) : -1], refs[-1]
    lines = DH // 2
    for ref in before_refs:
        lse_ref[...] = ref[...]

    def body(seen):
        for m, (b, slabs) in enumerate(zip(blocks, slabs_of(row_refs))):
            count = len(slabs) * lines
            q = lines_of(slabs, 0, lines)
            ends = ends_ref[:, first + m * count : first + (m + 1) * count]
            scores = []
            for i, ref in enumerate(pair_refs):
                part = lax.dot_general(
                    pair_keys(ref, tokens),
                    q,
                    (((1,), (1,)), ((), ())),
                    preferred_element_type=jnp.float32,
                )
                scores.append(part if seen else hide(part, ends, at, i, tokens, MASKED_SCORE))
            scores = jnp.concatenate(scores, axis=0)
            peak = jnp.max(scores, axis=0, keepdims=True)
            total = jnp.sum(jnp.exp2((scores - peak) * (SCALE * LOG2E)), axis=0, keepdims=True)
            lse = peak * SCALE + jnp.log(total)
            if count < DH:
                lse = jnp.concatenate([lse] * (DH // count), axis=1)
            held = lse_rows(count)
            for k in range(held):
                lse_ref[pl.ds((at[3] ^ b) * held + k, 1), :] = lse[:, k * DH : (k + 1) * DH]

    in_branches(all_visible(at, ends_ref[...], tokens), body)


def line_values(slabs, lines, first_piece):
    low = lax.broadcasted_iota(jnp.int32, (1, 2 * lines), 1) < lines

    def stats_of(ref):
        first = ref.shape[0] - STAT_ROWS
        return ref[first : first + STAT_ROWS, :].astype(jnp.float32)

    out = []
    for n in range(0, len(slabs), 2):
        ref, m = slabs[n]
        total = None
        for k in range(first_piece, first_piece + PIECES):
            if ref.shape[0] > DH + STAT_ROWS:
                k = m // 2 * (2 * PIECES) + k
                piece = stats_of(ref)[k : k + 1]
            else:
                piece = jnp.where(low, stats_of(ref)[k : k + 1], stats_of(slabs[n + 1][0])[k : k + 1])
            total = piece if total is None else total + piece
        out.append(total)
    return jnp.concatenate(out, axis=1)


def lse_lines(lse_ref, at, blocks, size):
    held = lse_rows(size)
    tiles = []
    for b in blocks:
        for k in range(held):
            tile = lse_ref[pl.ds((at[3] ^ b) * held + k, 1), :]
            tiles.append(tile[:, : min(size, DH)])
    return jnp.concatenate(tiles, axis=1)


def steps_of(blocks, all_slabs, lines):
    size = len(all_slabs[0]) * lines
    step = min(len(blocks), STEP_LINES // size)
    for c in range(0, len(blocks), step):
        slabs = [slab for held in all_slabs[c : c + step] for slab in held]
        yield c * size, step * size, blocks[c : c + step], slabs


def part_kernel(blocks, nears, heads, tokens, ends_ref, *refs):
    at = place(nears, heads)
    row_refs, refs = refs[: len(blocks)], refs[len(blocks) :]
    pair_refs, (lse_ref, prob_ref, dscore_ref, dq_ref) = refs[: len(KEEP)], refs[len(KEEP) :]
    lines = DH // 2
    all_slabs = slabs_of(row_refs)
    size = len(all_slabs[0]) * lines

    def body(seen):
        for first, count, held, slabs in steps_of(blocks, all_slabs, lines):
            q, o_grad = lines_of(slabs, 0, lines), lines_of(slabs, lines, lines)
            dots = line_values(slabs, lines, PIECES)
            lse = lse_lines(lse_ref, at, held, size) * LOG2E
            lanes = slice(first, first + count)
            dq_t = jnp.zeros((DH, count), jnp.float32)
            for i, ref in enumerate(pair_refs):
                k, v = pair_keys(ref, tokens), pair_values(ref, tokens)
                scores = lax.dot_general(
                    k, q, (((1,), (1,)), ((), ())), preferred_element_type=jnp.float32
                )
                prob = jnp.exp2(scores * (SCALE * LOG2E) - lse)
                if not seen:
                    prob = hide(prob, ends_ref[:, lanes], at, i, tokens, 0.0)
                dprob = lax.dot_general(
                    v, o_grad, (((1,), (1,)), ((), ())), preferred_element_type=jnp.float32
                )
                dscore = (prob * (dprob - dots)).astype(jnp.bfloat16)
                prob_ref[i, :, lanes] = prob.astype(jnp.bfloat16)
                dscore_ref[i, :, lanes] = dscore
                dq_t = dq_t + jnp.dot(k.T, dscore, preferred_element_type=jnp.float32)
            dq_ref[:, lanes] = dq_t

    in_branches(all_visible(at, ends_ref[...], tokens), body)


def token_kernel(blocks, nears, heads, tokens, live_ref, *refs):
    at = place(nears, heads)
    row_refs, refs = refs[: len(blocks)], refs[len(blocks) :]
    (prob_ref, dscore_ref, dq_ref), refs = refs[:3], refs[3:]
    lse_refs, refs = refs[: len(blocks)], refs[len(blocks) :]
    dkv_refs, (*dq_refs, dk_acc, dv_acc) = refs[: len(KEEP)], refs[len(KEEP) :]
    lines = DH // 2
    all_slabs = slabs_of(row_refs)
    size = len(all_slabs[0]) * lines
    for first, count, held, slabs in steps_of(blocks, all_slabs, lines):
        lanes = slice(first, first + count)
        part_lse = [lse_lines(ref, at, held, size) for ref in lse_refs]
        self_lse = line_values(slabs, lines, 0)
        peak = functools.reduce(jnp.maximum, part_lse, self_lse)
        total = sum(jnp.exp(x - peak) for x in part_lse) + jnp.exp(self_lse - peak)
        lse = jnp.where(live_ref[:, lanes] > 0, peak + jnp.log(total), DEAD_LSE)
        weight = jnp.exp(part_lse[0] - lse)
        dq = (dq_ref[:, lanes] * (weight * SCALE)).T.astype(jnp.bfloat16)
        groups = len(all_slabs[0])
        for m in range(len(slabs)):
            block, j, n = first // size + m // groups, m % groups // nears, m % nears
            dq_refs[n][block, j] = dq[m * lines : (m + 1) * lines]
        weight_t = jnp.broadcast_to(weight, (DH, count)).T
        q, o_grad = (
            (lines_of(slabs, start, lines).astype(jnp.float32) * weight_t).astype(jnp.bfloat16)
            for start in (0, lines)
        )
        for i in range(len(KEEP)):
            dk = jnp.dot(dscore_ref[i, :, lanes], q, preferred_element_type=jnp.float32) * SCALE
            dv = jnp.dot(prob_ref[i, :, lanes], o_grad, preferred_element_type=jnp.float32)
            if first > 0:
                dk = dk + dk_acc[i]
                dv = dv + dv_acc[i]
            if first + count < len(blocks) * size:
                dk_acc[i] = dk
                dv_acc[i] = dv
            else:
                for n in range(2):
                    inner = slice(n * tokens, (n + 1) * tokens)
                    dkv_refs[i][n, 0:tokens, :] = dk[inner].astype(jnp.bfloat16)
                    dkv_refs[i][n, tokens : 2 * tokens, :] = dv[inner].astype(jnp.bfloat16)


def add_query_kernel(nears, *refs):
    own_refs, came_refs, out_refs = refs[:nears], refs[nears:-2], refs[-2:]
    for n in range(nears):
        for j in range(own_refs[0].shape[1]):
            total = own_refs[n][0, j].astype(jnp.float32)
            for ref in came_refs:
                total = total + ref[n, j].astype(jnp.float32)
            out_refs[min(j, 1)][n] = total.astype(jnp.bfloat16)


def tie_kernel(*refs):
    pass


def write_kernel(nears, heads, *refs):
    at = place(nears, heads)
    slab_refs, refs = refs[: -len(KEEP) - 5], refs[-len(KEEP) - 5 :]
    pair_refs, (came_ref, out_q_ref, out_k_ref, out_v_ref, sems) = refs[: len(KEEP)], refs[len(KEEP) :]
    groups, lines, tokens = len(slab_refs) * nears, slab_refs[0].shape[1], out_k_ref.shape[0]
    copies = []
    for i, ref in enumerate(pair_refs):
        for source, other in ((ref.at[0], 0), (came_ref.at[i], FIRST)):
            columns = pl.ds(column_of(at[0] ^ KEEP[i] ^ other, groups, heads), DH)
            copies.append((source.at[0:tokens, :], out_k_ref.at[:, columns]))
            copies.append((source.at[tokens : 2 * tokens, :], out_v_ref.at[:, columns]))
    for j, ref in enumerate(slab_refs):
        for n in range(nears):
            first = pl.multiple_of(group_at(at, j, n, nears) * lines, lines)
            copies.append((ref.at[n], out_q_ref.at[pl.ds(first, lines), :]))
    copies = [pltpu.make_async_copy(s, t, sems.at[n]) for n, (s, t) in enumerate(copies)]
    for copy in copies:
        copy.start()
    for copy in copies:
        copy.wait()


def swap(x, axis, distance, size):
    return lax.ppermute(x, axis, [(i, i ^ distance) for i in range(size)])


def swap_pairs(keep, send):
    members = ("row", "near", "head")
    came = swap(send, members, FIRST, KVH)
    pairs = [jnp.stack([keep[i], came[i]]) for i in range(len(KEEP))]
    return [swap(x, members, j, KVH) if j else x for x, j in zip(pairs, KEEP)]


def tie(x, others):
    return pl.pallas_call(
        tie_kernel,
        in_specs=[ANY] * (1 + len(others)),
        out_specs=ANY,
        out_shape=jax.ShapeDtypeStruct(x.shape, x.dtype),
        input_output_aliases={0: 0},
        compiler_params=PARAMS,
    )(x, *others)


def swap_back(pairs, after):
    members = ("row", "near", "head")
    pairs = [swap(x, members, j, KVH) if j else x for x, j in zip(pairs, KEEP)]
    beyond = tie(jnp.stack([x[1] for x in pairs]), after)
    return [*pairs, swap(beyond, members, FIRST, KVH)]


def swap_slabs(slabs, groups):
    return [swap(x, ("row", "near"), m, groups) if m else x for m, x in enumerate(slabs)]


def line_limits(parts, row_count, nears, rows, lines, resp_len, prompt_end):
    line = lax.broadcasted_iota(jnp.int32, (1, parts * nears * row_count * lines), 1)
    slab = line >> shift_of(lines)
    near_xor = slab & (nears - 1)
    row_xor = (slab >> shift_of(nears)) & (row_count - 1)
    place_of_block = slab >> shift_of(row_count * nears)
    block, bits = jnp.zeros_like(line), shift_of(parts)
    for k in range(bits):
        block = block | (((place_of_block >> k) & 1) << (bits - 1 - k))
    device = (lax.axis_index("part") ^ block) * row_count + (lax.axis_index("row") ^ row_xor)
    device = device * nears + (lax.axis_index("near") ^ near_xor)
    row = device * rows + (line & (rows - 1))
    ends, lengths = jnp.zeros_like(row), jnp.zeros_like(row)
    for r in range(resp_len.shape[0]):
        own = row >> shift_of(RESP_LEN) == r
        ends, lengths = jnp.where(own, prompt_end[r], ends), jnp.where(own, resp_len[r], lengths)
    return ends, ((row & (RESP_LEN - 1)) < lengths).astype(jnp.int32)


def shards(parts, row_count, nears, heads, queries, grad_out, outputs, lse_self, keys, values, resp_len, prompt_end):
    rows = queries.shape[0]
    own_heads = queries.shape[1] // DH
    own_lines = rows * own_heads
    groups = row_count * nears
    lines = own_lines // groups
    tokens = keys.shape[0]
    assert 2 * lines == DH and RESP_LEN % (groups * rows) == 0 and row_count <= 2 and nears <= 2

    def as_lines(x):
        return x.reshape(rows, own_heads, DH).transpose(1, 0, 2).reshape(own_lines, DH)

    def in_hbm(x):
        return pltpu.with_memory_space_constraint(x, pltpu.HBM)

    half_shape = jax.ShapeDtypeStruct((len(KEEP), 2 * tokens, DH), jnp.bfloat16)
    slab_shape = jax.ShapeDtypeStruct((2 * lines + STAT_ROWS, DH), jnp.bfloat16)
    *slabs, kv_keep, kv_send = pl.pallas_call(
        functools.partial(pack_kernel, row_count, nears, heads),
        in_specs=[HBM] * 6,
        out_specs=[VMEM] * (groups + 2),
        out_shape=[slab_shape] * groups + [half_shape] * 2,
        scratch_shapes=[
            pltpu.VMEM((own_lines, DH), jnp.bfloat16),
            pltpu.VMEM(lse_self.shape, jnp.float32),
            pltpu.SemaphoreType.DMA((2 + 2 * groups + 4 * len(KEEP),)),
        ],
        compiler_params=PARAMS,
    )(
        in_hbm(as_lines(queries)),
        in_hbm(as_lines(grad_out)),
        in_hbm(as_lines(outputs)),
        in_hbm(lse_self),
        in_hbm(keys),
        in_hbm(values),
    )
    slabs = swap_slabs(slabs, groups)
    own_block = jnp.concatenate([x[:DH] for x in slabs] + [sum(x[DH:] for x in slabs)], axis=0)
    pairs = swap_pairs(kv_keep, kv_send)
    far = [1 << n for n in reversed(range(shift_of(parts)))]

    blocks, came = [0], [own_block]
    for d in far:
        if d == 1:
            came = came[:1] + [tie(x, pairs[1:3]) for x in came[1:]]
        came = came + [swap(x, "part", d, parts) for x in came]
        blocks = blocks + [b ^ d for b in blocks]
    ends, live = line_limits(parts, row_count, nears, rows, lines, resp_len, prompt_end)

    def part_lse(held, first, refs, before):
        return pl.pallas_call(
            functools.partial(stat_kernel, held, first, nears, heads, tokens),
            in_specs=[VMEM] * (1 + len(refs) + len(KEEP) + len(before)),
            out_shape=jax.ShapeDtypeStruct((parts * lse_rows(groups * lines), DH), jnp.float32),
            compiler_params=PARAMS,
        )(ends, *refs, *pairs, *before)

    lse = [part_lse(blocks[:-1], 0, came[:-1], [])]
    row_refs = [*came[:-1], tie(came[-1], lse)]
    lse = [part_lse(blocks[-1:], (parts - 1) * groups * lines, row_refs[-1:], lse)]
    every_lse = lse + [swap(lse[0], "part", d, parts) for d in range(1, parts)]

    all_lines = parts * groups * lines
    score_shape = jax.ShapeDtypeStruct((len(KEEP), 2 * tokens, all_lines), jnp.bfloat16)
    prob, dscore, dq = pl.pallas_call(
        functools.partial(part_kernel, blocks, nears, heads, tokens),
        in_specs=[VMEM] * (1 + len(row_refs) + len(KEEP) + 1),
        out_specs=[VMEM] * 3,
        out_shape=[score_shape] * 2 + [jax.ShapeDtypeStruct((DH, all_lines), jnp.float32)],
        compiler_params=PARAMS,
    )(ends, *row_refs, *pairs, *lse)
    dq_shape = jax.ShapeDtypeStruct((parts, row_count, lines, DH), jnp.bfloat16)
    acc = pltpu.VMEM((len(KEEP), 2 * tokens, DH), jnp.float32)
    outs = pl.pallas_call(
        functools.partial(token_kernel, blocks, nears, heads, tokens),
        in_specs=[VMEM] * (1 + len(row_refs) + 3 + parts),
        out_shape=[jax.ShapeDtypeStruct((2, 2 * tokens, DH), jnp.bfloat16)] * len(KEEP)
        + [dq_shape] * nears,
        scratch_shapes=[acc] * 2,
        compiler_params=PARAMS,
    )(live, *row_refs, prob, dscore, dq, *every_lse)
    dkv, dq = outs[: len(KEEP)], outs[len(KEEP) :]
    dq = [swap(x, "near", n, nears) if n else x for n, x in enumerate(dq)]
    from_parts = [
        swap(jnp.stack([x[blocks.index(b)] for x in dq]), "part", b, parts)
        for b in range(parts - 1, 0, -1)
    ]
    sum_shape = jax.ShapeDtypeStruct((nears, lines, DH), jnp.bfloat16)
    sums = pl.pallas_call(
        functools.partial(add_query_kernel, nears),
        in_specs=[VMEM] * (nears + len(from_parts)),
        out_shape=[sum_shape] * 2,
        compiler_params=PARAMS,
    )(*dq, *from_parts)
    pairs = swap_back(dkv, from_parts)
    sums = [swap(x, "row", j, row_count) if j else x for j, x in enumerate(sums[:row_count])]
    out_q, out_k, out_v = pl.pallas_call(
        functools.partial(write_kernel, nears, heads),
        in_specs=[VMEM] * (row_count + len(pairs)),
        out_specs=[HBM] * 3,
        out_shape=[
            jax.ShapeDtypeStruct((own_lines, DH), jnp.bfloat16),
            jax.ShapeDtypeStruct(keys.shape, jnp.bfloat16),
            jax.ShapeDtypeStruct(values.shape, jnp.bfloat16),
        ],
        scratch_shapes=[pltpu.SemaphoreType.DMA((4 * len(KEEP) + groups,))],
        compiler_params=PARAMS,
    )(*sums, *pairs)
    out_q = out_q.reshape(own_heads, rows, DH).transpose(1, 0, 2).reshape(rows, own_heads * DH)
    return out_q, out_k, out_v


def solution(mesh):
    ctx, heads = mesh.shape["ctx"], mesh.shape["head"]
    groups = KVH // heads
    parts = ctx // groups
    nears = min(2, groups)
    row_count = groups // nears
    fine = Mesh(
        mesh.devices.reshape(parts, row_count, nears, heads), ("part", "row", "near", "head")
    )
    rows = P(("part", "row", "near"), "head")
    tokens = P(("part", "row", "near", "head"), None)
    return jax.shard_map(
        functools.partial(shards, parts, row_count, nears, heads),
        mesh=fine,
        in_specs=(rows, rows, rows, rows, tokens, tokens, P(), P()),
        out_specs=(rows, tokens, tokens),
        check_vma=False,
    )
```
